32 devices in a mesh: groups: 2 (over y), req: 16 (over z, x, core), tp: 1.
Axes of the slice: x: 2, y: 2, z: 4, core: 2. Of those that a mesh axis runs over, the one named last changes fastest.
Arguments:
- tokens: bfloat16 [16384, 8192], P(('groups', 'req'), 'tp'), parts along dimension 0, may hold values from -6 to 6
- row_adapter_index: int32 [16384, 1], P(('groups', 'req')), parts along dimension 0, may hold values from 0 to 63; in each aligned block of 512 rows (0 to 511, 512 to 1023, ...) at most 10 rows name the same one
- adapter_storage_slot: int32 [64], replicated, may hold values from 0 to 63, each once
- base_value_weight: bfloat16 [8192, 1024], P('tp'), may hold values from -0.0625 to 0.0625
- adapter_down_weight: bfloat16 [64, 16, 8192], P('req', None, 'tp'), may hold values from -0.0625 to 0.0625
- adapter_up_weight: bfloat16 [64, 16, 1024], P('req', None, 'tp'), may hold values from -1.5 to 1.5
Outputs:
- values_out: bfloat16 [16384, 1024], P(('groups', 'req'), 'tp'), parts along dimension 0
The draws below stay inside these ranges and needn't reach their ends.
There are 2 independent parts, one for each index of `groups`. The reference program is written for one: setup_inputs(seed, part) draws one part's arguments, and reference() takes and returns one part's arrays. A program takes and returns all parts, laid end to end along the dimension named above; an argument that names none is the same for every part. Nothing has to cross between parts.
Inputs may be any that keep to these rules, and one draw needn't show every extreme that they name: `row_adapter_index`: within each device's aligned block of 512 rows no adapter is named by more than 10 rows. `adapter_storage_slot`: each slot appears once.
All inputs are finite; a program needn't handle non-finite values.
Results may differ from the reference program's by a relative error of at most 0.001.
Values may be sent and summed in bfloat16 or wider, within the bound.
No kernel may reach another device: no remote copies, remote signals or barrier semaphores. Data moves between devices by JAX's collectives and lax.ppermute only.
A program may use at most 128 MiB of HBM per device.

```python
import math
import jax
import jax.numpy as jnp
import numpy as np
from jax import lax

MODEL_WIDTH = 8192
VALUE_WIDTH = 1024
ADAPTER_RANK = 16
TOK_DEV = 512
ADAPTER_COUNT = 64
PROMPT_ROWS = 8192
MOST = 10


def steps_of(key, dims, cuts, least, largest):
    level = 1.0
    for axis_at, shards_of in cuts:
        draws = jax.random.uniform(jax.random.fold_in(jax.random.fold_in(key, 6), axis_at), (shards_of,), jnp.float32, least / len(cuts), largest / len(cuts))
        level = level * jnp.repeat(jnp.exp(draws), dims[axis_at] // shards_of).reshape((-1,) + (1,) * (len(dims) - 1 - axis_at))
    return level


def assign_block(stream_key, own, number, rows, amount, top, bound, slope):
    order = jax.random.permutation(stream_key, amount)
    packed, common = portions_of(amount, rows * top, bound, slope, True), portions_of(amount, rows * top, bound, slope, False)
    places = jnp.arange(amount)

    def named(tallies, offset_by):
        used = int((tallies > 0).sum())
        fixed = max(1, used // 4)
        moved = fixed + (places - fixed + offset_by * (used - fixed)) % max(1, amount - fixed)
        return jnp.zeros((amount,), jnp.int32).at[order[jnp.where(places < fixed, places, moved)]].set(jnp.asarray(tallies, jnp.int32))

    tallies = jnp.where(number % 4 == 0, named(packed, number // 4), named(common, number - number // 4 - 1))
    mixed = jax.random.permutation(jax.random.fold_in(own, 3), amount)
    giver, sink = mixed[0:amount // 2 * 2:2], mixed[1:amount // 2 * 2:2]
    slack = jnp.minimum(tallies[giver] - 1, bound - tallies[sink]) // 2
    slack = jnp.where((giver == order[0]) | (sink == order[0]) | (tallies[sink] == 0), 0, jnp.maximum(slack, 0))
    moved = jax.random.randint(jax.random.fold_in(own, 4), (amount // 2,), 0, 1 << 20) % (slack + 1)
    tallies = tallies.at[giver].add(-moved).at[sink].add(moved)
    labels = jnp.searchsorted(jnp.cumsum(tallies), jnp.arange(rows * top), side="right").astype(jnp.int32)
    grid = labels.reshape(top, rows).T
    grid = grid[jax.random.permutation(jax.random.fold_in(own, 1), rows)]
    offset_by = jax.random.randint(jax.random.fold_in(own, 2), (rows, 1), 0, top)
    return jnp.take_along_axis(grid, (jnp.arange(top)[None, :] + offset_by) % top, axis=1)


def portions_of(count, total, limit, slope, full):
    weights = [(1 << 20) // math.isqrt(standing ** slope) + 1 for standing in range(1, count + 1)]
    largest = limit if full else min(limit, max(-(-total // count), total * weights[0] // sum(weights)))
    least = 1 if total - largest >= count - 1 else 0
    holding, spare = [largest] + [least] * (count - 1), total - largest - least * (count - 1)
    while spare > 0:
        candidates = [i for i in range(1, count) if holding[i] < largest] or [i for i in range(1, count) if holding[i] < limit]
        mass, budget = sum([weights[i] for i in candidates]), spare
        for i in candidates:
            more = min(limit - holding[i], max(1, budget * weights[i] // mass), spare)
            holding[i] = holding[i] + more
            spare = spare - more
    return np.array(holding)


def scatter_about(rng, dims, scale, most, split=(), kind=jnp.bfloat16):
    values = jax.random.normal(rng, dims, jnp.float32) * scale
    if len(split) > 0:
        values = steps_of(rng, dims, split, -0.22, 0.18) * values
    return jnp.clip(values, min=-most, max=most).astype(kind)


def setup_inputs(seed: int = 0, part: int = 0) -> dict:
    key_list = jax.random.split(jax.random.key(seed), 7)
    part_splits = jax.random.split(jax.random.fold_in(key_list[6], part), 7)
    tokens = scatter_about(part_splits[0], (PROMPT_ROWS, MODEL_WIDTH), 1.0, 6.0, ((0, 16),))
    row_adapter_index_keys = jax.random.split(jax.random.fold_in(part_splits[1], 1), PROMPT_ROWS // TOK_DEV)
    row_adapter_index_turns = jax.random.permutation(jax.random.fold_in(part_splits[1], 3), PROMPT_ROWS // TOK_DEV)
    row_adapter_index = jax.vmap(lambda own, number: assign_block(jax.random.fold_in(part_splits[1], 2), own, number, TOK_DEV, ADAPTER_COUNT, 1, MOST, 2))(row_adapter_index_keys, row_adapter_index_turns).reshape((PROMPT_ROWS, 1))
    adapter_storage_slot = jax.random.permutation(key_list[2], ADAPTER_COUNT).astype(jnp.int32)
    base_value_weight = scatter_about(key_list[3], (MODEL_WIDTH, VALUE_WIDTH), MODEL_WIDTH ** -0.5, 0.0625)
    adapter_down_weight = scatter_about(key_list[4], (ADAPTER_COUNT, ADAPTER_RANK, MODEL_WIDTH), MODEL_WIDTH ** -0.5, 0.0625, ((0, 16),))
    adapter_up_weight = scatter_about(key_list[5], (ADAPTER_COUNT, ADAPTER_RANK, VALUE_WIDTH), ADAPTER_RANK ** -0.5, 1.5, ((0, 16),))
    return {"tokens": tokens, "row_adapter_index": row_adapter_index, "adapter_storage_slot": adapter_storage_slot, "base_value_weight": base_value_weight, "adapter_down_weight": adapter_down_weight, "adapter_up_weight": adapter_up_weight}


def reference(tokens, row_adapter_index, adapter_storage_slot, base_value_weight, adapter_down_weight, adapter_up_weight):
    base_output = jnp.dot(tokens, base_value_weight, preferred_element_type=jnp.float32)
    slot_of = adapter_storage_slot[row_adapter_index[:, 0]].astype(jnp.int32)
    blocks = PROMPT_ROWS // 128
    token_block_count = tokens.reshape(blocks, 128, MODEL_WIDTH)
    blocks_per_slot = slot_of.reshape(blocks, 128)

    def single_block(pair):
        block_rows, block_slot_table = pair
        down_weights = adapter_down_weight[block_slot_table].astype(jnp.float32)
        down_projected = jnp.einsum("id,ikd->ik", block_rows.astype(jnp.float32), down_weights, precision=lax.Precision.HIGHEST)
        up_weights = adapter_up_weight[block_slot_table].astype(jnp.float32)
        return jnp.einsum("ik,ikc->ic", down_projected, up_weights, precision=lax.Precision.HIGHEST)

    adapter_output = lax.map(single_block, (token_block_count, blocks_per_slot)).reshape(PROMPT_ROWS, VALUE_WIDTH)
    return (base_output + adapter_output).astype(jnp.bfloat16)
```

```python
import jax
import jax.numpy as jnp
from jax import lax
from jax.sharding import PartitionSpec as P


def per_device(
    tokens,
    row_adapter_index,
    adapter_storage_slot,
    base_value_weight,
    adapter_down_weight,
    adapter_up_weight,
):
    adapter_count = adapter_storage_slot.shape[0]
    rank = adapter_down_weight.shape[1]
    adapter_rows = row_adapter_index[:, 0]
    catalog = jnp.arange(adapter_count, dtype=jnp.int32)
    slot_of = jnp.sum(
        jnp.where(adapter_rows[:, None] == catalog[None, :], adapter_storage_slot[None, :], 0),
        axis=1,
    )
    down_all = lax.all_gather(
        adapter_down_weight.reshape(-1, adapter_down_weight.shape[2]), "req", axis=0, tiled=True
    )
    up_all = lax.all_gather(
        adapter_up_weight.reshape(-1, adapter_up_weight.shape[2]), "req", axis=0, tiled=True
    )
    base_partial = jnp.dot(tokens, base_value_weight, preferred_element_type=jnp.float32)
    base_output = lax.psum_scatter(base_partial, "tp", scatter_dimension=1, tiled=True)
    shrink = lax.dot_general(
        tokens, down_all, (((1,), (1,)), ((), ())), preferred_element_type=jnp.float32
    )
    column_slot = jnp.arange(adapter_count * rank, dtype=jnp.int32) // rank
    shrink = jnp.where(slot_of[:, None] == column_slot[None, :], shrink, 0.0)
    shrink = lax.psum(shrink, "tp")
    high = lax.reduce_precision(shrink, 8, 7)
    rest = shrink - high
    middle = lax.reduce_precision(rest, 8, 7)
    low = rest - middle
    lora = sum(
        jnp.dot(piece.astype(jnp.bfloat16), up_all, preferred_element_type=jnp.float32)
        for piece in (low, middle, high)
    )
    return (base_output + lora).astype(jnp.bfloat16)


def solution(mesh):
    placed = (
        P(("groups", "req"), "tp"),
        P(("groups", "req"), None),
        P(),
        P("tp", None),
        P("req", None, "tp"),
        P("req", None, "tp"),
    )
    return jax.shard_map(
        per_device,
        mesh=mesh,
        in_specs=placed,
        out_specs=P(("groups", "req"), "tp"),
        check_vma=False,
    )
```

```python
import functools

import jax
import jax.numpy as jnp
from jax import lax
from jax.experimental import pallas as pl
from jax.experimental.pallas import tpu as pltpu
from jax.sharding import PartitionSpec as P

RING = (0, 1, 3, 2)
PLACE_IN_RING = (0, 1, 3, 2)
DEPTH_TILE = 2048


def slots_of_rows(row_adapter_index, adapter_storage_slot):
    catalog = jnp.arange(adapter_storage_slot.shape[0], dtype=jnp.int32)
    return jnp.sum(
        jnp.where(row_adapter_index == catalog[None, :], adapter_storage_slot[None, :], 0),
        axis=1,
        keepdims=True,
    )


def gathered(
    tokens,
    row_adapter_index,
    adapter_storage_slot,
    base_value_weight,
    adapter_down_weight,
    adapter_up_weight,
):
    adapter_count = adapter_storage_slot.shape[0]
    rank = adapter_down_weight.shape[1]
    slot_of = slots_of_rows(row_adapter_index, adapter_storage_slot)
    down_all = lax.all_gather(
        adapter_down_weight.reshape(-1, adapter_down_weight.shape[2]), "req", axis=0, tiled=True
    )
    up_all = lax.all_gather(
        adapter_up_weight.reshape(-1, adapter_up_weight.shape[2]), "req", axis=0, tiled=True
    )
    base_partial = jnp.dot(tokens, base_value_weight, preferred_element_type=jnp.float32)
    base_output = lax.psum_scatter(base_partial, "tp", scatter_dimension=1, tiled=True)
    shrink = lax.dot_general(
        tokens, down_all, (((1,), (1,)), ((), ())), preferred_element_type=jnp.float32
    )
    column_slot = jnp.arange(adapter_count * rank, dtype=jnp.int32) // rank
    shrink = jnp.where(slot_of == column_slot[None, :], shrink, 0.0)
    shrink = lax.psum(shrink, "tp")
    high = lax.reduce_precision(shrink, 8, 7)
    rest = shrink - high
    middle = lax.reduce_precision(rest, 8, 7)
    low = rest - middle
    lora = sum(
        jnp.dot(piece.astype(jnp.bfloat16), up_all, preferred_element_type=jnp.float32)
        for piece in (low, middle, high)
    )
    return (base_output + lora).astype(jnp.bfloat16)


def absorb_kernel(count, steps, *refs):
    tokens_ref, row_slot_ref, column_slot_ref, total_ref = refs[:4]
    downs = refs[4 : 4 + count]
    ups = refs[4 + count : 4 + 2 * count]
    out_ref, shrink_ref = refs[4 + 2 * count :]
    step = pl.program_id(0)
    part = lax.dot_general(
        tokens_ref[...],
        jnp.concatenate([down[...] for down in downs], axis=0),
        (((1,), (1,)), ((), ())),
        preferred_element_type=jnp.float32,
    )

    @pl.when(step == 0)
    def _():
        shrink_ref[...] = part

    @pl.when(step > 0)
    def _():
        shrink_ref[...] += part

    @pl.when(step == steps - 1)
    def _():
        kept = jnp.where(row_slot_ref[...] == column_slot_ref[...], shrink_ref[...], 0.0)
        high = kept.astype(jnp.bfloat16)
        low = (kept - high.astype(jnp.float32)).astype(jnp.bfloat16)
        up = jnp.concatenate([up[...] for up in ups], axis=0)
        lora = jnp.dot(low, up, preferred_element_type=jnp.float32)
        lora += jnp.dot(high, up, preferred_element_type=jnp.float32)
        out_ref[...] = (total_ref[...] + lora).astype(out_ref.dtype)


def absorb(tokens, row_slot, total, pieces, slots, out_dtype):
    rows, depth = tokens.shape
    width = total.shape[1]
    columns = sum(piece.shape[0] for piece in pieces)
    rank = columns // len(slots)
    column_slot = jnp.repeat(jnp.stack(slots).astype(jnp.int32), rank)[None, :]
    tile = min(DEPTH_TILE, depth)
    steps = depth // tile
    whole = lambda *shape: pl.BlockSpec(shape, lambda k: (0, 0))
    return pl.pallas_call(
        functools.partial(absorb_kernel, len(pieces), steps),
        out_shape=jax.ShapeDtypeStruct(total.shape, out_dtype),
        grid=(steps,),
        in_specs=[
            pl.BlockSpec((rows, tile), lambda k: (0, k)),
            whole(rows, 1),
            whole(1, columns),
            whole(rows, width),
        ]
        + [pl.BlockSpec((piece.shape[0], tile), lambda k: (0, k)) for piece in pieces]
        + [pl.BlockSpec((piece.shape[0], width), lambda k: (0, depth // width)) for piece in pieces],
        out_specs=whole(rows, width),
        scratch_shapes=[pltpu.VMEM((rows, columns), jnp.float32)],
        cost_estimate=pl.CostEstimate(
            flops=2 * rows * columns * (depth + 2 * width),
            bytes_accessed=2 * (rows + columns) * depth + 8 * rows * width,
            transcendentals=0,
        ),
        compiler_params=pltpu.CompilerParams(vmem_limit_bytes=48 * 1024 * 1024),
    )(tokens, row_slot, column_slot, total, *pieces, *pieces)


def passed_round(
    tokens,
    row_adapter_index,
    adapter_storage_slot,
    base_value_weight,
    adapter_down_weight,
    adapter_up_weight,
):
    held, rank, depth = adapter_down_weight.shape
    axes = ("groups", "req")
    planes, owners = lax.axis_size("groups"), lax.axis_size("req")
    y, at = lax.axis_index("groups"), lax.axis_index("req")
    z, x, core = at // 4, (at // 2) % 2, at % 2
    ring = jnp.array(RING, jnp.int32)
    place = jnp.array(PLACE_IN_RING, jnp.int32)[z]

    def permuted(array, target):
        pairs = [
            (g * owners + r, target(g, r)) for g in range(planes) for r in range(owners)
        ]
        return lax.ppermute(array, axes, pairs)

    def next_z(g, r):
        to = RING[(PLACE_IN_RING[r // 4] + 1) % 4]
        return g * owners + to * 4 + r % 4

    z_ring = lambda array: permuted(array, next_z)
    x_swap = lambda array: permuted(array, lambda g, r: g * owners + (r ^ 2))
    y_swap = lambda array: permuted(array, lambda g, r: (1 - g) * owners + r)
    core_swap = lambda array: permuted(array, lambda g, r: g * owners + (r ^ 1))

    own = jnp.concatenate(
        [adapter_down_weight, adapter_up_weight], axis=2
    )
    own = jnp.where(y == 0, own, own[::-1])
    front = own[:2].reshape(2 * rank, -1)
    third = own[2]
    back = own[2:].reshape(2 * rank, -1)

    def slots(step, other_x, other_y, other_core, units):
        from_z = ring[(place - step) % 4]
        from_x = 1 - x if other_x else x
        from_y = 1 - y if other_y else y
        from_core = 1 - core if other_core else core
        first = held * ((from_z * 2 + from_x) * 2 + from_core)
        return [first + jnp.where(from_y == 0, unit, held - 1 - unit) for unit in units]

    row_slot = slots_of_rows(row_adapter_index, adapter_storage_slot)
    base = jnp.dot(tokens, base_value_weight, preferred_element_type=jnp.float32)

    z1 = z_ring(front)
    x0 = x_swap(front)
    z2 = z_ring(z1)
    x1 = x_swap(z1)
    m1 = y_swap(z1[:rank])
    z3 = z_ring(z2)
    x2 = x_swap(z2)
    m2 = y_swap(z2[:rank])
    y1 = y_swap(x1)
    third, _ = lax.optimization_barrier((third, z2))
    t1 = z_ring(third)
    x3 = x_swap(z3)
    y2 = y_swap(x2)
    m3 = y_swap(z3[:rank])
    t2 = z_ring(t1)
    y3 = y_swap(x3)
    back_late, _ = lax.optimization_barrier((back, z3))
    xr = x_swap(back_late)
    t3 = z_ring(t2)

    pair = (0, 1)
    groups = [
        [
            (front, slots, (0, False, False), pair),
            (back, slots, (0, False, False), (2, 3)),
            (x0, slots, (0, True, False), pair),
            (z1, slots, (1, False, False), pair),
        ],
        [
            (z2, slots, (2, False, False), pair),
            (x1, slots, (1, True, False), pair),
            (m1, slots, (1, False, True), (0,)),
            (m2, slots, (2, False, True), (0,)),
            (x2, slots, (2, True, False), pair),
        ],
        [
            (z3, slots, (3, False, False), pair),
            (m3, slots, (3, False, True), (0,)),
            (t1, slots, (1, False, False), (2,)),
            (x3, slots, (3, True, False), pair),
            (y1, slots, (1, True, True), pair),
        ],
        [
            (t2, slots, (2, False, False), (2,)),
            (t3, slots, (3, False, False), (2,)),
            (y2, slots, (2, True, True), pair),
            (xr, slots, (0, True, False), (2, 3)),
            (y3, slots, (3, True, True), pair),
        ],
    ]
    total = base
    for number, group in enumerate(groups):
        pieces, held_slots = [], []
        for array, lookup, (step, other_x, other_y), units in group:
            for other_core in (False, True):
                pieces.append(core_swap(array) if other_core else array)
                held_slots += lookup(step, other_x, other_y, other_core, units)
        last = number == len(groups) - 1
        total = absorb(
            tokens, row_slot, total, pieces, held_slots, jnp.bfloat16 if last else jnp.float32
        )
    return total


def solution(mesh):
    placed = (
        P(("groups", "req"), "tp"),
        P(("groups", "req"), None),
        P(),
        P("tp", None),
        P("req", None, "tp"),
        P("req", None, "tp"),
    )
    sizes = mesh.shape
    small = sizes["groups"] == 2 and sizes["req"] == 16 and sizes["tp"] == 1
    return jax.shard_map(
        passed_round if small else gathered,
        mesh=mesh,
        in_specs=placed,
        out_specs=P(("groups", "req"), "tp"),
        check_vma=False,
    )
```

```python
import functools

import jax
import jax.numpy as jnp
from jax import lax
from jax.experimental import pallas as pl
from jax.experimental.pallas import tpu as pltpu
from jax.sharding import PartitionSpec as P

RING = (0, 1, 3, 2)
PLACE_IN_RING = (0, 1, 3, 2)
DEPTH_TILE = 2048


def slots_of_rows(row_adapter_index, adapter_storage_slot):
    catalog = jnp.arange(adapter_storage_slot.shape[0], dtype=jnp.int32)
    return jnp.sum(
        jnp.where(row_adapter_index == catalog[None, :], adapter_storage_slot[None, :], 0),
        axis=1,
        keepdims=True,
    )


def gathered(
    tokens,
    row_adapter_index,
    adapter_storage_slot,
    base_value_weight,
    adapter_down_weight,
    adapter_up_weight,
):
    adapter_count = adapter_storage_slot.shape[0]
    rank = adapter_down_weight.shape[1]
    slot_of = slots_of_rows(row_adapter_index, adapter_storage_slot)
    down_all = lax.all_gather(
        adapter_down_weight.reshape(-1, adapter_down_weight.shape[2]), "req", axis=0, tiled=True
    )
    up_all = lax.all_gather(
        adapter_up_weight.reshape(-1, adapter_up_weight.shape[2]), "req", axis=0, tiled=True
    )
    base_partial = jnp.dot(tokens, base_value_weight, preferred_element_type=jnp.float32)
    base_output = lax.psum_scatter(base_partial, "tp", scatter_dimension=1, tiled=True)
    shrink = lax.dot_general(
        tokens, down_all, (((1,), (1,)), ((), ())), preferred_element_type=jnp.float32
    )
    column_slot = jnp.arange(adapter_count * rank, dtype=jnp.int32) // rank
    shrink = jnp.where(slot_of == column_slot[None, :], shrink, 0.0)
    shrink = lax.psum(shrink, "tp")
    high = lax.reduce_precision(shrink, 8, 7)
    rest = shrink - high
    middle = lax.reduce_precision(rest, 8, 7)
    low = rest - middle
    lora = sum(
        jnp.dot(piece.astype(jnp.bfloat16), up_all, preferred_element_type=jnp.float32)
        for piece in (low, middle, high)
    )
    return (base_output + lora).astype(jnp.bfloat16)


def absorb_kernel(totals, count, steps, *refs):
    tokens_ref, row_slot_ref, column_slot_ref = refs[:3]
    total_refs, refs = refs[3 : 3 + totals], refs[3 + totals :]
    downs, ups, (out_ref, shrink_ref) = refs[:count], refs[count : 2 * count], refs[2 * count :]
    step = pl.program_id(0)
    part = lax.dot_general(
        tokens_ref[...],
        jnp.concatenate([down[...] for down in downs], axis=0),
        (((1,), (1,)), ((), ())),
        preferred_element_type=jnp.float32,
    )

    @pl.when(step == 0)
    def _():
        shrink_ref[...] = part

    @pl.when(step > 0)
    def _():
        shrink_ref[...] += part

    @pl.when(step == steps - 1)
    def _():
        kept = jnp.where(row_slot_ref[...] == column_slot_ref[...], shrink_ref[...], 0.0)
        high = kept.astype(jnp.bfloat16)
        low = (kept - high.astype(jnp.float32)).astype(jnp.bfloat16)
        up = jnp.concatenate([up[...] for up in ups], axis=0)
        lora = jnp.dot(low, up, preferred_element_type=jnp.float32)
        lora += jnp.dot(high, up, preferred_element_type=jnp.float32)
        total = jnp.concatenate([total[...] for total in total_refs], axis=1)
        out_ref[...] = (total + lora).astype(out_ref.dtype)


def absorb(tokens, row_slot, totals, pieces, out_dtype):
    rows, depth = tokens.shape
    width = sum(total.shape[1] for total in totals)
    block = pieces[0][2]
    columns = block * len(pieces)
    slots = [slot for piece in pieces for slot in piece[3]]
    column_slot = jnp.repeat(jnp.stack(slots).astype(jnp.int32), columns // len(slots))[None, :]
    tile = min(DEPTH_TILE, depth)
    steps = depth // tile
    whole = lambda *shape: pl.BlockSpec(shape, lambda k: (0, 0))

    def down_spec(piece):
        return pl.BlockSpec((block, tile), lambda k: (piece[1], k))

    def up_spec(piece):
        return pl.BlockSpec((block, width), lambda k: (piece[1], depth // width))

    return pl.pallas_call(
        functools.partial(absorb_kernel, len(totals), len(pieces), steps),
        out_shape=jax.ShapeDtypeStruct((rows, width), out_dtype),
        grid=(steps,),
        in_specs=[
            pl.BlockSpec((rows, tile), lambda k: (0, k)),
            whole(rows, 1),
            whole(1, columns),
        ]
        + [whole(*total.shape) for total in totals]
        + [down_spec(piece) for piece in pieces]
        + [up_spec(piece) for piece in pieces],
        out_specs=whole(rows, width),
        scratch_shapes=[pltpu.VMEM((rows, columns), jnp.float32)],
        cost_estimate=pl.CostEstimate(
            flops=2 * rows * columns * (depth + 2 * width),
            bytes_accessed=2 * (rows + columns) * depth + 8 * rows * width,
            transcendentals=0,
        ),
        compiler_params=pltpu.CompilerParams(vmem_limit_bytes=20 * 1024 * 1024),
    )(tokens, row_slot, column_slot, *totals, *[piece[0] for piece in pieces * 2])


def passed_round(
    tokens,
    row_adapter_index,
    adapter_storage_slot,
    base_value_weight,
    adapter_down_weight,
    adapter_up_weight,
):
    held, rank, depth = adapter_down_weight.shape
    axes = ("groups", "req")
    planes, owners = lax.axis_size("groups"), lax.axis_size("req")
    y, at = lax.axis_index("groups"), lax.axis_index("req")
    z, x, core = at // 4, (at // 2) % 2, at % 2
    ring = jnp.array(RING, jnp.int32)
    ring_place = jnp.array(PLACE_IN_RING, jnp.int32)[z]

    def permuted(array, target):
        pairs = [
            (g * owners + r, target(g, r)) for g in range(planes) for r in range(owners)
        ]
        return lax.ppermute(array, axes, pairs)

    def along_z(g, r, by):
        to = RING[(PLACE_IN_RING[r // 4] + by) % 4]
        return g * owners + to * 4 + r % 4

    z_ring = lambda array: permuted(array, lambda g, r: along_z(g, r, 1))
    z_back = lambda array: permuted(array, lambda g, r: along_z(g, r, -1))
    x_swap = lambda array: permuted(array, lambda g, r: g * owners + (r ^ 2))
    y_swap = lambda array: permuted(array, lambda g, r: (1 - g) * owners + r)
    core_swap = lambda array: permuted(array, lambda g, r: g * owners + (r ^ 1))

    own = jnp.concatenate(
        [adapter_down_weight, adapter_up_weight], axis=2
    )
    own = jnp.where(y == 0, own, own[::-1])
    front = own[:2].reshape(2 * rank, -1)
    back = own[2:].reshape(2 * rank, -1)

    def slots(step, other_x, other_y, other_core, units):
        from_z = ring[(ring_place - step) % 4]
        from_x = 1 - x if other_x else x
        from_y = 1 - y if other_y else y
        from_core = 1 - core if other_core else core
        first = held * ((from_z * 2 + from_x) * 2 + from_core)
        return [first + jnp.where(from_y == 0, unit, held - 1 - unit) for unit in units]

    block = 2 * rank
    pair, rest = (0, 1), (2, 3)

    def pieces_of(arrived, batch):
        here = [(array, 0, block, slots(*place[:3], 0, place[3])) for array, place in arrived]
        batch = core_swap(batch)
        there = [
            (batch, number, block, slots(*place[:3], 1, place[3]))
            for number, (_, place) in enumerate(arrived)
        ]
        return here, there

    def joined(*arrived):
        return pieces_of(arrived, jnp.concatenate([array for array, _ in arrived], axis=0))

    row_slot = slots_of_rows(row_adapter_index, adapter_storage_slot)
    half = base_value_weight.shape[1] // 2
    update = functools.partial(absorb, tokens, row_slot)

    z1, x0 = z_ring(front), x_swap(front)
    here_0, there_0 = pieces_of(
        [(front, (0, 0, 0, pair)), (back, (0, 0, 0, rest))], own.reshape(held * rank, -1)
    )
    base_left = jnp.dot(
        tokens, base_value_weight[:, :half], preferred_element_type=jnp.float32
    )
    z1, x0, base_left = lax.optimization_barrier((z1, x0, base_left))

    z2, x1, yx0 = z_ring(z1), x_swap(z1), y_swap(x0)
    here_1, there_1 = joined((z1, (1, 0, 0, pair)), (x0, (0, 1, 0, pair)))
    tokens_late, base_left = lax.optimization_barrier((tokens, base_left))
    base_right = jnp.dot(
        tokens_late, base_value_weight[:, half:], preferred_element_type=jnp.float32
    )
    z2, x1, yx0, front, base_right = lax.optimization_barrier((z2, x1, yx0, front, base_right))

    z3, x2, yz2 = z_back(front), x_swap(z2), y_swap(z2)
    here_2, there_2 = joined((z2, (2, 0, 0, pair)), (x1, (1, 1, 0, pair)), (yx0, (0, 1, 1, pair)))
    total = update([base_left, base_right], here_0 + there_0 + here_1 + there_1, jnp.float32)
    z3, x2, yz2, x1, back, total = lax.optimization_barrier((z3, x2, yz2, x1, back, total))

    zb1, x3, yx1 = z_ring(back), x_swap(z3), y_swap(x1)
    here_3, there_3 = joined((z3, (3, 0, 0, pair)), (x2, (2, 1, 0, pair)), (yz2, (2, 0, 1, pair)))
    total = update([total], here_2 + there_2 + here_3[:1] + there_3[:1], jnp.float32)
    zb1, x3, yx1, yz2, back, total = lax.optimization_barrier((zb1, x3, yx1, yz2, back, total))

    zb3, xyz2, yx3 = z_back(back), x_swap(yz2), y_swap(x3)
    here_4, there_4 = joined((zb1, (1, 0, 0, rest)), (x3, (3, 1, 0, pair)), (yx1, (1, 1, 1, pair)))
    total = update(
        [total], here_3[1:] + there_3[1:] + here_4[:2] + there_4[:2], jnp.float32
    )
    zb3, xyz2, yx3, total = lax.optimization_barrier((zb3, xyz2, yx3, total))

    pieces = here_4[2:] + there_4[2:]
    for array, place in (
        (zb3, (3, 0, 0, rest)),
        (xyz2, (2, 1, 1, pair)),
        (yx3, (3, 1, 1, pair)),
    ):
        here, there = pieces_of([(array, place)], array)
        pieces += here + there
    return update([total], pieces, jnp.bfloat16)


def solution(mesh):
    placed = (
        P(("groups", "req"), "tp"),
        P(("groups", "req"), None),
        P(),
        P("tp", None),
        P("req", None, "tp"),
        P("req", None, "tp"),
    )
    sizes = mesh.shape
    small = sizes["groups"] == 2 and sizes["req"] == 16 and sizes["tp"] == 1
    return jax.shard_map(
        passed_round if small else gathered,
        mesh=mesh,
        in_specs=placed,
        out_specs=P(("groups", "req"), "tp"),
        check_vma=False,
    )
```

```python
import functools

import jax
import jax.numpy as jnp
import numpy as np
from jax import lax
from jax.experimental import pallas as pl
from jax.experimental.pallas import tpu as pltpu
from jax.sharding import PartitionSpec as P

RING = (0, 1, 3, 2)
PLACE_IN_RING = (0, 1, 3, 2)
DEPTH_TILE = 1024
VMEM_BYTES = 64 * 1024 * 1024 - 512 * 1024


def slots_of_rows(row_adapter_index, adapter_storage_slot):
    catalog = jnp.arange(adapter_storage_slot.shape[0], dtype=jnp.int32)
    return jnp.sum(
        jnp.where(row_adapter_index == catalog[None, :], adapter_storage_slot[None, :], 0),
        axis=1,
        keepdims=True,
    )


def gathered(
    tokens,
    row_adapter_index,
    adapter_storage_slot,
    base_value_weight,
    adapter_down_weight,
    adapter_up_weight,
):
    adapter_count = adapter_storage_slot.shape[0]
    rank = adapter_down_weight.shape[1]
    slot_of = slots_of_rows(row_adapter_index, adapter_storage_slot)
    down_all = lax.all_gather(
        adapter_down_weight.reshape(-1, adapter_down_weight.shape[2]), "req", axis=0, tiled=True
    )
    up_all = lax.all_gather(
        adapter_up_weight.reshape(-1, adapter_up_weight.shape[2]), "req", axis=0, tiled=True
    )
    base_partial = jnp.dot(tokens, base_value_weight, preferred_element_type=jnp.float32)
    base_output = lax.psum_scatter(base_partial, "tp", scatter_dimension=1, tiled=True)
    shrink = lax.dot_general(
        tokens, down_all, (((1,), (1,)), ((), ())), preferred_element_type=jnp.float32
    )
    column_slot = jnp.arange(adapter_count * rank, dtype=jnp.int32) // rank
    shrink = jnp.where(slot_of == column_slot[None, :], shrink, 0.0)
    shrink = lax.psum(shrink, "tp")
    high = lax.reduce_precision(shrink, 8, 7)
    rest = shrink - high
    middle = lax.reduce_precision(rest, 8, 7)
    low = rest - middle
    lora = sum(
        jnp.dot(piece.astype(jnp.bfloat16), up_all, preferred_element_type=jnp.float32)
        for piece in (low, middle, high)
    )
    return (base_output + lora).astype(jnp.bfloat16)


def params():
    return pltpu.CompilerParams(vmem_limit_bytes=VMEM_BYTES)


def started(copies):
    for copy in copies:
        copy.start()


def awaited(copies):
    for copy in copies:
        copy.wait()


def own_kernel(y_ref, down_ref, up_ref, front_ref, back_ref):
    depth = down_ref.shape[2]
    count = down_ref.shape[0] // 2
    for out_ref, first in ((front_ref, y_ref[0] * count), (back_ref, (1 - y_ref[0]) * count)):
        rows = out_ref.shape[0]
        out_ref[:, :depth] = down_ref[pl.ds(first, count)].reshape(rows, depth)
        out_ref[:, depth:] = up_ref[pl.ds(first, count)].reshape(rows, up_ref.shape[2])


def own_pieces(y, down, up):
    held, rank, depth = down.shape
    piece = jax.ShapeDtypeStruct((held // 2 * rank, depth + up.shape[2]), down.dtype)
    vmem = pl.BlockSpec(memory_space=pltpu.VMEM)
    return pl.pallas_call(
        own_kernel,
        out_shape=(piece, piece),
        in_specs=[pl.BlockSpec(memory_space=pltpu.SMEM), vmem, vmem],
        out_specs=(vmem, vmem),
        compiler_params=params(),
    )(y[None], down, up)


def join_kernel(count, *refs):
    sources, out_ref, sems = refs[:count], refs[count], refs[count + 1]
    rows = sources[0].shape[0]
    copies = [
        pltpu.make_async_copy(source, out_ref.at[pl.ds(n * rows, rows)], sems.at[n])
        for n, source in enumerate(sources)
    ]
    started(copies)
    awaited(copies)


def join(*arrays):
    rows, width = arrays[0].shape
    count = len(arrays)
    anywhere = pl.BlockSpec(memory_space=pl.ANY)
    return pl.pallas_call(
        functools.partial(join_kernel, count),
        out_shape=jax.ShapeDtypeStruct((count * rows, width), arrays[0].dtype),
        in_specs=[anywhere] * count,
        out_specs=anywhere,
        scratch_shapes=[pltpu.SemaphoreType.DMA((count,))],
        cost_estimate=pl.CostEstimate(
            flops=0, bytes_accessed=4 * count * rows * width, transcendentals=0
        ),
        compiler_params=params(),
    )(*arrays)


def base_kernel(steps, tokens_ref, weight_ref, *refs):
    step = pl.program_id(0)
    more = len(refs) > 1
    out_ref = refs[1] if more else refs[0]
    copies = [pltpu.make_async_copy(refs[0], refs[2], refs[3].at[0])] if more else []
    part = jnp.dot(tokens_ref[...], weight_ref[...], preferred_element_type=jnp.float32)

    @pl.when(step == 0)
    def _():
        started(copies)
        out_ref[...] = part

    @pl.when(step > 0)
    def _():
        out_ref[...] += part

    if more:

        @pl.when(step == steps - 1)
        def _():
            awaited(copies)
            out_ref[...] += refs[2][...]


def base_part(tokens, weight, begin, end, total=None):
    rows, depth = tokens.shape
    width = weight.shape[1]
    steps, first = (end - begin) // DEPTH_TILE, begin // DEPTH_TILE
    result = jax.ShapeDtypeStruct((rows, width), jnp.float32)
    more = total is not None
    return pl.pallas_call(
        functools.partial(base_kernel, steps),
        out_shape=result,
        grid=(steps,),
        in_specs=[
            pl.BlockSpec((rows, DEPTH_TILE), lambda k: (0, first + k)),
            pl.BlockSpec((DEPTH_TILE, width), lambda k: (first + k, 0)),
        ]
        + [pl.BlockSpec(memory_space=pl.ANY)] * more,
        out_specs=pl.BlockSpec((rows, width), lambda k: (0, 0)),
        scratch_shapes=[pltpu.VMEM((rows, width), jnp.float32), pltpu.SemaphoreType.DMA((1,))]
        if more
        else [],
        cost_estimate=pl.CostEstimate(
            flops=2 * rows * width * (end - begin),
            bytes_accessed=2 * (rows + width) * (end - begin) + 4 * rows * width,
            transcendentals=0,
        ),
        compiler_params=params(),
    )(tokens, weight, *([total] if more else []))


def absorb_kernel(places, steps, tokens_ref, row_slot_ref, column_slot_ref, total_ref, *refs):
    count = len(places)
    downs, sources = refs[:count], refs[count : 2 * count]
    out_ref, shrink_ref, total, up, sems = refs[2 * count :]
    step = pl.program_id(0)
    block = downs[0].shape[0]
    width = up.shape[1]
    depth = sources[0].shape[1] - width
    copies = [pltpu.make_async_copy(total_ref, total, sems.at[count])] + [
        pltpu.make_async_copy(
            source.at[pl.ds(place * block, block), pl.ds(depth, width)],
            up.at[pl.ds(n * block, block)],
            sems.at[n],
        )
        for n, (source, place) in enumerate(zip(sources, places))
    ]

    @pl.when(step == 0)
    def _():
        started(copies)

    part = lax.dot_general(
        tokens_ref[...],
        jnp.concatenate([down[...] for down in downs], axis=0),
        (((1,), (1,)), ((), ())),
        preferred_element_type=jnp.float32,
    )

    @pl.when(step == 0)
    def _():
        shrink_ref[...] = part

    @pl.when(step > 0)
    def _():
        shrink_ref[...] += part

    @pl.when(step == steps - 1)
    def _():
        kept = jnp.where(row_slot_ref[...] == column_slot_ref[...], shrink_ref[...], 0.0)
        high = kept.astype(jnp.bfloat16)
        low = (kept - high.astype(jnp.float32)).astype(jnp.bfloat16)
        awaited(copies)
        lora = jnp.dot(low, up[...], preferred_element_type=jnp.float32)
        lora += jnp.dot(high, up[...], preferred_element_type=jnp.float32)
        out_ref[...] = (total[...] + lora).astype(out_ref.dtype)


def absorb(tokens, row_slot, column_slot, total, pieces, out_dtype):
    rows, depth = tokens.shape
    width = total.shape[1]
    columns = column_slot.shape[1]
    block = columns // len(pieces)
    places = [place for _, place in pieces]
    steps = depth // DEPTH_TILE
    whole = lambda *shape: pl.BlockSpec(shape, lambda k: (0, 0))
    anywhere = pl.BlockSpec(memory_space=pl.ANY)

    def down_spec(place):
        return pl.BlockSpec((block, DEPTH_TILE), lambda k: (place, k))

    return pl.pallas_call(
        functools.partial(absorb_kernel, places, steps),
        out_shape=jax.ShapeDtypeStruct((rows, width), out_dtype),
        grid=(steps,),
        in_specs=[
            pl.BlockSpec((rows, DEPTH_TILE), lambda k: (0, k)),
            whole(rows, 1),
            whole(1, columns),
            anywhere,
        ]
        + [down_spec(place) for place in places]
        + [anywhere] * len(pieces),
        out_specs=whole(rows, width),
        scratch_shapes=[
            pltpu.VMEM((rows, columns), jnp.float32),
            pltpu.VMEM((rows, width), jnp.float32),
            pltpu.VMEM((columns, width), jnp.bfloat16),
            pltpu.SemaphoreType.DMA((len(pieces) + 1,)),
        ],
        cost_estimate=pl.CostEstimate(
            flops=2 * rows * columns * (depth + 2 * width),
            bytes_accessed=2 * (rows + columns) * depth + 8 * rows * width,
            transcendentals=0,
        ),
        compiler_params=params(),
    )(tokens, row_slot, column_slot, total, *[array for array, _ in pieces * 2])


def passed_round(
    tokens,
    row_adapter_index,
    adapter_storage_slot,
    base_value_weight,
    adapter_down_weight,
    adapter_up_weight,
):
    held, rank, depth = adapter_down_weight.shape
    axes = ("groups", "req")
    planes, owners = lax.axis_size("groups"), lax.axis_size("req")
    y, at = lax.axis_index("groups"), lax.axis_index("req")

    def permuted(array, target):
        pairs = [
            (g * owners + r, target(g, r)) for g in range(planes) for r in range(owners)
        ]
        return lax.ppermute(array, axes, pairs)

    def along_z(r, by):
        return RING[(PLACE_IN_RING[r // 4] + by) % 4] * 4 + r % 4

    z_ring = lambda array: permuted(array, lambda g, r: g * owners + along_z(r, 1))
    z_back = lambda array: permuted(array, lambda g, r: g * owners + along_z(r, -1))
    x_swap = lambda array: permuted(array, lambda g, r: g * owners + (r ^ 2))
    y_swap = lambda array: permuted(array, lambda g, r: (1 - g) * owners + r)
    core_swap = lambda array: permuted(array, lambda g, r: g * owners + (r ^ 1))

    def slots(g, r, step, other_x, other_core, back):
        owner = along_z(r, -step) ^ (2 * other_x) ^ other_core
        return [owner * held + (g ^ back) * (held // 2) + unit for unit in range(held // 2)]

    groups = (
        ((0, 0, 0), (0, 0, 1), (1, 0, 0), (0, 1, 0)),
        ((2, 0, 0), (1, 1, 0), (0, 1, 1), (3, 0, 0)),
        ((2, 1, 0), (2, 0, 1), (1, 0, 1), (3, 1, 0)),
        ((1, 1, 1), (3, 0, 1), (2, 1, 1), (3, 1, 1)),
    )
    table = np.array(
        [
            [
                [
                    np.repeat(
                        [
                            slot
                            for step, other_x, back in group
                            for other_core in (0, 1)
                            for slot in slots(g, r, step, other_x, other_core, back)
                        ],
                        rank,
                    )
                ]
                for group in groups
            ]
            for g in range(planes)
            for r in range(owners)
        ],
        np.int32,
    )
    column_slots = lax.dynamic_index_in_dim(jnp.array(table), y * owners + at, 0, keepdims=False)
    row_slot = slots_of_rows(row_adapter_index, adapter_storage_slot)
    front, back = own_pieces(y, adapter_down_weight, adapter_up_weight)

    def update(number, total, pieces, out_dtype=jnp.float32):
        return absorb(tokens, row_slot, column_slots[number], total, pieces, out_dtype)

    def interleaved(here, there):
        return [piece for both in zip(here, there) for piece in both]

    def shared(*arrays):
        batch = core_swap(join(*arrays))
        return interleaved(
            [(array, 0) for array in arrays], [(batch, n) for n in range(len(arrays))]
        )

    def shared_singly(*arrays):
        there = [core_swap(array) for array in arrays]
        return interleaved([(array, 0) for array in arrays], [(array, 0) for array in there])

    def together(*values):
        leaves, tree = jax.tree.flatten(values)
        arrays = {id(leaf): leaf for leaf in leaves if not isinstance(leaf, int)}
        arrays = dict(zip(arrays, lax.optimization_barrier(tuple(arrays.values()))))
        return tree.unflatten([arrays.get(id(leaf), leaf) for leaf in leaves])

    z1, x0 = z_ring(front), x_swap(front)
    own = shared_singly(front, back)
    total = base_part(tokens, base_value_weight, 0, depth // 2)
    z1, x0, own, front, back, total, row_slot, column_slots = together(
        z1, x0, own, front, back, total, row_slot, column_slots
    )

    z2, x1, yx0 = z_ring(z1), x_swap(z1), y_swap(x0)
    first = shared(z1, x0)
    total = base_part(tokens, base_value_weight, depth // 2, depth, total)
    z2, x1, yx0, first, front, total = together(z2, x1, yx0, first, front, total)

    z3, x2, yz2 = z_back(front), x_swap(z2), y_swap(z2)
    second = shared(z2, x1, yx0)
    total = update(0, total, own + first)
    z3, x2, yz2, x1, second, back, total = together(z3, x2, yz2, x1, second, back, total)

    zb1, x3, yx1 = z_ring(back), x_swap(z3), y_swap(x1)
    third = shared(z3, x2, yz2)
    total = update(1, total, second + third[:2])
    zb1, x3, yx1, yz2, third, back, total = together(zb1, x3, yx1, yz2, third, back, total)

    zb3, xyz2, yx3 = z_back(back), x_swap(yz2), y_swap(x3)
    fourth = shared(zb1, x3, yx1)
    total = update(2, total, third[2:] + fourth[:4])
    zb3, xyz2, yx3, fourth, total = together(zb3, xyz2, yx3, fourth, total)

    return update(3, total, fourth[4:] + shared_singly(zb3, xyz2, yx3), jnp.bfloat16)


def solution(mesh):
    placed = (
        P(("groups", "req"), "tp"),
        P(("groups", "req"), None),
        P(),
        P("tp", None),
        P("req", None, "tp"),
        P("req", None, "tp"),
    )
    sizes = mesh.shape
    small = sizes["groups"] == 2 and sizes["req"] == 16 and sizes["tp"] == 1
    return jax.shard_map(
        passed_round if small else gathered,
        mesh=mesh,
        in_specs=placed,
        out_specs=P(("groups", "req"), "tp"),
        check_vma=False,
    )
```

```python
import functools

import jax
import jax.numpy as jnp
import numpy as np
from jax import lax
from jax.experimental import pallas as pl
from jax.experimental.pallas import tpu as pltpu
from jax.sharding import PartitionSpec as P

RING = (0, 1, 3, 2)
PLACE_IN_RING = (0, 1, 3, 2)
DEPTH_TILE = 1024
LANES = 128
RANK = 16
VMEM_BYTES = 64 * 1024 * 1024 - 512 * 1024


def slots_of_rows(row_adapter_index, adapter_storage_slot):
    catalog = jnp.arange(adapter_storage_slot.shape[0], dtype=jnp.int32)
    return jnp.sum(
        jnp.where(row_adapter_index == catalog[None, :], adapter_storage_slot[None, :], 0),
        axis=1,
        keepdims=True,
    )


def gathered(
    tokens,
    row_adapter_index,
    adapter_storage_slot,
    base_value_weight,
    adapter_down_weight,
    adapter_up_weight,
):
    adapter_count = adapter_storage_slot.shape[0]
    rank = adapter_down_weight.shape[1]
    slot_of = slots_of_rows(row_adapter_index, adapter_storage_slot)
    down_all = lax.all_gather(
        adapter_down_weight.reshape(-1, adapter_down_weight.shape[2]), "req", axis=0, tiled=True
    )
    up_all = lax.all_gather(
        adapter_up_weight.reshape(-1, adapter_up_weight.shape[2]), "req", axis=0, tiled=True
    )
    base_partial = jnp.dot(tokens, base_value_weight, preferred_element_type=jnp.float32)
    base_output = lax.psum_scatter(base_partial, "tp", scatter_dimension=1, tiled=True)
    shrink = lax.dot_general(
        tokens, down_all, (((1,), (1,)), ((), ())), preferred_element_type=jnp.float32
    )
    column_slot = jnp.arange(adapter_count * rank, dtype=jnp.int32) // rank
    shrink = jnp.where(slot_of == column_slot[None, :], shrink, 0.0)
    shrink = lax.psum(shrink, "tp")
    high = lax.reduce_precision(shrink, 8, 7)
    rest = shrink - high
    middle = lax.reduce_precision(rest, 8, 7)
    low = rest - middle
    lora = sum(
        jnp.dot(piece.astype(jnp.bfloat16), up_all, preferred_element_type=jnp.float32)
        for piece in (low, middle, high)
    )
    return (base_output + lora).astype(jnp.bfloat16)


def params():
    return pltpu.CompilerParams(vmem_limit_bytes=VMEM_BYTES)


def started(copies):
    for copy in copies:
        copy.start()


def awaited(copies):
    for copy in copies:
        copy.wait()


def assemble_kernel(at_ref, here_ref, there_ref, front_ref, back_ref, sems):
    y, core = at_ref[0], at_ref[1]
    count, _, half = front_ref.shape
    count //= 2
    columns = pl.ds(pl.multiple_of(core * half, half), half)
    copies = []
    for back, out_ref in ((0, front_ref), (1, back_ref)):
        first = count * (y + back - 2 * y * back)
        for source, of_core in ((here_ref, core), (there_ref, 1 - core)):
            copies.append(
                pltpu.make_async_copy(
                    source.at[pl.ds(first, count), :, columns],
                    out_ref.at[pl.ds(of_core * count, count)],
                    sems.at[len(copies)],
                )
            )
    started(copies)
    awaited(copies)


def assemble(y, core, here, there):
    held, rank, depth = here.shape
    piece = jax.ShapeDtypeStruct((held, rank, depth // 2), here.dtype)
    anywhere = pl.BlockSpec(memory_space=pl.ANY)
    vmem = pl.BlockSpec(memory_space=pltpu.VMEM)
    return pl.pallas_call(
        assemble_kernel,
        out_shape=(piece, piece),
        in_specs=[pl.BlockSpec(memory_space=pltpu.SMEM), anywhere, anywhere],
        out_specs=(vmem, vmem),
        scratch_shapes=[pltpu.SemaphoreType.DMA((4,))],
        compiler_params=params(),
    )(jnp.stack([y, core]), here, there)


def base_kernel(steps, tokens_ref, weight_ref, *refs):
    step = pl.program_id(0)
    more = len(refs) > 1
    out_ref = refs[1] if more else refs[0]
    copies = [pltpu.make_async_copy(refs[0], refs[2], refs[3].at[0])] if more else []
    part = jnp.dot(tokens_ref[...], weight_ref[...], preferred_element_type=jnp.float32)

    @pl.when(step == 0)
    def _():
        started(copies)
        out_ref[...] = part

    @pl.when(step > 0)
    def _():
        out_ref[...] += part

    if more:

        @pl.when(step == steps - 1)
        def _():
            awaited(copies)
            out_ref[...] += refs[2][...]


def base_part(tokens, weight, begin, end, total=None):
    rows, depth = tokens.shape
    width = weight.shape[1]
    steps, first = (end - begin) // DEPTH_TILE, begin // DEPTH_TILE
    result = jax.ShapeDtypeStruct((rows, width), jnp.float32)
    more = total is not None
    return pl.pallas_call(
        functools.partial(base_kernel, steps),
        out_shape=result,
        grid=(steps,),
        in_specs=[
            pl.BlockSpec((rows, DEPTH_TILE), lambda k: (0, first + k)),
            pl.BlockSpec((DEPTH_TILE, width), lambda k: (first + k, 0)),
        ]
        + [pl.BlockSpec(memory_space=pl.ANY)] * more,
        out_specs=pl.BlockSpec((rows, width), lambda k: (0, 0)),
        scratch_shapes=[pltpu.VMEM((rows, width), jnp.float32), pltpu.SemaphoreType.DMA((1,))]
        if more
        else [],
        cost_estimate=pl.CostEstimate(
            flops=2 * rows * width * (end - begin),
            bytes_accessed=2 * (rows + width) * (end - begin) + 4 * rows * width,
            transcendentals=0,
        ),
        compiler_params=params(),
    )(tokens, weight, *([total] if more else []))


def absorb_kernel(
    count, more, at_ref, row_slot_ref, column_slot_ref, tokens_ref, other_ref, *refs
):
    sources, refs = refs[:count], refs[count:]
    before, refs = refs[: 2 * more], refs[2 * more :]
    outs, (rows_ref, down_ref, sems) = refs[:2], refs[2:]
    rows = tokens_ref.shape[0]
    block, half = sources[0].shape
    core = at_ref[1]
    downs = [
        pltpu.make_async_copy(source, down_ref.at[pl.ds(n * block, block)], sems.at[n])
        for n, source in enumerate(sources)
    ]
    started(downs)
    tiles = []
    for k in range(half // DEPTH_TILE):
        source_columns = pl.ds(
            pl.multiple_of(core * half + k * DEPTH_TILE, DEPTH_TILE), DEPTH_TILE
        )
        columns = pl.ds(k * DEPTH_TILE, DEPTH_TILE)
        pair = [
            pltpu.make_async_copy(
                source.at[:, source_columns],
                rows_ref.at[pl.ds(n * rows, rows), columns],
                sems.at[count + 2 * k + n],
            )
            for n, source in enumerate((tokens_ref, other_ref))
        ]
        started(pair)
        tiles.append((pair, columns))
    awaited(downs)
    shrink = None
    for pair, columns in tiles:
        awaited(pair)
        part = lax.dot_general(
            rows_ref[:, columns],
            down_ref[:, columns],
            (((1,), (1,)), ((), ())),
            preferred_element_type=jnp.float32,
        )
        shrink = part if shrink is None else shrink + part
    kept = jnp.where(row_slot_ref[...] == column_slot_ref[...], shrink, 0.0)
    folded = sum(kept[:, n : n + LANES] for n in range(0, kept.shape[1], LANES))
    shift = LANES // 2
    while shift >= RANK:
        folded += pltpu.roll(folded, shift, 1)
        shift //= 2
    for n, out_ref in enumerate(outs):
        own = folded[n * rows : (n + 1) * rows]
        out_ref[...] = own + before[n][...] if more else own


def absorb(at, row_slots, column_slot, tokens, other, pieces, before=None):
    rows, depth = tokens.shape
    block, half = pieces[0].shape
    columns = block * len(pieces)
    anywhere = pl.BlockSpec(memory_space=pl.ANY)
    vmem = pl.BlockSpec(memory_space=pltpu.VMEM)
    more = before is not None
    state = jax.ShapeDtypeStruct((rows, LANES), jnp.float32)
    return pl.pallas_call(
        functools.partial(absorb_kernel, len(pieces), more),
        out_shape=(state, state),
        in_specs=[pl.BlockSpec(memory_space=pltpu.SMEM), vmem, vmem]
        + [anywhere] * (2 + len(pieces))
        + [vmem] * (2 * more),
        out_specs=(vmem, vmem),
        scratch_shapes=[
            pltpu.VMEM((2 * rows, half), jnp.bfloat16),
            pltpu.VMEM((columns, half), jnp.bfloat16),
            pltpu.SemaphoreType.DMA((len(pieces) + 2 * (half // DEPTH_TILE),)),
        ],
        cost_estimate=pl.CostEstimate(
            flops=4 * rows * columns * half,
            bytes_accessed=2 * (2 * rows + columns) * half,
            transcendentals=0,
        ),
        compiler_params=params(),
    )(at, row_slots, column_slot, tokens, other, *pieces, *(before or ()))


def finish_kernel(row_slot_ref, mine_ref, theirs_ref, total_ref, up_ref, out_ref, total, up, sems):
    rows = out_ref.shape[0]
    copies = [
        pltpu.make_async_copy(up_ref, up, sems.at[0]),
        pltpu.make_async_copy(total_ref, total, sems.at[1]),
    ]
    started(copies)
    shrink = mine_ref[...] + theirs_ref[...]
    lane_slot = lax.broadcasted_iota(jnp.int32, (rows, LANES), 1) // RANK
    high, low = [], []
    for n in range(up.shape[0] // LANES):
        kept = jnp.where(row_slot_ref[...] == lane_slot + n * (LANES // RANK), shrink, 0.0)
        high.append(kept.astype(jnp.bfloat16))
        low.append((kept - high[-1].astype(jnp.float32)).astype(jnp.bfloat16))
    awaited(copies)
    lora = jnp.dot(jnp.concatenate(low, axis=1), up[...], preferred_element_type=jnp.float32)
    lora += jnp.dot(jnp.concatenate(high, axis=1), up[...], preferred_element_type=jnp.float32)
    out_ref[...] = (total[...] + lora).astype(out_ref.dtype)


def finish(row_slot, mine, theirs, total, up):
    rows, width = total.shape
    anywhere = pl.BlockSpec(memory_space=pl.ANY)
    vmem = pl.BlockSpec(memory_space=pltpu.VMEM)
    return pl.pallas_call(
        finish_kernel,
        out_shape=jax.ShapeDtypeStruct((rows, width), jnp.bfloat16),
        in_specs=[vmem, vmem, vmem, anywhere, anywhere],
        out_specs=vmem,
        scratch_shapes=[
            pltpu.VMEM((rows, width), jnp.float32),
            pltpu.VMEM(up.shape, up.dtype),
            pltpu.SemaphoreType.DMA((2,)),
        ],
        cost_estimate=pl.CostEstimate(
            flops=4 * rows * width * up.shape[0],
            bytes_accessed=6 * rows * width + 2 * up.size,
            transcendentals=0,
        ),
        compiler_params=params(),
    )(row_slot, mine, theirs, total, up)


def passed_round(
    tokens,
    row_adapter_index,
    adapter_storage_slot,
    base_value_weight,
    adapter_down_weight,
    adapter_up_weight,
):
    rows, depth = tokens.shape
    held, rank, _ = adapter_down_weight.shape
    axes = ("groups", "req")
    planes, owners = lax.axis_size("groups"), lax.axis_size("req")
    y, owner = lax.axis_index("groups"), lax.axis_index("req")
    at = jnp.stack([y, owner % 2])

    def permuted(array, target):
        pairs = [
            (g * owners + r, target(g, r)) for g in range(planes) for r in range(owners)
        ]
        return lax.ppermute(array, axes, pairs)

    def along_z(r, by):
        return RING[(PLACE_IN_RING[r // 4] + by) % 4] * 4 + r % 4

    z_ring = lambda array: permuted(array, lambda g, r: g * owners + along_z(r, 1))
    z_back = lambda array: permuted(array, lambda g, r: g * owners + along_z(r, -1))
    x_swap = lambda array: permuted(array, lambda g, r: g * owners + (r ^ 2))
    y_swap = lambda array: permuted(array, lambda g, r: (1 - g) * owners + r)
    core_swap = lambda array: permuted(array, lambda g, r: g * owners + (r ^ 1))

    def slots(g, r, step, other_x, back):
        chip = (along_z(r, -step) ^ (2 * other_x)) & ~1
        half = held // 2
        return [
            (chip + core) * held + (g ^ back) * half + unit
            for core in (0, 1)
            for unit in range(half)
        ]

    groups = (
        ((0, 0, 0), (0, 0, 1), (1, 0, 0), (0, 1, 0)),
        ((2, 0, 0), (1, 1, 0), (0, 1, 1), (3, 0, 0)),
        ((2, 1, 0), (2, 0, 1), (1, 0, 1), (3, 1, 0)),
        ((1, 1, 1), (3, 0, 1), (2, 1, 1), (3, 1, 1)),
    )
    table = np.array(
        [
            [
                [np.repeat([slot for piece in group for slot in slots(g, r, *piece)], rank)]
                for group in groups
            ]
            for g in range(planes)
            for r in range(owners)
        ],
        np.int32,
    )

    def together(*values):
        return lax.optimization_barrier(values)

    there = core_swap(adapter_down_weight)
    up = lax.all_gather(
        adapter_up_weight.reshape(held * rank, -1), "req", axis=0, tiled=True
    )
    column_slots = lax.dynamic_index_in_dim(jnp.array(table), y * owners + owner, 0, keepdims=False)
    row_slot = slots_of_rows(row_adapter_index, adapter_storage_slot)
    there, tokens_late = together(there, tokens)
    other = core_swap(tokens_late)
    other_slot = core_swap(row_slot[:, 0])
    front, back = [
        piece.reshape(held * rank, -1)
        for piece in assemble(y, owner % 2, adapter_down_weight, there)
    ]

    z1, x0 = z_ring(front), x_swap(front)
    total = base_part(tokens, base_value_weight, 0, depth // 2)
    row_slots = jnp.concatenate([row_slot, other_slot[:, None]], axis=0)
    z1, x0, front, back, total, row_slots, column_slots = together(
        z1, x0, front, back, total, row_slots, column_slots
    )

    z2, x1, yx0 = z_ring(z1), x_swap(z1), y_swap(x0)
    total = base_part(tokens, base_value_weight, depth // 2, depth, total)
    z2, x1, yx0, front, other, total = together(z2, x1, yx0, front, other, total)
    update = lambda number, pieces, before=None: absorb(
        at, row_slots, column_slots[number], tokens, other, pieces, before
    )

    z3, x2, yz2 = z_back(front), x_swap(z2), y_swap(z2)
    state = update(0, [front, back, z1, x0])
    z3, x2, yz2, x1, back, state = together(z3, x2, yz2, x1, back, state)

    zb1, x3, yx1 = z_ring(back), x_swap(z3), y_swap(x1)
    state = update(1, [z2, x1, yx0, z3], state)
    zb1, x3, yx1, yz2, back, state, up = together(zb1, x3, yx1, yz2, back, state, up)

    zb3, xyz2, yx3 = z_back(back), x_swap(yz2), y_swap(x3)
    state = update(2, [x2, yz2, zb1, x3], state)
    zb3, xyz2, yx3, state = together(zb3, xyz2, yx3, state)

    state = update(3, [yx1, zb3, xyz2, yx3], state)
    mine, others = state
    return finish(row_slot, mine, core_swap(others), total, up)


def solution(mesh):
    placed = (
        P(("groups", "req"), "tp"),
        P(("groups", "req"), None),
        P(),
        P("tp", None),
        P("req", None, "tp"),
        P("req", None, "tp"),
    )
    sizes = mesh.shape
    small = sizes["groups"] == 2 and sizes["req"] == 16 and sizes["tp"] == 1
    return jax.shard_map(
        passed_round if small else gathered,
        mesh=mesh,
        in_specs=placed,
        out_specs=P(("groups", "req"), "tp"),
        check_vma=False,
    )
```

```python
import functools

import jax
import jax.numpy as jnp
import numpy as np
from jax import lax
from jax.experimental import pallas as pl
from jax.experimental.pallas import tpu as pltpu
from jax.sharding import PartitionSpec as P

RING = (0, 1, 3, 2)
PLACE_IN_RING = (0, 1, 3, 2)
DEPTH_TILE = 1024
LANES = 128
RANK = 16

PIECES = (
    *((0, 0, 0), (1, 0, 0), (0, 0, 1), (0, 1, 1)),
    *((0, 1, 0), (2, 0, 0), (1, 1, 0), (3, 0, 0)),
    *((2, 1, 0), (3, 1, 0), (2, 0, 1), (1, 0, 1)),
    *((1, 1, 1), (3, 0, 1), (2, 1, 1), (3, 1, 1)),
)
VMEM_BYTES = 64 * 1024 * 1024 - 512 * 1024


def slots_of_rows(row_adapter_index, adapter_storage_slot):
    catalog = jnp.arange(adapter_storage_slot.shape[0], dtype=jnp.int32)
    return jnp.sum(
        jnp.where(row_adapter_index == catalog[None, :], adapter_storage_slot[None, :], 0),
        axis=1,
        keepdims=True,
    )


def gathered(
    tokens,
    row_adapter_index,
    adapter_storage_slot,
    base_value_weight,
    adapter_down_weight,
    adapter_up_weight,
):
    adapter_count = adapter_storage_slot.shape[0]
    rank = adapter_down_weight.shape[1]
    slot_of = slots_of_rows(row_adapter_index, adapter_storage_slot)
    down_all = lax.all_gather(
        adapter_down_weight.reshape(-1, adapter_down_weight.shape[2]), "req", axis=0, tiled=True
    )
    up_all = lax.all_gather(
        adapter_up_weight.reshape(-1, adapter_up_weight.shape[2]), "req", axis=0, tiled=True
    )
    base_partial = jnp.dot(tokens, base_value_weight, preferred_element_type=jnp.float32)
    base_output = lax.psum_scatter(base_partial, "tp", scatter_dimension=1, tiled=True)
    shrink = lax.dot_general(
        tokens, down_all, (((1,), (1,)), ((), ())), preferred_element_type=jnp.float32
    )
    column_slot = jnp.arange(adapter_count * rank, dtype=jnp.int32) // rank
    shrink = jnp.where(slot_of == column_slot[None, :], shrink, 0.0)
    shrink = lax.psum(shrink, "tp")
    high = lax.reduce_precision(shrink, 8, 7)
    rest = shrink - high
    middle = lax.reduce_precision(rest, 8, 7)
    low = rest - middle
    lora = sum(
        jnp.dot(piece.astype(jnp.bfloat16), up_all, preferred_element_type=jnp.float32)
        for piece in (low, middle, high)
    )
    return (base_output + lora).astype(jnp.bfloat16)


def params():
    return pltpu.CompilerParams(vmem_limit_bytes=VMEM_BYTES)


def started(copies):
    for copy in copies:
        copy.start()


def awaited(copies):
    for copy in copies:
        copy.wait()


def assemble_kernel(
    info_ref, here_ref, there_ref, up_ref, front_ref, back_ref, down_ref, sems
):
    y, core = info_ref[0], info_ref[1]
    held, rank, half = down_ref.shape
    held //= 2
    columns = pl.ds(pl.multiple_of(core * half, half), half)
    copies = [
        pltpu.make_async_copy(
            source.at[:, :, columns], down_ref.at[pl.ds(of_core * held, held)], sems.at[n]
        )
        for n, (source, of_core) in enumerate(((here_ref, core), (there_ref, 1 - core)))
    ]
    started(copies)
    awaited(copies)
    quarter = half // 2
    for out_ref, place in ((front_ref, y), (back_ref, 1 - y)):
        for n in range(0, quarter, LANES):
            columns = pl.ds(pl.multiple_of(place * quarter + n, LANES), LANES)
            block = down_ref[:, :, columns].reshape(2 * held * rank, LANES)
            out_ref[n : n + LANES] = block.T
        up = up_ref[pl.ds(place * (held // 2), held // 2)].reshape(held // 2 * rank, -1)
        rows = up.shape[0]
        for n in range(up.shape[1] // LANES):
            first = quarter + n * rows
            out_ref[first : first + rows] = up[:, n * LANES : (n + 1) * LANES]


def assemble(info, here, there, up):
    held, rank, depth = here.shape
    width = up.shape[2]
    rows = depth // 4 + held // 2 * rank * width // LANES
    piece = jax.ShapeDtypeStruct((rows, LANES), here.dtype)
    anywhere = pl.BlockSpec(memory_space=pl.ANY)
    vmem = pl.BlockSpec(memory_space=pltpu.VMEM)
    return pl.pallas_call(
        assemble_kernel,
        out_shape=(piece, piece),
        in_specs=[pl.BlockSpec(memory_space=pltpu.SMEM), anywhere, anywhere, vmem],
        out_specs=(vmem, vmem),
        scratch_shapes=[
            pltpu.VMEM((2 * held, rank, depth // 2), here.dtype),
            pltpu.SemaphoreType.DMA((2,)),
        ],
        compiler_params=params(),
    )(info, here, there, up)


def base_kernel(steps, tokens_ref, weight_ref, *refs):
    step = pl.program_id(0)
    more = len(refs) > 1
    out_ref = refs[1] if more else refs[0]
    copies = [pltpu.make_async_copy(refs[0], refs[2], refs[3].at[0])] if more else []
    part = jnp.dot(tokens_ref[...], weight_ref[...], preferred_element_type=jnp.float32)

    @pl.when(step == 0)
    def _():
        started(copies)
        out_ref[...] = part

    @pl.when(step > 0)
    def _():
        out_ref[...] += part

    if more:

        @pl.when(step == steps - 1)
        def _():
            awaited(copies)
            out_ref[...] += refs[2][...]


def base_part(tokens, weight, begin, end, total=None):
    rows, depth = tokens.shape
    width = weight.shape[1]
    steps, first = (end - begin) // DEPTH_TILE, begin // DEPTH_TILE
    result = jax.ShapeDtypeStruct((rows, width), jnp.float32)
    more = total is not None
    return pl.pallas_call(
        functools.partial(base_kernel, steps),
        out_shape=result,
        grid=(steps,),
        in_specs=[
            pl.BlockSpec((rows, DEPTH_TILE), lambda k: (0, first + k)),
            pl.BlockSpec((DEPTH_TILE, width), lambda k: (first + k, 0)),
        ]
        + [pl.BlockSpec(memory_space=pl.ANY)] * more,
        out_specs=pl.BlockSpec((rows, width), lambda k: (0, 0)),
        scratch_shapes=[pltpu.VMEM((rows, width), jnp.float32), pltpu.SemaphoreType.DMA((1,))]
        if more
        else [],
        cost_estimate=pl.CostEstimate(
            flops=2 * rows * width * (end - begin),
            bytes_accessed=2 * (rows + width) * (end - begin) + 4 * rows * width,
            transcendentals=0,
        ),
        compiler_params=params(),
    )(tokens, weight, *([total] if more else []))


def absorb_kernel(
    backs, more, info_ref, row_slot_ref, column_slot_ref, tokens_ref, other_ref, *refs
):
    count = 2 * len(backs)
    sources, refs = refs[:count], refs[count:]
    before, refs = refs[: 2 * more], refs[2 * more :]
    outs, up_ref, (rows_ref, down_ref, sems) = refs[:2], refs[2], refs[3:]
    rows = tokens_ref.shape[0]
    quarter = rows_ref.shape[2]
    y, core = info_ref[0], info_ref[1]
    copies = 0
    downs, tiles = [], {}

    def begin(source, target):
        nonlocal copies
        copy = pltpu.make_async_copy(source, target, sems.at[copies])
        copies += 1
        copy.start()
        return copy

    for n, back in enumerate(backs):
        downs.append(
            [
                begin(sources[2 * n + i], down_ref.at[n, :, pl.ds(i * LANES, LANES)])
                for i in range(2)
            ]
        )
        if back in tiles:
            continue
        place = len(tiles)
        tiles[back] = []
        first = core * 2 * quarter + (1 - y if back else y) * quarter
        for k in range(0, quarter, DEPTH_TILE):
            columns = pl.ds(pl.multiple_of(first + k, DEPTH_TILE), DEPTH_TILE)
            pair = [
                begin(
                    source.at[:, columns],
                    rows_ref.at[place, pl.ds(i * rows, rows), pl.ds(k, DEPTH_TILE)],
                )
                for i, source in enumerate((tokens_ref, other_ref))
            ]
            tiles[back].append([place, k, pair])
    state = None
    for n, back in enumerate(backs):
        awaited(downs[n])
        shrink = None
        for tile in tiles[back]:
            place, k, pair = tile
            awaited(pair)
            tile[2] = []
            part = jnp.dot(
                rows_ref[place, :, k : k + DEPTH_TILE],
                down_ref[n, k : k + DEPTH_TILE, :],
                preferred_element_type=jnp.float32,
            )
            shrink = part if shrink is None else shrink + part
        for i in range(2):
            lanes = slice(i * LANES, (i + 1) * LANES)
            wanted = column_slot_ref[:, 2 * n * LANES + i * LANES : 2 * n * LANES + (i + 1) * LANES]
            kept = jnp.where(row_slot_ref[...] == wanted, shrink[:, lanes], 0.0)
            state = kept if state is None else state + kept
            height = up_ref.shape[0] // count
            for j in range(up_ref.shape[1] // LANES):
                first = quarter + j * height
                up_ref[
                    (2 * n + i) * height : (2 * n + i + 1) * height,
                    j * LANES : (j + 1) * LANES,
                ] = down_ref[n, first : first + height, lanes]
    for i, out_ref in enumerate(outs):
        own = state[i * rows : (i + 1) * rows]
        out_ref[...] = own + before[i][...] if more else own


def absorb(info, row_slots, column_slot, tokens, other, width, pairs, before=None):
    rows, depth = tokens.shape
    pieces = [piece for pair, _ in pairs for piece in pair]
    backs = [back for _, back in pairs]
    quarter = depth // 4
    height = pieces[0].shape[0]
    anywhere = pl.BlockSpec(memory_space=pl.ANY)
    vmem = pl.BlockSpec(memory_space=pltpu.VMEM)
    more = before is not None
    state = jax.ShapeDtypeStruct((rows, LANES), jnp.float32)
    up_rows = len(pieces) * (height - quarter) * LANES // width
    quarters = len(set(backs))
    copies = len(pieces) + 2 * quarters * (quarter // DEPTH_TILE)
    return pl.pallas_call(
        functools.partial(absorb_kernel, backs, more),
        out_shape=(state, state, jax.ShapeDtypeStruct((up_rows, width), tokens.dtype)),
        in_specs=[pl.BlockSpec(memory_space=pltpu.SMEM), vmem, vmem]
        + [anywhere] * (2 + len(pieces))
        + [vmem] * (2 * more),
        out_specs=(vmem, vmem, vmem),
        scratch_shapes=[
            pltpu.VMEM((quarters, 2 * rows, quarter), tokens.dtype),
            pltpu.VMEM((len(pairs), height, 2 * LANES), tokens.dtype),
            pltpu.SemaphoreType.DMA((copies,)),
        ],
        cost_estimate=pl.CostEstimate(
            flops=4 * rows * len(pieces) * LANES * quarter,
            bytes_accessed=4 * rows * quarters * quarter + 2 * len(pieces) * LANES * height,
            transcendentals=0,
        ),
        compiler_params=params(),
    )(info, row_slots, column_slot, tokens, other, *pieces, *(before or ()))


def finish_kernel(
    count, info_ref, row_slot_ref, mine_ref, theirs_ref, total_ref, *refs
):
    sources, (out_ref, total, up, sems) = refs[:count], refs[count:]
    rows = out_ref.shape[0]
    height = up.shape[0] // (len(PIECES) * 2)
    per = sources[0].shape[0] // height
    copies = [pltpu.make_async_copy(total_ref, total, sems.at[0])]
    for n in range(count * per):
        first = pl.multiple_of(info_ref[2 + n], height)
        copies.append(
            pltpu.make_async_copy(
                sources[n // per].at[pl.ds(n % per * height, height)],
                up.at[pl.ds(first, height)],
                sems.at[1 + n],
            )
        )
    started(copies)
    shrink = mine_ref[...] + theirs_ref[...]
    lane_slot = lax.broadcasted_iota(jnp.int32, (rows, LANES), 1) // RANK
    high, low = [], []
    for n in range(up.shape[0] // LANES):
        kept = jnp.where(row_slot_ref[...] == lane_slot + n * (LANES // RANK), shrink, 0.0)
        high.append(kept.astype(jnp.bfloat16))
        low.append((kept - high[-1].astype(jnp.float32)).astype(jnp.bfloat16))
    awaited(copies)
    lora = jnp.dot(jnp.concatenate(low, axis=1), up[...], preferred_element_type=jnp.float32)
    lora += jnp.dot(jnp.concatenate(high, axis=1), up[...], preferred_element_type=jnp.float32)
    out_ref[...] = (total[...] + lora).astype(out_ref.dtype)


def finish(info, row_slot, mine, theirs, total, ups):
    rows, width = total.shape
    anywhere = pl.BlockSpec(memory_space=pl.ANY)
    vmem = pl.BlockSpec(memory_space=pltpu.VMEM)
    up_rows = sum(up.shape[0] for up in ups)
    return pl.pallas_call(
        functools.partial(finish_kernel, len(ups)),
        out_shape=jax.ShapeDtypeStruct((rows, width), jnp.bfloat16),
        in_specs=[pl.BlockSpec(memory_space=pltpu.SMEM), vmem, vmem, vmem]
        + [anywhere] * (1 + len(ups)),
        out_specs=vmem,
        scratch_shapes=[
            pltpu.VMEM((rows, width), jnp.float32),
            pltpu.VMEM((up_rows, width), ups[0].dtype),
            pltpu.SemaphoreType.DMA((1 + 2 * len(PIECES),)),
        ],
        cost_estimate=pl.CostEstimate(
            flops=4 * rows * width * up_rows,
            bytes_accessed=6 * rows * width + 2 * up_rows * width,
            transcendentals=0,
        ),
        compiler_params=params(),
    )(info, row_slot, mine, theirs, total, *ups)


def passed_round(
    tokens,
    row_adapter_index,
    adapter_storage_slot,
    base_value_weight,
    adapter_down_weight,
    adapter_up_weight,
):
    rows, depth = tokens.shape
    held, rank, _ = adapter_down_weight.shape
    width = adapter_up_weight.shape[2]
    axes = ("groups", "req")
    planes, owners = lax.axis_size("groups"), lax.axis_size("req")
    device = lax.axis_index("groups") * owners + lax.axis_index("req")

    def permuted(array, target):
        pairs = [
            (g * owners + r, target(g, r)) for g in range(planes) for r in range(owners)
        ]
        return lax.ppermute(array, axes, pairs)

    def along_z(r, by):
        return RING[(PLACE_IN_RING[r // 4] + by) % 4] * 4 + r % 4

    z_ring = lambda array: permuted(array, lambda g, r: g * owners + along_z(r, 1))
    z_back = lambda array: permuted(array, lambda g, r: g * owners + along_z(r, -1))
    x_swap = lambda array: permuted(array, lambda g, r: g * owners + (r ^ 2))
    y_swap = lambda array: permuted(array, lambda g, r: (1 - g) * owners + r)
    core_swap = lambda array: permuted(array, lambda g, r: g * owners + (r ^ 1))

    def chip(r, piece):
        return (along_z(r, -piece[0]) ^ (2 * piece[1])) // 2

    per_chip = LANES // rank
    column_table, info_table = [], []
    for g in range(planes):
        for r in range(owners):
            column_table.append(
                [
                    [
                        np.repeat(
                            [chip(r, p) * per_chip + n for p in PIECES[k : k + 4] for n in range(per_chip)],
                            rank,
                        )
                    ]
                    for k in range(0, len(PIECES), 4)
                ]
            )
            info = [g, r % 2]
            for k in range(0, len(PIECES), 4):
                for core in (r % 2, 1 - r % 2):
                    for p in PIECES[k : k + 4]:
                        info.append(
                            chip(r, p) * LANES
                            + core * held * rank
                            + (g ^ p[2]) * (held // 2 * rank)
                        )
            info_table.append(info)
    here_of = lambda table: lax.dynamic_index_in_dim(
        jnp.array(np.array(table, np.int32)), device, 0, keepdims=False
    )
    info, column_slots = here_of(info_table), here_of(column_table)

    def together(*values):
        return lax.optimization_barrier(values)

    there = core_swap(adapter_down_weight)
    row_slot = slots_of_rows(row_adapter_index, adapter_storage_slot)
    there, tokens_late = together(there, tokens)
    other = core_swap(tokens_late)
    other_slot = core_swap(row_slot[:, 0])
    front, back = assemble(info, adapter_down_weight, there, adapter_up_weight)

    z1, x0 = z_ring(front), x_swap(front)
    total = base_part(tokens, base_value_weight, 0, depth // 2)
    row_slots = jnp.concatenate([row_slot, other_slot[:, None]], axis=0)
    z1, x0, front, back, total, row_slots, column_slots = together(
        z1, x0, front, back, total, row_slots, column_slots
    )

    z2, x1, yx0 = z_ring(z1), x_swap(z1), y_swap(x0)
    total = base_part(tokens, base_value_weight, depth // 2, depth, total)
    z2, x1, yx0, front, other, total = together(z2, x1, yx0, front, other, total)
    ups = []

    def update(number, pairs, before=None):
        mine, others, up = absorb(
            info, row_slots, column_slots[number], tokens, other, width, pairs, before
        )
        ups.extend([up, core_swap(up)])
        return mine, others

    z3, x2, yz2 = z_back(front), x_swap(z2), y_swap(z2)
    state = update(0, [((front, z1), 0), ((back, yx0), 1)])
    z3, x2, yz2, x1, back, state = together(z3, x2, yz2, x1, back, state)

    zb1, x3, yx1 = z_ring(back), x_swap(z3), y_swap(x1)
    state = update(1, [((x0, z2), 0), ((x1, z3), 0)], state)
    zb1, x3, yx1, yz2, back, state = together(zb1, x3, yx1, yz2, back, state)

    zb3, xyz2, yx3 = z_back(back), x_swap(yz2), y_swap(x3)
    state = update(2, [((x2, x3), 0), ((yz2, zb1), 1)], state)
    zb3, xyz2, yx3, state = together(zb3, xyz2, yx3, state)

    mine, others = update(3, [((yx1, zb3), 1), ((xyz2, yx3), 1)], state)
    return finish(info, row_slot, mine, core_swap(others), total, ups)


def solution(mesh):
    placed = (
        P(("groups", "req"), "tp"),
        P(("groups", "req"), None),
        P(),
        P("tp", None),
        P("req", None, "tp"),
        P("req", None, "tp"),
    )
    sizes = mesh.shape
    small = sizes["groups"] == 2 and sizes["req"] == 16 and sizes["tp"] == 1
    return jax.shard_map(
        passed_round if small else gathered,
        mesh=mesh,
        in_specs=placed,
        out_specs=P(("groups", "req"), "tp"),
        check_vma=False,
    )
```

```python
import functools

import jax
import jax.numpy as jnp
import numpy as np
from jax import lax
from jax.experimental import pallas as pl
from jax.experimental.pallas import tpu as pltpu
from jax.sharding import PartitionSpec as P

RING = (0, 1, 3, 2)
PLACE_IN_RING = (0, 1, 3, 2)
DEPTH_TILE = 1024
LANES = 128
RANK = 16

PIECES = (
    *((0, 0, 0), (1, 0, 0), (0, 1, 0), (2, 0, 0)),
    *((1, 1, 0), (3, 0, 0), (2, 1, 0), (3, 1, 0)),
    *((0, 0, 1), (0, 1, 1), (2, 0, 1), (1, 0, 1)),
    *((1, 1, 1), (3, 0, 1), (2, 1, 1), (3, 1, 1)),
)
TOGETHER = 4
VMEM_BYTES = 64 * 1024 * 1024 - 512 * 1024


def slots_of_rows(row_adapter_index, adapter_storage_slot):
    catalog = jnp.arange(adapter_storage_slot.shape[0], dtype=jnp.int32)
    return jnp.sum(
        jnp.where(row_adapter_index == catalog[None, :], adapter_storage_slot[None, :], 0),
        axis=1,
        keepdims=True,
    )


def gathered(
    tokens,
    row_adapter_index,
    adapter_storage_slot,
    base_value_weight,
    adapter_down_weight,
    adapter_up_weight,
):
    adapter_count = adapter_storage_slot.shape[0]
    rank = adapter_down_weight.shape[1]
    slot_of = slots_of_rows(row_adapter_index, adapter_storage_slot)
    down_all = lax.all_gather(
        adapter_down_weight.reshape(-1, adapter_down_weight.shape[2]), "req", axis=0, tiled=True
    )
    up_all = lax.all_gather(
        adapter_up_weight.reshape(-1, adapter_up_weight.shape[2]), "req", axis=0, tiled=True
    )
    base_partial = jnp.dot(tokens, base_value_weight, preferred_element_type=jnp.float32)
    base_output = lax.psum_scatter(base_partial, "tp", scatter_dimension=1, tiled=True)
    shrink = lax.dot_general(
        tokens, down_all, (((1,), (1,)), ((), ())), preferred_element_type=jnp.float32
    )
    column_slot = jnp.arange(adapter_count * rank, dtype=jnp.int32) // rank
    shrink = jnp.where(slot_of == column_slot[None, :], shrink, 0.0)
    shrink = lax.psum(shrink, "tp")
    high = lax.reduce_precision(shrink, 8, 7)
    rest = shrink - high
    middle = lax.reduce_precision(rest, 8, 7)
    low = rest - middle
    lora = sum(
        jnp.dot(piece.astype(jnp.bfloat16), up_all, preferred_element_type=jnp.float32)
        for piece in (low, middle, high)
    )
    return (base_output + lora).astype(jnp.bfloat16)


def params():
    return pltpu.CompilerParams(vmem_limit_bytes=VMEM_BYTES)


def started(copies):
    for copy in copies:
        copy.start()


def awaited(copies):
    for copy in copies:
        copy.wait()


def assemble_kernel(back, info_ref, here_ref, there_ref, up_ref, out_ref, down_ref, sems):
    y, core = info_ref[0], info_ref[1]
    place = 1 - y if back else y
    held, rank, quarter = down_ref.shape
    held //= 2
    columns = pl.ds(pl.multiple_of((2 * core + place) * quarter, quarter), quarter)
    copies = [
        pltpu.make_async_copy(
            source.at[:, :, columns], down_ref.at[pl.ds(of_core * held, held)], sems.at[n]
        )
        for n, (source, of_core) in enumerate(((here_ref, core), (there_ref, 1 - core)))
    ]
    started(copies)
    up = up_ref[pl.ds(place * (held // 2), held // 2)].reshape(held // 2 * rank, -1)
    rows = up.shape[0]
    for n in range(up.shape[1] // LANES):
        first = quarter + n * rows
        out_ref[first : first + rows] = up[:, n * LANES : (n + 1) * LANES]
    awaited(copies)
    for n in range(0, quarter, LANES):
        block = down_ref[:, :, n : n + LANES].reshape(2 * held * rank, LANES)
        out_ref[n : n + LANES] = block.T


def assemble(back, info, here, there, up):
    held, rank, depth = here.shape
    width = up.shape[2]
    rows = depth // 4 + held // 2 * rank * width // LANES
    anywhere = pl.BlockSpec(memory_space=pl.ANY)
    vmem = pl.BlockSpec(memory_space=pltpu.VMEM)
    return pl.pallas_call(
        functools.partial(assemble_kernel, back),
        out_shape=jax.ShapeDtypeStruct((rows, LANES), here.dtype),
        in_specs=[pl.BlockSpec(memory_space=pltpu.SMEM), anywhere, anywhere, vmem],
        out_specs=vmem,
        scratch_shapes=[
            pltpu.VMEM((2 * held, rank, depth // 4), here.dtype),
            pltpu.SemaphoreType.DMA((2,)),
        ],
        compiler_params=params(),
    )(info, here, there, up)


def base_kernel(steps, tokens_ref, weight_ref, *refs):
    step = pl.program_id(0)
    more = len(refs) > 1
    out_ref = refs[1] if more else refs[0]
    copies = [pltpu.make_async_copy(refs[0], refs[2], refs[3].at[0])] if more else []
    part = jnp.dot(tokens_ref[...], weight_ref[...], preferred_element_type=jnp.float32)

    @pl.when(step == 0)
    def _():
        started(copies)
        out_ref[...] = part

    @pl.when(step > 0)
    def _():
        out_ref[...] += part

    if more:

        @pl.when(step == steps - 1)
        def _():
            awaited(copies)
            out_ref[...] += refs[2][...]


def base_part(tokens, weight, begin, end, total=None):
    rows, depth = tokens.shape
    width = weight.shape[1]
    steps, first = (end - begin) // DEPTH_TILE, begin // DEPTH_TILE
    result = jax.ShapeDtypeStruct((rows, width), jnp.float32)
    more = total is not None
    return pl.pallas_call(
        functools.partial(base_kernel, steps),
        out_shape=result,
        grid=(steps,),
        in_specs=[
            pl.BlockSpec((rows, DEPTH_TILE), lambda k: (0, first + k)),
            pl.BlockSpec((DEPTH_TILE, width), lambda k: (first + k, 0)),
        ]
        + [pl.BlockSpec(memory_space=pl.ANY)] * more,
        out_specs=pl.BlockSpec((rows, width), lambda k: (0, 0)),
        scratch_shapes=[pltpu.VMEM((rows, width), jnp.float32), pltpu.SemaphoreType.DMA((1,))]
        if more
        else [],
        cost_estimate=pl.CostEstimate(
            flops=2 * rows * width * (end - begin),
            bytes_accessed=2 * (rows + width) * (end - begin) + 4 * rows * width,
            transcendentals=0,
        ),
        compiler_params=params(),
    )(tokens, weight, *([total] if more else []))


def absorb_kernel(
    backs, more, info_ref, row_slot_ref, column_slot_ref, tokens_ref, other_ref, *refs
):
    count = TOGETHER * len(backs)
    sources, refs = refs[:count], refs[count:]
    before, refs = refs[: 2 * more], refs[2 * more :]
    outs, up_ref, (rows_ref, down_ref, sems) = refs[:2], refs[2], refs[3:]
    rows = tokens_ref.shape[0]
    quarter = rows_ref.shape[2]
    y, core = info_ref[0], info_ref[1]
    copies = 0
    downs, tiles = [], {}

    def begin(source, target):
        nonlocal copies
        copy = pltpu.make_async_copy(source, target, sems.at[copies])
        copies += 1
        copy.start()
        return copy

    for n, back in enumerate(backs):
        downs.append(
            [
                begin(sources[TOGETHER * n + i], down_ref.at[n, :, pl.ds(i * LANES, LANES)])
                for i in range(TOGETHER)
            ]
        )
        if back in tiles:
            continue
        place = len(tiles)
        tiles[back] = []
        first = core * 2 * quarter + (1 - y if back else y) * quarter
        for k in range(0, quarter, DEPTH_TILE):
            columns = pl.ds(pl.multiple_of(first + k, DEPTH_TILE), DEPTH_TILE)
            pair = [
                begin(
                    source.at[:, columns],
                    rows_ref.at[place, pl.ds(i * rows, rows), pl.ds(k, DEPTH_TILE)],
                )
                for i, source in enumerate((tokens_ref, other_ref))
            ]
            tiles[back].append([place, k, pair])
    state = None
    for n, back in enumerate(backs):
        awaited(downs[n])
        shrink = None
        for tile in tiles[back]:
            place, k, pair = tile
            awaited(pair)
            tile[2] = []
            part = jnp.dot(
                rows_ref[place, :, k : k + DEPTH_TILE],
                down_ref[n, k : k + DEPTH_TILE, :],
                preferred_element_type=jnp.float32,
            )
            shrink = part if shrink is None else shrink + part
        height = up_ref.shape[0] // count
        for i in range(TOGETHER):
            lanes, which = slice(i * LANES, (i + 1) * LANES), TOGETHER * n + i
            wanted = column_slot_ref[:, which * LANES : (which + 1) * LANES]
            kept = jnp.where(row_slot_ref[...] == wanted, shrink[:, lanes], 0.0)
            state = kept if state is None else state + kept
            for j in range(up_ref.shape[1] // LANES):
                first = quarter + j * height
                up_ref[
                    which * height : (which + 1) * height, j * LANES : (j + 1) * LANES
                ] = down_ref[n, first : first + height, lanes]
    for i, out_ref in enumerate(outs):
        own = state[i * rows : (i + 1) * rows]
        out_ref[...] = own + before[i][...] if more else own


def absorb(info, row_slots, column_slot, tokens, other, width, fours, before=None):
    rows, depth = tokens.shape
    pieces = [piece for four, _ in fours for piece in four]
    backs = [back for _, back in fours]
    quarter = depth // 4
    height = pieces[0].shape[0]
    anywhere = pl.BlockSpec(memory_space=pl.ANY)
    vmem = pl.BlockSpec(memory_space=pltpu.VMEM)
    more = before is not None
    state = jax.ShapeDtypeStruct((rows, LANES), jnp.float32)
    up_rows = len(pieces) * (height - quarter) * LANES // width
    quarters = len(set(backs))
    copies = len(pieces) + 2 * quarters * (quarter // DEPTH_TILE)
    return pl.pallas_call(
        functools.partial(absorb_kernel, backs, more),
        out_shape=(state, state, jax.ShapeDtypeStruct((up_rows, width), tokens.dtype)),
        in_specs=[pl.BlockSpec(memory_space=pltpu.SMEM), vmem, vmem]
        + [anywhere] * (2 + len(pieces))
        + [vmem] * (2 * more),
        out_specs=(vmem, vmem, vmem),
        scratch_shapes=[
            pltpu.VMEM((quarters, 2 * rows, quarter), tokens.dtype),
            pltpu.VMEM((len(fours), height, TOGETHER * LANES), tokens.dtype),
            pltpu.SemaphoreType.DMA((copies,)),
        ],
        cost_estimate=pl.CostEstimate(
            flops=4 * rows * len(pieces) * LANES * quarter,
            bytes_accessed=4 * rows * quarters * quarter + 2 * len(pieces) * LANES * height,
            transcendentals=0,
        ),
        compiler_params=params(),
    )(info, row_slots, column_slot, tokens, other, *pieces, *(before or ()))


def finish_kernel(
    count, info_ref, row_slot_ref, mine_ref, theirs_ref, total_ref, *refs
):
    sources, (out_ref, total, up, sems) = refs[:count], refs[count:]
    rows = out_ref.shape[0]
    height = up.shape[0] // (len(PIECES) * 2)
    copies = [pltpu.make_async_copy(total_ref, total, sems.at[0])]
    for source in sources:
        for n in range(0, source.shape[0], height):
            first = pl.multiple_of(info_ref[1 + len(copies)], height)
            copies.append(
                pltpu.make_async_copy(
                    source.at[pl.ds(n, height)], up.at[pl.ds(first, height)], sems.at[len(copies)]
                )
            )
    started(copies)
    shrink = mine_ref[...] + theirs_ref[...]
    lane_slot = lax.broadcasted_iota(jnp.int32, (rows, LANES), 1) // RANK
    high, low = [], []
    for n in range(up.shape[0] // LANES):
        kept = jnp.where(row_slot_ref[...] == lane_slot + n * (LANES // RANK), shrink, 0.0)
        high.append(kept.astype(jnp.bfloat16))
        low.append((kept - high[-1].astype(jnp.float32)).astype(jnp.bfloat16))
    awaited(copies)
    both = jnp.concatenate([jnp.concatenate(part, axis=1) for part in (low, high)], axis=0)
    lora = jnp.dot(both, up[...], preferred_element_type=jnp.float32)
    out_ref[...] = (total[...] + (lora[:rows] + lora[rows:])).astype(out_ref.dtype)


def finish(info, row_slot, mine, theirs, total, ups):
    rows, width = total.shape
    anywhere = pl.BlockSpec(memory_space=pl.ANY)
    vmem = pl.BlockSpec(memory_space=pltpu.VMEM)
    up_rows = sum(up.shape[0] for up in ups)
    return pl.pallas_call(
        functools.partial(finish_kernel, len(ups)),
        out_shape=jax.ShapeDtypeStruct((rows, width), jnp.bfloat16),
        in_specs=[pl.BlockSpec(memory_space=pltpu.SMEM), vmem, vmem, vmem]
        + [anywhere] * (1 + len(ups)),
        out_specs=vmem,
        scratch_shapes=[
            pltpu.VMEM((rows, width), jnp.float32),
            pltpu.VMEM((up_rows, width), ups[0].dtype),
            pltpu.SemaphoreType.DMA((1 + 2 * len(PIECES),)),
        ],
        cost_estimate=pl.CostEstimate(
            flops=4 * rows * width * up_rows,
            bytes_accessed=6 * rows * width + 2 * up_rows * width,
            transcendentals=0,
        ),
        compiler_params=params(),
    )(info, row_slot, mine, theirs, total, *ups)


def passed_round(
    tokens,
    row_adapter_index,
    adapter_storage_slot,
    base_value_weight,
    adapter_down_weight,
    adapter_up_weight,
):
    rows, depth = tokens.shape
    held, rank, _ = adapter_down_weight.shape
    width = adapter_up_weight.shape[2]
    axes = ("groups", "req")
    planes, owners = lax.axis_size("groups"), lax.axis_size("req")
    device = lax.axis_index("groups") * owners + lax.axis_index("req")

    def permuted(array, target):
        pairs = [
            (g * owners + r, target(g, r)) for g in range(planes) for r in range(owners)
        ]
        return lax.ppermute(array, axes, pairs)

    def along_z(r, by):
        return RING[(PLACE_IN_RING[r // 4] + by) % 4] * 4 + r % 4

    z_ring = lambda array: permuted(array, lambda g, r: g * owners + along_z(r, 1))
    z_back = lambda array: permuted(array, lambda g, r: g * owners + along_z(r, -1))
    x_swap = lambda array: permuted(array, lambda g, r: g * owners + (r ^ 2))
    y_swap = lambda array: permuted(array, lambda g, r: (1 - g) * owners + r)
    core_swap = lambda array: permuted(array, lambda g, r: g * owners + (r ^ 1))

    def chip(r, piece):
        return (along_z(r, -piece[0]) ^ (2 * piece[1])) // 2

    per_chip = LANES // rank
    kernels = (PIECES[:4], PIECES[4:12], PIECES[12:])
    column_table, info_table = [], []
    for g in range(planes):
        for r in range(owners):
            column_table.append(
                [chip(r, p) * per_chip + n // rank for p in PIECES for n in range(LANES)]
            )
            info_table.append(
                [g, r % 2]
                + [
                    chip(r, p) * LANES + core * held * rank + (g ^ p[2]) * (held // 2 * rank)
                    for pieces in kernels
                    for core in (r % 2, 1 - r % 2)
                    for p in pieces
                ]
            )
    here_of = lambda table: lax.dynamic_index_in_dim(
        jnp.array(np.array(table, np.int32)), device, 0, keepdims=False
    )
    info, column_slots = here_of(info_table), here_of(column_table)[None, :]

    def together(*values):
        return lax.optimization_barrier(values)

    there = core_swap(adapter_down_weight)
    row_slot = slots_of_rows(row_adapter_index, adapter_storage_slot)
    there, tokens_late, info, row_slot, column_slots = together(
        there, tokens, info, row_slot, column_slots
    )
    piece = lambda back: assemble(back, info, adapter_down_weight, there, adapter_up_weight)
    front = piece(0)

    z1, x0 = z_ring(front), x_swap(front)
    other = core_swap(tokens_late)
    other_slot = core_swap(row_slot[:, 0])
    back = piece(1)
    third = 3 * DEPTH_TILE
    total = base_part(tokens, base_value_weight, 0, third)
    row_slots = jnp.concatenate([row_slot, other_slot[:, None]], axis=0)
    z1, x0, front, back, total, row_slots = together(z1, x0, front, back, total, row_slots)

    z2, x1, yx0 = z_ring(z1), x_swap(z1), y_swap(x0)
    total = base_part(tokens, base_value_weight, third, 2 * third, total)
    z2, x1, yx0, front, other, total = together(z2, x1, yx0, front, other, total)
    ups = []

    def update(first, fours, before=None):
        lanes = slice(first * LANES, (first + TOGETHER * len(fours)) * LANES)
        mine, others, up = absorb(
            info, row_slots, column_slots[:, lanes], tokens, other, width, fours, before
        )
        ups.extend([up, core_swap(up)])
        return mine, others

    z3, x2, yz2 = z_back(front), x_swap(z2), y_swap(z2)
    state = update(0, [((front, z1, x0, z2), 0)])
    z3, x2, yz2, x1, back, state, total = together(z3, x2, yz2, x1, back, state, total)

    zb1, x3, yx1 = z_ring(back), x_swap(z3), y_swap(x1)
    total = base_part(tokens, base_value_weight, 2 * third, depth, total)
    zb1, x3, yx1, yz2, back, state, total = together(zb1, x3, yx1, yz2, back, state, total)

    zb3, xyz2, yx3 = z_back(back), x_swap(yz2), y_swap(x3)
    state = update(4, [((x1, z3, x2, x3), 0), ((back, yx0, yz2, zb1), 1)], state)
    zb3, xyz2, yx3, state = together(zb3, xyz2, yx3, state)

    mine, others = update(12, [((yx1, zb3, xyz2, yx3), 1)], state)
    return finish(info, row_slot, mine, core_swap(others), total, ups)


def solution(mesh):
    placed = (
        P(("groups", "req"), "tp"),
        P(("groups", "req"), None),
        P(),
        P("tp", None),
        P("req", None, "tp"),
        P("req", None, "tp"),
    )
    sizes = mesh.shape
    small = sizes["groups"] == 2 and sizes["req"] == 16 and sizes["tp"] == 1
    return jax.shard_map(
        passed_round if small else gathered,
        mesh=mesh,
        in_specs=placed,
        out_specs=P(("groups", "req"), "tp"),
        check_vma=False,
    )
```

```python
import functools

import jax
import jax.numpy as jnp
import numpy as np
from jax import lax
from jax.experimental import pallas as pl
from jax.experimental.pallas import tpu as pltpu
from jax.sharding import PartitionSpec as P

RING = (0, 1, 3, 2)
PLACE_IN_RING = (0, 1, 3, 2)
DEPTH_TILE = 1024
LANES = 128
RANK = 16

PIECES = (
    *((0, 0, 0), (1, 0, 0), (0, 1, 0)),
    *((2, 0, 0), (1, 1, 0), (3, 0, 0), (2, 1, 0)),
    *((0, 0, 1), (0, 1, 1), (2, 0, 1), (1, 0, 1), (3, 1, 0)),
    *((1, 1, 1), (3, 0, 1), (2, 1, 1), (3, 1, 1)),
)
KERNEL_BOUNDS = (0, 3, 7, 12, 16)
QUARTER_CUTS = (0, 512, 1024, 2048)
VMEM_BYTES = 64 * 1024 * 1024 - 512 * 1024


def slots_of_rows(row_adapter_index, adapter_storage_slot):
    catalog = jnp.arange(adapter_storage_slot.shape[0], dtype=jnp.int32)
    return jnp.sum(
        jnp.where(row_adapter_index == catalog[None, :], adapter_storage_slot[None, :], 0),
        axis=1,
        keepdims=True,
    )


def gathered(
    tokens,
    row_adapter_index,
    adapter_storage_slot,
    base_value_weight,
    adapter_down_weight,
    adapter_up_weight,
):
    adapter_count = adapter_storage_slot.shape[0]
    rank = adapter_down_weight.shape[1]
    slot_of = slots_of_rows(row_adapter_index, adapter_storage_slot)
    down_all = lax.all_gather(
        adapter_down_weight.reshape(-1, adapter_down_weight.shape[2]), "req", axis=0, tiled=True
    )
    up_all = lax.all_gather(
        adapter_up_weight.reshape(-1, adapter_up_weight.shape[2]), "req", axis=0, tiled=True
    )
    base_partial = jnp.dot(tokens, base_value_weight, preferred_element_type=jnp.float32)
    base_output = lax.psum_scatter(base_partial, "tp", scatter_dimension=1, tiled=True)
    shrink = lax.dot_general(
        tokens, down_all, (((1,), (1,)), ((), ())), preferred_element_type=jnp.float32
    )
    column_slot = jnp.arange(adapter_count * rank, dtype=jnp.int32) // rank
    shrink = jnp.where(slot_of == column_slot[None, :], shrink, 0.0)
    shrink = lax.psum(shrink, "tp")
    high = lax.reduce_precision(shrink, 8, 7)
    rest = shrink - high
    middle = lax.reduce_precision(rest, 8, 7)
    low = rest - middle
    lora = sum(
        jnp.dot(piece.astype(jnp.bfloat16), up_all, preferred_element_type=jnp.float32)
        for piece in (low, middle, high)
    )
    return (base_output + lora).astype(jnp.bfloat16)


def params():
    return pltpu.CompilerParams(vmem_limit_bytes=VMEM_BYTES)


def started(copies):
    for copy in copies:
        copy.start()


def awaited(copies):
    for copy in copies:
        copy.wait()


def assemble_kernel(back, info_ref, here_ref, there_ref, up_ref, out_ref, down_ref, sems):
    y, core = info_ref[0], info_ref[1]
    place = 1 - y if back else y
    held, rank, quarter = down_ref.shape
    held //= 2
    columns = pl.ds(pl.multiple_of((2 * core + place) * quarter, quarter), quarter)
    copies = [
        pltpu.make_async_copy(
            source.at[:, :, columns], down_ref.at[pl.ds(of_core * held, held)], sems.at[n]
        )
        for n, (source, of_core) in enumerate(((here_ref, core), (there_ref, 1 - core)))
    ]
    started(copies)
    up = up_ref[pl.ds(place * (held // 2), held // 2)].reshape(held // 2 * rank, -1)
    rows = up.shape[0]
    for n in range(up.shape[1] // LANES):
        first = quarter + n * rows
        out_ref[first : first + rows] = up[:, n * LANES : (n + 1) * LANES]
    awaited(copies)
    for n in range(0, quarter, LANES):
        block = down_ref[:, :, n : n + LANES].reshape(2 * held * rank, LANES)
        out_ref[n : n + LANES] = block.T


def assemble(back, info, here, there, up):
    held, rank, depth = here.shape
    width = up.shape[2]
    rows = depth // 4 + held // 2 * rank * width // LANES
    anywhere = pl.BlockSpec(memory_space=pl.ANY)
    vmem = pl.BlockSpec(memory_space=pltpu.VMEM)
    return pl.pallas_call(
        functools.partial(assemble_kernel, back),
        out_shape=jax.ShapeDtypeStruct((rows, LANES), here.dtype),
        in_specs=[pl.BlockSpec(memory_space=pltpu.SMEM), anywhere, anywhere, vmem],
        out_specs=vmem,
        scratch_shapes=[
            pltpu.VMEM((2 * held, rank, depth // 4), here.dtype),
            pltpu.SemaphoreType.DMA((2,)),
        ],
        compiler_params=params(),
    )(info, here, there, up)


def base_kernel(tokens_ref, weight_ref, out_ref):
    step = pl.program_id(0)
    part = jnp.dot(tokens_ref[...], weight_ref[...], preferred_element_type=jnp.float32)

    @pl.when(step == 0)
    def _():
        out_ref[...] = part

    @pl.when(step > 0)
    def _():
        out_ref[...] += part


def base_half(tokens, weight, half):
    rows, depth = tokens.shape
    width = weight.shape[1] // 2
    return pl.pallas_call(
        base_kernel,
        out_shape=jax.ShapeDtypeStruct((rows, width), jnp.float32),
        grid=(depth // DEPTH_TILE,),
        in_specs=[
            pl.BlockSpec((rows, DEPTH_TILE), lambda k: (0, k)),
            pl.BlockSpec((DEPTH_TILE, width), lambda k: (k, half)),
        ],
        out_specs=pl.BlockSpec((rows, width), lambda k: (0, 0)),
        cost_estimate=pl.CostEstimate(
            flops=2 * rows * width * depth,
            bytes_accessed=2 * (rows + width) * depth + 4 * rows * width,
            transcendentals=0,
        ),
        compiler_params=params(),
    )(tokens, weight)


def absorb_kernel(
    groups, start, more, info_ref, row_slot_ref, column_slot_ref, tokens_ref, other_ref, *refs
):
    count = sum(size for size, _ in groups)
    sources, refs = refs[:count], refs[count:]
    before, refs = refs[: 2 * more], refs[2 * more :]
    outs, up_ref, rows_ref, refs = refs[:2], refs[2], refs[3], refs[4:]
    down_refs, sems = refs[: len(groups)], refs[len(groups)]
    rows = tokens_ref.shape[0]
    quarter = rows_ref.shape[2]
    y, core = info_ref[0], info_ref[1]
    cuts = list(zip(QUARTER_CUTS, QUARTER_CUTS[1:]))
    copies, waits = [], {}

    def begin(key, source, target):
        copy = pltpu.make_async_copy(source, target, sems.at[len(copies)])
        copies.append(copy)
        waits.setdefault(key, []).append(copy)
        copy.start()

    places = {}
    first = 0
    for n, ((size, back), down_ref) in enumerate(zip(groups, down_refs)):
        load = back not in places
        place = places.setdefault(back, len(places))
        column = (2 * core + (1 - y if back else y)) * quarter
        ends = cuts + [(quarter, sources[0].shape[0])]
        for low, high in ends:
            for i in range(size):
                begin(
                    (n, low),
                    sources[first + i].at[pl.ds(low, high - low)],
                    down_ref.at[pl.ds(low, high - low), pl.ds(i * LANES, LANES)],
                )
            if not load or low == quarter:
                continue
            columns = pl.ds(pl.multiple_of(column + low, QUARTER_CUTS[1]), high - low)
            for i, source in enumerate((tokens_ref, other_ref)):
                begin(
                    (n, low),
                    source.at[:, columns],
                    rows_ref.at[place, pl.ds(i * rows, rows), pl.ds(low, high - low)],
                )
        first += size
    state = None
    first = 0
    for n, ((size, back), down_ref) in enumerate(zip(groups, down_refs)):
        shrink = None
        for low, high in cuts:
            awaited(waits[n, low])
            part = jnp.dot(
                rows_ref[places[back], :, low:high],
                down_ref[low:high],
                preferred_element_type=jnp.float32,
            )
            shrink = part if shrink is None else shrink + part
        awaited(waits[n, quarter])
        height = up_ref.shape[0] // count
        for i in range(size):
            lanes, which = slice(i * LANES, (i + 1) * LANES), first + i
            wanted = column_slot_ref[:, (start + which) * LANES : (start + which + 1) * LANES]
            kept = jnp.where(row_slot_ref[...] == wanted, shrink[:, lanes], 0.0)
            state = kept if state is None else state + kept
            for j in range(up_ref.shape[1] // LANES):
                top = quarter + j * height
                up_ref[
                    which * height : (which + 1) * height, j * LANES : (j + 1) * LANES
                ] = down_ref[top : top + height, lanes]
        first += size
    for i, out_ref in enumerate(outs):
        own = state[i * rows : (i + 1) * rows]
        out_ref[...] = own + before[i][...] if more else own


def absorb(info, row_slots, column_slots, tokens, other, width, groups, start, before):
    rows, depth = tokens.shape
    pieces = [piece for group, _ in groups for piece in group]
    sizes = [(len(group), back) for group, back in groups]
    quarter = depth // 4
    height = pieces[0].shape[0]
    anywhere = pl.BlockSpec(memory_space=pl.ANY)
    vmem = pl.BlockSpec(memory_space=pltpu.VMEM)
    more = before is not None
    state = jax.ShapeDtypeStruct((rows, LANES), jnp.float32)
    up_rows = len(pieces) * (height - quarter) * LANES // width
    quarters = len({back for _, back in groups})
    cuts = len(QUARTER_CUTS) - 1
    copies = len(pieces) * (cuts + 1) + 2 * quarters * cuts
    return pl.pallas_call(
        functools.partial(absorb_kernel, sizes, start, more),
        out_shape=(state, state, jax.ShapeDtypeStruct((up_rows, width), tokens.dtype)),
        in_specs=[pl.BlockSpec(memory_space=pltpu.SMEM), vmem, vmem]
        + [anywhere] * (2 + len(pieces))
        + [vmem] * (2 * more),
        out_specs=(vmem, vmem, vmem),
        scratch_shapes=[pltpu.VMEM((quarters, 2 * rows, quarter), tokens.dtype)]
        + [pltpu.VMEM((height, size * LANES), tokens.dtype) for size, _ in sizes]
        + [pltpu.SemaphoreType.DMA((copies,))],
        cost_estimate=pl.CostEstimate(
            flops=4 * rows * len(pieces) * LANES * quarter,
            bytes_accessed=4 * rows * quarters * quarter + 2 * len(pieces) * LANES * height,
            transcendentals=0,
        ),
        compiler_params=params(),
    )(info, row_slots, column_slots, tokens, other, *pieces, *(before or ()))


def finish_kernel(
    count, info_ref, row_slot_ref, mine_ref, theirs_ref, left_ref, right_ref, *refs
):
    sources, (out_ref, total, up, sems) = refs[:count], refs[count:]
    rows = out_ref.shape[0]
    height = up.shape[0] // (len(PIECES) * 2)
    half = left_ref.shape[1]
    copies = [
        pltpu.make_async_copy(source, total.at[:, pl.ds(n * half, half)], sems.at[n])
        for n, source in enumerate((left_ref, right_ref))
    ]
    for source in sources:
        for n in range(0, source.shape[0], height):
            first = pl.multiple_of(info_ref[len(copies)], height)
            copies.append(
                pltpu.make_async_copy(
                    source.at[pl.ds(n, height)], up.at[pl.ds(first, height)], sems.at[len(copies)]
                )
            )
    started(copies)
    shrink = mine_ref[...] + theirs_ref[...]
    lane_slot = lax.broadcasted_iota(jnp.int32, (rows, LANES), 1) // RANK
    high, low = [], []
    for n in range(up.shape[0] // LANES):
        kept = jnp.where(row_slot_ref[...] == lane_slot + n * (LANES // RANK), shrink, 0.0)
        high.append(kept.astype(jnp.bfloat16))
        low.append((kept - high[-1].astype(jnp.float32)).astype(jnp.bfloat16))
    awaited(copies)
    both = jnp.concatenate([jnp.concatenate(part, axis=1) for part in (low, high)], axis=0)
    lora = jnp.dot(both, up[...], preferred_element_type=jnp.float32)
    out_ref[...] = (total[...] + (lora[:rows] + lora[rows:])).astype(out_ref.dtype)


def finish(info, row_slot, mine, theirs, left, right, ups):
    rows, width = left.shape[0], 2 * left.shape[1]
    anywhere = pl.BlockSpec(memory_space=pl.ANY)
    vmem = pl.BlockSpec(memory_space=pltpu.VMEM)
    up_rows = sum(up.shape[0] for up in ups)
    return pl.pallas_call(
        functools.partial(finish_kernel, len(ups)),
        out_shape=jax.ShapeDtypeStruct((rows, width), jnp.bfloat16),
        in_specs=[pl.BlockSpec(memory_space=pltpu.SMEM), vmem, vmem, vmem]
        + [anywhere] * (2 + len(ups)),
        out_specs=vmem,
        scratch_shapes=[
            pltpu.VMEM((rows, width), jnp.float32),
            pltpu.VMEM((up_rows, width), ups[0].dtype),
            pltpu.SemaphoreType.DMA((2 + 2 * len(PIECES),)),
        ],
        cost_estimate=pl.CostEstimate(
            flops=4 * rows * width * up_rows,
            bytes_accessed=6 * rows * width + 2 * up_rows * width,
            transcendentals=0,
        ),
        compiler_params=params(),
    )(info, row_slot, mine, theirs, left, right, *ups)


def passed_round(
    tokens,
    row_adapter_index,
    adapter_storage_slot,
    base_value_weight,
    adapter_down_weight,
    adapter_up_weight,
):
    rows, depth = tokens.shape
    held, rank, _ = adapter_down_weight.shape
    width = adapter_up_weight.shape[2]
    axes = ("groups", "req")
    planes, owners = lax.axis_size("groups"), lax.axis_size("req")
    device = lax.axis_index("groups") * owners + lax.axis_index("req")

    def permuted(array, target):
        pairs = [
            (g * owners + r, target(g, r)) for g in range(planes) for r in range(owners)
        ]
        return lax.ppermute(array, axes, pairs)

    def along_z(r, by):
        return RING[(PLACE_IN_RING[r // 4] + by) % 4] * 4 + r % 4

    z_ring = lambda array: permuted(array, lambda g, r: g * owners + along_z(r, 1))
    z_back = lambda array: permuted(array, lambda g, r: g * owners + along_z(r, -1))
    x_swap = lambda array: permuted(array, lambda g, r: g * owners + (r ^ 2))
    y_swap = lambda array: permuted(array, lambda g, r: (1 - g) * owners + r)
    core_swap = lambda array: permuted(array, lambda g, r: g * owners + (r ^ 1))

    def chip(r, piece):
        return (along_z(r, -piece[0]) ^ (2 * piece[1])) // 2

    per_chip = LANES // rank
    kernels = [PIECES[low:high] for low, high in zip(KERNEL_BOUNDS, KERNEL_BOUNDS[1:])]
    column_table, info_table = [], []
    for g in range(planes):
        for r in range(owners):
            column_table.append(
                [chip(r, p) * per_chip + n // rank for p in PIECES for n in range(LANES)]
            )
            info_table.append(
                [g, r % 2]
                + [
                    chip(r, p) * LANES + core * held * rank + (g ^ p[2]) * (held // 2 * rank)
                    for pieces in kernels
                    for core in (r % 2, 1 - r % 2)
                    for p in pieces
                ]
            )
    here_of = lambda table: lax.dynamic_index_in_dim(
        jnp.array(np.array(table, np.int32)), device, 0, keepdims=False
    )
    info, column_slots = here_of(info_table), here_of(column_table)[None, :]

    def together(*values):
        return lax.optimization_barrier(values)

    def after(value, *others):
        return lax.optimization_barrier((value, *others))[0]

    there = core_swap(adapter_down_weight)
    row_slot = slots_of_rows(row_adapter_index, adapter_storage_slot)
    there, tokens_late, info, row_slot, column_slots = together(
        there, tokens, info, row_slot, column_slots
    )

    def piece(back, *others):
        return assemble(
            back, after(info, *others), adapter_down_weight, there, adapter_up_weight
        )

    front = piece(0)

    z1, x0 = z_ring(front), x_swap(front)
    other = core_swap(tokens_late)
    other_slot = core_swap(row_slot[:, 0])
    left = base_half(after(tokens, front), base_value_weight, 0)
    row_slots = jnp.concatenate([row_slot, other_slot[:, None]], axis=0)

    z2 = z_ring(after(z1, left))
    x1 = x_swap(after(z1, x0, left))
    yx0 = y_swap(after(x0, left))
    right = base_half(after(tokens, z1, x0, left, row_slots), base_value_weight, 1)
    ups = []

    def update(number, groups, before, *others):
        mine, others, up = absorb(
            after(info, *others),
            row_slots,
            column_slots,
            tokens,
            other,
            width,
            groups,
            KERNEL_BOUNDS[number],
            before,
        )
        ups.extend([up, core_swap(up)])
        return mine, others

    z3 = z_back(after(front, z2, right))
    x2 = x_swap(after(z2, x1, right))
    yz2 = y_swap(after(z2, yx0, right))
    state = update(0, [((front, z1, x0), 0)], None, z2, x1, yx0, right)
    back = piece(1, z2, x1, yx0, right)

    zb1 = z_ring(after(back, z3, state[0]))
    x3 = x_swap(after(z3, x2, state[0]))
    yx1 = y_swap(after(x1, yz2, state[0]))
    state = update(1, [((z2, x1, z3, x2), 0)], state, z3, x2, yz2, back)

    zb3 = z_back(after(back, zb1, state[0]))
    xyz2 = x_swap(after(yz2, x3, state[0]))
    yx3 = y_swap(after(x3, yx1, state[0]))
    state = update(2, [((back, yx0, yz2, zb1), 1), ((x3,), 0)], state, zb1, x3, yx1, ups[1])

    mine, others = update(3, [((yx1, zb3, xyz2, yx3), 1)], state, ups[3], ups[5])
    return finish(info, row_slot, mine, core_swap(others), left, right, ups)


def solution(mesh):
    placed = (
        P(("groups", "req"), "tp"),
        P(("groups", "req"), None),
        P(),
        P("tp", None),
        P("req", None, "tp"),
        P("req", None, "tp"),
    )
    sizes = mesh.shape
    small = sizes["groups"] == 2 and sizes["req"] == 16 and sizes["tp"] == 1
    return jax.shard_map(
        passed_round if small else gathered,
        mesh=mesh,
        in_specs=placed,
        out_specs=P(("groups", "req"), "tp"),
        check_vma=False,
    )
```

```python
import functools

import jax
import jax.numpy as jnp
import numpy as np
from jax import lax
from jax.experimental import pallas as pl
from jax.experimental.pallas import tpu as pltpu
from jax.sharding import PartitionSpec as P

RING = (0, 1, 3, 2)
PLACE_IN_RING = (0, 1, 3, 2)
DEPTH_TILE = 1024
LANES = 128
RANK = 16

PIECES = (
    *((0, 0, 0), (1, 0, 0), (0, 1, 0), (2, 0, 0)),
    *((1, 1, 0), (3, 0, 0), (2, 1, 0), (3, 1, 0)),
    *((0, 0, 1), (0, 1, 1), (2, 0, 1), (1, 0, 1)),
    *((1, 1, 1), (3, 0, 1), (2, 1, 1), (3, 1, 1)),
)
KERNEL_BOUNDS = (0, 4, 12, 16)
QUARTER_CUTS = (0, 512, 1024, 2048)
VMEM_BYTES = 64 * 1024 * 1024 - 512 * 1024


def slots_of_rows(row_adapter_index, adapter_storage_slot):
    catalog = jnp.arange(adapter_storage_slot.shape[0], dtype=jnp.int32)
    return jnp.sum(
        jnp.where(row_adapter_index == catalog[None, :], adapter_storage_slot[None, :], 0),
        axis=1,
        keepdims=True,
    )


def gathered(
    tokens,
    row_adapter_index,
    adapter_storage_slot,
    base_value_weight,
    adapter_down_weight,
    adapter_up_weight,
):
    adapter_count = adapter_storage_slot.shape[0]
    rank = adapter_down_weight.shape[1]
    slot_of = slots_of_rows(row_adapter_index, adapter_storage_slot)
    down_all = lax.all_gather(
        adapter_down_weight.reshape(-1, adapter_down_weight.shape[2]), "req", axis=0, tiled=True
    )
    up_all = lax.all_gather(
        adapter_up_weight.reshape(-1, adapter_up_weight.shape[2]), "req", axis=0, tiled=True
    )
    base_partial = jnp.dot(tokens, base_value_weight, preferred_element_type=jnp.float32)
    base_output = lax.psum_scatter(base_partial, "tp", scatter_dimension=1, tiled=True)
    shrink = lax.dot_general(
        tokens, down_all, (((1,), (1,)), ((), ())), preferred_element_type=jnp.float32
    )
    column_slot = jnp.arange(adapter_count * rank, dtype=jnp.int32) // rank
    shrink = jnp.where(slot_of == column_slot[None, :], shrink, 0.0)
    shrink = lax.psum(shrink, "tp")
    high = lax.reduce_precision(shrink, 8, 7)
    rest = shrink - high
    middle = lax.reduce_precision(rest, 8, 7)
    low = rest - middle
    lora = sum(
        jnp.dot(piece.astype(jnp.bfloat16), up_all, preferred_element_type=jnp.float32)
        for piece in (low, middle, high)
    )
    return (base_output + lora).astype(jnp.bfloat16)


def params():
    return pltpu.CompilerParams(vmem_limit_bytes=VMEM_BYTES)


def started(copies):
    for copy in copies:
        copy.start()


def awaited(copies):
    for copy in copies:
        copy.wait()


def assemble_kernel(back, info_ref, here_ref, there_ref, up_ref, out_ref, down_ref, sems):
    y, core = info_ref[0], info_ref[1]
    place = 1 - y if back else y
    held, rank, quarter = down_ref.shape
    held //= 2
    columns = pl.ds(pl.multiple_of((2 * core + place) * quarter, quarter), quarter)
    copies = [
        pltpu.make_async_copy(
            source.at[:, :, columns], down_ref.at[pl.ds(of_core * held, held)], sems.at[n]
        )
        for n, (source, of_core) in enumerate(((here_ref, core), (there_ref, 1 - core)))
    ]
    started(copies)
    up = up_ref[pl.ds(place * (held // 2), held // 2)].reshape(held // 2 * rank, -1)
    rows = up.shape[0]
    for n in range(up.shape[1] // LANES):
        first = quarter + n * rows
        out_ref[first : first + rows] = up[:, n * LANES : (n + 1) * LANES]
    awaited(copies)
    for n in range(0, quarter, LANES):
        block = down_ref[:, :, n : n + LANES].reshape(2 * held * rank, LANES)
        out_ref[n : n + LANES] = block.T


def assemble(back, info, here, there, up):
    held, rank, depth = here.shape
    width = up.shape[2]
    rows = depth // 4 + held // 2 * rank * width // LANES
    anywhere = pl.BlockSpec(memory_space=pl.ANY)
    vmem = pl.BlockSpec(memory_space=pltpu.VMEM)
    return pl.pallas_call(
        functools.partial(assemble_kernel, back),
        out_shape=jax.ShapeDtypeStruct((rows, LANES), here.dtype),
        in_specs=[pl.BlockSpec(memory_space=pltpu.SMEM), anywhere, anywhere, vmem],
        out_specs=vmem,
        scratch_shapes=[
            pltpu.VMEM((2 * held, rank, depth // 4), here.dtype),
            pltpu.SemaphoreType.DMA((2,)),
        ],
        compiler_params=params(),
    )(info, here, there, up)


def base_kernel(steps, tokens_ref, weight_ref, *refs):
    step = pl.program_id(0)
    more = len(refs) > 1
    out_ref = refs[1] if more else refs[0]
    copies = [pltpu.make_async_copy(refs[0], refs[2], refs[3].at[0])] if more else []
    part = jnp.dot(tokens_ref[...], weight_ref[...], preferred_element_type=jnp.float32)

    @pl.when(step == 0)
    def _():
        started(copies)
        out_ref[...] = part

    @pl.when(step > 0)
    def _():
        out_ref[...] += part

    if more:

        @pl.when(step == steps - 1)
        def _():
            awaited(copies)
            out_ref[...] += refs[2][...]


def base_part(tokens, weight, begin, end, total=None):
    rows, depth = tokens.shape
    width = weight.shape[1]
    steps, first = (end - begin) // DEPTH_TILE, begin // DEPTH_TILE
    result = jax.ShapeDtypeStruct((rows, width), jnp.float32)
    more = total is not None
    return pl.pallas_call(
        functools.partial(base_kernel, steps),
        out_shape=result,
        grid=(steps,),
        in_specs=[
            pl.BlockSpec((rows, DEPTH_TILE), lambda k: (0, first + k)),
            pl.BlockSpec((DEPTH_TILE, width), lambda k: (first + k, 0)),
        ]
        + [pl.BlockSpec(memory_space=pl.ANY)] * more,
        out_specs=pl.BlockSpec((rows, width), lambda k: (0, 0)),
        scratch_shapes=[pltpu.VMEM((rows, width), jnp.float32), pltpu.SemaphoreType.DMA((1,))]
        if more
        else [],
        cost_estimate=pl.CostEstimate(
            flops=2 * rows * width * (end - begin),
            bytes_accessed=2 * (rows + width) * (end - begin) + 4 * rows * width,
            transcendentals=0,
        ),
        compiler_params=params(),
    )(tokens, weight, *([total] if more else []))


def absorb_kernel(
    groups, start, more, info_ref, row_slot_ref, column_slot_ref, tokens_ref, other_ref, *refs
):
    count = sum(size for size, _ in groups)
    sources, refs = refs[:count], refs[count:]
    before, refs = refs[: 2 * more], refs[2 * more :]
    outs, up_ref, rows_ref, refs = refs[:2], refs[2], refs[3], refs[4:]
    down_refs, sems = refs[: len(groups)], refs[len(groups)]
    rows = tokens_ref.shape[0]
    quarter = rows_ref.shape[2]
    y, core = info_ref[0], info_ref[1]
    cuts = list(zip(QUARTER_CUTS, QUARTER_CUTS[1:]))
    copies, waits = [], {}

    def begin(key, source, target):
        copy = pltpu.make_async_copy(source, target, sems.at[len(copies)])
        copies.append(copy)
        waits.setdefault(key, []).append(copy)
        copy.start()

    places = {}
    first = 0
    for n, ((size, back), down_ref) in enumerate(zip(groups, down_refs)):
        load = back not in places
        place = places.setdefault(back, len(places))
        column = (2 * core + (1 - y if back else y)) * quarter
        ends = cuts + [(quarter, sources[0].shape[0])]
        for low, high in ends:
            for i in range(size):
                begin(
                    (n, low),
                    sources[first + i].at[pl.ds(low, high - low)],
                    down_ref.at[pl.ds(low, high - low), pl.ds(i * LANES, LANES)],
                )
            if not load or low == quarter:
                continue
            columns = pl.ds(pl.multiple_of(column + low, QUARTER_CUTS[1]), high - low)
            for i, source in enumerate((tokens_ref, other_ref)):
                begin(
                    (n, low),
                    source.at[:, columns],
                    rows_ref.at[place, pl.ds(i * rows, rows), pl.ds(low, high - low)],
                )
        first += size
    state = None
    first = 0
    for n, ((size, back), down_ref) in enumerate(zip(groups, down_refs)):
        shrink = None
        for low, high in cuts:
            awaited(waits[n, low])
            part = jnp.dot(
                rows_ref[places[back], :, low:high],
                down_ref[low:high],
                preferred_element_type=jnp.float32,
            )
            shrink = part if shrink is None else shrink + part
        awaited(waits[n, quarter])
        height = up_ref.shape[0] // count
        for i in range(size):
            lanes, which = slice(i * LANES, (i + 1) * LANES), first + i
            wanted = column_slot_ref[:, (start + which) * LANES : (start + which + 1) * LANES]
            kept = jnp.where(row_slot_ref[...] == wanted, shrink[:, lanes], 0.0)
            state = kept if state is None else state + kept
            for j in range(up_ref.shape[1] // LANES):
                top = quarter + j * height
                up_ref[
                    which * height : (which + 1) * height, j * LANES : (j + 1) * LANES
                ] = down_ref[top : top + height, lanes]
        first += size
    for i, out_ref in enumerate(outs):
        own = state[i * rows : (i + 1) * rows]
        out_ref[...] = own + before[i][...] if more else own


def absorb(info, row_slots, column_slots, tokens, other, width, groups, start, before):
    rows, depth = tokens.shape
    pieces = [piece for group, _ in groups for piece in group]
    sizes = [(len(group), back) for group, back in groups]
    quarter = depth // 4
    height = pieces[0].shape[0]
    anywhere = pl.BlockSpec(memory_space=pl.ANY)
    vmem = pl.BlockSpec(memory_space=pltpu.VMEM)
    more = before is not None
    state = jax.ShapeDtypeStruct((rows, LANES), jnp.float32)
    up_rows = len(pieces) * (height - quarter) * LANES // width
    quarters = len({back for _, back in groups})
    cuts = len(QUARTER_CUTS) - 1
    copies = len(pieces) * (cuts + 1) + 2 * quarters * cuts
    return pl.pallas_call(
        functools.partial(absorb_kernel, sizes, start, more),
        out_shape=(state, state, jax.ShapeDtypeStruct((up_rows, width), tokens.dtype)),
        in_specs=[pl.BlockSpec(memory_space=pltpu.SMEM), vmem, vmem]
        + [anywhere] * (2 + len(pieces))
        + [vmem] * (2 * more),
        out_specs=(vmem, vmem, vmem),
        scratch_shapes=[pltpu.VMEM((quarters, 2 * rows, quarter), tokens.dtype)]
        + [pltpu.VMEM((height, size * LANES), tokens.dtype) for size, _ in sizes]
        + [pltpu.SemaphoreType.DMA((copies,))],
        cost_estimate=pl.CostEstimate(
            flops=4 * rows * len(pieces) * LANES * quarter,
            bytes_accessed=4 * rows * quarters * quarter + 2 * len(pieces) * LANES * height,
            transcendentals=0,
        ),
        compiler_params=params(),
    )(info, row_slots, column_slots, tokens, other, *pieces, *(before or ()))


def finish_kernel(
    count, info_ref, row_slot_ref, mine_ref, theirs_ref, total_ref, *refs
):
    sources, (out_ref, total, up, sems) = refs[:count], refs[count:]
    rows = out_ref.shape[0]
    height = up.shape[0] // (len(PIECES) * 2)
    copies = [pltpu.make_async_copy(total_ref, total, sems.at[0])]
    for source in sources:
        for n in range(0, source.shape[0], height):
            first = pl.multiple_of(info_ref[1 + len(copies)], height)
            copies.append(
                pltpu.make_async_copy(
                    source.at[pl.ds(n, height)], up.at[pl.ds(first, height)], sems.at[len(copies)]
                )
            )
    started(copies)
    shrink = mine_ref[...] + theirs_ref[...]
    lane_slot = lax.broadcasted_iota(jnp.int32, (rows, LANES), 1) // RANK
    high, low = [], []
    for n in range(up.shape[0] // LANES):
        kept = jnp.where(row_slot_ref[...] == lane_slot + n * (LANES // RANK), shrink, 0.0)
        high.append(kept.astype(jnp.bfloat16))
        low.append((kept - high[-1].astype(jnp.float32)).astype(jnp.bfloat16))
    awaited(copies)
    both = jnp.concatenate([jnp.concatenate(part, axis=1) for part in (low, high)], axis=0)
    lora = jnp.dot(both, up[...], preferred_element_type=jnp.float32)
    out_ref[...] = (total[...] + (lora[:rows] + lora[rows:])).astype(out_ref.dtype)


def finish(info, row_slot, mine, theirs, total, ups):
    rows, width = total.shape
    anywhere = pl.BlockSpec(memory_space=pl.ANY)
    vmem = pl.BlockSpec(memory_space=pltpu.VMEM)
    up_rows = sum(up.shape[0] for up in ups)
    return pl.pallas_call(
        functools.partial(finish_kernel, len(ups)),
        out_shape=jax.ShapeDtypeStruct((rows, width), jnp.bfloat16),
        in_specs=[pl.BlockSpec(memory_space=pltpu.SMEM), vmem, vmem, vmem]
        + [anywhere] * (1 + len(ups)),
        out_specs=vmem,
        scratch_shapes=[
            pltpu.VMEM((rows, width), jnp.float32),
            pltpu.VMEM((up_rows, width), ups[0].dtype),
            pltpu.SemaphoreType.DMA((1 + 2 * len(PIECES),)),
        ],
        cost_estimate=pl.CostEstimate(
            flops=4 * rows * width * up_rows,
            bytes_accessed=6 * rows * width + 2 * up_rows * width,
            transcendentals=0,
        ),
        compiler_params=params(),
    )(info, row_slot, mine, theirs, total, *ups)


def passed_round(
    tokens,
    row_adapter_index,
    adapter_storage_slot,
    base_value_weight,
    adapter_down_weight,
    adapter_up_weight,
):
    rows, depth = tokens.shape
    held, rank, _ = adapter_down_weight.shape
    width = adapter_up_weight.shape[2]
    axes = ("groups", "req")
    planes, owners = lax.axis_size("groups"), lax.axis_size("req")
    device = lax.axis_index("groups") * owners + lax.axis_index("req")

    def permuted(array, target):
        pairs = [
            (g * owners + r, target(g, r)) for g in range(planes) for r in range(owners)
        ]
        return lax.ppermute(array, axes, pairs)

    def along_z(r, by):
        return RING[(PLACE_IN_RING[r // 4] + by) % 4] * 4 + r % 4

    z_ring = lambda array: permuted(array, lambda g, r: g * owners + along_z(r, 1))
    z_back = lambda array: permuted(array, lambda g, r: g * owners + along_z(r, -1))
    x_swap = lambda array: permuted(array, lambda g, r: g * owners + (r ^ 2))
    y_swap = lambda array: permuted(array, lambda g, r: (1 - g) * owners + r)
    core_swap = lambda array: permuted(array, lambda g, r: g * owners + (r ^ 1))

    def chip(r, piece):
        return (along_z(r, -piece[0]) ^ (2 * piece[1])) // 2

    per_chip = LANES // rank
    kernels = [PIECES[low:high] for low, high in zip(KERNEL_BOUNDS, KERNEL_BOUNDS[1:])]
    column_table, info_table = [], []
    for g in range(planes):
        for r in range(owners):
            column_table.append(
                [chip(r, p) * per_chip + n // rank for p in PIECES for n in range(LANES)]
            )
            info_table.append(
                [g, r % 2]
                + [
                    chip(r, p) * LANES + core * held * rank + (g ^ p[2]) * (held // 2 * rank)
                    for pieces in kernels
                    for core in (r % 2, 1 - r % 2)
                    for p in pieces
                ]
            )
    here_of = lambda table, which: lax.dynamic_index_in_dim(
        jnp.array(np.array(table, np.int32)), which, 0, keepdims=False
    )

    def together(*values):
        return lax.optimization_barrier(values)

    def after(value, *others):
        return lax.optimization_barrier((value, *others))[0]

    there = core_swap(adapter_down_weight)
    at = jnp.stack([lax.axis_index("groups"), lax.axis_index("req") % 2])
    there, at, tokens_late = together(there, at, tokens)

    def piece(back, *others):
        return assemble(
            back, after(at, *others), adapter_down_weight, there, adapter_up_weight
        )

    front = piece(0)

    z1, x0 = z_ring(front), x_swap(front)
    other = core_swap(tokens_late)
    row_index = after(row_adapter_index, front)
    row_slot = slots_of_rows(row_index, adapter_storage_slot)
    other_slot = core_swap(row_slot[:, 0])
    device = after(device, front)
    info, column_slots = here_of(info_table, device), here_of(column_table, device)[None, :]
    total = base_part(after(tokens, front), base_value_weight, 0, depth // 2)
    row_slots = jnp.concatenate([row_slot, other_slot[:, None]], axis=0)

    z2 = z_ring(after(z1, total))
    x1 = x_swap(after(z1, x0, total))
    yx0 = y_swap(after(x0, total))
    tokens_late = after(tokens, z1, x0, total, row_slots, info, column_slots)
    total = base_part(tokens_late, base_value_weight, depth // 2, depth, total)
    ups = []

    def update(number, groups, before, *others):
        mine, others, up = absorb(
            after(info, *others),
            row_slots,
            column_slots,
            tokens,
            other,
            width,
            groups,
            KERNEL_BOUNDS[number],
            before,
        )
        ups.extend([up, core_swap(up)])
        return mine, others

    z3 = z_back(after(front, z2, total))
    x2 = x_swap(after(z2, x1, total))
    yz2 = y_swap(after(z2, yx0, total))
    state = update(0, [((front, z1, x0, z2), 0)], None, x1, yx0, total)
    back = piece(1, z2, x1, yx0, total)

    zb1 = z_ring(after(back, z3, state[0]))
    x3 = x_swap(after(z3, x2, state[0]))
    yx1 = y_swap(after(x1, yz2, state[0]))

    zb3 = z_back(after(back, zb1))
    xyz2 = x_swap(after(yz2, x3))
    yx3 = y_swap(after(x3, yx1))
    state = update(
        1, [((x1, z3, x2, x3), 0), ((back, yx0, yz2, zb1), 1)], state, yx1, ups[1]
    )

    mine, others = update(2, [((yx1, zb3, xyz2, yx3), 1)], state, ups[3])
    return finish(info, row_slot, mine, core_swap(others), total, ups)


def solution(mesh):
    placed = (
        P(("groups", "req"), "tp"),
        P(("groups", "req"), None),
        P(),
        P("tp", None),
        P("req", None, "tp"),
        P("req", None, "tp"),
    )
    sizes = mesh.shape
    small = sizes["groups"] == 2 and sizes["req"] == 16 and sizes["tp"] == 1
    return jax.shard_map(
        passed_round if small else gathered,
        mesh=mesh,
        in_specs=placed,
        out_specs=P(("groups", "req"), "tp"),
        check_vma=False,
    )
```

```python
import functools

import jax
import jax.numpy as jnp
import numpy as np
from jax import lax
from jax.experimental import pallas as pl
from jax.experimental.pallas import tpu as pltpu
from jax.sharding import PartitionSpec as P

RING = (0, 1, 3, 2)
PLACE_IN_RING = (0, 1, 3, 2)
DEPTH_TILE = 1024
LANES = 128
RANK = 16

PIECES = (
    *((0, 0, 0), (1, 0, 0), (0, 1, 0), (2, 0, 0), (0, 0, 1), (0, 1, 1), (2, 0, 1)),
    *((1, 1, 0), (3, 0, 0), (2, 1, 0), (3, 1, 0), (1, 0, 1), (1, 1, 1)),
    *((3, 0, 1), (2, 1, 1), (3, 1, 1)),
)
KERNEL_BOUNDS = (0, 7, 13, 16)
QUARTER_CUTS = (0, 512, 1024, 2048)
VMEM_BYTES = 64 * 1024 * 1024 - 512 * 1024


def slots_of_rows(row_adapter_index, adapter_storage_slot):
    catalog = jnp.arange(adapter_storage_slot.shape[0], dtype=jnp.int32)
    return jnp.sum(
        jnp.where(row_adapter_index == catalog[None, :], adapter_storage_slot[None, :], 0),
        axis=1,
        keepdims=True,
    )


def gathered(
    tokens,
    row_adapter_index,
    adapter_storage_slot,
    base_value_weight,
    adapter_down_weight,
    adapter_up_weight,
):
    adapter_count = adapter_storage_slot.shape[0]
    rank = adapter_down_weight.shape[1]
    slot_of = slots_of_rows(row_adapter_index, adapter_storage_slot)
    down_all = lax.all_gather(
        adapter_down_weight.reshape(-1, adapter_down_weight.shape[2]), "req", axis=0, tiled=True
    )
    up_all = lax.all_gather(
        adapter_up_weight.reshape(-1, adapter_up_weight.shape[2]), "req", axis=0, tiled=True
    )
    base_partial = jnp.dot(tokens, base_value_weight, preferred_element_type=jnp.float32)
    base_output = lax.psum_scatter(base_partial, "tp", scatter_dimension=1, tiled=True)
    shrink = lax.dot_general(
        tokens, down_all, (((1,), (1,)), ((), ())), preferred_element_type=jnp.float32
    )
    column_slot = jnp.arange(adapter_count * rank, dtype=jnp.int32) // rank
    shrink = jnp.where(slot_of == column_slot[None, :], shrink, 0.0)
    shrink = lax.psum(shrink, "tp")
    high = lax.reduce_precision(shrink, 8, 7)
    rest = shrink - high
    middle = lax.reduce_precision(rest, 8, 7)
    low = rest - middle
    lora = sum(
        jnp.dot(piece.astype(jnp.bfloat16), up_all, preferred_element_type=jnp.float32)
        for piece in (low, middle, high)
    )
    return (base_output + lora).astype(jnp.bfloat16)


def params():
    return pltpu.CompilerParams(vmem_limit_bytes=VMEM_BYTES)


def started(copies):
    for copy in copies:
        copy.start()


def awaited(copies):
    for copy in copies:
        copy.wait()


def assemble_kernel(back, info_ref, here_ref, there_ref, up_ref, out_ref, down_ref, sems):
    y, core = info_ref[0], info_ref[1]
    place = 1 - y if back else y
    held, rank, quarter = down_ref.shape
    held //= 2
    columns = pl.ds(pl.multiple_of((2 * core + place) * quarter, quarter), quarter)
    copies = [
        pltpu.make_async_copy(
            source.at[:, :, columns], down_ref.at[pl.ds(of_core * held, held)], sems.at[n]
        )
        for n, (source, of_core) in enumerate(((here_ref, core), (there_ref, 1 - core)))
    ]
    started(copies)
    up = up_ref[pl.ds(place * (held // 2), held // 2)].reshape(held // 2 * rank, -1)
    rows = up.shape[0]
    for n in range(up.shape[1] // LANES):
        first = quarter + n * rows
        out_ref[first : first + rows] = up[:, n * LANES : (n + 1) * LANES]
    awaited(copies)
    for n in range(0, quarter, LANES):
        block = down_ref[:, :, n : n + LANES].reshape(2 * held * rank, LANES)
        out_ref[n : n + LANES] = block.T


def assemble(back, info, here, there, up):
    held, rank, depth = here.shape
    width = up.shape[2]
    rows = depth // 4 + held // 2 * rank * width // LANES
    anywhere = pl.BlockSpec(memory_space=pl.ANY)
    vmem = pl.BlockSpec(memory_space=pltpu.VMEM)
    return pl.pallas_call(
        functools.partial(assemble_kernel, back),
        out_shape=jax.ShapeDtypeStruct((rows, LANES), here.dtype),
        in_specs=[pl.BlockSpec(memory_space=pltpu.SMEM), anywhere, anywhere, vmem],
        out_specs=vmem,
        scratch_shapes=[
            pltpu.VMEM((2 * held, rank, depth // 4), here.dtype),
            pltpu.SemaphoreType.DMA((2,)),
        ],
        compiler_params=params(),
    )(info, here, there, up)


def base_kernel(steps, tokens_ref, weight_ref, *refs):
    step = pl.program_id(0)
    more = len(refs) > 1
    out_ref = refs[1] if more else refs[0]
    copies = [pltpu.make_async_copy(refs[0], refs[2], refs[3].at[0])] if more else []
    part = jnp.dot(tokens_ref[...], weight_ref[...], preferred_element_type=jnp.float32)

    @pl.when(step == 0)
    def _():
        started(copies)
        out_ref[...] = part

    @pl.when(step > 0)
    def _():
        out_ref[...] += part

    if more:

        @pl.when(step == steps - 1)
        def _():
            awaited(copies)
            out_ref[...] += refs[2][...]


def base_part(tokens, weight, begin, end, total=None):
    rows, depth = tokens.shape
    width = weight.shape[1]
    steps, first = (end - begin) // DEPTH_TILE, begin // DEPTH_TILE
    result = jax.ShapeDtypeStruct((rows, width), jnp.float32)
    more = total is not None
    return pl.pallas_call(
        functools.partial(base_kernel, steps),
        out_shape=result,
        grid=(steps,),
        in_specs=[
            pl.BlockSpec((rows, DEPTH_TILE), lambda k: (0, first + k)),
            pl.BlockSpec((DEPTH_TILE, width), lambda k: (first + k, 0)),
        ]
        + [pl.BlockSpec(memory_space=pl.ANY)] * more,
        out_specs=pl.BlockSpec((rows, width), lambda k: (0, 0)),
        scratch_shapes=[pltpu.VMEM((rows, width), jnp.float32), pltpu.SemaphoreType.DMA((1,))]
        if more
        else [],
        cost_estimate=pl.CostEstimate(
            flops=2 * rows * width * (end - begin),
            bytes_accessed=2 * (rows + width) * (end - begin) + 4 * rows * width,
            transcendentals=0,
        ),
        compiler_params=params(),
    )(tokens, weight, *([total] if more else []))


def absorb_kernel(
    groups, start, more, info_ref, row_slot_ref, tokens_ref, other_ref, *refs
):
    count = sum(size for size, _ in groups)
    sources, refs = refs[:count], refs[count:]
    before, refs = refs[: 2 * more], refs[2 * more :]
    outs, up_ref, rows_ref, refs = refs[:2], refs[2], refs[3], refs[4:]
    down_refs, sems = refs[: len(groups)], refs[len(groups)]
    rows = tokens_ref.shape[0]
    quarter = rows_ref.shape[2]
    y, core = info_ref[0], info_ref[1]
    cuts = list(zip(QUARTER_CUTS, QUARTER_CUTS[1:]))
    copies, waits = [], {}

    def begin(key, source, target):
        copy = pltpu.make_async_copy(source, target, sems.at[len(copies)])
        copies.append(copy)
        waits.setdefault(key, []).append(copy)
        copy.start()

    places = {}
    first = 0
    for n, ((size, back), down_ref) in enumerate(zip(groups, down_refs)):
        load = back not in places
        place = places.setdefault(back, len(places))
        column = (2 * core + (1 - y if back else y)) * quarter
        ends = cuts + [(quarter, sources[0].shape[0])]
        for low, high in ends:
            for i in range(size):
                begin(
                    (n, low),
                    sources[first + i].at[pl.ds(low, high - low)],
                    down_ref.at[pl.ds(low, high - low), pl.ds(i * LANES, LANES)],
                )
            if not load or low == quarter:
                continue
            columns = pl.ds(pl.multiple_of(column + low, QUARTER_CUTS[1]), high - low)
            for i, source in enumerate((tokens_ref, other_ref)):
                begin(
                    (n, low),
                    source.at[:, columns],
                    rows_ref.at[place, pl.ds(i * rows, rows), pl.ds(low, high - low)],
                )
        first += size
    lane_slot = lax.broadcasted_iota(jnp.int32, (1, LANES), 1) // RANK
    state = None
    first = 0
    for n, ((size, back), down_ref) in enumerate(zip(groups, down_refs)):
        shrink = None
        for low, high in cuts:
            awaited(waits[n, low])
            part = jnp.dot(
                rows_ref[places[back], :, low:high],
                down_ref[low:high],
                preferred_element_type=jnp.float32,
            )
            shrink = part if shrink is None else shrink + part
        awaited(waits[n, quarter])
        height = up_ref.shape[0] // count
        for i in range(size):
            lanes, which = slice(i * LANES, (i + 1) * LANES), first + i
            chip = info_ref[2 + 2 * len(PIECES) + start + which]
            wanted = lane_slot + chip * (LANES // RANK)
            kept = jnp.where(row_slot_ref[...] == wanted, shrink[:, lanes], 0.0)
            state = kept if state is None else state + kept
            for j in range(up_ref.shape[1] // LANES):
                top = quarter + j * height
                up_ref[
                    which * height : (which + 1) * height, j * LANES : (j + 1) * LANES
                ] = down_ref[top : top + height, lanes]
        first += size
    for i, out_ref in enumerate(outs):
        own = state[i * rows : (i + 1) * rows]
        out_ref[...] = own + before[i][...] if more else own


def absorb(info, row_slots, tokens, other, width, groups, start, before):
    rows, depth = tokens.shape
    pieces = [piece for group, _ in groups for piece in group]
    sizes = [(len(group), back) for group, back in groups]
    quarter = depth // 4
    height = pieces[0].shape[0]
    anywhere = pl.BlockSpec(memory_space=pl.ANY)
    vmem = pl.BlockSpec(memory_space=pltpu.VMEM)
    more = before is not None
    state = jax.ShapeDtypeStruct((rows, LANES), jnp.float32)
    up_rows = len(pieces) * (height - quarter) * LANES // width
    quarters = len({back for _, back in groups})
    cuts = len(QUARTER_CUTS) - 1
    copies = len(pieces) * (cuts + 1) + 2 * quarters * cuts
    return pl.pallas_call(
        functools.partial(absorb_kernel, sizes, start, more),
        out_shape=(state, state, jax.ShapeDtypeStruct((up_rows, width), tokens.dtype)),
        in_specs=[pl.BlockSpec(memory_space=pltpu.SMEM), vmem]
        + [anywhere] * (2 + len(pieces))
        + [vmem] * (2 * more),
        out_specs=(vmem, vmem, vmem),
        scratch_shapes=[pltpu.VMEM((quarters, 2 * rows, quarter), tokens.dtype)]
        + [pltpu.VMEM((height, size * LANES), tokens.dtype) for size, _ in sizes]
        + [pltpu.SemaphoreType.DMA((copies,))],
        cost_estimate=pl.CostEstimate(
            flops=4 * rows * len(pieces) * LANES * quarter,
            bytes_accessed=4 * rows * quarters * quarter + 2 * len(pieces) * LANES * height,
            transcendentals=0,
        ),
        compiler_params=params(),
    )(info, row_slots, tokens, other, *pieces, *(before or ()))


def finish_kernel(
    count, info_ref, row_slot_ref, mine_ref, theirs_ref, total_ref, *refs
):
    sources, (out_ref, total, up, sems) = refs[:count], refs[count:]
    rows = out_ref.shape[0]
    height = up.shape[0] // (len(PIECES) * 2)
    copies = [pltpu.make_async_copy(total_ref, total, sems.at[0])]
    for source in sources:
        for n in range(0, source.shape[0], height):
            first = pl.multiple_of(info_ref[1 + len(copies)], height)
            copies.append(
                pltpu.make_async_copy(
                    source.at[pl.ds(n, height)], up.at[pl.ds(first, height)], sems.at[len(copies)]
                )
            )
    started(copies)
    shrink = mine_ref[...] + theirs_ref[...]
    lane_slot = lax.broadcasted_iota(jnp.int32, (rows, LANES), 1) // RANK
    high, low = [], []
    for n in range(up.shape[0] // LANES):
        kept = jnp.where(row_slot_ref[:rows] == lane_slot + n * (LANES // RANK), shrink, 0.0)
        high.append(kept.astype(jnp.bfloat16))
        low.append((kept - high[-1].astype(jnp.float32)).astype(jnp.bfloat16))
    awaited(copies)
    both = jnp.concatenate([jnp.concatenate(part, axis=1) for part in (low, high)], axis=0)
    lora = jnp.dot(both, up[...], preferred_element_type=jnp.float32)
    out_ref[...] = (total[...] + (lora[:rows] + lora[rows:])).astype(out_ref.dtype)


def finish(info, row_slots, mine, theirs, total, ups):
    rows, width = total.shape
    anywhere = pl.BlockSpec(memory_space=pl.ANY)
    vmem = pl.BlockSpec(memory_space=pltpu.VMEM)
    up_rows = sum(up.shape[0] for up in ups)
    return pl.pallas_call(
        functools.partial(finish_kernel, len(ups)),
        out_shape=jax.ShapeDtypeStruct((rows, width), jnp.bfloat16),
        in_specs=[pl.BlockSpec(memory_space=pltpu.SMEM), vmem, vmem, vmem]
        + [anywhere] * (1 + len(ups)),
        out_specs=vmem,
        scratch_shapes=[
            pltpu.VMEM((rows, width), jnp.float32),
            pltpu.VMEM((up_rows, width), ups[0].dtype),
            pltpu.SemaphoreType.DMA((1 + 2 * len(PIECES),)),
        ],
        cost_estimate=pl.CostEstimate(
            flops=4 * rows * width * up_rows,
            bytes_accessed=6 * rows * width + 2 * up_rows * width,
            transcendentals=0,
        ),
        compiler_params=params(),
    )(info, row_slots, mine, theirs, total, *ups)


def passed_round(
    tokens,
    row_adapter_index,
    adapter_storage_slot,
    base_value_weight,
    adapter_down_weight,
    adapter_up_weight,
):
    rows, depth = tokens.shape
    held, rank, _ = adapter_down_weight.shape
    width = adapter_up_weight.shape[2]
    axes = ("groups", "req")
    planes, owners = lax.axis_size("groups"), lax.axis_size("req")
    device = lax.axis_index("groups") * owners + lax.axis_index("req")

    def permuted(array, target):
        pairs = [
            (g * owners + r, target(g, r)) for g in range(planes) for r in range(owners)
        ]
        return lax.ppermute(array, axes, pairs)

    def along_z(r, by):
        return RING[(PLACE_IN_RING[r // 4] + by) % 4] * 4 + r % 4

    z_ring = lambda array: permuted(array, lambda g, r: g * owners + along_z(r, 1))
    z_back = lambda array: permuted(array, lambda g, r: g * owners + along_z(r, -1))
    x_swap = lambda array: permuted(array, lambda g, r: g * owners + (r ^ 2))
    y_swap = lambda array: permuted(array, lambda g, r: (1 - g) * owners + r)
    core_swap = lambda array: permuted(array, lambda g, r: g * owners + (r ^ 1))

    def chip(r, piece):
        return (along_z(r, -piece[0]) ^ (2 * piece[1])) // 2

    kernels = [PIECES[low:high] for low, high in zip(KERNEL_BOUNDS, KERNEL_BOUNDS[1:])]
    info_table = [
        [g, r % 2]
        + [
            chip(r, p) * LANES + core * held * rank + (g ^ p[2]) * (held // 2 * rank)
            for pieces in kernels
            for core in (r % 2, 1 - r % 2)
            for p in pieces
        ]
        + [chip(r, p) for p in PIECES]
        for g in range(planes)
        for r in range(owners)
    ]
    info = lax.dynamic_index_in_dim(
        jnp.array(np.array(info_table, np.int32)), device, 0, keepdims=False
    )

    def together(*values):
        return lax.optimization_barrier(values)

    def after(value, *others):
        return lax.optimization_barrier((value, *others))[0]

    there = core_swap(adapter_down_weight)
    row_slot = slots_of_rows(row_adapter_index, adapter_storage_slot)
    there, info, row_slot, tokens_late = together(there, info, row_slot, tokens)

    def piece(back, *others):
        return assemble(
            back, after(info, *others), adapter_down_weight, there, adapter_up_weight
        )

    front = piece(0)
    cuts = (0, 3 * DEPTH_TILE, 6 * DEPTH_TILE, depth)

    def base(number, before, *others):
        low, high = cuts[number : number + 2]
        return base_part(after(tokens, *others), base_value_weight, low, high, before)

    z1, x0 = z_ring(front), x_swap(front)
    other = core_swap(tokens_late)
    other_slot = core_swap(row_slot[:, 0])
    total = base(0, None, front)
    row_slots = jnp.concatenate([row_slot, other_slot[:, None]], axis=0)

    z2 = z_ring(after(z1, total))
    x1 = x_swap(after(z1, x0, total))
    yx0 = y_swap(after(x0, total))
    total = base(1, total, z1, x0, total, row_slots)

    z3 = z_back(after(front, z2, total))
    x2 = x_swap(after(z2, x1, total))
    yz2 = y_swap(after(z2, yx0, total))
    back = piece(1, z2, x1, yx0, total)
    total = base(2, total, z2, x1, yx0, back, other)
    ups = []

    def update(number, groups, before, *others):
        mine, others, up = absorb(
            after(info, *others),
            row_slots,
            tokens,
            other,
            width,
            groups,
            KERNEL_BOUNDS[number],
            before,
        )
        ups.extend([up, core_swap(up)])
        return mine, others

    zb1 = z_ring(after(back, z3, total))
    x3 = x_swap(after(z3, x2, total))
    yx1 = y_swap(after(x1, yz2, total))
    state = update(
        0, [((front, z1, x0, z2), 0), ((back, yx0, yz2), 1)], None, z3, x2, yz2, total
    )

    zb3 = z_back(after(back, zb1, state[0]))
    xyz2 = x_swap(after(yz2, x3, state[0]))
    yx3 = y_swap(after(x3, yx1, state[0]))
    state = update(1, [((x1, z3, x2, x3), 0), ((zb1, yx1), 1)], state, zb1, x3, yx1)

    mine, others = update(2, [((zb3, xyz2, yx3), 1)], state, ups[1], ups[3])
    return finish(info, row_slots, mine, core_swap(others), total, ups)


def solution(mesh):
    placed = (
        P(("groups", "req"), "tp"),
        P(("groups", "req"), None),
        P(),
        P("tp", None),
        P("req", None, "tp"),
        P("req", None, "tp"),
    )
    sizes = mesh.shape
    small = sizes["groups"] == 2 and sizes["req"] == 16 and sizes["tp"] == 1
    return jax.shard_map(
        passed_round if small else gathered,
        mesh=mesh,
        in_specs=placed,
        out_specs=P(("groups", "req"), "tp"),
        check_vma=False,
    )
```

```python
import functools

import jax
import jax.numpy as jnp
import numpy as np
from jax import lax
from jax.experimental import pallas as pl
from jax.experimental.pallas import tpu as pltpu
from jax.sharding import PartitionSpec as P

RING = (0, 1, 3, 2)
PLACE_IN_RING = (0, 1, 3, 2)
DEPTH_TILE = 1024
LANES = 128
RANK = 16

PIECES = (
    *((0, 0, 0), (1, 0, 0), (0, 1, 0), (2, 0, 0)),
    *((1, 1, 0), (3, 0, 0), (2, 1, 0), (3, 1, 0), (0, 0, 1), (0, 1, 1), (2, 0, 1), (1, 0, 1)),
    *((1, 1, 1), (3, 0, 1), (2, 1, 1), (3, 1, 1)),
)
KERNEL_BOUNDS = (0, 4, 12, 16)
QUARTER_CUTS = (0, 512, 1024, 2048)
VMEM_BYTES = 64 * 1024 * 1024 - 512 * 1024


def slots_of_rows(row_adapter_index, adapter_storage_slot):
    catalog = jnp.arange(adapter_storage_slot.shape[0], dtype=jnp.int32)
    return jnp.sum(
        jnp.where(row_adapter_index == catalog[None, :], adapter_storage_slot[None, :], 0),
        axis=1,
        keepdims=True,
    )


def gathered(
    tokens,
    row_adapter_index,
    adapter_storage_slot,
    base_value_weight,
    adapter_down_weight,
    adapter_up_weight,
):
    adapter_count = adapter_storage_slot.shape[0]
    rank = adapter_down_weight.shape[1]
    slot_of = slots_of_rows(row_adapter_index, adapter_storage_slot)
    down_all = lax.all_gather(
        adapter_down_weight.reshape(-1, adapter_down_weight.shape[2]), "req", axis=0, tiled=True
    )
    up_all = lax.all_gather(
        adapter_up_weight.reshape(-1, adapter_up_weight.shape[2]), "req", axis=0, tiled=True
    )
    base_partial = jnp.dot(tokens, base_value_weight, preferred_element_type=jnp.float32)
    base_output = lax.psum_scatter(base_partial, "tp", scatter_dimension=1, tiled=True)
    shrink = lax.dot_general(
        tokens, down_all, (((1,), (1,)), ((), ())), preferred_element_type=jnp.float32
    )
    column_slot = jnp.arange(adapter_count * rank, dtype=jnp.int32) // rank
    shrink = jnp.where(slot_of == column_slot[None, :], shrink, 0.0)
    shrink = lax.psum(shrink, "tp")
    high = lax.reduce_precision(shrink, 8, 7)
    rest = shrink - high
    middle = lax.reduce_precision(rest, 8, 7)
    low = rest - middle
    lora = sum(
        jnp.dot(piece.astype(jnp.bfloat16), up_all, preferred_element_type=jnp.float32)
        for piece in (low, middle, high)
    )
    return (base_output + lora).astype(jnp.bfloat16)


def params():
    return pltpu.CompilerParams(vmem_limit_bytes=VMEM_BYTES)


def started(copies):
    for copy in copies:
        copy.start()


def awaited(copies):
    for copy in copies:
        copy.wait()


def assemble_kernel(back, info_ref, here_ref, there_ref, up_ref, out_ref, down_ref, sems):
    y, core = info_ref[0], info_ref[1]
    place = 1 - y if back else y
    held, rank, quarter = down_ref.shape
    held //= 2
    columns = pl.ds(pl.multiple_of((2 * core + place) * quarter, quarter), quarter)
    copies = [
        pltpu.make_async_copy(
            source.at[:, :, columns], down_ref.at[pl.ds(of_core * held, held)], sems.at[n]
        )
        for n, (source, of_core) in enumerate(((here_ref, core), (there_ref, 1 - core)))
    ]
    started(copies)
    up = up_ref[pl.ds(place * (held // 2), held // 2)].reshape(held // 2 * rank, -1)
    rows = up.shape[0]
    for n in range(up.shape[1] // LANES):
        first = quarter + n * rows
        out_ref[first : first + rows] = up[:, n * LANES : (n + 1) * LANES]
    awaited(copies)
    for n in range(0, quarter, LANES):
        block = down_ref[:, :, n : n + LANES].reshape(2 * held * rank, LANES)
        out_ref[n : n + LANES] = block.T


def assemble(back, info, here, there, up):
    held, rank, depth = here.shape
    width = up.shape[2]
    rows = depth // 4 + held // 2 * rank * width // LANES
    anywhere = pl.BlockSpec(memory_space=pl.ANY)
    vmem = pl.BlockSpec(memory_space=pltpu.VMEM)
    return pl.pallas_call(
        functools.partial(assemble_kernel, back),
        out_shape=jax.ShapeDtypeStruct((rows, LANES), here.dtype),
        in_specs=[pl.BlockSpec(memory_space=pltpu.SMEM), anywhere, anywhere, vmem],
        out_specs=vmem,
        scratch_shapes=[
            pltpu.VMEM((2 * held, rank, depth // 4), here.dtype),
            pltpu.SemaphoreType.DMA((2,)),
        ],
        compiler_params=params(),
    )(info, here, there, up)


def copy_kernel(info_ref, in_ref, out_ref):
    out_ref[...] = in_ref[...]


def half_for_partner(info, tokens):
    rows, depth = tokens.shape
    height = rows // 4
    return pl.pallas_call(
        copy_kernel,
        out_shape=jax.ShapeDtypeStruct((rows, depth // 2), tokens.dtype),
        grid_spec=pltpu.PrefetchScalarGridSpec(
            num_scalar_prefetch=1,
            grid=(rows // height,),
            in_specs=[pl.BlockSpec((height, depth // 2), lambda n, info: (n, 1 - info[1]))],
            out_specs=pl.BlockSpec((height, depth // 2), lambda n, info: (n, 0)),
        ),
        cost_estimate=pl.CostEstimate(
            flops=0, bytes_accessed=2 * rows * depth, transcendentals=0
        ),
        compiler_params=params(),
    )(info, tokens)


def base_kernel(steps, tokens_ref, weight_ref, *refs):
    step = pl.program_id(0)
    more = len(refs) > 1
    out_ref = refs[1] if more else refs[0]
    copies = [pltpu.make_async_copy(refs[0], refs[2], refs[3].at[0])] if more else []
    part = jnp.dot(tokens_ref[...], weight_ref[...], preferred_element_type=jnp.float32)

    @pl.when(step == 0)
    def _():
        started(copies)
        out_ref[...] = part

    @pl.when(step > 0)
    def _():
        out_ref[...] += part

    if more:

        @pl.when(step == steps - 1)
        def _():
            awaited(copies)
            out_ref[...] += refs[2][...]


def base_part(tokens, weight, begin, end, total=None):
    rows, depth = tokens.shape
    width = weight.shape[1]
    steps, first = (end - begin) // DEPTH_TILE, begin // DEPTH_TILE
    result = jax.ShapeDtypeStruct((rows, width), jnp.float32)
    more = total is not None
    return pl.pallas_call(
        functools.partial(base_kernel, steps),
        out_shape=result,
        grid=(steps,),
        in_specs=[
            pl.BlockSpec((rows, DEPTH_TILE), lambda k: (0, first + k)),
            pl.BlockSpec((DEPTH_TILE, width), lambda k: (first + k, 0)),
        ]
        + [pl.BlockSpec(memory_space=pl.ANY)] * more,
        out_specs=pl.BlockSpec((rows, width), lambda k: (0, 0)),
        scratch_shapes=[pltpu.VMEM((rows, width), jnp.float32), pltpu.SemaphoreType.DMA((1,))]
        if more
        else [],
        cost_estimate=pl.CostEstimate(
            flops=2 * rows * width * (end - begin),
            bytes_accessed=2 * (rows + width) * (end - begin) + 4 * rows * width,
            transcendentals=0,
        ),
        compiler_params=params(),
    )(tokens, weight, *([total] if more else []))


def absorb_kernel(groups, start, sides, more, has_up, info_ref, row_slot_ref, *refs):
    count = sum(size for size, _ in groups)
    token_refs, sources, refs = refs[: len(sides)], refs[len(sides) :][:count], refs[len(sides) + count :]
    before, refs = refs[: len(sides) * more], refs[len(sides) * more :]
    outs, refs = refs[: len(sides)], refs[len(sides) :]
    up_ref, refs = (refs[0], refs[1:]) if has_up else (None, refs)
    rows_ref, down_refs, sems = refs[0], refs[1:-1], refs[-1]
    rows = token_refs[0].shape[0]
    quarter = rows_ref.shape[2]
    y, core = info_ref[0], info_ref[1]
    cuts = list(zip(QUARTER_CUTS, QUARTER_CUTS[1:]))
    copies, waits = [], {}

    def begin(key, source, target):
        copy = pltpu.make_async_copy(source, target, sems.at[len(copies)])
        copies.append(copy)
        waits.setdefault(key, []).append(copy)
        copy.start()

    places = {}
    first = 0
    for n, ((size, back), down_ref) in enumerate(zip(groups, down_refs)):
        load = back not in places
        place = places.setdefault(back, len(places))
        ends = cuts + [(quarter, sources[0].shape[0])] * has_up
        for low, high in ends:
            for i in range(size):
                begin(
                    (n, low),
                    sources[first + i].at[pl.ds(low, high - low)],
                    down_ref.at[pl.ds(low, high - low), pl.ds(i * LANES, LANES)],
                )
            if not load or low == quarter:
                continue
            for i, (side, source) in enumerate(zip(sides, token_refs)):
                column = (1 - y if back else y) * quarter + low
                if side == 0:
                    column += core * 2 * quarter
                begin(
                    (n, low),
                    source.at[:, pl.ds(pl.multiple_of(column, QUARTER_CUTS[1]), high - low)],
                    rows_ref.at[place, pl.ds(i * rows, rows), pl.ds(low, high - low)],
                )
        first += size
    lane_slot = lax.broadcasted_iota(jnp.int32, (1, LANES), 1) // RANK
    row_slot = jnp.concatenate(
        [row_slot_ref[side * rows : (side + 1) * rows] for side in sides], axis=0
    )
    state = None
    first = 0
    for n, ((size, back), down_ref) in enumerate(zip(groups, down_refs)):
        shrink = None
        for low, high in cuts:
            awaited(waits[n, low])
            part = jnp.dot(
                rows_ref[places[back], :, low:high],
                down_ref[low:high],
                preferred_element_type=jnp.float32,
            )
            shrink = part if shrink is None else shrink + part
        for i in range(size):
            lanes, which = slice(i * LANES, (i + 1) * LANES), first + i
            chip = info_ref[2 + 2 * len(PIECES) + start + which]
            wanted = lane_slot + chip * (LANES // RANK)
            kept = jnp.where(row_slot == wanted, shrink[:, lanes], 0.0)
            state = kept if state is None else state + kept
        if has_up:
            awaited(waits[n, quarter])
            height = up_ref.shape[0] // count
            for i in range(size):
                lanes, which = slice(i * LANES, (i + 1) * LANES), first + i
                for j in range(up_ref.shape[1] // LANES):
                    top = quarter + j * height
                    up_ref[
                        which * height : (which + 1) * height, j * LANES : (j + 1) * LANES
                    ] = down_ref[top : top + height, lanes]
        first += size
    for i, out_ref in enumerate(outs):
        own = state[i * rows : (i + 1) * rows]
        out_ref[...] = own + before[i][...] if more else own


def absorb(info, row_slots, sides, tokens, width, groups, start, before, has_up):
    rows = tokens[0].shape[0]
    pieces = [piece for group, _ in groups for piece in group]
    sizes = [(len(group), back) for group, back in groups]
    quarter = tokens[-1].shape[1] // (4 if sides == (0,) else 2)
    height = pieces[0].shape[0]
    anywhere = pl.BlockSpec(memory_space=pl.ANY)
    vmem = pl.BlockSpec(memory_space=pltpu.VMEM)
    more = before is not None
    state = jax.ShapeDtypeStruct((rows, LANES), jnp.float32)
    up_rows = len(pieces) * (height - quarter) * LANES // width
    up = jax.ShapeDtypeStruct((up_rows, width), tokens[0].dtype)
    quarters = len({back for _, back in groups})
    cuts = len(QUARTER_CUTS) - 1
    copies = len(pieces) * (cuts + has_up) + len(sides) * quarters * cuts
    outs = (state,) * len(sides) + (up,) * has_up
    return pl.pallas_call(
        functools.partial(absorb_kernel, sizes, start, sides, more, has_up),
        out_shape=outs,
        in_specs=[pl.BlockSpec(memory_space=pltpu.SMEM), vmem]
        + [anywhere] * (len(sides) + len(pieces))
        + [vmem] * (len(sides) * more),
        out_specs=(vmem,) * len(outs),
        scratch_shapes=[pltpu.VMEM((quarters, len(sides) * rows, quarter), tokens[0].dtype)]
        + [pltpu.VMEM((height, size * LANES), tokens[0].dtype) for size, _ in sizes]
        + [pltpu.SemaphoreType.DMA((copies,))],
        cost_estimate=pl.CostEstimate(
            flops=2 * len(sides) * rows * len(pieces) * LANES * quarter,
            bytes_accessed=2 * len(sides) * rows * quarters * quarter
            + 2 * len(pieces) * LANES * height,
            transcendentals=0,
        ),
        compiler_params=params(),
    )(info, row_slots, *tokens, *pieces, *(before or ()))


def finish_kernel(
    count, info_ref, row_slot_ref, mine_ref, theirs_ref, total_ref, *refs
):
    sources, (out_ref, total, up, sems) = refs[:count], refs[count:]
    rows = out_ref.shape[0]
    height = up.shape[0] // (len(PIECES) * 2)
    copies = [pltpu.make_async_copy(total_ref, total, sems.at[0])]
    for source in sources:
        for n in range(0, source.shape[0], height):
            first = pl.multiple_of(info_ref[1 + len(copies)], height)
            copies.append(
                pltpu.make_async_copy(
                    source.at[pl.ds(n, height)], up.at[pl.ds(first, height)], sems.at[len(copies)]
                )
            )
    started(copies)
    shrink = mine_ref[...] + theirs_ref[...]
    lane_slot = lax.broadcasted_iota(jnp.int32, (rows, LANES), 1) // RANK
    high, low = [], []
    for n in range(up.shape[0] // LANES):
        kept = jnp.where(row_slot_ref[:rows] == lane_slot + n * (LANES // RANK), shrink, 0.0)
        high.append(kept.astype(jnp.bfloat16))
        low.append((kept - high[-1].astype(jnp.float32)).astype(jnp.bfloat16))
    awaited(copies)
    both = jnp.concatenate([jnp.concatenate(part, axis=1) for part in (low, high)], axis=0)
    lora = jnp.dot(both, up[...], preferred_element_type=jnp.float32)
    out_ref[...] = (total[...] + (lora[:rows] + lora[rows:])).astype(out_ref.dtype)


def finish(info, row_slots, mine, theirs, total, ups):
    rows, width = total.shape
    anywhere = pl.BlockSpec(memory_space=pl.ANY)
    vmem = pl.BlockSpec(memory_space=pltpu.VMEM)
    up_rows = sum(up.shape[0] for up in ups)
    return pl.pallas_call(
        functools.partial(finish_kernel, len(ups)),
        out_shape=jax.ShapeDtypeStruct((rows, width), jnp.bfloat16),
        in_specs=[pl.BlockSpec(memory_space=pltpu.SMEM), vmem, vmem, vmem]
        + [anywhere] * (1 + len(ups)),
        out_specs=vmem,
        scratch_shapes=[
            pltpu.VMEM((rows, width), jnp.float32),
            pltpu.VMEM((up_rows, width), ups[0].dtype),
            pltpu.SemaphoreType.DMA((1 + 2 * len(PIECES),)),
        ],
        cost_estimate=pl.CostEstimate(
            flops=4 * rows * width * up_rows,
            bytes_accessed=6 * rows * width + 2 * up_rows * width,
            transcendentals=0,
        ),
        compiler_params=params(),
    )(info, row_slots, mine, theirs, total, *ups)


def passed_round(
    tokens,
    row_adapter_index,
    adapter_storage_slot,
    base_value_weight,
    adapter_down_weight,
    adapter_up_weight,
):
    rows, depth = tokens.shape
    held, rank, _ = adapter_down_weight.shape
    width = adapter_up_weight.shape[2]
    axes = ("groups", "req")
    planes, owners = lax.axis_size("groups"), lax.axis_size("req")
    device = lax.axis_index("groups") * owners + lax.axis_index("req")

    def permuted(array, target):
        pairs = [
            (g * owners + r, target(g, r)) for g in range(planes) for r in range(owners)
        ]
        return lax.ppermute(array, axes, pairs)

    def along_z(r, by):
        return RING[(PLACE_IN_RING[r // 4] + by) % 4] * 4 + r % 4

    z_ring = lambda array: permuted(array, lambda g, r: g * owners + along_z(r, 1))
    z_back = lambda array: permuted(array, lambda g, r: g * owners + along_z(r, -1))
    x_swap = lambda array: permuted(array, lambda g, r: g * owners + (r ^ 2))
    y_swap = lambda array: permuted(array, lambda g, r: (1 - g) * owners + r)
    core_swap = lambda array: permuted(array, lambda g, r: g * owners + (r ^ 1))

    def chip(r, piece):
        return (along_z(r, -piece[0]) ^ (2 * piece[1])) // 2

    kernels = [PIECES[low:high] for low, high in zip(KERNEL_BOUNDS, KERNEL_BOUNDS[1:])]
    info_table = [
        [g, r % 2]
        + [
            chip(r, p) * LANES + core * held * rank + (g ^ p[2]) * (held // 2 * rank)
            for pieces in kernels
            for core in (r % 2, 1 - r % 2)
            for p in pieces
        ]
        + [chip(r, p) for p in PIECES]
        for g in range(planes)
        for r in range(owners)
    ]
    info = lax.dynamic_index_in_dim(
        jnp.array(np.array(info_table, np.int32)), device, 0, keepdims=False
    )

    def together(*values):
        return lax.optimization_barrier(values)

    def after(value, *others):
        return lax.optimization_barrier((value, *others))[0]

    there = core_swap(adapter_down_weight)
    row_slot = slots_of_rows(row_adapter_index, adapter_storage_slot)
    there, info, row_slot = together(there, info, row_slot)

    def piece(back, *others):
        return assemble(
            back, after(info, *others), adapter_down_weight, there, adapter_up_weight
        )

    front = piece(0)
    cuts = (0, 3 * DEPTH_TILE, 6 * DEPTH_TILE, depth)

    def base(number, before, *others):
        low, high = cuts[number : number + 2]
        return base_part(after(tokens, *others), base_value_weight, low, high, before)

    z1, x0 = z_ring(front), x_swap(front)
    other_slot = core_swap(row_slot[:, 0])
    total = base(0, None, front)
    half = half_for_partner(after(info, total), tokens)
    other = core_swap(half)
    row_slots = jnp.concatenate([row_slot, other_slot[:, None]], axis=0)

    z2 = z_ring(after(z1, half))
    x1 = x_swap(after(z1, x0, half))
    yx0 = y_swap(after(x0, half))
    total = base(1, total, z1, x0, total, row_slots)

    z3 = z_back(after(front, z2, total))
    x2 = x_swap(after(z2, x1, total))
    yz2 = y_swap(after(z2, yx0, total))
    back = piece(1, z2, x1, yx0, total)
    total = base(2, total, z2, x1, yx0, back, other)

    def update(number, sides, groups, before, has_up, *others):
        return absorb(
            after(info, *others),
            row_slots,
            sides,
            [(tokens, other)[side] for side in sides],
            width,
            groups,
            KERNEL_BOUNDS[number],
            before,
            has_up,
        )

    zb1 = z_ring(after(back, z3, total))
    x3 = x_swap(after(z3, x2, total))
    yx1 = y_swap(after(x1, yz2, total))
    *state, up_a = update(0, (0, 1), [((front, z1, x0, z2), 0)], None, True, z3, x2, yz2, total)
    there_a = core_swap(up_a)

    zb3 = z_back(after(back, zb1, state[0]))
    xyz2 = x_swap(after(yz2, x3, state[0]))
    yx3 = y_swap(after(x3, yx1, state[0]))
    *state, up_b = update(
        1,
        (0, 1),
        [((x1, z3, x2, x3), 0), ((back, yx0, yz2, zb1), 1)],
        state,
        True,
        zb1,
        x3,
        yx1,
    )
    there_b = core_swap(up_b)

    last = [((yx1, zb3, xyz2, yx3), 1)]
    others, up_c = update(2, (1,), last, state[1:], True)
    theirs, there_c = core_swap(others), core_swap(up_c)
    (mine,) = update(2, (0,), last, state[:1], False, others, there_a, there_b)
    ups = (up_a, there_a, up_b, there_b, up_c, there_c)
    return finish(info, row_slots, mine, theirs, total, ups)


def solution(mesh):
    placed = (
        P(("groups", "req"), "tp"),
        P(("groups", "req"), None),
        P(),
        P("tp", None),
        P("req", None, "tp"),
        P("req", None, "tp"),
    )
    sizes = mesh.shape
    small = sizes["groups"] == 2 and sizes["req"] == 16 and sizes["tp"] == 1
    return jax.shard_map(
        passed_round if small else gathered,
        mesh=mesh,
        in_specs=placed,
        out_specs=P(("groups", "req"), "tp"),
        check_vma=False,
    )
```

```python
import functools

import jax
import jax.numpy as jnp
import numpy as np
from jax import lax
from jax.experimental import pallas as pl
from jax.experimental.pallas import tpu as pltpu
from jax.sharding import PartitionSpec as P

RING = (0, 1, 3, 2)
PLACE_IN_RING = (0, 1, 3, 2)
DEPTH_TILE = 1024
LANES = 128
RANK = 16

PIECES = (
    *((0, 0, 0), (1, 0, 0), (0, 1, 0), (2, 0, 0)),
    *((1, 1, 0), (3, 0, 0), (2, 1, 0), (3, 1, 0)),
    *((0, 0, 1), (0, 1, 1), (2, 0, 1), (1, 0, 1), (1, 1, 1)),
    *((3, 0, 1), (2, 1, 1), (3, 1, 1)),
)
KERNEL_BOUNDS = (0, 4, 13, 16)
QUARTER_CUTS = (0, 512, 1024, 2048)
VMEM_BYTES = 64 * 1024 * 1024 - 512 * 1024


def slots_of_rows(row_adapter_index, adapter_storage_slot):
    catalog = jnp.arange(adapter_storage_slot.shape[0], dtype=jnp.int32)
    return jnp.sum(
        jnp.where(row_adapter_index == catalog[None, :], adapter_storage_slot[None, :], 0),
        axis=1,
        keepdims=True,
    )


def gathered(
    tokens,
    row_adapter_index,
    adapter_storage_slot,
    base_value_weight,
    adapter_down_weight,
    adapter_up_weight,
):
    adapter_count = adapter_storage_slot.shape[0]
    rank = adapter_down_weight.shape[1]
    slot_of = slots_of_rows(row_adapter_index, adapter_storage_slot)
    down_all = lax.all_gather(
        adapter_down_weight.reshape(-1, adapter_down_weight.shape[2]), "req", axis=0, tiled=True
    )
    up_all = lax.all_gather(
        adapter_up_weight.reshape(-1, adapter_up_weight.shape[2]), "req", axis=0, tiled=True
    )
    base_partial = jnp.dot(tokens, base_value_weight, preferred_element_type=jnp.float32)
    base_output = lax.psum_scatter(base_partial, "tp", scatter_dimension=1, tiled=True)
    shrink = lax.dot_general(
        tokens, down_all, (((1,), (1,)), ((), ())), preferred_element_type=jnp.float32
    )
    column_slot = jnp.arange(adapter_count * rank, dtype=jnp.int32) // rank
    shrink = jnp.where(slot_of == column_slot[None, :], shrink, 0.0)
    shrink = lax.psum(shrink, "tp")
    high = lax.reduce_precision(shrink, 8, 7)
    rest = shrink - high
    middle = lax.reduce_precision(rest, 8, 7)
    low = rest - middle
    lora = sum(
        jnp.dot(piece.astype(jnp.bfloat16), up_all, preferred_element_type=jnp.float32)
        for piece in (low, middle, high)
    )
    return (base_output + lora).astype(jnp.bfloat16)


def params():
    return pltpu.CompilerParams(vmem_limit_bytes=VMEM_BYTES)


def started(copies):
    for copy in copies:
        copy.start()


def awaited(copies):
    for copy in copies:
        copy.wait()


def assemble_kernel(back, info_ref, here_ref, there_ref, up_ref, out_ref, down_ref, sems):
    y, core = info_ref[0], info_ref[1]
    place = 1 - y if back else y
    held, rank, quarter = down_ref.shape
    held //= 2
    columns = pl.ds(pl.multiple_of((2 * core + place) * quarter, quarter), quarter)
    copies = [
        pltpu.make_async_copy(
            source.at[:, :, columns], down_ref.at[pl.ds(of_core * held, held)], sems.at[n]
        )
        for n, (source, of_core) in enumerate(((here_ref, core), (there_ref, 1 - core)))
    ]
    started(copies)
    up = up_ref[pl.ds(place * (held // 2), held // 2)].reshape(held // 2 * rank, -1)
    rows = up.shape[0]
    for n in range(up.shape[1] // LANES):
        first = quarter + n * rows
        out_ref[first : first + rows] = up[:, n * LANES : (n + 1) * LANES]
    awaited(copies)
    for n in range(0, quarter, LANES):
        block = down_ref[:, :, n : n + LANES].reshape(2 * held * rank, LANES)
        out_ref[n : n + LANES] = block.T


def assemble(back, info, here, there, up):
    held, rank, depth = here.shape
    width = up.shape[2]
    rows = depth // 4 + held // 2 * rank * width // LANES
    anywhere = pl.BlockSpec(memory_space=pl.ANY)
    vmem = pl.BlockSpec(memory_space=pltpu.VMEM)
    return pl.pallas_call(
        functools.partial(assemble_kernel, back),
        out_shape=jax.ShapeDtypeStruct((rows, LANES), here.dtype),
        in_specs=[pl.BlockSpec(memory_space=pltpu.SMEM), anywhere, anywhere, vmem],
        out_specs=vmem,
        scratch_shapes=[
            pltpu.VMEM((2 * held, rank, depth // 4), here.dtype),
            pltpu.SemaphoreType.DMA((2,)),
        ],
        compiler_params=params(),
    )(info, here, there, up)


def base_kernel(steps, tokens_ref, weight_ref, *refs):
    step = pl.program_id(0)
    more = len(refs) > 1
    out_ref = refs[1] if more else refs[0]
    copies = [pltpu.make_async_copy(refs[0], refs[2], refs[3].at[0])] if more else []
    part = jnp.dot(tokens_ref[...], weight_ref[...], preferred_element_type=jnp.float32)

    @pl.when(step == 0)
    def _():
        started(copies)
        out_ref[...] = part

    @pl.when(step > 0)
    def _():
        out_ref[...] += part

    if more:

        @pl.when(step == steps - 1)
        def _():
            awaited(copies)
            out_ref[...] += refs[2][...]


def base_part(tokens, weight, begin, end, total=None):
    rows, depth = tokens.shape
    width = weight.shape[1]
    steps, first = (end - begin) // DEPTH_TILE, begin // DEPTH_TILE
    result = jax.ShapeDtypeStruct((rows, width), jnp.float32)
    more = total is not None
    return pl.pallas_call(
        functools.partial(base_kernel, steps),
        out_shape=result,
        grid=(steps,),
        in_specs=[
            pl.BlockSpec((rows, DEPTH_TILE), lambda k: (0, first + k)),
            pl.BlockSpec((DEPTH_TILE, width), lambda k: (first + k, 0)),
        ]
        + [pl.BlockSpec(memory_space=pl.ANY)] * more,
        out_specs=pl.BlockSpec((rows, width), lambda k: (0, 0)),
        scratch_shapes=[pltpu.VMEM((rows, width), jnp.float32), pltpu.SemaphoreType.DMA((1,))]
        if more
        else [],
        cost_estimate=pl.CostEstimate(
            flops=2 * rows * width * (end - begin),
            bytes_accessed=2 * (rows + width) * (end - begin) + 4 * rows * width,
            transcendentals=0,
        ),
        compiler_params=params(),
    )(tokens, weight, *([total] if more else []))


def absorb_kernel(groups, start, sides, more, has_up, info_ref, row_slot_ref, *refs):
    count = sum(size for size, _ in groups)
    token_refs, sources, refs = refs[: len(sides)], refs[len(sides) :][:count], refs[len(sides) + count :]
    before, refs = refs[: len(sides) * more], refs[len(sides) * more :]
    outs, refs = refs[: len(sides)], refs[len(sides) :]
    up_ref, refs = (refs[0], refs[1:]) if has_up else (None, refs)
    rows_ref, down_refs, sems = refs[0], refs[1:-1], refs[-1]
    rows = token_refs[0].shape[0]
    quarter = rows_ref.shape[2]
    y, core = info_ref[0], info_ref[1]
    cuts = list(zip(QUARTER_CUTS, QUARTER_CUTS[1:]))
    copies, waits = [], {}

    def begin(key, source, target):
        copy = pltpu.make_async_copy(source, target, sems.at[len(copies)])
        copies.append(copy)
        waits.setdefault(key, []).append(copy)
        copy.start()

    places = {}
    first = 0
    for n, ((size, back), down_ref) in enumerate(zip(groups, down_refs)):
        load = back not in places
        place = places.setdefault(back, len(places))
        ends = cuts + [(quarter, sources[0].shape[0])] * has_up
        for low, high in ends:
            for i in range(size):
                begin(
                    (n, low),
                    sources[first + i].at[pl.ds(low, high - low)],
                    down_ref.at[pl.ds(low, high - low), pl.ds(i * LANES, LANES)],
                )
            if not load or low == quarter:
                continue
            for i, source in enumerate(token_refs):
                column = (2 * core + (1 - y if back else y)) * quarter + low
                begin(
                    (n, low),
                    source.at[:, pl.ds(pl.multiple_of(column, QUARTER_CUTS[1]), high - low)],
                    rows_ref.at[place, pl.ds(i * rows, rows), pl.ds(low, high - low)],
                )
        first += size
    lane_slot = lax.broadcasted_iota(jnp.int32, (1, LANES), 1) // RANK
    row_slot = jnp.concatenate(
        [row_slot_ref[side * rows : (side + 1) * rows] for side in sides], axis=0
    )
    state = None
    first = 0
    for n, ((size, back), down_ref) in enumerate(zip(groups, down_refs)):
        shrink = None
        for low, high in cuts:
            awaited(waits[n, low])
            part = jnp.dot(
                rows_ref[places[back], :, low:high],
                down_ref[low:high],
                preferred_element_type=jnp.float32,
            )
            shrink = part if shrink is None else shrink + part
        for i in range(size):
            lanes, which = slice(i * LANES, (i + 1) * LANES), first + i
            chip = info_ref[2 + 2 * len(PIECES) + start + which]
            wanted = lane_slot + chip * (LANES // RANK)
            kept = jnp.where(row_slot == wanted, shrink[:, lanes], 0.0)
            state = kept if state is None else state + kept
        if has_up:
            awaited(waits[n, quarter])
            height = up_ref.shape[0] // count
            for i in range(size):
                lanes, which = slice(i * LANES, (i + 1) * LANES), first + i
                for j in range(up_ref.shape[1] // LANES):
                    top = quarter + j * height
                    up_ref[
                        which * height : (which + 1) * height, j * LANES : (j + 1) * LANES
                    ] = down_ref[top : top + height, lanes]
        first += size
    for i, out_ref in enumerate(outs):
        own = state[i * rows : (i + 1) * rows]
        out_ref[...] = own + before[i][...] if more else own


def absorb(info, row_slots, sides, tokens, width, groups, start, before, has_up):
    rows = tokens[0].shape[0]
    pieces = [piece for group, _ in groups for piece in group]
    sizes = [(len(group), back) for group, back in groups]
    quarter = tokens[0].shape[1] // 4
    height = pieces[0].shape[0]
    anywhere = pl.BlockSpec(memory_space=pl.ANY)
    vmem = pl.BlockSpec(memory_space=pltpu.VMEM)
    more = before is not None
    state = jax.ShapeDtypeStruct((rows, LANES), jnp.float32)
    up_rows = len(pieces) * (height - quarter) * LANES // width
    up = jax.ShapeDtypeStruct((up_rows, width), tokens[0].dtype)
    quarters = len({back for _, back in groups})
    cuts = len(QUARTER_CUTS) - 1
    copies = len(pieces) * (cuts + has_up) + len(sides) * quarters * cuts
    outs = (state,) * len(sides) + (up,) * has_up
    return pl.pallas_call(
        functools.partial(absorb_kernel, sizes, start, sides, more, has_up),
        out_shape=outs,
        in_specs=[pl.BlockSpec(memory_space=pltpu.SMEM), vmem]
        + [anywhere] * (len(sides) + len(pieces))
        + [vmem] * (len(sides) * more),
        out_specs=(vmem,) * len(outs),
        scratch_shapes=[pltpu.VMEM((quarters, len(sides) * rows, quarter), tokens[0].dtype)]
        + [pltpu.VMEM((height, size * LANES), tokens[0].dtype) for size, _ in sizes]
        + [pltpu.SemaphoreType.DMA((copies,))],
        cost_estimate=pl.CostEstimate(
            flops=2 * len(sides) * rows * len(pieces) * LANES * quarter,
            bytes_accessed=2 * len(sides) * rows * quarters * quarter
            + 2 * len(pieces) * LANES * height,
            transcendentals=0,
        ),
        compiler_params=params(),
    )(info, row_slots, *tokens, *pieces, *(before or ()))


def finish_kernel(count, info_ref, row_slot_ref, mine_ref, theirs_ref, total_ref, *refs):
    sources, refs = refs[:count], refs[count:]
    out_ref, row_slot, mine, theirs, total, up, sems = refs
    rows = out_ref.shape[0]
    height = up.shape[0] // (len(PIECES) * 2)
    copies = []

    def begin(source, target):
        copies.append(pltpu.make_async_copy(source, target, sems.at[len(copies)]))
        copies[-1].start()

    begin(row_slot_ref.at[pl.ds(0, rows)], row_slot)
    begin(mine_ref, mine)
    begin(theirs_ref, theirs)
    begin(total_ref, total)
    for source in sources:
        for n in range(0, source.shape[0], height):
            first = pl.multiple_of(info_ref[len(copies) - 2], height)
            begin(source.at[pl.ds(n, height)], up.at[pl.ds(first, height)])
    awaited(copies[:3])
    shrink = mine[...] + theirs[...]
    lane_slot = lax.broadcasted_iota(jnp.int32, (1, LANES), 1) // RANK
    high, low = [], []
    for n in range(up.shape[0] // LANES):
        kept = jnp.where(row_slot[...] == lane_slot + n * (LANES // RANK), shrink, 0.0)
        high.append(kept.astype(jnp.bfloat16))
        low.append((kept - high[-1].astype(jnp.float32)).astype(jnp.bfloat16))
    both = jnp.concatenate([jnp.concatenate(part, axis=1) for part in (low, high)], axis=0)
    awaited(copies[3:])
    lora = jnp.dot(both, up[...], preferred_element_type=jnp.float32)
    out_ref[...] = (total[...] + (lora[:rows] + lora[rows:])).astype(out_ref.dtype)


def finish(info, row_slots, mine, theirs, total, ups):
    rows, width = total.shape
    anywhere = pl.BlockSpec(memory_space=pl.ANY)
    up_rows = sum(up.shape[0] for up in ups)
    return pl.pallas_call(
        functools.partial(finish_kernel, len(ups)),
        out_shape=jax.ShapeDtypeStruct((rows, width), jnp.bfloat16),
        in_specs=[pl.BlockSpec(memory_space=pltpu.SMEM)] + [anywhere] * (4 + len(ups)),
        out_specs=pl.BlockSpec(memory_space=pltpu.VMEM),
        scratch_shapes=[
            pltpu.VMEM((rows, 1), jnp.int32),
            pltpu.VMEM((rows, LANES), jnp.float32),
            pltpu.VMEM((rows, LANES), jnp.float32),
            pltpu.VMEM((rows, width), jnp.float32),
            pltpu.VMEM((up_rows, width), ups[0].dtype),
            pltpu.SemaphoreType.DMA((4 + 2 * len(PIECES),)),
        ],
        cost_estimate=pl.CostEstimate(
            flops=4 * rows * width * up_rows,
            bytes_accessed=6 * rows * width + 2 * up_rows * width,
            transcendentals=0,
        ),
        compiler_params=params(),
    )(info, row_slots, mine, theirs, total, *ups)


def passed_round(
    tokens,
    row_adapter_index,
    adapter_storage_slot,
    base_value_weight,
    adapter_down_weight,
    adapter_up_weight,
):
    rows, depth = tokens.shape
    held, rank, _ = adapter_down_weight.shape
    width = adapter_up_weight.shape[2]
    axes = ("groups", "req")
    planes, owners = lax.axis_size("groups"), lax.axis_size("req")
    device = lax.axis_index("groups") * owners + lax.axis_index("req")

    def permuted(array, target):
        pairs = [
            (g * owners + r, target(g, r)) for g in range(planes) for r in range(owners)
        ]
        return lax.ppermute(array, axes, pairs)

    def along_z(r, by):
        return RING[(PLACE_IN_RING[r // 4] + by) % 4] * 4 + r % 4

    z_ring = lambda array: permuted(array, lambda g, r: g * owners + along_z(r, 1))
    z_back = lambda array: permuted(array, lambda g, r: g * owners + along_z(r, -1))
    x_swap = lambda array: permuted(array, lambda g, r: g * owners + (r ^ 2))
    y_swap = lambda array: permuted(array, lambda g, r: (1 - g) * owners + r)
    core_swap = lambda array: permuted(array, lambda g, r: g * owners + (r ^ 1))

    def chip(r, piece):
        return (along_z(r, -piece[0]) ^ (2 * piece[1])) // 2

    kernels = [PIECES[low:high] for low, high in zip(KERNEL_BOUNDS, KERNEL_BOUNDS[1:])]
    info_table = [
        [g, r % 2]
        + [
            chip(r, p) * LANES + core * held * rank + (g ^ p[2]) * (held // 2 * rank)
            for pieces in kernels
            for core in (r % 2, 1 - r % 2)
            for p in pieces
        ]
        + [chip(r, p) for p in PIECES]
        for g in range(planes)
        for r in range(owners)
    ]
    info = lax.dynamic_index_in_dim(
        jnp.array(np.array(info_table, np.int32)), device, 0, keepdims=False
    )

    def together(*values):
        return lax.optimization_barrier(values)

    def after(value, *others):
        return lax.optimization_barrier((value, *others))[0]

    there = core_swap(adapter_down_weight)
    row_slot = slots_of_rows(row_adapter_index, adapter_storage_slot)
    there, info, row_slot, tokens_late = together(there, info, row_slot, tokens)

    def piece(back, *others):
        return assemble(
            back, after(info, *others), adapter_down_weight, there, adapter_up_weight
        )

    front = piece(0)
    cuts = (0, 3 * DEPTH_TILE, 6 * DEPTH_TILE, depth)

    def base(number, before, *others):
        low, high = cuts[number : number + 2]
        return base_part(after(tokens, *others), base_value_weight, low, high, before)

    z1, x0 = z_ring(front), x_swap(front)
    other = core_swap(tokens_late)
    other_slot = core_swap(row_slot[:, 0])
    total = base(0, None, front)
    row_slots = jnp.concatenate([row_slot, other_slot[:, None]], axis=0)

    z2 = z_ring(after(z1, total))
    x1 = x_swap(after(z1, x0, total))
    yx0 = y_swap(after(x0, total))
    total = base(1, total, z1, x0, total, row_slots)

    z3 = z_back(after(front, z2, total))
    x2 = x_swap(after(z2, x1, total))
    yz2 = y_swap(after(z2, yx0, total))
    back = piece(1, z2, x1, yx0, total)
    total = base(2, total, z2, x1, yx0, back, other)

    def update(number, groups, before, *others):
        return absorb(
            after(info, *others),
            row_slots,
            (0, 1),
            [tokens, other],
            width,
            groups,
            KERNEL_BOUNDS[number],
            before,
            True,
        )

    zb1 = z_ring(after(back, z3, total))
    x3 = x_swap(after(z3, x2, total))
    yx1 = y_swap(after(x1, yz2, total))
    *state, up_a = update(0, [((front, z1, x0, z2), 0)], None, z3, x2, yz2, total)
    there_a = core_swap(up_a)

    zb3 = z_back(after(back, state[0]))
    xyz2 = x_swap(after(yz2, x3, state[0]))
    yx3 = y_swap(after(x3, yx1, state[0]))
    *state, up_b = update(
        1,
        [((x1, z3, x2, x3), 0), ((back, yx0, yz2, zb1, yx1), 1)],
        state,
        zb1,
        x3,
        yx1,
        there_a,
    )
    there_b = core_swap(up_b)

    mine, others, up_c = update(2, [((zb3, xyz2, yx3), 1)], state)
    ups = (up_a, there_a, up_b, there_b, up_c, core_swap(up_c))
    return finish(info, row_slots, mine, core_swap(others), total, ups)


def solution(mesh):
    placed = (
        P(("groups", "req"), "tp"),
        P(("groups", "req"), None),
        P(),
        P("tp", None),
        P("req", None, "tp"),
        P("req", None, "tp"),
    )
    sizes = mesh.shape
    small = sizes["groups"] == 2 and sizes["req"] == 16 and sizes["tp"] == 1
    return jax.shard_map(
        passed_round if small else gathered,
        mesh=mesh,
        in_specs=placed,
        out_specs=P(("groups", "req"), "tp"),
        check_vma=False,
    )
```

```python
import functools

import jax
import jax.numpy as jnp
import numpy as np
from jax import lax
from jax.experimental import pallas as pl
from jax.experimental.pallas import tpu as pltpu
from jax.sharding import PartitionSpec as P

RING = (0, 1, 3, 2)
PLACE_IN_RING = (0, 1, 3, 2)
DEPTH_TILE = 1024
LANES = 128
RANK = 16

PIECES = (
    *((0, 0, 0), (1, 0, 0), (0, 1, 0), (2, 0, 0)),
    *((0, 0, 1), (0, 1, 1), (2, 0, 1)),
    *((1, 1, 0), (3, 0, 0), (2, 1, 0), (3, 1, 0), (1, 0, 1), (1, 1, 1)),
    *((3, 0, 1), (2, 1, 1), (3, 1, 1)),
)
KERNEL_BOUNDS = (0, 4, 7, 13, 16)
QUARTER_CUTS = (0, 512, 1024, 2048)
VMEM_BYTES = 64 * 1024 * 1024 - 512 * 1024


def slots_of_rows(row_adapter_index, adapter_storage_slot):
    catalog = jnp.arange(adapter_storage_slot.shape[0], dtype=jnp.int32)
    return jnp.sum(
        jnp.where(row_adapter_index == catalog[None, :], adapter_storage_slot[None, :], 0),
        axis=1,
        keepdims=True,
    )


def gathered(
    tokens,
    row_adapter_index,
    adapter_storage_slot,
    base_value_weight,
    adapter_down_weight,
    adapter_up_weight,
):
    adapter_count = adapter_storage_slot.shape[0]
    rank = adapter_down_weight.shape[1]
    slot_of = slots_of_rows(row_adapter_index, adapter_storage_slot)
    down_all = lax.all_gather(
        adapter_down_weight.reshape(-1, adapter_down_weight.shape[2]), "req", axis=0, tiled=True
    )
    up_all = lax.all_gather(
        adapter_up_weight.reshape(-1, adapter_up_weight.shape[2]), "req", axis=0, tiled=True
    )
    base_partial = jnp.dot(tokens, base_value_weight, preferred_element_type=jnp.float32)
    base_output = lax.psum_scatter(base_partial, "tp", scatter_dimension=1, tiled=True)
    shrink = lax.dot_general(
        tokens, down_all, (((1,), (1,)), ((), ())), preferred_element_type=jnp.float32
    )
    column_slot = jnp.arange(adapter_count * rank, dtype=jnp.int32) // rank
    shrink = jnp.where(slot_of == column_slot[None, :], shrink, 0.0)
    shrink = lax.psum(shrink, "tp")
    high = lax.reduce_precision(shrink, 8, 7)
    rest = shrink - high
    middle = lax.reduce_precision(rest, 8, 7)
    low = rest - middle
    lora = sum(
        jnp.dot(piece.astype(jnp.bfloat16), up_all, preferred_element_type=jnp.float32)
        for piece in (low, middle, high)
    )
    return (base_output + lora).astype(jnp.bfloat16)


def params():
    return pltpu.CompilerParams(vmem_limit_bytes=VMEM_BYTES)


def started(copies):
    for copy in copies:
        copy.start()


def awaited(copies):
    for copy in copies:
        copy.wait()


def assemble_kernel(back, info_ref, here_ref, there_ref, up_ref, out_ref, down_ref, sems):
    y, core = info_ref[0], info_ref[1]
    place = 1 - y if back else y
    held, rank, quarter = down_ref.shape
    held //= 2
    columns = pl.ds(pl.multiple_of((2 * core + place) * quarter, quarter), quarter)
    copies = [
        pltpu.make_async_copy(
            source.at[:, :, columns], down_ref.at[pl.ds(of_core * held, held)], sems.at[n]
        )
        for n, (source, of_core) in enumerate(((here_ref, core), (there_ref, 1 - core)))
    ]
    started(copies)
    up = up_ref[pl.ds(place * (held // 2), held // 2)].reshape(held // 2 * rank, -1)
    rows = up.shape[0]
    for n in range(up.shape[1] // LANES):
        first = quarter + n * rows
        out_ref[first : first + rows] = up[:, n * LANES : (n + 1) * LANES]
    awaited(copies)
    for n in range(0, quarter, LANES):
        block = down_ref[:, :, n : n + LANES].reshape(2 * held * rank, LANES)
        out_ref[n : n + LANES] = block.T


def assemble(back, info, here, there, up):
    held, rank, depth = here.shape
    width = up.shape[2]
    rows = depth // 4 + held // 2 * rank * width // LANES
    anywhere = pl.BlockSpec(memory_space=pl.ANY)
    vmem = pl.BlockSpec(memory_space=pltpu.VMEM)
    return pl.pallas_call(
        functools.partial(assemble_kernel, back),
        out_shape=jax.ShapeDtypeStruct((rows, LANES), here.dtype),
        in_specs=[pl.BlockSpec(memory_space=pltpu.SMEM), anywhere, anywhere, vmem],
        out_specs=vmem,
        scratch_shapes=[
            pltpu.VMEM((2 * held, rank, depth // 4), here.dtype),
            pltpu.SemaphoreType.DMA((2,)),
        ],
        compiler_params=params(),
    )(info, here, there, up)


def base_kernel(steps, tokens_ref, weight_ref, *refs):
    step = pl.program_id(0)
    more = len(refs) > 1
    out_ref = refs[1] if more else refs[0]
    copies = [pltpu.make_async_copy(refs[0], refs[2], refs[3].at[0])] if more else []
    part = jnp.dot(tokens_ref[...], weight_ref[...], preferred_element_type=jnp.float32)

    @pl.when(step == 0)
    def _():
        started(copies)
        out_ref[...] = part

    @pl.when(step > 0)
    def _():
        out_ref[...] += part

    if more:

        @pl.when(step == steps - 1)
        def _():
            awaited(copies)
            out_ref[...] += refs[2][...]


def base_part(tokens, weight, begin, end, total=None):
    rows, depth = tokens.shape
    width = weight.shape[1]
    steps, first = (end - begin) // DEPTH_TILE, begin // DEPTH_TILE
    result = jax.ShapeDtypeStruct((rows, width), jnp.float32)
    more = total is not None
    return pl.pallas_call(
        functools.partial(base_kernel, steps),
        out_shape=result,
        grid=(steps,),
        in_specs=[
            pl.BlockSpec((rows, DEPTH_TILE), lambda k: (0, first + k)),
            pl.BlockSpec((DEPTH_TILE, width), lambda k: (first + k, 0)),
        ]
        + [pl.BlockSpec(memory_space=pl.ANY)] * more,
        out_specs=pl.BlockSpec((rows, width), lambda k: (0, 0)),
        scratch_shapes=[pltpu.VMEM((rows, width), jnp.float32), pltpu.SemaphoreType.DMA((1,))]
        if more
        else [],
        cost_estimate=pl.CostEstimate(
            flops=2 * rows * width * (end - begin),
            bytes_accessed=2 * (rows + width) * (end - begin) + 4 * rows * width,
            transcendentals=0,
        ),
        compiler_params=params(),
    )(tokens, weight, *([total] if more else []))


def absorb_kernel(groups, start, sides, more, has_up, info_ref, row_slot_ref, *refs):
    count = sum(size for size, _ in groups)
    token_refs, sources, refs = refs[: len(sides)], refs[len(sides) :][:count], refs[len(sides) + count :]
    before, refs = refs[: len(sides) * more], refs[len(sides) * more :]
    outs, refs = refs[: len(sides)], refs[len(sides) :]
    up_ref, refs = (refs[0], refs[1:]) if has_up else (None, refs)
    rows_ref, down_refs, sems = refs[0], refs[1:-1], refs[-1]
    rows = token_refs[0].shape[0]
    quarter = rows_ref.shape[2]
    y, core = info_ref[0], info_ref[1]
    cuts = list(zip(QUARTER_CUTS, QUARTER_CUTS[1:]))
    copies, waits = [], {}

    def begin(key, source, target):
        copy = pltpu.make_async_copy(source, target, sems.at[len(copies)])
        copies.append(copy)
        waits.setdefault(key, []).append(copy)
        copy.start()

    places = {}
    first = 0
    for n, ((size, back), down_ref) in enumerate(zip(groups, down_refs)):
        load = back not in places
        place = places.setdefault(back, len(places))
        ends = cuts + [(quarter, sources[0].shape[0])] * has_up
        for low, high in ends:
            for i in range(size):
                begin(
                    (n, low),
                    sources[first + i].at[pl.ds(low, high - low)],
                    down_ref.at[pl.ds(low, high - low), pl.ds(i * LANES, LANES)],
                )
            if not load or low == quarter:
                continue
            for i, source in enumerate(token_refs):
                column = (2 * core + (1 - y if back else y)) * quarter + low
                begin(
                    (n, low),
                    source.at[:, pl.ds(pl.multiple_of(column, QUARTER_CUTS[1]), high - low)],
                    rows_ref.at[place, pl.ds(i * rows, rows), pl.ds(low, high - low)],
                )
        first += size
    lane_slot = lax.broadcasted_iota(jnp.int32, (1, LANES), 1) // RANK
    row_slot = jnp.concatenate(
        [row_slot_ref[side * rows : (side + 1) * rows] for side in sides], axis=0
    )
    state = None
    first = 0
    for n, ((size, back), down_ref) in enumerate(zip(groups, down_refs)):
        shrink = None
        for low, high in cuts:
            awaited(waits[n, low])
            part = jnp.dot(
                rows_ref[places[back], :, low:high],
                down_ref[low:high],
                preferred_element_type=jnp.float32,
            )
            shrink = part if shrink is None else shrink + part
        for i in range(size):
            lanes, which = slice(i * LANES, (i + 1) * LANES), first + i
            chip = info_ref[2 + 2 * len(PIECES) + start + which]
            wanted = lane_slot + chip * (LANES // RANK)
            kept = jnp.where(row_slot == wanted, shrink[:, lanes], 0.0)
            state = kept if state is None else state + kept
        if has_up:
            awaited(waits[n, quarter])
            height = up_ref.shape[0] // count
            for i in range(size):
                lanes, which = slice(i * LANES, (i + 1) * LANES), first + i
                for j in range(up_ref.shape[1] // LANES):
                    top = quarter + j * height
                    up_ref[
                        which * height : (which + 1) * height, j * LANES : (j + 1) * LANES
                    ] = down_ref[top : top + height, lanes]
        first += size
    for i, out_ref in enumerate(outs):
        own = state[i * rows : (i + 1) * rows]
        out_ref[...] = own + before[i][...] if more else own


def absorb(info, row_slots, sides, tokens, width, groups, start, before, has_up):
    rows = tokens[0].shape[0]
    pieces = [piece for group, _ in groups for piece in group]
    sizes = [(len(group), back) for group, back in groups]
    quarter = tokens[0].shape[1] // 4
    height = pieces[0].shape[0]
    anywhere = pl.BlockSpec(memory_space=pl.ANY)
    vmem = pl.BlockSpec(memory_space=pltpu.VMEM)
    more = before is not None
    state = jax.ShapeDtypeStruct((rows, LANES), jnp.float32)
    up_rows = len(pieces) * (height - quarter) * LANES // width
    up = jax.ShapeDtypeStruct((up_rows, width), tokens[0].dtype)
    quarters = len({back for _, back in groups})
    cuts = len(QUARTER_CUTS) - 1
    copies = len(pieces) * (cuts + has_up) + len(sides) * quarters * cuts
    outs = (state,) * len(sides) + (up,) * has_up
    return pl.pallas_call(
        functools.partial(absorb_kernel, sizes, start, sides, more, has_up),
        out_shape=outs,
        in_specs=[pl.BlockSpec(memory_space=pltpu.SMEM), vmem]
        + [anywhere] * (len(sides) + len(pieces))
        + [vmem] * (len(sides) * more),
        out_specs=(vmem,) * len(outs),
        scratch_shapes=[pltpu.VMEM((quarters, len(sides) * rows, quarter), tokens[0].dtype)]
        + [pltpu.VMEM((height, size * LANES), tokens[0].dtype) for size, _ in sizes]
        + [pltpu.SemaphoreType.DMA((copies,))],
        cost_estimate=pl.CostEstimate(
            flops=2 * len(sides) * rows * len(pieces) * LANES * quarter,
            bytes_accessed=2 * len(sides) * rows * quarters * quarter
            + 2 * len(pieces) * LANES * height,
            transcendentals=0,
        ),
        compiler_params=params(),
    )(info, row_slots, *tokens, *pieces, *(before or ()))


def finish_kernel(count, info_ref, row_slot_ref, mine_ref, theirs_ref, total_ref, *refs):
    sources, refs = refs[:count], refs[count:]
    out_ref, row_slot, mine, theirs, total, up, sems = refs
    rows = out_ref.shape[0]
    height = up.shape[0] // (len(PIECES) * 2)
    copies = []

    def begin(source, target):
        copies.append(pltpu.make_async_copy(source, target, sems.at[len(copies)]))
        copies[-1].start()

    begin(row_slot_ref.at[pl.ds(0, rows)], row_slot)
    begin(mine_ref, mine)
    begin(theirs_ref, theirs)
    begin(total_ref, total)
    for source in sources:
        for n in range(0, source.shape[0], height):
            first = pl.multiple_of(info_ref[len(copies) - 2], height)
            begin(source.at[pl.ds(n, height)], up.at[pl.ds(first, height)])
    awaited(copies[:3])
    shrink = mine[...] + theirs[...]
    lane_slot = lax.broadcasted_iota(jnp.int32, (1, LANES), 1) // RANK
    high, low = [], []
    for n in range(up.shape[0] // LANES):
        kept = jnp.where(row_slot[...] == lane_slot + n * (LANES // RANK), shrink, 0.0)
        high.append(kept.astype(jnp.bfloat16))
        low.append((kept - high[-1].astype(jnp.float32)).astype(jnp.bfloat16))
    both = jnp.concatenate([jnp.concatenate(part, axis=1) for part in (low, high)], axis=0)
    awaited(copies[3:])
    lora = jnp.dot(both, up[...], preferred_element_type=jnp.float32)
    out_ref[...] = (total[...] + (lora[:rows] + lora[rows:])).astype(out_ref.dtype)


def finish(info, row_slots, mine, theirs, total, ups):
    rows, width = total.shape
    anywhere = pl.BlockSpec(memory_space=pl.ANY)
    up_rows = sum(up.shape[0] for up in ups)
    return pl.pallas_call(
        functools.partial(finish_kernel, len(ups)),
        out_shape=jax.ShapeDtypeStruct((rows, width), jnp.bfloat16),
        in_specs=[pl.BlockSpec(memory_space=pltpu.SMEM)] + [anywhere] * (4 + len(ups)),
        out_specs=pl.BlockSpec(memory_space=pltpu.VMEM),
        scratch_shapes=[
            pltpu.VMEM((rows, 1), jnp.int32),
            pltpu.VMEM((rows, LANES), jnp.float32),
            pltpu.VMEM((rows, LANES), jnp.float32),
            pltpu.VMEM((rows, width), jnp.float32),
            pltpu.VMEM((up_rows, width), ups[0].dtype),
            pltpu.SemaphoreType.DMA((4 + 2 * len(PIECES),)),
        ],
        cost_estimate=pl.CostEstimate(
            flops=4 * rows * width * up_rows,
            bytes_accessed=6 * rows * width + 2 * up_rows * width,
            transcendentals=0,
        ),
        compiler_params=params(),
    )(info, row_slots, mine, theirs, total, *ups)


def passed_round(
    tokens,
    row_adapter_index,
    adapter_storage_slot,
    base_value_weight,
    adapter_down_weight,
    adapter_up_weight,
):
    rows, depth = tokens.shape
    held, rank, _ = adapter_down_weight.shape
    width = adapter_up_weight.shape[2]
    axes = ("groups", "req")
    planes, owners = lax.axis_size("groups"), lax.axis_size("req")
    device = lax.axis_index("groups") * owners + lax.axis_index("req")

    def permuted(array, target):
        pairs = [
            (g * owners + r, target(g, r)) for g in range(planes) for r in range(owners)
        ]
        return lax.ppermute(array, axes, pairs)

    def along_z(r, by):
        return RING[(PLACE_IN_RING[r // 4] + by) % 4] * 4 + r % 4

    z_ring = lambda array: permuted(array, lambda g, r: g * owners + along_z(r, 1))
    z_back = lambda array: permuted(array, lambda g, r: g * owners + along_z(r, -1))
    x_swap = lambda array: permuted(array, lambda g, r: g * owners + (r ^ 2))
    y_swap = lambda array: permuted(array, lambda g, r: (1 - g) * owners + r)
    core_swap = lambda array: permuted(array, lambda g, r: g * owners + (r ^ 1))

    def chip(r, piece):
        return (along_z(r, -piece[0]) ^ (2 * piece[1])) // 2

    kernels = [PIECES[low:high] for low, high in zip(KERNEL_BOUNDS, KERNEL_BOUNDS[1:])]
    info_table = [
        [g, r % 2]
        + [
            chip(r, p) * LANES + core * held * rank + (g ^ p[2]) * (held // 2 * rank)
            for pieces in kernels
            for core in (r % 2, 1 - r % 2)
            for p in pieces
        ]
        + [chip(r, p) for p in PIECES]
        for g in range(planes)
        for r in range(owners)
    ]
    info = lax.dynamic_index_in_dim(
        jnp.array(np.array(info_table, np.int32)), device, 0, keepdims=False
    )

    def together(*values):
        return lax.optimization_barrier(values)

    def after(value, *others):
        return lax.optimization_barrier((value, *others))[0]

    there = core_swap(adapter_down_weight)
    row_slot = slots_of_rows(row_adapter_index, adapter_storage_slot)
    there, info, row_slot, tokens_late = together(there, info, row_slot, tokens)

    def piece(back, *others):
        return assemble(
            back, after(info, *others), adapter_down_weight, there, adapter_up_weight
        )

    front = piece(0)
    cuts = (0, depth // 2, depth)

    def base(number, before, *others):
        low, high = cuts[number : number + 2]
        return base_part(after(tokens, *others), base_value_weight, low, high, before)

    z1, x0 = z_ring(front), x_swap(front)
    other = core_swap(tokens_late)
    other_slot = core_swap(row_slot[:, 0])
    total = base(0, None, front)
    row_slots = jnp.concatenate([row_slot, other_slot[:, None]], axis=0)

    z2 = z_ring(after(z1, total))
    x1 = x_swap(after(z1, x0, total))
    yx0 = y_swap(after(x0, total))
    total = base(1, total, z1, x0, total, row_slots)

    def update(number, groups, before, *others):
        return absorb(
            after(info, *others),
            row_slots,
            (0, 1),
            [tokens, other],
            width,
            groups,
            KERNEL_BOUNDS[number],
            before,
            True,
        )

    z3 = z_back(after(front, z2, total))
    x2 = x_swap(after(z2, x1, total))
    yz2 = y_swap(after(z2, yx0, total))
    back = piece(1, z2, x1, yx0, total, other)
    *state, up_a = update(0, [((front, z1, x0, z2), 0)], None, x1, yx0, total, back)
    there_a = core_swap(up_a)

    zb1 = z_ring(after(back, z3, state[0]))
    x3 = x_swap(after(z3, x2, state[0]))
    yx1 = y_swap(after(x1, yz2, state[0]))
    *state, up_b = update(1, [((back, yx0, yz2), 1)], state, z3, x2, there_a)
    there_b = core_swap(up_b)

    zb3 = z_back(after(back, zb1, state[0]))
    xyz2 = x_swap(after(yz2, x3, state[0]))
    yx3 = y_swap(after(x3, yx1, state[0]))
    *state, up_c = update(
        2,
        [((x1, z3, x2, x3), 0), ((zb1, yx1), 1)],
        state,
        there_b,
    )
    there_c = core_swap(up_c)

    mine, others, up_d = update(3, [((zb3, xyz2, yx3), 1)], state)
    ups = (up_a, there_a, up_b, there_b, up_c, there_c, up_d, core_swap(up_d))
    return finish(info, row_slots, mine, core_swap(others), total, ups)


def solution(mesh):
    placed = (
        P(("groups", "req"), "tp"),
        P(("groups", "req"), None),
        P(),
        P("tp", None),
        P("req", None, "tp"),
        P("req", None, "tp"),
    )
    sizes = mesh.shape
    small = sizes["groups"] == 2 and sizes["req"] == 16 and sizes["tp"] == 1
    return jax.shard_map(
        passed_round if small else gathered,
        mesh=mesh,
        in_specs=placed,
        out_specs=P(("groups", "req"), "tp"),
        check_vma=False,
    )
```

```python
import functools

import jax
import jax.numpy as jnp
import numpy as np
from jax import lax
from jax.experimental import pallas as pl
from jax.experimental.pallas import tpu as pltpu
from jax.sharding import PartitionSpec as P

RING = (0, 1, 3, 2)
PLACE_IN_RING = (0, 1, 3, 2)
DEPTH_TILE = 1024
LANES = 128
RANK = 16

PIECES = (
    *((0, 0, 0), (1, 0, 0), (0, 1, 0), (2, 0, 0)),
    *((0, 0, 1), (0, 1, 1), (2, 0, 1), (1, 1, 0), (3, 0, 0), (2, 1, 0)),
    *((3, 1, 0), (1, 0, 1), (1, 1, 1)),
    *((3, 0, 1), (2, 1, 1), (3, 1, 1)),
)
KERNEL_BOUNDS = (0, 4, 10, 13, 16)
EARLY_CHIPS = ((0, 0), (0, 1), (2, 0))
LATE_CHIPS = ((1, 0), (3, 0), (1, 1), (2, 1), (3, 1))
QUARTER_CUTS = (0, 512, 1024, 2048)
VMEM_BYTES = 64 * 1024 * 1024 - 512 * 1024


def slots_of_rows(row_adapter_index, adapter_storage_slot):
    catalog = jnp.arange(adapter_storage_slot.shape[0], dtype=jnp.int32)
    return jnp.sum(
        jnp.where(row_adapter_index == catalog[None, :], adapter_storage_slot[None, :], 0),
        axis=1,
        keepdims=True,
    )


def gathered(
    tokens,
    row_adapter_index,
    adapter_storage_slot,
    base_value_weight,
    adapter_down_weight,
    adapter_up_weight,
):
    adapter_count = adapter_storage_slot.shape[0]
    rank = adapter_down_weight.shape[1]
    slot_of = slots_of_rows(row_adapter_index, adapter_storage_slot)
    down_all = lax.all_gather(
        adapter_down_weight.reshape(-1, adapter_down_weight.shape[2]), "req", axis=0, tiled=True
    )
    up_all = lax.all_gather(
        adapter_up_weight.reshape(-1, adapter_up_weight.shape[2]), "req", axis=0, tiled=True
    )
    base_partial = jnp.dot(tokens, base_value_weight, preferred_element_type=jnp.float32)
    base_output = lax.psum_scatter(base_partial, "tp", scatter_dimension=1, tiled=True)
    shrink = lax.dot_general(
        tokens, down_all, (((1,), (1,)), ((), ())), preferred_element_type=jnp.float32
    )
    column_slot = jnp.arange(adapter_count * rank, dtype=jnp.int32) // rank
    shrink = jnp.where(slot_of == column_slot[None, :], shrink, 0.0)
    shrink = lax.psum(shrink, "tp")
    high = lax.reduce_precision(shrink, 8, 7)
    rest = shrink - high
    middle = lax.reduce_precision(rest, 8, 7)
    low = rest - middle
    lora = sum(
        jnp.dot(piece.astype(jnp.bfloat16), up_all, preferred_element_type=jnp.float32)
        for piece in (low, middle, high)
    )
    return (base_output + lora).astype(jnp.bfloat16)


def params():
    return pltpu.CompilerParams(vmem_limit_bytes=VMEM_BYTES)


def started(copies):
    for copy in copies:
        copy.start()


def awaited(copies):
    for copy in copies:
        copy.wait()


def assemble_kernel(back, info_ref, here_ref, there_ref, up_ref, out_ref, down_ref, own_ref, sems):
    y, core = info_ref[0], info_ref[1]
    place = 1 - y if back else y
    held, rank, quarter = down_ref.shape
    held //= 2
    columns = pl.ds(pl.multiple_of((2 * core + place) * quarter, quarter), quarter)
    copies = [
        pltpu.make_async_copy(
            source.at[:, :, columns], down_ref.at[pl.ds(of_core * held, held)], sems.at[n]
        )
        for n, (source, of_core) in enumerate(((here_ref, core), (there_ref, 1 - core)))
    ]
    copies.append(
        pltpu.make_async_copy(up_ref.at[pl.ds(place * (held // 2), held // 2)], own_ref, sems.at[2])
    )
    started(copies)
    awaited(copies)
    up = own_ref[...].reshape(held // 2 * rank, -1)
    rows = up.shape[0]
    for n in range(up.shape[1] // LANES):
        first = quarter + n * rows
        out_ref[first : first + rows] = up[:, n * LANES : (n + 1) * LANES]
    for n in range(0, quarter, LANES):
        block = down_ref[:, :, n : n + LANES].reshape(2 * held * rank, LANES)
        out_ref[n : n + LANES] = block.T


def assemble(back, info, here, there, up):
    held, rank, depth = here.shape
    width = up.shape[2]
    rows = depth // 4 + held // 2 * rank * width // LANES
    anywhere = pl.BlockSpec(memory_space=pl.ANY)
    return pl.pallas_call(
        functools.partial(assemble_kernel, back),
        out_shape=jax.ShapeDtypeStruct((rows, LANES), here.dtype),
        in_specs=[pl.BlockSpec(memory_space=pltpu.SMEM)] + [anywhere] * 3,
        out_specs=pl.BlockSpec(memory_space=pltpu.VMEM),
        scratch_shapes=[
            pltpu.VMEM((2 * held, rank, depth // 4), here.dtype),
            pltpu.VMEM((held // 2, rank, width), up.dtype),
            pltpu.SemaphoreType.DMA((3,)),
        ],
        compiler_params=params(),
    )(info, here, there, up)


def base_kernel(steps, tokens_ref, weight_ref, *refs):
    step = pl.program_id(0)
    more = len(refs) > 1
    out_ref = refs[1] if more else refs[0]
    copies = [pltpu.make_async_copy(refs[0], refs[2], refs[3].at[0])] if more else []
    part = jnp.dot(tokens_ref[...], weight_ref[...], preferred_element_type=jnp.float32)

    @pl.when(step == 0)
    def _():
        started(copies)
        out_ref[...] = part

    @pl.when(step > 0)
    def _():
        out_ref[...] += part

    if more:

        @pl.when(step == steps - 1)
        def _():
            awaited(copies)
            out_ref[...] += refs[2][...]


def base_part(tokens, weight, begin, end, total=None):
    rows, depth = tokens.shape
    width = weight.shape[1]
    steps, first = (end - begin) // DEPTH_TILE, begin // DEPTH_TILE
    result = jax.ShapeDtypeStruct((rows, width), jnp.float32)
    more = total is not None
    return pl.pallas_call(
        functools.partial(base_kernel, steps),
        out_shape=result,
        grid=(steps,),
        in_specs=[
            pl.BlockSpec((rows, DEPTH_TILE), lambda k: (0, first + k)),
            pl.BlockSpec((DEPTH_TILE, width), lambda k: (first + k, 0)),
        ]
        + [pl.BlockSpec(memory_space=pl.ANY)] * more,
        out_specs=pl.BlockSpec((rows, width), lambda k: (0, 0)),
        scratch_shapes=[pltpu.VMEM((rows, width), jnp.float32), pltpu.SemaphoreType.DMA((1,))]
        if more
        else [],
        cost_estimate=pl.CostEstimate(
            flops=2 * rows * width * (end - begin),
            bytes_accessed=2 * (rows + width) * (end - begin) + 4 * rows * width,
            transcendentals=0,
        ),
        compiler_params=params(),
    )(tokens, weight, *([total] if more else []))


def absorb_kernel(groups, start, sides, more, has_up, info_ref, row_slot_ref, *refs):
    count = sum(size for size, _ in groups)
    token_refs, sources, refs = refs[: len(sides)], refs[len(sides) :][:count], refs[len(sides) + count :]
    before, refs = refs[: len(sides) * more], refs[len(sides) * more :]
    outs, refs = refs[: len(sides)], refs[len(sides) :]
    up_ref, refs = (refs[0], refs[1:]) if has_up else (None, refs)
    rows_ref, down_refs, sems = refs[0], refs[1:-1], refs[-1]
    rows = token_refs[0].shape[0]
    quarter = rows_ref.shape[2]
    y, core = info_ref[0], info_ref[1]
    cuts = list(zip(QUARTER_CUTS, QUARTER_CUTS[1:]))
    copies, waits = [], {}

    def begin(key, source, target):
        copy = pltpu.make_async_copy(source, target, sems.at[len(copies)])
        copies.append(copy)
        waits.setdefault(key, []).append(copy)
        copy.start()

    places = {}
    first = 0
    for n, ((size, back), down_ref) in enumerate(zip(groups, down_refs)):
        load = back not in places
        place = places.setdefault(back, len(places))
        ends = cuts + [(quarter, sources[0].shape[0])] * has_up
        for low, high in ends:
            for i in range(size):
                begin(
                    (n, low),
                    sources[first + i].at[pl.ds(low, high - low)],
                    down_ref.at[pl.ds(low, high - low), pl.ds(i * LANES, LANES)],
                )
            if not load or low == quarter:
                continue
            for i, source in enumerate(token_refs):
                column = (2 * core + (1 - y if back else y)) * quarter + low
                begin(
                    (n, low),
                    source.at[:, pl.ds(pl.multiple_of(column, QUARTER_CUTS[1]), high - low)],
                    rows_ref.at[place, pl.ds(i * rows, rows), pl.ds(low, high - low)],
                )
        first += size
    lane_slot = lax.broadcasted_iota(jnp.int32, (1, LANES), 1) // RANK
    row_slot = jnp.concatenate(
        [row_slot_ref[side * rows : (side + 1) * rows] for side in sides], axis=0
    )
    state = None
    first = 0
    for n, ((size, back), down_ref) in enumerate(zip(groups, down_refs)):
        shrink = None
        for low, high in cuts:
            awaited(waits[n, low])
            part = jnp.dot(
                rows_ref[places[back], :, low:high],
                down_ref[low:high],
                preferred_element_type=jnp.float32,
            )
            shrink = part if shrink is None else shrink + part
        for i in range(size):
            lanes, which = slice(i * LANES, (i + 1) * LANES), first + i
            chip = info_ref[2 + 2 * len(PIECES) + start + which]
            wanted = lane_slot + chip * (LANES // RANK)
            kept = jnp.where(row_slot == wanted, shrink[:, lanes], 0.0)
            state = kept if state is None else state + kept
        if has_up:
            awaited(waits[n, quarter])
            height = up_ref.shape[0] // count
            for i in range(size):
                lanes, which = slice(i * LANES, (i + 1) * LANES), first + i
                for j in range(up_ref.shape[1] // LANES):
                    top = quarter + j * height
                    up_ref[
                        which * height : (which + 1) * height, j * LANES : (j + 1) * LANES
                    ] = down_ref[top : top + height, lanes]
        first += size
    for i, out_ref in enumerate(outs):
        own = state[i * rows : (i + 1) * rows]
        out_ref[...] = own + before[i][...] if more else own


def absorb(info, row_slots, sides, tokens, width, groups, start, before, has_up):
    rows = tokens[0].shape[0]
    pieces = [piece for group, _ in groups for piece in group]
    sizes = [(len(group), back) for group, back in groups]
    quarter = tokens[0].shape[1] // 4
    height = pieces[0].shape[0]
    anywhere = pl.BlockSpec(memory_space=pl.ANY)
    vmem = pl.BlockSpec(memory_space=pltpu.VMEM)
    more = before is not None
    state = jax.ShapeDtypeStruct((rows, LANES), jnp.float32)
    up_rows = len(pieces) * (height - quarter) * LANES // width
    up = jax.ShapeDtypeStruct((up_rows, width), tokens[0].dtype)
    quarters = len({back for _, back in groups})
    cuts = len(QUARTER_CUTS) - 1
    copies = len(pieces) * (cuts + has_up) + len(sides) * quarters * cuts
    outs = (state,) * len(sides) + (up,) * has_up
    return pl.pallas_call(
        functools.partial(absorb_kernel, sizes, start, sides, more, has_up),
        out_shape=outs,
        in_specs=[pl.BlockSpec(memory_space=pltpu.SMEM), vmem]
        + [anywhere] * (len(sides) + len(pieces))
        + [vmem] * (len(sides) * more),
        out_specs=(vmem,) * len(outs),
        scratch_shapes=[pltpu.VMEM((quarters, len(sides) * rows, quarter), tokens[0].dtype)]
        + [pltpu.VMEM((height, size * LANES), tokens[0].dtype) for size, _ in sizes]
        + [pltpu.SemaphoreType.DMA((copies,))],
        cost_estimate=pl.CostEstimate(
            flops=2 * len(sides) * rows * len(pieces) * LANES * quarter,
            bytes_accessed=2 * len(sides) * rows * quarters * quarter
            + 2 * len(pieces) * LANES * height,
            transcendentals=0,
        ),
        compiler_params=params(),
    )(info, row_slots, *tokens, *pieces, *(before or ()))


def expand_kernel(
    count, chips, blocks, info_ref, row_slot_ref, mine_ref, theirs_ref, total_ref, *refs
):
    sources, refs = refs[:count], refs[count:]
    out_ref, row_slot, mine, theirs, total, up, sems = refs
    rows = out_ref.shape[0]
    height = LANES // 4
    copies = []

    def begin(source, target):
        copies.append(pltpu.make_async_copy(source, target, sems.at[len(copies)]))
        copies[-1].start()

    begin(row_slot_ref.at[pl.ds(0, rows)], row_slot)
    begin(mine_ref, mine)
    begin(theirs_ref, theirs)
    begin(total_ref, total)
    for array, at, chip, which in blocks:
        first = pl.multiple_of(chip * LANES + info_ref[which], height)
        begin(sources[array].at[pl.ds(at * height, height)], up.at[pl.ds(first, height)])
    awaited(copies[:3])
    shrink = mine[...] + theirs[...]
    lane_slot = lax.broadcasted_iota(jnp.int32, (1, LANES), 1) // RANK
    high, low = [], []
    for which in chips:
        wanted = lane_slot + info_ref[which] * (LANES // RANK)
        kept = jnp.where(row_slot[...] == wanted, shrink, 0.0)
        high.append(kept.astype(jnp.bfloat16))
        low.append((kept - high[-1].astype(jnp.float32)).astype(jnp.bfloat16))
    both = jnp.concatenate([jnp.concatenate(part, axis=1) for part in (low, high)], axis=0)
    awaited(copies[3:])
    lora = jnp.dot(both, up[...], preferred_element_type=jnp.float32)
    out_ref[...] = (total[...] + (lora[:rows] + lora[rows:])).astype(out_ref.dtype)


def expand(info, row_slots, mine, theirs, total, ups, chips, out_dtype):
    rows, width = total.shape
    anywhere = pl.BlockSpec(memory_space=pl.ANY)
    blocks, chip_places = [], []
    for kernel, (low, high) in enumerate(zip(KERNEL_BOUNDS, KERNEL_BOUNDS[1:])):
        for n in range(low, high):
            if PIECES[n][:2] in chips:
                for side in (0, 1):
                    blocks.append(
                        (2 * kernel + side, n - low, chips.index(PIECES[n][:2]), 2 + 2 * n + side)
                    )
    for chip in chips:
        chip_places.append(2 + 2 * len(PIECES) + PIECES.index((*chip, 0)))
    arrays = [array for pair in ups for array in pair]
    up_rows = len(chips) * LANES
    return pl.pallas_call(
        functools.partial(expand_kernel, len(arrays), chip_places, blocks),
        out_shape=jax.ShapeDtypeStruct((rows, width), out_dtype),
        in_specs=[pl.BlockSpec(memory_space=pltpu.SMEM)] + [anywhere] * (4 + len(arrays)),
        out_specs=pl.BlockSpec(memory_space=pltpu.VMEM),
        scratch_shapes=[
            pltpu.VMEM((rows, 1), jnp.int32),
            pltpu.VMEM((rows, LANES), jnp.float32),
            pltpu.VMEM((rows, LANES), jnp.float32),
            pltpu.VMEM((rows, width), jnp.float32),
            pltpu.VMEM((up_rows, width), arrays[0].dtype),
            pltpu.SemaphoreType.DMA((4 + len(blocks),)),
        ],
        cost_estimate=pl.CostEstimate(
            flops=4 * rows * width * up_rows,
            bytes_accessed=8 * rows * width + 2 * up_rows * width,
            transcendentals=0,
        ),
        compiler_params=params(),
    )(info, row_slots, mine, theirs, total, *arrays)


def passed_round(
    tokens,
    row_adapter_index,
    adapter_storage_slot,
    base_value_weight,
    adapter_down_weight,
    adapter_up_weight,
):
    rows, depth = tokens.shape
    held, rank, _ = adapter_down_weight.shape
    width = adapter_up_weight.shape[2]
    axes = ("groups", "req")
    planes, owners = lax.axis_size("groups"), lax.axis_size("req")
    device = lax.axis_index("groups") * owners + lax.axis_index("req")

    def permuted(array, target):
        pairs = [
            (g * owners + r, target(g, r)) for g in range(planes) for r in range(owners)
        ]
        return lax.ppermute(array, axes, pairs)

    def along_z(r, by):
        return RING[(PLACE_IN_RING[r // 4] + by) % 4] * 4 + r % 4

    z_ring = lambda array: permuted(array, lambda g, r: g * owners + along_z(r, 1))
    z_back = lambda array: permuted(array, lambda g, r: g * owners + along_z(r, -1))
    x_swap = lambda array: permuted(array, lambda g, r: g * owners + (r ^ 2))
    y_swap = lambda array: permuted(array, lambda g, r: (1 - g) * owners + r)
    core_swap = lambda array: permuted(array, lambda g, r: g * owners + (r ^ 1))

    def chip(r, piece):
        return (along_z(r, -piece[0]) ^ (2 * piece[1])) // 2

    info_table = [
        [g, r % 2]
        + [
            core * held * rank + (g ^ p[2]) * (held // 2 * rank)
            for p in PIECES
            for core in (r % 2, 1 - r % 2)
        ]
        + [chip(r, p) for p in PIECES]
        for g in range(planes)
        for r in range(owners)
    ]
    info = lax.dynamic_index_in_dim(
        jnp.array(np.array(info_table, np.int32)), device, 0, keepdims=False
    )

    def together(*values):
        return lax.optimization_barrier(values)

    def after(value, *others):
        return lax.optimization_barrier((value, *others))[0]

    there = core_swap(adapter_down_weight)
    row_slot = slots_of_rows(row_adapter_index, adapter_storage_slot)
    there, info, row_slot, tokens_late = together(there, info, row_slot, tokens)

    def piece(back, *others):
        return assemble(
            back, after(info, *others), adapter_down_weight, there, adapter_up_weight
        )

    front = piece(0)
    cuts = (0, depth // 2, depth)

    def base(number, before, *others):
        low, high = cuts[number : number + 2]
        return base_part(after(tokens, *others), base_value_weight, low, high, before)

    z1, x0 = z_ring(front), x_swap(front)
    other = core_swap(tokens_late)
    other_slot = core_swap(row_slot[:, 0])
    total = base(0, None, front)
    row_slots = jnp.concatenate([row_slot, other_slot[:, None]], axis=0)

    z2 = z_ring(after(z1, total))
    x1 = x_swap(after(z1, x0, total))
    yx0 = y_swap(after(x0, total))
    total = base(1, total, z1, x0, total, row_slots)

    def update(number, groups, before, *others):
        return absorb(
            after(info, *others),
            row_slots,
            (0, 1),
            [tokens, other],
            width,
            groups,
            KERNEL_BOUNDS[number],
            before,
            True,
        )

    z3 = z_back(after(front, z2, total))
    x2 = x_swap(after(z2, x1, total))
    yz2 = y_swap(after(z2, yx0, total))
    back = piece(1, z2, x1, yx0, total, other)
    *state, up_a = update(0, [((front, z1, x0, z2), 0)], None, x1, yx0, total, back)
    there_a = core_swap(up_a)

    zb1 = z_ring(after(back, z3, state[0]))
    x3 = x_swap(after(z3, x2, state[0]))
    yx1 = y_swap(after(x1, yz2, state[0]))
    *state, up_b = update(
        1, [((back, yx0, yz2), 1), ((x1, z3, x2), 0)], state, there_a
    )
    there_b, theirs = core_swap(up_b), core_swap(state[1])
    early = state[0]

    zb3 = z_back(after(back, zb1, state[0]))
    xyz2 = x_swap(after(yz2, x3, state[0]))
    yx3 = y_swap(after(x3, yx1, state[0]))
    *state, up_c = update(2, [((x3,), 0), ((zb1, yx1), 1)], state)
    there_c = core_swap(up_c)
    ups = [(up_a, there_a), (up_b, there_b)]
    total = expand(
        after(info, state[0]), row_slots, early, theirs, total, ups, EARLY_CHIPS, jnp.float32
    )

    mine, others, up_d = update(3, [((zb3, xyz2, yx3), 1)], state, total, there_c)
    ups += [(up_c, there_c), (up_d, core_swap(up_d))]
    return expand(
        info, row_slots, mine, core_swap(others), total, ups, LATE_CHIPS, jnp.bfloat16
    )


def solution(mesh):
    placed = (
        P(("groups", "req"), "tp"),
        P(("groups", "req"), None),
        P(),
        P("tp", None),
        P("req", None, "tp"),
        P("req", None, "tp"),
    )
    sizes = mesh.shape
    small = sizes["groups"] == 2 and sizes["req"] == 16 and sizes["tp"] == 1
    return jax.shard_map(
        passed_round if small else gathered,
        mesh=mesh,
        in_specs=placed,
        out_specs=P(("groups", "req"), "tp"),
        check_vma=False,
    )
```

```python
import functools

import jax
import jax.numpy as jnp
import numpy as np
from jax import lax
from jax.experimental import pallas as pl
from jax.experimental.pallas import tpu as pltpu
from jax.sharding import PartitionSpec as P

RING = (0, 1, 3, 2)
PLACE_IN_RING = (0, 1, 3, 2)
DEPTH_TILE = 1024
LANES = 128
RANK = 16

PIECES = (
    *((0, 0, 0), (1, 0, 0), (0, 1, 0), (2, 0, 0)),
    *((0, 0, 1), (0, 1, 1), (2, 0, 1)),
    *((1, 1, 0), (3, 0, 0), (2, 1, 0), (3, 1, 0), (1, 0, 1), (1, 1, 1)),
    *((3, 0, 1), (2, 1, 1), (3, 1, 1)),
)
KERNEL_BOUNDS = (0, 4, 7, 13, 16)
QUARTER_CUTS = (0, 512, 1024, 2048)
VMEM_BYTES = 64 * 1024 * 1024 - 512 * 1024


def slots_of_rows(row_adapter_index, adapter_storage_slot):
    catalog = jnp.arange(adapter_storage_slot.shape[0], dtype=jnp.int32)
    return jnp.sum(
        jnp.where(row_adapter_index == catalog[None, :], adapter_storage_slot[None, :], 0),
        axis=1,
        keepdims=True,
    )


def gathered(
    tokens,
    row_adapter_index,
    adapter_storage_slot,
    base_value_weight,
    adapter_down_weight,
    adapter_up_weight,
):
    adapter_count = adapter_storage_slot.shape[0]
    rank = adapter_down_weight.shape[1]
    slot_of = slots_of_rows(row_adapter_index, adapter_storage_slot)
    down_all = lax.all_gather(
        adapter_down_weight.reshape(-1, adapter_down_weight.shape[2]), "req", axis=0, tiled=True
    )
    up_all = lax.all_gather(
        adapter_up_weight.reshape(-1, adapter_up_weight.shape[2]), "req", axis=0, tiled=True
    )
    base_partial = jnp.dot(tokens, base_value_weight, preferred_element_type=jnp.float32)
    base_output = lax.psum_scatter(base_partial, "tp", scatter_dimension=1, tiled=True)
    shrink = lax.dot_general(
        tokens, down_all, (((1,), (1,)), ((), ())), preferred_element_type=jnp.float32
    )
    column_slot = jnp.arange(adapter_count * rank, dtype=jnp.int32) // rank
    shrink = jnp.where(slot_of == column_slot[None, :], shrink, 0.0)
    shrink = lax.psum(shrink, "tp")
    high = lax.reduce_precision(shrink, 8, 7)
    rest = shrink - high
    middle = lax.reduce_precision(rest, 8, 7)
    low = rest - middle
    lora = sum(
        jnp.dot(piece.astype(jnp.bfloat16), up_all, preferred_element_type=jnp.float32)
        for piece in (low, middle, high)
    )
    return (base_output + lora).astype(jnp.bfloat16)


def params():
    return pltpu.CompilerParams(vmem_limit_bytes=VMEM_BYTES)


def started(copies):
    for copy in copies:
        copy.start()


def awaited(copies):
    for copy in copies:
        copy.wait()


def assemble_kernel(back, info_ref, here_ref, there_ref, up_ref, out_ref, down_ref, own_ref, sems):
    y, core = info_ref[0], info_ref[1]
    place = 1 - y if back else y
    held, rank, quarter = down_ref.shape
    held //= 2
    columns = pl.ds(pl.multiple_of((2 * core + place) * quarter, quarter), quarter)
    copies = [
        pltpu.make_async_copy(
            source.at[:, :, columns], down_ref.at[pl.ds(of_core * held, held)], sems.at[n]
        )
        for n, (source, of_core) in enumerate(((here_ref, core), (there_ref, 1 - core)))
    ]
    copies.append(
        pltpu.make_async_copy(up_ref.at[pl.ds(place * (held // 2), held // 2)], own_ref, sems.at[2])
    )
    started(copies)
    awaited(copies)
    up = own_ref[...].reshape(held // 2 * rank, -1)
    rows = up.shape[0]
    for n in range(up.shape[1] // LANES):
        first = quarter + n * rows
        out_ref[first : first + rows] = up[:, n * LANES : (n + 1) * LANES]
    for n in range(0, quarter, LANES):
        block = down_ref[:, :, n : n + LANES].reshape(2 * held * rank, LANES)
        out_ref[n : n + LANES] = block.T


def assemble(back, info, here, there, up):
    held, rank, depth = here.shape
    width = up.shape[2]
    rows = depth // 4 + held // 2 * rank * width // LANES
    anywhere = pl.BlockSpec(memory_space=pl.ANY)
    return pl.pallas_call(
        functools.partial(assemble_kernel, back),
        out_shape=jax.ShapeDtypeStruct((rows, LANES), here.dtype),
        in_specs=[pl.BlockSpec(memory_space=pltpu.SMEM)] + [anywhere] * 3,
        out_specs=pl.BlockSpec(memory_space=pltpu.VMEM),
        scratch_shapes=[
            pltpu.VMEM((2 * held, rank, depth // 4), here.dtype),
            pltpu.VMEM((held // 2, rank, width), up.dtype),
            pltpu.SemaphoreType.DMA((3,)),
        ],
        compiler_params=params(),
    )(info, here, there, up)


def base_kernel(steps, tokens_ref, weight_ref, *refs):
    step = pl.program_id(0)
    more = len(refs) > 1
    out_ref = refs[1] if more else refs[0]
    copies = [pltpu.make_async_copy(refs[0], refs[2], refs[3].at[0])] if more else []
    part = jnp.dot(tokens_ref[...], weight_ref[...], preferred_element_type=jnp.float32)

    @pl.when(step == 0)
    def _():
        started(copies)
        out_ref[...] = part

    @pl.when(step > 0)
    def _():
        out_ref[...] += part

    if more:

        @pl.when(step == steps - 1)
        def _():
            awaited(copies)
            out_ref[...] += refs[2][...]


def base_part(tokens, weight, begin, end, total=None):
    rows, depth = tokens.shape
    width = weight.shape[1]
    steps, first = (end - begin) // DEPTH_TILE, begin // DEPTH_TILE
    result = jax.ShapeDtypeStruct((rows, width), jnp.float32)
    more = total is not None
    return pl.pallas_call(
        functools.partial(base_kernel, steps),
        out_shape=result,
        grid=(steps,),
        in_specs=[
            pl.BlockSpec((rows, DEPTH_TILE), lambda k: (0, first + k)),
            pl.BlockSpec((DEPTH_TILE, width), lambda k: (first + k, 0)),
        ]
        + [pl.BlockSpec(memory_space=pl.ANY)] * more,
        out_specs=pl.BlockSpec((rows, width), lambda k: (0, 0)),
        scratch_shapes=[pltpu.VMEM((rows, width), jnp.float32), pltpu.SemaphoreType.DMA((1,))]
        if more
        else [],
        cost_estimate=pl.CostEstimate(
            flops=2 * rows * width * (end - begin),
            bytes_accessed=2 * (rows + width) * (end - begin) + 4 * rows * width,
            transcendentals=0,
        ),
        compiler_params=params(),
    )(tokens, weight, *([total] if more else []))


def absorb_kernel(groups, start, sides, more, has_up, info_ref, row_slot_ref, *refs):
    count = sum(size for size, _ in groups)
    token_refs, sources, refs = refs[: len(sides)], refs[len(sides) :][:count], refs[len(sides) + count :]
    before, refs = refs[: len(sides) * more], refs[len(sides) * more :]
    outs, refs = refs[: len(sides)], refs[len(sides) :]
    up_ref, refs = (refs[0], refs[1:]) if has_up else (None, refs)
    rows_ref, down_refs, sems = refs[0], refs[1:-1], refs[-1]
    rows = token_refs[0].shape[0]
    quarter = rows_ref.shape[2]
    y, core = info_ref[0], info_ref[1]
    cuts = list(zip(QUARTER_CUTS, QUARTER_CUTS[1:]))
    copies, waits = [], {}

    def begin(key, source, target):
        copy = pltpu.make_async_copy(source, target, sems.at[len(copies)])
        copies.append(copy)
        waits.setdefault(key, []).append(copy)
        copy.start()

    places = {}
    first = 0
    for n, ((size, back), down_ref) in enumerate(zip(groups, down_refs)):
        load = back not in places
        place = places.setdefault(back, len(places))
        ends = cuts + [(quarter, sources[0].shape[0])] * has_up
        for low, high in ends:
            for i in range(size):
                begin(
                    (n, low),
                    sources[first + i].at[pl.ds(low, high - low)],
                    down_ref.at[pl.ds(low, high - low), pl.ds(i * LANES, LANES)],
                )
            if not load or low == quarter:
                continue
            for i, source in enumerate(token_refs):
                column = (2 * core + (1 - y if back else y)) * quarter + low
                begin(
                    (n, low),
                    source.at[:, pl.ds(pl.multiple_of(column, QUARTER_CUTS[1]), high - low)],
                    rows_ref.at[place, pl.ds(i * rows, rows), pl.ds(low, high - low)],
                )
        first += size
    lane_slot = lax.broadcasted_iota(jnp.int32, (1, LANES), 1) // RANK
    row_slot = jnp.concatenate(
        [row_slot_ref[side * rows : (side + 1) * rows] for side in sides], axis=0
    )
    state = None
    first = 0
    for n, ((size, back), down_ref) in enumerate(zip(groups, down_refs)):
        shrink = None
        for low, high in cuts:
            awaited(waits[n, low])
            part = jnp.dot(
                rows_ref[places[back], :, low:high],
                down_ref[low:high],
                preferred_element_type=jnp.float32,
            )
            shrink = part if shrink is None else shrink + part
        for i in range(size):
            lanes, which = slice(i * LANES, (i + 1) * LANES), first + i
            chip = info_ref[2 + 2 * len(PIECES) + start + which]
            wanted = lane_slot + chip * (LANES // RANK)
            kept = jnp.where(row_slot == wanted, shrink[:, lanes], 0.0)
            state = kept if state is None else state + kept
        if has_up:
            awaited(waits[n, quarter])
            height = up_ref.shape[0] // count
            for i in range(size):
                lanes, which = slice(i * LANES, (i + 1) * LANES), first + i
                for j in range(up_ref.shape[1] // LANES):
                    top = quarter + j * height
                    up_ref[
                        which * height : (which + 1) * height, j * LANES : (j + 1) * LANES
                    ] = down_ref[top : top + height, lanes]
        first += size
    for i, out_ref in enumerate(outs):
        own = state[i * rows : (i + 1) * rows]
        out_ref[...] = own + before[i][...] if more else own


def absorb(info, row_slots, sides, tokens, width, groups, start, before, has_up):
    rows = tokens[0].shape[0]
    pieces = [piece for group, _ in groups for piece in group]
    sizes = [(len(group), back) for group, back in groups]
    quarter = tokens[0].shape[1] // 4
    height = pieces[0].shape[0]
    anywhere = pl.BlockSpec(memory_space=pl.ANY)
    vmem = pl.BlockSpec(memory_space=pltpu.VMEM)
    more = before is not None
    state = jax.ShapeDtypeStruct((rows, LANES), jnp.float32)
    up_rows = len(pieces) * (height - quarter) * LANES // width
    up = jax.ShapeDtypeStruct((up_rows, width), tokens[0].dtype)
    quarters = len({back for _, back in groups})
    cuts = len(QUARTER_CUTS) - 1
    copies = len(pieces) * (cuts + has_up) + len(sides) * quarters * cuts
    outs = (state,) * len(sides) + (up,) * has_up
    return pl.pallas_call(
        functools.partial(absorb_kernel, sizes, start, sides, more, has_up),
        out_shape=outs,
        in_specs=[pl.BlockSpec(memory_space=pltpu.SMEM), vmem]
        + [anywhere] * (len(sides) + len(pieces))
        + [vmem] * (len(sides) * more),
        out_specs=(vmem,) * len(outs),
        scratch_shapes=[pltpu.VMEM((quarters, len(sides) * rows, quarter), tokens[0].dtype)]
        + [pltpu.VMEM((height, size * LANES), tokens[0].dtype) for size, _ in sizes]
        + [pltpu.SemaphoreType.DMA((copies,))],
        cost_estimate=pl.CostEstimate(
            flops=2 * len(sides) * rows * len(pieces) * LANES * quarter,
            bytes_accessed=2 * len(sides) * rows * quarters * quarter
            + 2 * len(pieces) * LANES * height,
            transcendentals=0,
        ),
        compiler_params=params(),
    )(info, row_slots, *tokens, *pieces, *(before or ()))


def finish_kernel(count, info_ref, row_slot_ref, mine_ref, theirs_ref, total_ref, *refs):
    sources, refs = refs[:count], refs[count:]
    out_ref, row_slot, mine, theirs, total, up, sems = refs
    rows = out_ref.shape[0]
    height = up.shape[0] // (len(PIECES) * 2)
    copies = []

    def begin(source, target):
        copies.append(pltpu.make_async_copy(source, target, sems.at[len(copies)]))
        copies[-1].start()

    begin(row_slot_ref.at[pl.ds(0, rows)], row_slot)
    begin(mine_ref, mine)
    begin(theirs_ref, theirs)
    begin(total_ref, total)
    for source in sources:
        for n in range(0, source.shape[0], height):
            first = pl.multiple_of(info_ref[len(copies) - 2], height)
            begin(source.at[pl.ds(n, height)], up.at[pl.ds(first, height)])
    awaited(copies[:3])
    shrink = mine[...] + theirs[...]
    lane_slot = lax.broadcasted_iota(jnp.int32, (1, LANES), 1) // RANK
    high, low = [], []
    for n in range(up.shape[0] // LANES):
        kept = jnp.where(row_slot[...] == lane_slot + n * (LANES // RANK), shrink, 0.0)
        high.append(kept.astype(jnp.bfloat16))
        low.append((kept - high[-1].astype(jnp.float32)).astype(jnp.bfloat16))
    both = jnp.concatenate([jnp.concatenate(part, axis=1) for part in (low, high)], axis=0)
    awaited(copies[3:])
    lora = jnp.dot(both, up[...], preferred_element_type=jnp.float32)
    out_ref[...] = (total[...] + (lora[:rows] + lora[rows:])).astype(out_ref.dtype)


def finish(info, row_slots, mine, theirs, total, ups):
    rows, width = total.shape
    anywhere = pl.BlockSpec(memory_space=pl.ANY)
    up_rows = sum(up.shape[0] for up in ups)
    return pl.pallas_call(
        functools.partial(finish_kernel, len(ups)),
        out_shape=jax.ShapeDtypeStruct((rows, width), jnp.bfloat16),
        in_specs=[pl.BlockSpec(memory_space=pltpu.SMEM)] + [anywhere] * (4 + len(ups)),
        out_specs=pl.BlockSpec(memory_space=pltpu.VMEM),
        scratch_shapes=[
            pltpu.VMEM((rows, 1), jnp.int32),
            pltpu.VMEM((rows, LANES), jnp.float32),
            pltpu.VMEM((rows, LANES), jnp.float32),
            pltpu.VMEM((rows, width), jnp.float32),
            pltpu.VMEM((up_rows, width), ups[0].dtype),
            pltpu.SemaphoreType.DMA((4 + 2 * len(PIECES),)),
        ],
        cost_estimate=pl.CostEstimate(
            flops=4 * rows * width * up_rows,
            bytes_accessed=6 * rows * width + 2 * up_rows * width,
            transcendentals=0,
        ),
        compiler_params=params(),
    )(info, row_slots, mine, theirs, total, *ups)


def passed_round(
    tokens,
    row_adapter_index,
    adapter_storage_slot,
    base_value_weight,
    adapter_down_weight,
    adapter_up_weight,
):
    rows, depth = tokens.shape
    held, rank, _ = adapter_down_weight.shape
    width = adapter_up_weight.shape[2]
    axes = ("groups", "req")
    planes, owners = lax.axis_size("groups"), lax.axis_size("req")
    device = lax.axis_index("groups") * owners + lax.axis_index("req")

    def permuted(array, target):
        pairs = [
            (g * owners + r, target(g, r)) for g in range(planes) for r in range(owners)
        ]
        return lax.ppermute(array, axes, pairs)

    def along_z(r, by):
        return RING[(PLACE_IN_RING[r // 4] + by) % 4] * 4 + r % 4

    z_ring = lambda array: permuted(array, lambda g, r: g * owners + along_z(r, 1))
    z_back = lambda array: permuted(array, lambda g, r: g * owners + along_z(r, -1))
    x_swap = lambda array: permuted(array, lambda g, r: g * owners + (r ^ 2))
    y_swap = lambda array: permuted(array, lambda g, r: (1 - g) * owners + r)
    core_swap = lambda array: permuted(array, lambda g, r: g * owners + (r ^ 1))

    def chip(r, piece):
        return (along_z(r, -piece[0]) ^ (2 * piece[1])) // 2

    kernels = [PIECES[low:high] for low, high in zip(KERNEL_BOUNDS, KERNEL_BOUNDS[1:])]
    info_table = [
        [g, r % 2]
        + [
            chip(r, p) * LANES + core * held * rank + (g ^ p[2]) * (held // 2 * rank)
            for pieces in kernels
            for core in (r % 2, 1 - r % 2)
            for p in pieces
        ]
        + [chip(r, p) for p in PIECES]
        for g in range(planes)
        for r in range(owners)
    ]
    info = lax.dynamic_index_in_dim(
        jnp.array(np.array(info_table, np.int32)), device, 0, keepdims=False
    )

    def together(*values):
        return lax.optimization_barrier(values)

    def after(value, *others):
        return lax.optimization_barrier((value, *others))[0]

    there = core_swap(adapter_down_weight)
    row_slot = slots_of_rows(row_adapter_index, adapter_storage_slot)
    there, info, row_slot, tokens_late = together(there, info, row_slot, tokens)

    def piece(back, *others):
        return assemble(
            back, after(info, *others), adapter_down_weight, there, adapter_up_weight
        )

    front = piece(0)
    cuts = (0, depth // 2, depth)

    def base(number, before, *others):
        low, high = cuts[number : number + 2]
        return base_part(after(tokens, *others), base_value_weight, low, high, before)

    z1, x0 = z_ring(front), x_swap(front)
    other = core_swap(tokens_late)
    other_slot = core_swap(row_slot[:, 0])
    total = base(0, None, front)
    row_slots = jnp.concatenate([row_slot, other_slot[:, None]], axis=0)
    z1, x0, front, total, row_slots = together(z1, x0, front, total, row_slots)

    z2, x1, yx0 = z_ring(z1), x_swap(z1), y_swap(x0)
    total = base(1, total, total)
    z2, x1, yx0, front, other, total, info = together(z2, x1, yx0, front, other, total, info)

    def update(number, groups, before):
        return absorb(
            info,
            row_slots,
            (0, 1),
            [tokens, other],
            width,
            groups,
            KERNEL_BOUNDS[number],
            before,
            True,
        )

    z3, x2, yz2 = z_back(front), x_swap(z2), y_swap(z2)
    back = piece(1, z2)
    *state, up_a = update(0, [((front, z1, x0, z2), 0)], None)
    z3, x2, yz2, x1, back, state, total = together(z3, x2, yz2, x1, back, state, total)
    there_a = core_swap(up_a)

    zb1, x3, yx1 = z_ring(back), x_swap(z3), y_swap(x1)
    *state, up_b = update(1, [((back, yx0, yz2), 1)], state)
    zb1, x3, yx1, yz2, back, state, there_a = together(
        zb1, x3, yx1, yz2, back, state, there_a
    )
    there_b = core_swap(up_b)

    zb3, xyz2, yx3 = z_back(back), x_swap(yz2), y_swap(x3)
    *state, up_c = update(2, [((x1, z3, x2, x3), 0), ((zb1, yx1), 1)], state)
    zb3, xyz2, yx3, state, there_b = together(zb3, xyz2, yx3, state, there_b)
    there_c = core_swap(up_c)

    mine, others, up_d = update(3, [((zb3, xyz2, yx3), 1)], state)
    ups = (up_a, there_a, up_b, there_b, up_c, there_c, up_d, core_swap(up_d))
    return finish(info, row_slots, mine, core_swap(others), total, ups)


def solution(mesh):
    placed = (
        P(("groups", "req"), "tp"),
        P(("groups", "req"), None),
        P(),
        P("tp", None),
        P("req", None, "tp"),
        P("req", None, "tp"),
    )
    sizes = mesh.shape
    small = sizes["groups"] == 2 and sizes["req"] == 16 and sizes["tp"] == 1
    return jax.shard_map(
        passed_round if small else gathered,
        mesh=mesh,
        in_specs=placed,
        out_specs=P(("groups", "req"), "tp"),
        check_vma=False,
    )
```

```python
import functools

import jax
import jax.numpy as jnp
import numpy as np
from jax import lax
from jax.experimental import pallas as pl
from jax.experimental.pallas import tpu as pltpu
from jax.sharding import PartitionSpec as P

RING = (0, 1, 3, 2)
PLACE_IN_RING = (0, 1, 3, 2)
DEPTH_TILE = 1024
LANES = 128
RANK = 16

PIECES = (
    *((0, 0, 0), (1, 0, 0), (0, 1, 0), (2, 0, 0)),
    *((0, 0, 1), (0, 1, 1), (2, 0, 1)),
    *((1, 1, 0), (3, 0, 0), (2, 1, 0), (3, 1, 0), (1, 0, 1), (1, 1, 1)),
    *((3, 0, 1), (2, 1, 1), (3, 1, 1)),
)
KERNEL_BOUNDS = (0, 4, 7, 13, 16)
QUARTER_CUTS = (0, 512, 1024, 2048)
VMEM_BYTES = 64 * 1024 * 1024 - 512 * 1024


def slots_of_rows(row_adapter_index, adapter_storage_slot):
    catalog = jnp.arange(adapter_storage_slot.shape[0], dtype=jnp.int32)
    return jnp.sum(
        jnp.where(row_adapter_index == catalog[None, :], adapter_storage_slot[None, :], 0),
        axis=1,
        keepdims=True,
    )


def gathered(
    tokens,
    row_adapter_index,
    adapter_storage_slot,
    base_value_weight,
    adapter_down_weight,
    adapter_up_weight,
):
    adapter_count = adapter_storage_slot.shape[0]
    rank = adapter_down_weight.shape[1]
    slot_of = slots_of_rows(row_adapter_index, adapter_storage_slot)
    down_all = lax.all_gather(
        adapter_down_weight.reshape(-1, adapter_down_weight.shape[2]), "req", axis=0, tiled=True
    )
    up_all = lax.all_gather(
        adapter_up_weight.reshape(-1, adapter_up_weight.shape[2]), "req", axis=0, tiled=True
    )
    base_partial = jnp.dot(tokens, base_value_weight, preferred_element_type=jnp.float32)
    base_output = lax.psum_scatter(base_partial, "tp", scatter_dimension=1, tiled=True)
    shrink = lax.dot_general(
        tokens, down_all, (((1,), (1,)), ((), ())), preferred_element_type=jnp.float32
    )
    column_slot = jnp.arange(adapter_count * rank, dtype=jnp.int32) // rank
    shrink = jnp.where(slot_of == column_slot[None, :], shrink, 0.0)
    shrink = lax.psum(shrink, "tp")
    high = lax.reduce_precision(shrink, 8, 7)
    rest = shrink - high
    middle = lax.reduce_precision(rest, 8, 7)
    low = rest - middle
    lora = sum(
        jnp.dot(piece.astype(jnp.bfloat16), up_all, preferred_element_type=jnp.float32)
        for piece in (low, middle, high)
    )
    return (base_output + lora).astype(jnp.bfloat16)


def params():
    return pltpu.CompilerParams(vmem_limit_bytes=VMEM_BYTES)


def started(copies):
    for copy in copies:
        copy.start()


def awaited(copies):
    for copy in copies:
        copy.wait()


def assemble_kernel(back, info_ref, here_ref, there_ref, up_ref, out_ref, down_ref, own_ref, sems):
    y, core = info_ref[0], info_ref[1]
    place = 1 - y if back else y
    held, rank, quarter = down_ref.shape
    held //= 2
    columns = pl.ds(pl.multiple_of((2 * core + place) * quarter, quarter), quarter)
    copies = [
        pltpu.make_async_copy(
            source.at[:, :, columns], down_ref.at[pl.ds(of_core * held, held)], sems.at[n]
        )
        for n, (source, of_core) in enumerate(((here_ref, core), (there_ref, 1 - core)))
    ]
    copies.append(
        pltpu.make_async_copy(up_ref.at[pl.ds(place * (held // 2), held // 2)], own_ref, sems.at[2])
    )
    started(copies)
    awaited(copies)
    up = own_ref[...].reshape(held // 2 * rank, -1)
    rows = up.shape[0]
    for n in range(up.shape[1] // LANES):
        first = quarter + n * rows
        out_ref[first : first + rows] = up[:, n * LANES : (n + 1) * LANES]
    for n in range(0, quarter, LANES):
        block = down_ref[:, :, n : n + LANES].reshape(2 * held * rank, LANES)
        out_ref[n : n + LANES] = block.T


def assemble(back, info, here, there, up):
    held, rank, depth = here.shape
    width = up.shape[2]
    rows = depth // 4 + held // 2 * rank * width // LANES
    anywhere = pl.BlockSpec(memory_space=pl.ANY)
    return pl.pallas_call(
        functools.partial(assemble_kernel, back),
        out_shape=jax.ShapeDtypeStruct((rows, LANES), here.dtype),
        in_specs=[pl.BlockSpec(memory_space=pltpu.SMEM)] + [anywhere] * 3,
        out_specs=pl.BlockSpec(memory_space=pltpu.VMEM),
        scratch_shapes=[
            pltpu.VMEM((2 * held, rank, depth // 4), here.dtype),
            pltpu.VMEM((held // 2, rank, width), up.dtype),
            pltpu.SemaphoreType.DMA((3,)),
        ],
        compiler_params=params(),
    )(info, here, there, up)


def base_kernel(steps, tokens_ref, weight_ref, *refs):
    step = pl.program_id(0)
    more = len(refs) > 1
    out_ref = refs[1] if more else refs[0]
    copies = [pltpu.make_async_copy(refs[0], refs[2], refs[3].at[0])] if more else []
    part = jnp.dot(tokens_ref[...], weight_ref[...], preferred_element_type=jnp.float32)

    @pl.when(step == 0)
    def _():
        started(copies)
        out_ref[...] = part

    @pl.when(step > 0)
    def _():
        out_ref[...] += part

    if more:

        @pl.when(step == steps - 1)
        def _():
            awaited(copies)
            out_ref[...] += refs[2][...]


def base_part(tokens, weight, begin, end, total=None):
    rows, depth = tokens.shape
    width = weight.shape[1]
    steps, first = (end - begin) // DEPTH_TILE, begin // DEPTH_TILE
    result = jax.ShapeDtypeStruct((rows, width), jnp.float32)
    more = total is not None
    return pl.pallas_call(
        functools.partial(base_kernel, steps),
        out_shape=result,
        grid=(steps,),
        in_specs=[
            pl.BlockSpec((rows, DEPTH_TILE), lambda k: (0, first + k)),
            pl.BlockSpec((DEPTH_TILE, width), lambda k: (first + k, 0)),
        ]
        + [pl.BlockSpec(memory_space=pl.ANY)] * more,
        out_specs=pl.BlockSpec((rows, width), lambda k: (0, 0)),
        scratch_shapes=[pltpu.VMEM((rows, width), jnp.float32), pltpu.SemaphoreType.DMA((1,))]
        if more
        else [],
        cost_estimate=pl.CostEstimate(
            flops=2 * rows * width * (end - begin),
            bytes_accessed=2 * (rows + width) * (end - begin) + 4 * rows * width,
            transcendentals=0,
        ),
        compiler_params=params(),
    )(tokens, weight, *([total] if more else []))


def absorb_kernel(groups, start, sides, more, has_up, info_ref, row_slot_ref, *refs):
    count = sum(size for size, _ in groups)
    token_refs, sources, refs = refs[: len(sides)], refs[len(sides) :][:count], refs[len(sides) + count :]
    before, refs = refs[: len(sides) * more], refs[len(sides) * more :]
    outs, refs = refs[: len(sides)], refs[len(sides) :]
    up_ref, refs = (refs[0], refs[1:]) if has_up else (None, refs)
    rows_ref, row_slot, held_refs, refs = refs[0], refs[1], refs[2 : 2 + len(before)], refs[2 + len(before) :]
    down_refs, sems = refs[:-1], refs[-1]
    rows = token_refs[0].shape[0]
    quarter = rows_ref.shape[2]
    y, core = info_ref[0], info_ref[1]
    cuts = list(zip(QUARTER_CUTS, QUARTER_CUTS[1:]))
    copies, waits = [], {}

    def begin(key, source, target):
        copy = pltpu.make_async_copy(source, target, sems.at[len(copies)])
        copies.append(copy)
        waits.setdefault(key, []).append(copy)
        copy.start()

    places = {}
    first = 0
    for n, ((size, back), down_ref) in enumerate(zip(groups, down_refs)):
        load = back not in places
        place = places.setdefault(back, len(places))
        ends = cuts + [(quarter, sources[0].shape[0])] * has_up
        for low, high in ends:
            for i in range(size):
                begin(
                    (n, low),
                    sources[first + i].at[pl.ds(low, high - low)],
                    down_ref.at[pl.ds(low, high - low), pl.ds(i * LANES, LANES)],
                )
            if not load or low == quarter:
                continue
            for i, source in enumerate(token_refs):
                column = (2 * core + (1 - y if back else y)) * quarter + low
                begin(
                    (n, low),
                    source.at[:, pl.ds(pl.multiple_of(column, QUARTER_CUTS[1]), high - low)],
                    rows_ref.at[place, pl.ds(i * rows, rows), pl.ds(low, high - low)],
                )
        first += size
    begin("late", row_slot_ref, row_slot)
    for source, target in zip(before, held_refs):
        begin("late", source, target)
    lane_slot = lax.broadcasted_iota(jnp.int32, (1, LANES), 1) // RANK
    state = None
    first = 0
    for n, ((size, back), down_ref) in enumerate(zip(groups, down_refs)):
        shrink = None
        for low, high in cuts:
            awaited(waits[n, low])
            part = jnp.dot(
                rows_ref[places[back], :, low:high],
                down_ref[low:high],
                preferred_element_type=jnp.float32,
            )
            shrink = part if shrink is None else shrink + part
        if n == 0:
            awaited(waits["late"])
        for i in range(size):
            lanes, which = slice(i * LANES, (i + 1) * LANES), first + i
            chip = info_ref[2 + 2 * len(PIECES) + start + which]
            wanted = lane_slot + chip * (LANES // RANK)
            kept = jnp.where(row_slot[...] == wanted, shrink[:, lanes], 0.0)
            state = kept if state is None else state + kept
        if has_up:
            awaited(waits[n, quarter])
            height = up_ref.shape[0] // count
            for i in range(size):
                lanes, which = slice(i * LANES, (i + 1) * LANES), first + i
                for j in range(up_ref.shape[1] // LANES):
                    top = quarter + j * height
                    up_ref[
                        which * height : (which + 1) * height, j * LANES : (j + 1) * LANES
                    ] = down_ref[top : top + height, lanes]
        first += size
    for i, out_ref in enumerate(outs):
        own = state[i * rows : (i + 1) * rows]
        out_ref[...] = own + held_refs[i][...] if more else own


def absorb(info, row_slots, sides, tokens, width, groups, start, before, has_up):
    rows = tokens[0].shape[0]
    pieces = [piece for group, _ in groups for piece in group]
    sizes = [(len(group), back) for group, back in groups]
    quarter = tokens[0].shape[1] // 4
    height = pieces[0].shape[0]
    anywhere = pl.BlockSpec(memory_space=pl.ANY)
    vmem = pl.BlockSpec(memory_space=pltpu.VMEM)
    more = before is not None
    state = jax.ShapeDtypeStruct((rows, LANES), jnp.float32)
    up_rows = len(pieces) * (height - quarter) * LANES // width
    up = jax.ShapeDtypeStruct((up_rows, width), tokens[0].dtype)
    quarters = len({back for _, back in groups})
    cuts = len(QUARTER_CUTS) - 1
    copies = len(pieces) * (cuts + has_up) + len(sides) * (quarters * cuts + more) + 1
    outs = (state,) * len(sides) + (up,) * has_up
    return pl.pallas_call(
        functools.partial(absorb_kernel, sizes, start, sides, more, has_up),
        out_shape=outs,
        in_specs=[pl.BlockSpec(memory_space=pltpu.SMEM)]
        + [anywhere] * (1 + len(sides) + len(pieces) + len(sides) * more),
        out_specs=(vmem,) * len(outs),
        scratch_shapes=[
            pltpu.VMEM((quarters, len(sides) * rows, quarter), tokens[0].dtype),
            pltpu.VMEM(row_slots.shape, row_slots.dtype),
        ]
        + [pltpu.VMEM((rows, LANES), jnp.float32)] * (len(sides) * more)
        + [pltpu.VMEM((height, size * LANES), tokens[0].dtype) for size, _ in sizes]
        + [pltpu.SemaphoreType.DMA((copies,))],
        cost_estimate=pl.CostEstimate(
            flops=2 * len(sides) * rows * len(pieces) * LANES * quarter,
            bytes_accessed=2 * len(sides) * rows * quarters * quarter
            + 2 * len(pieces) * LANES * height,
            transcendentals=0,
        ),
        compiler_params=params(),
    )(info, row_slots, *tokens, *pieces, *(before or ()))


def finish_kernel(count, info_ref, row_slot_ref, mine_ref, theirs_ref, total_ref, *refs):
    sources, refs = refs[:count], refs[count:]
    out_ref, row_slot, mine, theirs, total, up, sems = refs
    rows = out_ref.shape[0]
    height = up.shape[0] // (len(PIECES) * 2)
    copies = []

    def begin(source, target):
        copies.append(pltpu.make_async_copy(source, target, sems.at[len(copies)]))
        copies[-1].start()

    begin(row_slot_ref.at[pl.ds(0, rows)], row_slot)
    begin(mine_ref, mine)
    begin(theirs_ref, theirs)
    begin(total_ref, total)
    for source in sources:
        for n in range(0, source.shape[0], height):
            first = pl.multiple_of(info_ref[len(copies) - 2], height)
            begin(source.at[pl.ds(n, height)], up.at[pl.ds(first, height)])
    awaited(copies[:3])
    shrink = mine[...] + theirs[...]
    lane_slot = lax.broadcasted_iota(jnp.int32, (1, LANES), 1) // RANK
    high, low = [], []
    for n in range(up.shape[0] // LANES):
        kept = jnp.where(row_slot[...] == lane_slot + n * (LANES // RANK), shrink, 0.0)
        high.append(kept.astype(jnp.bfloat16))
        low.append((kept - high[-1].astype(jnp.float32)).astype(jnp.bfloat16))
    both = jnp.concatenate([jnp.concatenate(part, axis=1) for part in (low, high)], axis=0)
    awaited(copies[3:])
    lora = jnp.dot(both, up[...], preferred_element_type=jnp.float32)
    out_ref[...] = (total[...] + (lora[:rows] + lora[rows:])).astype(out_ref.dtype)


def finish(info, row_slots, mine, theirs, total, ups):
    rows, width = total.shape
    anywhere = pl.BlockSpec(memory_space=pl.ANY)
    up_rows = sum(up.shape[0] for up in ups)
    return pl.pallas_call(
        functools.partial(finish_kernel, len(ups)),
        out_shape=jax.ShapeDtypeStruct((rows, width), jnp.bfloat16),
        in_specs=[pl.BlockSpec(memory_space=pltpu.SMEM)] + [anywhere] * (4 + len(ups)),
        out_specs=pl.BlockSpec(memory_space=pltpu.VMEM),
        scratch_shapes=[
            pltpu.VMEM((rows, 1), jnp.int32),
            pltpu.VMEM((rows, LANES), jnp.float32),
            pltpu.VMEM((rows, LANES), jnp.float32),
            pltpu.VMEM((rows, width), jnp.float32),
            pltpu.VMEM((up_rows, width), ups[0].dtype),
            pltpu.SemaphoreType.DMA((4 + 2 * len(PIECES),)),
        ],
        cost_estimate=pl.CostEstimate(
            flops=4 * rows * width * up_rows,
            bytes_accessed=6 * rows * width + 2 * up_rows * width,
            transcendentals=0,
        ),
        compiler_params=params(),
    )(info, row_slots, mine, theirs, total, *ups)


def passed_round(
    tokens,
    row_adapter_index,
    adapter_storage_slot,
    base_value_weight,
    adapter_down_weight,
    adapter_up_weight,
):
    rows, depth = tokens.shape
    held, rank, _ = adapter_down_weight.shape
    width = adapter_up_weight.shape[2]
    axes = ("groups", "req")
    planes, owners = lax.axis_size("groups"), lax.axis_size("req")
    device = lax.axis_index("groups") * owners + lax.axis_index("req")

    def permuted(array, target):
        pairs = [
            (g * owners + r, target(g, r)) for g in range(planes) for r in range(owners)
        ]
        return lax.ppermute(array, axes, pairs)

    def along_z(r, by):
        return RING[(PLACE_IN_RING[r // 4] + by) % 4] * 4 + r % 4

    z_ring = lambda array: permuted(array, lambda g, r: g * owners + along_z(r, 1))
    z_back = lambda array: permuted(array, lambda g, r: g * owners + along_z(r, -1))
    x_swap = lambda array: permuted(array, lambda g, r: g * owners + (r ^ 2))
    y_swap = lambda array: permuted(array, lambda g, r: (1 - g) * owners + r)
    core_swap = lambda array: permuted(array, lambda g, r: g * owners + (r ^ 1))

    def chip(r, piece):
        return (along_z(r, -piece[0]) ^ (2 * piece[1])) // 2

    kernels = [PIECES[low:high] for low, high in zip(KERNEL_BOUNDS, KERNEL_BOUNDS[1:])]
    info_table = [
        [g, r % 2]
        + [
            chip(r, p) * LANES + core * held * rank + (g ^ p[2]) * (held // 2 * rank)
            for pieces in kernels
            for core in (r % 2, 1 - r % 2)
            for p in pieces
        ]
        + [chip(r, p) for p in PIECES]
        for g in range(planes)
        for r in range(owners)
    ]
    info = lax.dynamic_index_in_dim(
        jnp.array(np.array(info_table, np.int32)), device, 0, keepdims=False
    )

    def together(*values):
        return lax.optimization_barrier(values)

    def after(value, *others):
        return lax.optimization_barrier((value, *others))[0]

    there = core_swap(adapter_down_weight)
    row_slot = slots_of_rows(row_adapter_index, adapter_storage_slot)
    there, info, row_slot, tokens_late = together(there, info, row_slot, tokens)

    def piece(back, *others):
        return assemble(
            back, after(info, *others), adapter_down_weight, there, adapter_up_weight
        )

    front = piece(0)
    cuts = (0, depth // 2, depth)

    def base(number, before, *others):
        low, high = cuts[number : number + 2]
        return base_part(after(tokens, *others), base_value_weight, low, high, before)

    z1, x0 = z_ring(front), x_swap(front)
    other = core_swap(tokens_late)
    other_slot = core_swap(row_slot[:, 0])
    total = base(0, None, front)
    row_slots = jnp.concatenate([row_slot, other_slot[:, None]], axis=0)
    z1, x0, front, total, row_slots = together(z1, x0, front, total, row_slots)

    z2, x1, yx0 = z_ring(z1), x_swap(z1), y_swap(x0)
    total = base(1, total, total)
    z2, x1, yx0, front, other, total, info = together(z2, x1, yx0, front, other, total, info)

    def update(number, groups, before):
        return absorb(
            info,
            row_slots,
            (0, 1),
            [tokens, other],
            width,
            groups,
            KERNEL_BOUNDS[number],
            before,
            True,
        )

    z3, x2, yz2 = z_back(front), x_swap(z2), y_swap(z2)
    back = piece(1, z2)
    *state, up_a = update(0, [((front, z1, x0, z2), 0)], None)
    z3, x2, yz2, x1, back, state, total = together(z3, x2, yz2, x1, back, state, total)
    there_a = core_swap(up_a)

    zb1, x3, yx1 = z_ring(back), x_swap(z3), y_swap(x1)
    *state, up_b = update(1, [((back, yx0, yz2), 1)], state)
    zb1, x3, yx1, yz2, back, state, there_a = together(
        zb1, x3, yx1, yz2, back, state, there_a
    )
    there_b = core_swap(up_b)

    zb3, xyz2, yx3 = z_back(back), x_swap(yz2), y_swap(x3)
    *state, up_c = update(2, [((x1, z3, x2, x3), 0), ((zb1, yx1), 1)], state)
    zb3, xyz2, yx3, state, there_b = together(zb3, xyz2, yx3, state, there_b)
    there_c = core_swap(up_c)

    mine, others, up_d = update(3, [((zb3, xyz2, yx3), 1)], state)
    ups = (up_a, there_a, up_b, there_b, up_c, there_c, up_d, core_swap(up_d))
    return finish(info, row_slots, mine, core_swap(others), total, ups)


def solution(mesh):
    placed = (
        P(("groups", "req"), "tp"),
        P(("groups", "req"), None),
        P(),
        P("tp", None),
        P("req", None, "tp"),
        P("req", None, "tp"),
    )
    sizes = mesh.shape
    small = sizes["groups"] == 2 and sizes["req"] == 16 and sizes["tp"] == 1
    return jax.shard_map(
        passed_round if small else gathered,
        mesh=mesh,
        in_specs=placed,
        out_specs=P(("groups", "req"), "tp"),
        check_vma=False,
    )
```

```python
import functools

import jax
import jax.numpy as jnp
import numpy as np
from jax import lax
from jax.experimental import pallas as pl
from jax.experimental.pallas import tpu as pltpu
from jax.sharding import PartitionSpec as P

RING = (0, 1, 3, 2)
PLACE_IN_RING = (0, 1, 3, 2)
DEPTH_TILE = 1024
LANES = 128
RANK = 16

PIECES = (
    *((0, 0, 0), (1, 0, 0), (0, 1, 0), (2, 0, 0)),
    *((0, 0, 1), (0, 1, 1), (2, 0, 1)),
    *((1, 1, 0), (3, 0, 0), (2, 1, 0), (3, 1, 0), (1, 0, 1), (1, 1, 1)),
    *((3, 0, 1), (2, 1, 1), (3, 1, 1)),
)
KERNEL_BOUNDS = (0, 4, 7, 13, 16)
QUARTER_CUTS = (0, 512, 1024, 2048)
VMEM_BYTES = 64 * 1024 * 1024 - 512 * 1024


def slots_of_rows(row_adapter_index, adapter_storage_slot):
    catalog = jnp.arange(adapter_storage_slot.shape[0], dtype=jnp.int32)
    return jnp.sum(
        jnp.where(row_adapter_index == catalog[None, :], adapter_storage_slot[None, :], 0),
        axis=1,
        keepdims=True,
    )


def gathered(
    tokens,
    row_adapter_index,
    adapter_storage_slot,
    base_value_weight,
    adapter_down_weight,
    adapter_up_weight,
):
    adapter_count = adapter_storage_slot.shape[0]
    rank = adapter_down_weight.shape[1]
    slot_of = slots_of_rows(row_adapter_index, adapter_storage_slot)
    down_all = lax.all_gather(
        adapter_down_weight.reshape(-1, adapter_down_weight.shape[2]), "req", axis=0, tiled=True
    )
    up_all = lax.all_gather(
        adapter_up_weight.reshape(-1, adapter_up_weight.shape[2]), "req", axis=0, tiled=True
    )
    base_partial = jnp.dot(tokens, base_value_weight, preferred_element_type=jnp.float32)
    base_output = lax.psum_scatter(base_partial, "tp", scatter_dimension=1, tiled=True)
    shrink = lax.dot_general(
        tokens, down_all, (((1,), (1,)), ((), ())), preferred_element_type=jnp.float32
    )
    column_slot = jnp.arange(adapter_count * rank, dtype=jnp.int32) // rank
    shrink = jnp.where(slot_of == column_slot[None, :], shrink, 0.0)
    shrink = lax.psum(shrink, "tp")
    high = lax.reduce_precision(shrink, 8, 7)
    rest = shrink - high
    middle = lax.reduce_precision(rest, 8, 7)
    low = rest - middle
    lora = sum(
        jnp.dot(piece.astype(jnp.bfloat16), up_all, preferred_element_type=jnp.float32)
        for piece in (low, middle, high)
    )
    return (base_output + lora).astype(jnp.bfloat16)


def params():
    return pltpu.CompilerParams(vmem_limit_bytes=VMEM_BYTES)


def started(copies):
    for copy in copies:
        copy.start()


def awaited(copies):
    for copy in copies:
        copy.wait()


def assemble_kernel(back, info_ref, here_ref, there_ref, up_ref, out_ref, down_ref, own_ref, sems):
    y, core = info_ref[0], info_ref[1]
    place = 1 - y if back else y
    held, rank, quarter = down_ref.shape
    held //= 2
    columns = pl.ds(pl.multiple_of((2 * core + place) * quarter, quarter), quarter)
    copies = [
        pltpu.make_async_copy(
            source.at[:, :, columns], down_ref.at[pl.ds(of_core * held, held)], sems.at[n]
        )
        for n, (source, of_core) in enumerate(((here_ref, core), (there_ref, 1 - core)))
    ]
    copies.append(
        pltpu.make_async_copy(up_ref.at[pl.ds(place * (held // 2), held // 2)], own_ref, sems.at[2])
    )
    started(copies)
    awaited(copies)
    up = own_ref[...].reshape(held // 2 * rank, -1)
    rows = up.shape[0]
    for n in range(up.shape[1] // LANES):
        first = quarter + n * rows
        out_ref[first : first + rows] = up[:, n * LANES : (n + 1) * LANES]
    for n in range(0, quarter, LANES):
        block = down_ref[:, :, n : n + LANES].reshape(2 * held * rank, LANES)
        out_ref[n : n + LANES] = block.T


def assemble(back, info, here, there, up):
    held, rank, depth = here.shape
    width = up.shape[2]
    rows = depth // 4 + held // 2 * rank * width // LANES
    anywhere = pl.BlockSpec(memory_space=pl.ANY)
    return pl.pallas_call(
        functools.partial(assemble_kernel, back),
        out_shape=jax.ShapeDtypeStruct((rows, LANES), here.dtype),
        in_specs=[pl.BlockSpec(memory_space=pltpu.SMEM)] + [anywhere] * 3,
        out_specs=pl.BlockSpec(memory_space=pltpu.VMEM),
        scratch_shapes=[
            pltpu.VMEM((2 * held, rank, depth // 4), here.dtype),
            pltpu.VMEM((held // 2, rank, width), up.dtype),
            pltpu.SemaphoreType.DMA((3,)),
        ],
        compiler_params=params(),
    )(info, here, there, up)


def base_kernel(steps, tokens_ref, weight_ref, *refs):
    step = pl.program_id(0)
    more = len(refs) > 1
    out_ref = refs[1] if more else refs[0]
    copies = [pltpu.make_async_copy(refs[0], refs[2], refs[3].at[0])] if more else []
    part = jnp.dot(tokens_ref[...], weight_ref[...], preferred_element_type=jnp.float32)

    @pl.when(step == 0)
    def _():
        started(copies)
        out_ref[...] = part

    @pl.when(step > 0)
    def _():
        out_ref[...] += part

    if more:

        @pl.when(step == steps - 1)
        def _():
            awaited(copies)
            out_ref[...] += refs[2][...]


def base_part(tokens, weight, begin, end, total=None):
    rows, depth = tokens.shape
    width = weight.shape[1]
    steps, first = (end - begin) // DEPTH_TILE, begin // DEPTH_TILE
    result = jax.ShapeDtypeStruct((rows, width), jnp.float32)
    more = total is not None
    return pl.pallas_call(
        functools.partial(base_kernel, steps),
        out_shape=result,
        grid=(steps,),
        in_specs=[
            pl.BlockSpec((rows, DEPTH_TILE), lambda k: (0, first + k)),
            pl.BlockSpec((DEPTH_TILE, width), lambda k: (first + k, 0)),
        ]
        + [pl.BlockSpec(memory_space=pl.ANY)] * more,
        out_specs=pl.BlockSpec((rows, width), lambda k: (0, 0)),
        scratch_shapes=[pltpu.VMEM((rows, width), jnp.float32), pltpu.SemaphoreType.DMA((1,))]
        if more
        else [],
        cost_estimate=pl.CostEstimate(
            flops=2 * rows * width * (end - begin),
            bytes_accessed=2 * (rows + width) * (end - begin) + 4 * rows * width,
            transcendentals=0,
        ),
        compiler_params=params(),
    )(tokens, weight, *([total] if more else []))


def absorb_kernel(groups, start, sides, more, has_up, info_ref, row_slot_ref, *refs):
    count = sum(size for size, _ in groups)
    token_refs, sources, refs = refs[: len(sides)], refs[len(sides) :][:count], refs[len(sides) + count :]
    before, refs = refs[: len(sides) * more], refs[len(sides) * more :]
    outs, refs = refs[: len(sides)], refs[len(sides) :]
    up_ref, refs = (refs[0], refs[1:]) if has_up else (None, refs)
    rows_ref, row_slot, held_refs, refs = refs[0], refs[1], refs[2 : 2 + len(before)], refs[2 + len(before) :]
    down_refs, sems = refs[:-1], refs[-1]
    rows = token_refs[0].shape[0]
    quarter = rows_ref.shape[2]
    y, core = info_ref[0], info_ref[1]
    cuts = list(zip(QUARTER_CUTS, QUARTER_CUTS[1:]))
    copies, waits = [], {}

    def begin(key, source, target):
        copy = pltpu.make_async_copy(source, target, sems.at[len(copies)])
        copies.append(copy)
        waits.setdefault(key, []).append(copy)
        copy.start()

    places = {}
    first = 0
    for n, ((size, back), down_ref) in enumerate(zip(groups, down_refs)):
        load = back not in places
        place = places.setdefault(back, len(places))
        ends = cuts + [(quarter, sources[0].shape[0])] * has_up
        for low, high in ends:
            for i in range(size):
                begin(
                    (n, low),
                    sources[first + i].at[pl.ds(low, high - low)],
                    down_ref.at[pl.ds(low, high - low), pl.ds(i * LANES, LANES)],
                )
            if not load or low == quarter:
                continue
            for i, source in enumerate(token_refs):
                column = (2 * core + (1 - y if back else y)) * quarter + low
                begin(
                    (n, low),
                    source.at[:, pl.ds(pl.multiple_of(column, QUARTER_CUTS[1]), high - low)],
                    rows_ref.at[place, pl.ds(i * rows, rows), pl.ds(low, high - low)],
                )
        first += size
    begin("late", row_slot_ref, row_slot)
    for source, target in zip(before, held_refs):
        begin("late", source, target)
    lane_slot = lax.broadcasted_iota(jnp.int32, (1, LANES), 1) // RANK
    state = None
    first = 0
    for n, ((size, back), down_ref) in enumerate(zip(groups, down_refs)):
        shrink = None
        for low, high in cuts:
            awaited(waits[n, low])
            part = jnp.dot(
                rows_ref[places[back], :, low:high],
                down_ref[low:high],
                preferred_element_type=jnp.float32,
            )
            shrink = part if shrink is None else shrink + part
        if n == 0:
            awaited(waits["late"])
        for i in range(size):
            lanes, which = slice(i * LANES, (i + 1) * LANES), first + i
            chip = info_ref[2 + 2 * len(PIECES) + start + which]
            wanted = lane_slot + chip * (LANES // RANK)
            kept = jnp.where(row_slot[...] == wanted, shrink[:, lanes], 0.0)
            state = kept if state is None else state + kept
        if has_up:
            awaited(waits[n, quarter])
            height = up_ref.shape[0] // count
            for i in range(size):
                lanes, which = slice(i * LANES, (i + 1) * LANES), first + i
                for j in range(up_ref.shape[1] // LANES):
                    top = quarter + j * height
                    up_ref[
                        which * height : (which + 1) * height, j * LANES : (j + 1) * LANES
                    ] = down_ref[top : top + height, lanes]
        first += size
    for i, out_ref in enumerate(outs):
        own = state[i * rows : (i + 1) * rows]
        out_ref[...] = own + held_refs[i][...] if more else own


def absorb(info, row_slots, sides, tokens, width, groups, start, before, has_up):
    rows = tokens[0].shape[0]
    pieces = [piece for group, _ in groups for piece in group]
    sizes = [(len(group), back) for group, back in groups]
    quarter = tokens[0].shape[1] // 4
    height = pieces[0].shape[0]
    anywhere = pl.BlockSpec(memory_space=pl.ANY)
    vmem = pl.BlockSpec(memory_space=pltpu.VMEM)
    more = before is not None
    state = jax.ShapeDtypeStruct((rows, LANES), jnp.float32)
    up_rows = len(pieces) * (height - quarter) * LANES // width
    up = jax.ShapeDtypeStruct((up_rows, width), tokens[0].dtype)
    quarters = len({back for _, back in groups})
    cuts = len(QUARTER_CUTS) - 1
    copies = len(pieces) * (cuts + has_up) + len(sides) * (quarters * cuts + more) + 1
    outs = (state,) * len(sides) + (up,) * has_up
    return pl.pallas_call(
        functools.partial(absorb_kernel, sizes, start, sides, more, has_up),
        out_shape=outs,
        in_specs=[pl.BlockSpec(memory_space=pltpu.SMEM)]
        + [anywhere] * (1 + len(sides) + len(pieces) + len(sides) * more),
        out_specs=(vmem,) * len(outs),
        scratch_shapes=[
            pltpu.VMEM((quarters, len(sides) * rows, quarter), tokens[0].dtype),
            pltpu.VMEM(row_slots.shape, row_slots.dtype),
        ]
        + [pltpu.VMEM((rows, LANES), jnp.float32)] * (len(sides) * more)
        + [pltpu.VMEM((height, size * LANES), tokens[0].dtype) for size, _ in sizes]
        + [pltpu.SemaphoreType.DMA((copies,))],
        cost_estimate=pl.CostEstimate(
            flops=2 * len(sides) * rows * len(pieces) * LANES * quarter,
            bytes_accessed=2 * len(sides) * rows * quarters * quarter
            + 2 * len(pieces) * LANES * height,
            transcendentals=0,
        ),
        compiler_params=params(),
    )(info, row_slots, *tokens, *pieces, *(before or ()))


def finish_kernel(count, info_ref, row_slot_ref, mine_ref, theirs_ref, total_ref, *refs):
    sources, refs = refs[:count], refs[count:]
    out_ref, row_slot, mine, theirs, total, up, sems = refs
    rows = out_ref.shape[0]
    height = up.shape[0] // (len(PIECES) * 2)
    copies = []

    def begin(source, target):
        copies.append(pltpu.make_async_copy(source, target, sems.at[len(copies)]))
        copies[-1].start()

    begin(row_slot_ref.at[pl.ds(0, rows)], row_slot)
    begin(mine_ref, mine)
    begin(theirs_ref, theirs)
    for source in sources:
        for n in range(0, source.shape[0], height):
            first = pl.multiple_of(info_ref[len(copies) - 1], height)
            begin(source.at[pl.ds(n, height)], up.at[pl.ds(first, height)])
    begin(total_ref, total)
    awaited(copies[:3])
    shrink = mine[...] + theirs[...]
    lane_slot = lax.broadcasted_iota(jnp.int32, (1, LANES), 1) // RANK
    high, low = [], []
    for n in range(up.shape[0] // LANES):
        kept = jnp.where(row_slot[...] == lane_slot + n * (LANES // RANK), shrink, 0.0)
        high.append(kept.astype(jnp.bfloat16))
        low.append((kept - high[-1].astype(jnp.float32)).astype(jnp.bfloat16))
    both = jnp.concatenate([jnp.concatenate(part, axis=1) for part in (low, high)], axis=0)
    awaited(copies[3:-1])
    lora = jnp.dot(both, up[...], preferred_element_type=jnp.float32)
    awaited(copies[-1:])
    out_ref[...] = (total[...] + (lora[:rows] + lora[rows:])).astype(out_ref.dtype)


def finish(info, row_slots, mine, theirs, total, ups):
    rows, width = total.shape
    anywhere = pl.BlockSpec(memory_space=pl.ANY)
    up_rows = sum(up.shape[0] for up in ups)
    return pl.pallas_call(
        functools.partial(finish_kernel, len(ups)),
        out_shape=jax.ShapeDtypeStruct((rows, width), jnp.bfloat16),
        in_specs=[pl.BlockSpec(memory_space=pltpu.SMEM)] + [anywhere] * (4 + len(ups)),
        out_specs=pl.BlockSpec(memory_space=pltpu.VMEM),
        scratch_shapes=[
            pltpu.VMEM((rows, 1), jnp.int32),
            pltpu.VMEM((rows, LANES), jnp.float32),
            pltpu.VMEM((rows, LANES), jnp.float32),
            pltpu.VMEM((rows, width), jnp.float32),
            pltpu.VMEM((up_rows, width), ups[0].dtype),
            pltpu.SemaphoreType.DMA((4 + 2 * len(PIECES),)),
        ],
        cost_estimate=pl.CostEstimate(
            flops=4 * rows * width * up_rows,
            bytes_accessed=6 * rows * width + 2 * up_rows * width,
            transcendentals=0,
        ),
        compiler_params=params(),
    )(info, row_slots, mine, theirs, total, *ups)


def passed_round(
    tokens,
    row_adapter_index,
    adapter_storage_slot,
    base_value_weight,
    adapter_down_weight,
    adapter_up_weight,
):
    rows, depth = tokens.shape
    held, rank, _ = adapter_down_weight.shape
    width = adapter_up_weight.shape[2]
    axes = ("groups", "req")
    planes, owners = lax.axis_size("groups"), lax.axis_size("req")
    device = lax.axis_index("groups") * owners + lax.axis_index("req")

    def permuted(array, target):
        pairs = [
            (g * owners + r, target(g, r)) for g in range(planes) for r in range(owners)
        ]
        return lax.ppermute(array, axes, pairs)

    def along_z(r, by):
        return RING[(PLACE_IN_RING[r // 4] + by) % 4] * 4 + r % 4

    z_ring = lambda array: permuted(array, lambda g, r: g * owners + along_z(r, 1))
    z_back = lambda array: permuted(array, lambda g, r: g * owners + along_z(r, -1))
    x_swap = lambda array: permuted(array, lambda g, r: g * owners + (r ^ 2))
    y_swap = lambda array: permuted(array, lambda g, r: (1 - g) * owners + r)
    core_swap = lambda array: permuted(array, lambda g, r: g * owners + (r ^ 1))

    def chip(r, piece):
        return (along_z(r, -piece[0]) ^ (2 * piece[1])) // 2

    kernels = [PIECES[low:high] for low, high in zip(KERNEL_BOUNDS, KERNEL_BOUNDS[1:])]
    info_table = [
        [g, r % 2]
        + [
            chip(r, p) * LANES + core * held * rank + (g ^ p[2]) * (held // 2 * rank)
            for pieces in kernels
            for core in (r % 2, 1 - r % 2)
            for p in pieces
        ]
        + [chip(r, p) for p in PIECES]
        for g in range(planes)
        for r in range(owners)
    ]
    info = lax.dynamic_index_in_dim(
        jnp.array(np.array(info_table, np.int32)), device, 0, keepdims=False
    )

    def together(*values):
        return lax.optimization_barrier(values)

    def after(value, *others):
        return lax.optimization_barrier((value, *others))[0]

    there = core_swap(adapter_down_weight)
    row_slot = slots_of_rows(row_adapter_index, adapter_storage_slot)
    there, info, row_slot, tokens_late = together(there, info, row_slot, tokens)

    def piece(back, *others):
        return assemble(
            back, after(info, *others), adapter_down_weight, there, adapter_up_weight
        )

    front = piece(0)
    cuts = (0, depth // 2, depth)

    def base(number, before, *others):
        low, high = cuts[number : number + 2]
        return base_part(after(tokens, *others), base_value_weight, low, high, before)

    z1, x0 = z_ring(front), x_swap(front)
    other = core_swap(tokens_late)
    other_slot = core_swap(row_slot[:, 0])
    total = base(0, None, front)
    row_slots = jnp.concatenate([row_slot, other_slot[:, None]], axis=0)
    z1, x0, front, total, row_slots = together(z1, x0, front, total, row_slots)

    z2, x1, yx0 = z_ring(z1), x_swap(z1), y_swap(x0)
    total = base(1, total, total)
    z2, x1, yx0, front, other, total, info = together(z2, x1, yx0, front, other, total, info)

    def update(number, groups, before):
        return absorb(
            info,
            row_slots,
            (0, 1),
            [tokens, other],
            width,
            groups,
            KERNEL_BOUNDS[number],
            before,
            True,
        )

    z3, x2, yz2 = z_back(front), x_swap(z2), y_swap(z2)
    back = piece(1, z2)
    *state, up_a = update(0, [((front, z1, x0, z2), 0)], None)
    z3, x2, yz2, x1, back, state, total = together(z3, x2, yz2, x1, back, state, total)
    there_a = core_swap(up_a)

    zb1, x3, yx1 = z_ring(back), x_swap(z3), y_swap(x1)
    *state, up_b = update(1, [((back, yx0, yz2), 1)], state)
    zb1, x3, yx1, yz2, back, state, there_a = together(
        zb1, x3, yx1, yz2, back, state, there_a
    )
    there_b = core_swap(up_b)

    zb3, xyz2, yx3 = z_back(back), x_swap(yz2), y_swap(x3)
    *state, up_c = update(2, [((x1, z3, x2, x3), 0), ((zb1, yx1), 1)], state)
    zb3, xyz2, yx3, state, there_b = together(zb3, xyz2, yx3, state, there_b)
    there_c = core_swap(up_c)

    mine, others, up_d = update(3, [((zb3, xyz2, yx3), 1)], state)
    ups = (up_a, there_a, up_b, there_b, up_c, there_c, up_d, core_swap(up_d))
    return finish(info, row_slots, mine, core_swap(others), total, ups)


def solution(mesh):
    placed = (
        P(("groups", "req"), "tp"),
        P(("groups", "req"), None),
        P(),
        P("tp", None),
        P("req", None, "tp"),
        P("req", None, "tp"),
    )
    sizes = mesh.shape
    small = sizes["groups"] == 2 and sizes["req"] == 16 and sizes["tp"] == 1
    return jax.shard_map(
        passed_round if small else gathered,
        mesh=mesh,
        in_specs=placed,
        out_specs=P(("groups", "req"), "tp"),
        check_vma=False,
    )
```

```python
import functools

import jax
import jax.numpy as jnp
import numpy as np
from jax import lax
from jax.experimental import pallas as pl
from jax.experimental.pallas import tpu as pltpu
from jax.sharding import PartitionSpec as P

RING = (0, 1, 3, 2)
PLACE_IN_RING = (0, 1, 3, 2)
DEPTH_TILE = 1024
LANES = 128
RANK = 16

PIECES = (
    *((0, 0, 0), (1, 0, 0), (0, 1, 0), (2, 0, 0)),
    *((0, 0, 1), (0, 1, 1), (2, 0, 1)),
    *((1, 1, 0), (3, 0, 0), (2, 1, 0), (3, 1, 0), (1, 0, 1), (1, 1, 1)),
    *((3, 0, 1), (2, 1, 1), (3, 1, 1)),
)
KERNEL_BOUNDS = (0, 4, 7, 13, 16)
QUARTER_CUTS = (0, 512, 1024, 2048)
VMEM_BYTES = 64 * 1024 * 1024 - 512 * 1024


def slots_of_rows(row_adapter_index, adapter_storage_slot):
    catalog = jnp.arange(adapter_storage_slot.shape[0], dtype=jnp.int32)
    return jnp.sum(
        jnp.where(row_adapter_index == catalog[None, :], adapter_storage_slot[None, :], 0),
        axis=1,
        keepdims=True,
    )


def gathered(
    tokens,
    row_adapter_index,
    adapter_storage_slot,
    base_value_weight,
    adapter_down_weight,
    adapter_up_weight,
):
    adapter_count = adapter_storage_slot.shape[0]
    rank = adapter_down_weight.shape[1]
    slot_of = slots_of_rows(row_adapter_index, adapter_storage_slot)
    down_all = lax.all_gather(
        adapter_down_weight.reshape(-1, adapter_down_weight.shape[2]), "req", axis=0, tiled=True
    )
    up_all = lax.all_gather(
        adapter_up_weight.reshape(-1, adapter_up_weight.shape[2]), "req", axis=0, tiled=True
    )
    base_partial = jnp.dot(tokens, base_value_weight, preferred_element_type=jnp.float32)
    base_output = lax.psum_scatter(base_partial, "tp", scatter_dimension=1, tiled=True)
    shrink = lax.dot_general(
        tokens, down_all, (((1,), (1,)), ((), ())), preferred_element_type=jnp.float32
    )
    column_slot = jnp.arange(adapter_count * rank, dtype=jnp.int32) // rank
    shrink = jnp.where(slot_of == column_slot[None, :], shrink, 0.0)
    shrink = lax.psum(shrink, "tp")
    high = lax.reduce_precision(shrink, 8, 7)
    rest = shrink - high
    middle = lax.reduce_precision(rest, 8, 7)
    low = rest - middle
    lora = sum(
        jnp.dot(piece.astype(jnp.bfloat16), up_all, preferred_element_type=jnp.float32)
        for piece in (low, middle, high)
    )
    return (base_output + lora).astype(jnp.bfloat16)


def params():
    return pltpu.CompilerParams(vmem_limit_bytes=VMEM_BYTES)


def started(copies):
    for copy in copies:
        copy.start()


def awaited(copies):
    for copy in copies:
        copy.wait()


def assemble_kernel(back, info_ref, here_ref, there_ref, up_ref, out_ref, down_ref, own_ref, sems):
    y, core = info_ref[0], info_ref[1]
    place = 1 - y if back else y
    held, rank, quarter = down_ref.shape
    held //= 2
    columns = pl.ds(pl.multiple_of((2 * core + place) * quarter, quarter), quarter)
    copies = [
        pltpu.make_async_copy(
            source.at[:, :, columns], down_ref.at[pl.ds(of_core * held, held)], sems.at[n]
        )
        for n, (source, of_core) in enumerate(((here_ref, core), (there_ref, 1 - core)))
    ]
    copies.append(
        pltpu.make_async_copy(up_ref.at[pl.ds(place * (held // 2), held // 2)], own_ref, sems.at[2])
    )
    started(copies)
    awaited(copies)
    up = own_ref[...].reshape(held // 2 * rank, -1)
    rows = up.shape[0]
    for n in range(up.shape[1] // LANES):
        first = quarter + n * rows
        out_ref[first : first + rows] = up[:, n * LANES : (n + 1) * LANES]
    for n in range(0, quarter, LANES):
        block = down_ref[:, :, n : n + LANES].reshape(2 * held * rank, LANES)
        out_ref[n : n + LANES] = block.T


def assemble(back, info, here, there, up):
    held, rank, depth = here.shape
    width = up.shape[2]
    rows = depth // 4 + held // 2 * rank * width // LANES
    anywhere = pl.BlockSpec(memory_space=pl.ANY)
    return pl.pallas_call(
        functools.partial(assemble_kernel, back),
        out_shape=jax.ShapeDtypeStruct((rows, LANES), here.dtype),
        in_specs=[pl.BlockSpec(memory_space=pltpu.SMEM)] + [anywhere] * 3,
        out_specs=pl.BlockSpec(memory_space=pltpu.VMEM),
        scratch_shapes=[
            pltpu.VMEM((2 * held, rank, depth // 4), here.dtype),
            pltpu.VMEM((held // 2, rank, width), up.dtype),
            pltpu.SemaphoreType.DMA((3,)),
        ],
        compiler_params=params(),
    )(info, here, there, up)


def base_kernel(steps, tokens_ref, weight_ref, *refs):
    step = pl.program_id(0)
    more = len(refs) > 1
    out_ref = refs[1] if more else refs[0]
    copies = [pltpu.make_async_copy(refs[0], refs[2], refs[3].at[0])] if more else []
    part = jnp.dot(tokens_ref[...], weight_ref[...], preferred_element_type=jnp.float32)

    @pl.when(step == 0)
    def _():
        started(copies)
        out_ref[...] = part

    @pl.when(step > 0)
    def _():
        out_ref[...] += part

    if more:

        @pl.when(step == steps - 1)
        def _():
            awaited(copies)
            out_ref[...] += refs[2][...]


def base_part(tokens, weight, begin, end, total=None):
    rows, depth = tokens.shape
    width = weight.shape[1]
    steps, first = (end - begin) // DEPTH_TILE, begin // DEPTH_TILE
    result = jax.ShapeDtypeStruct((rows, width), jnp.float32)
    more = total is not None
    return pl.pallas_call(
        functools.partial(base_kernel, steps),
        out_shape=result,
        grid=(steps,),
        in_specs=[
            pl.BlockSpec((rows, DEPTH_TILE), lambda k: (0, first + k)),
            pl.BlockSpec((DEPTH_TILE, width), lambda k: (first + k, 0)),
        ]
        + [pl.BlockSpec(memory_space=pl.ANY)] * more,
        out_specs=pl.BlockSpec((rows, width), lambda k: (0, 0)),
        scratch_shapes=[pltpu.VMEM((rows, width), jnp.float32), pltpu.SemaphoreType.DMA((1,))]
        if more
        else [],
        cost_estimate=pl.CostEstimate(
            flops=2 * rows * width * (end - begin),
            bytes_accessed=2 * (rows + width) * (end - begin) + 4 * rows * width,
            transcendentals=0,
        ),
        compiler_params=params(),
    )(tokens, weight, *([total] if more else []))


def absorb_kernel(groups, start, sides, more, has_up, info_ref, row_slot_ref, *refs):
    count = sum(size for size, _ in groups)
    token_refs, sources, refs = refs[: len(sides)], refs[len(sides) :][:count], refs[len(sides) + count :]
    before, refs = refs[: len(sides) * more], refs[len(sides) * more :]
    outs, refs = refs[: len(sides)], refs[len(sides) :]
    up_ref, refs = (refs[0], refs[1:]) if has_up else (None, refs)
    rows_ref, row_slot, held_refs, refs = refs[0], refs[1], refs[2 : 2 + len(before)], refs[2 + len(before) :]
    down_refs, sems = refs[:-1], refs[-1]
    rows = token_refs[0].shape[0]
    quarter = rows_ref.shape[2]
    y, core = info_ref[0], info_ref[1]
    cuts = list(zip(QUARTER_CUTS, QUARTER_CUTS[1:]))
    copies, waits = [], {}

    def begin(key, source, target):
        copy = pltpu.make_async_copy(source, target, sems.at[len(copies)])
        copies.append(copy)
        waits.setdefault(key, []).append(copy)
        copy.start()

    places = {}
    first = 0
    for n, ((size, back), down_ref) in enumerate(zip(groups, down_refs)):
        load = back not in places
        place = places.setdefault(back, len(places))
        ends = cuts + [(quarter, sources[0].shape[0])] * has_up
        for low, high in ends:
            for i in range(size):
                begin(
                    (n, low),
                    sources[first + i].at[pl.ds(low, high - low)],
                    down_ref.at[pl.ds(low, high - low), pl.ds(i * LANES, LANES)],
                )
            if not load or low == quarter:
                continue
            for i, source in enumerate(token_refs):
                column = (2 * core + (1 - y if back else y)) * quarter + low
                begin(
                    (n, low),
                    source.at[:, pl.ds(pl.multiple_of(column, QUARTER_CUTS[1]), high - low)],
                    rows_ref.at[place, pl.ds(i * rows, rows), pl.ds(low, high - low)],
                )
        first += size
    begin("late", row_slot_ref, row_slot)
    for source, target in zip(before, held_refs):
        begin("late", source, target)
    lane_slot = lax.broadcasted_iota(jnp.int32, (1, LANES), 1) // RANK
    state = None
    first = 0
    for n, ((size, back), down_ref) in enumerate(zip(groups, down_refs)):
        shrink = None
        for low, high in cuts:
            awaited(waits[n, low])
            part = jnp.dot(
                rows_ref[places[back], :, low:high],
                down_ref[low:high],
                preferred_element_type=jnp.float32,
            )
            shrink = part if shrink is None else shrink + part
        if n == 0:
            awaited(waits["late"])
        for i in range(size):
            lanes, which = slice(i * LANES, (i + 1) * LANES), first + i
            chip = info_ref[2 + 2 * len(PIECES) + start + which]
            wanted = lane_slot + chip * (LANES // RANK)
            kept = jnp.where(row_slot[...] == wanted, shrink[:, lanes], 0.0)
            state = kept if state is None else state + kept
        if has_up:
            awaited(waits[n, quarter])
            height = up_ref.shape[0] // count
            for i in range(size):
                lanes, which = slice(i * LANES, (i + 1) * LANES), first + i
                for j in range(up_ref.shape[1] // LANES):
                    top = quarter + j * height
                    up_ref[
                        which * height : (which + 1) * height, j * LANES : (j + 1) * LANES
                    ] = down_ref[top : top + height, lanes]
        first += size
    for i, out_ref in enumerate(outs):
        own = state[i * rows : (i + 1) * rows]
        out_ref[...] = own + held_refs[i][...] if more else own


def absorb(info, row_slots, sides, tokens, width, groups, start, before, has_up):
    rows = tokens[0].shape[0]
    pieces = [piece for group, _ in groups for piece in group]
    sizes = [(len(group), back) for group, back in groups]
    quarter = tokens[0].shape[1] // 4
    height = pieces[0].shape[0]
    anywhere = pl.BlockSpec(memory_space=pl.ANY)
    vmem = pl.BlockSpec(memory_space=pltpu.VMEM)
    more = before is not None
    state = jax.ShapeDtypeStruct((rows, LANES), jnp.float32)
    up_rows = len(pieces) * (height - quarter) * LANES // width
    up = jax.ShapeDtypeStruct((up_rows, width), tokens[0].dtype)
    quarters = len({back for _, back in groups})
    cuts = len(QUARTER_CUTS) - 1
    copies = len(pieces) * (cuts + has_up) + len(sides) * (quarters * cuts + more) + 1
    outs = (state,) * len(sides) + (up,) * has_up
    return pl.pallas_call(
        functools.partial(absorb_kernel, sizes, start, sides, more, has_up),
        out_shape=outs,
        in_specs=[pl.BlockSpec(memory_space=pltpu.SMEM)]
        + [anywhere] * (1 + len(sides) + len(pieces) + len(sides) * more),
        out_specs=(vmem,) * len(outs),
        scratch_shapes=[
            pltpu.VMEM((quarters, len(sides) * rows, quarter), tokens[0].dtype),
            pltpu.VMEM(row_slots.shape, row_slots.dtype),
        ]
        + [pltpu.VMEM((rows, LANES), jnp.float32)] * (len(sides) * more)
        + [pltpu.VMEM((height, size * LANES), tokens[0].dtype) for size, _ in sizes]
        + [pltpu.SemaphoreType.DMA((copies,))],
        cost_estimate=pl.CostEstimate(
            flops=2 * len(sides) * rows * len(pieces) * LANES * quarter,
            bytes_accessed=2 * len(sides) * rows * quarters * quarter
            + 2 * len(pieces) * LANES * height,
            transcendentals=0,
        ),
        compiler_params=params(),
    )(info, row_slots, *tokens, *pieces, *(before or ()))


def finish_kernel(count, info_ref, row_slot_ref, mine_ref, theirs_ref, total_ref, *refs):
    sources, refs = refs[:count], refs[count:]
    out_ref, row_slot, mine, theirs, total, up, sems = refs
    rows = out_ref.shape[0]
    height = up.shape[0] // (len(PIECES) * 2)
    copies = []

    def begin(source, target):
        copies.append(pltpu.make_async_copy(source, target, sems.at[len(copies)]))
        copies[-1].start()

    begin(row_slot_ref.at[pl.ds(0, rows)], row_slot)
    begin(mine_ref, mine)
    begin(theirs_ref, theirs)
    for source in sources:
        for n in range(0, source.shape[0], height):
            first = pl.multiple_of(info_ref[len(copies) - 1], height)
            begin(source.at[pl.ds(n, height)], up.at[pl.ds(first, height)])
    begin(total_ref, total)
    awaited(copies[:3])
    shrink = mine[...] + theirs[...]
    lane_slot = lax.broadcasted_iota(jnp.int32, (1, LANES), 1) // RANK
    high, low = [], []
    for n in range(up.shape[0] // LANES):
        kept = jnp.where(row_slot[...] == lane_slot + n * (LANES // RANK), shrink, 0.0)
        high.append(kept.astype(jnp.bfloat16))
        low.append((kept - high[-1].astype(jnp.float32)).astype(jnp.bfloat16))
    both = jnp.concatenate([jnp.concatenate(part, axis=1) for part in (low, high)], axis=0)
    awaited(copies[3:-1])
    lora = jnp.dot(both, up[...], preferred_element_type=jnp.float32)
    awaited(copies[-1:])
    out_ref[...] = (total[...] + (lora[:rows] + lora[rows:])).astype(out_ref.dtype)


def finish(info, row_slots, mine, theirs, total, ups):
    rows, width = total.shape
    anywhere = pl.BlockSpec(memory_space=pl.ANY)
    up_rows = sum(up.shape[0] for up in ups)
    return pl.pallas_call(
        functools.partial(finish_kernel, len(ups)),
        out_shape=jax.ShapeDtypeStruct((rows, width), jnp.bfloat16),
        in_specs=[pl.BlockSpec(memory_space=pltpu.SMEM)] + [anywhere] * (4 + len(ups)),
        out_specs=pl.BlockSpec(memory_space=pltpu.VMEM),
        scratch_shapes=[
            pltpu.VMEM((rows, 1), jnp.int32),
            pltpu.VMEM((rows, LANES), jnp.float32),
            pltpu.VMEM((rows, LANES), jnp.float32),
            pltpu.VMEM((rows, width), jnp.float32),
            pltpu.VMEM((up_rows, width), ups[0].dtype),
            pltpu.SemaphoreType.DMA((4 + 2 * len(PIECES),)),
        ],
        cost_estimate=pl.CostEstimate(
            flops=4 * rows * width * up_rows,
            bytes_accessed=6 * rows * width + 2 * up_rows * width,
            transcendentals=0,
        ),
        compiler_params=params(),
    )(info, row_slots, mine, theirs, total, *ups)


def passed_round(
    tokens,
    row_adapter_index,
    adapter_storage_slot,
    base_value_weight,
    adapter_down_weight,
    adapter_up_weight,
):
    rows, depth = tokens.shape
    held, rank, _ = adapter_down_weight.shape
    width = adapter_up_weight.shape[2]
    axes = ("groups", "req")
    planes, owners = lax.axis_size("groups"), lax.axis_size("req")
    device = lax.axis_index("groups") * owners + lax.axis_index("req")

    def permuted(array, target):
        pairs = [
            (g * owners + r, target(g, r)) for g in range(planes) for r in range(owners)
        ]
        return lax.ppermute(array, axes, pairs)

    def along_z(r, by):
        return RING[(PLACE_IN_RING[r // 4] + by) % 4] * 4 + r % 4

    z_ring = lambda array: permuted(array, lambda g, r: g * owners + along_z(r, 1))
    z_back = lambda array: permuted(array, lambda g, r: g * owners + along_z(r, -1))
    x_swap = lambda array: permuted(array, lambda g, r: g * owners + (r ^ 2))
    y_swap = lambda array: permuted(array, lambda g, r: (1 - g) * owners + r)
    core_swap = lambda array: permuted(array, lambda g, r: g * owners + (r ^ 1))

    def chip(r, piece):
        return (along_z(r, -piece[0]) ^ (2 * piece[1])) // 2

    kernels = [PIECES[low:high] for low, high in zip(KERNEL_BOUNDS, KERNEL_BOUNDS[1:])]
    info_table = [
        [g, r % 2]
        + [
            chip(r, p) * LANES + core * held * rank + (g ^ p[2]) * (held // 2 * rank)
            for pieces in kernels
            for core in (r % 2, 1 - r % 2)
            for p in pieces
        ]
        + [chip(r, p) for p in PIECES]
        for g in range(planes)
        for r in range(owners)
    ]
    info = lax.dynamic_index_in_dim(
        jnp.array(np.array(info_table, np.int32)), device, 0, keepdims=False
    )

    def together(*values):
        return lax.optimization_barrier(values)

    def after(value, *others):
        return lax.optimization_barrier((value, *others))[0]

    there = core_swap(adapter_down_weight)
    row_slot = slots_of_rows(row_adapter_index, adapter_storage_slot)
    there, info, row_slot, tokens_late = together(there, info, row_slot, tokens)

    def piece(back, *others):
        return assemble(
            back, after(info, *others), adapter_down_weight, there, adapter_up_weight
        )

    front = piece(0)
    cuts = (0, depth // 2, depth)

    def base(number, before, *others):
        low, high = cuts[number : number + 2]
        return base_part(after(tokens, *others), base_value_weight, low, high, before)

    z1, x0 = z_ring(front), x_swap(front)
    other_slot = core_swap(row_slot[:, 0])
    total = base(0, None, front)
    row_slots = jnp.concatenate([row_slot, other_slot[:, None]], axis=0)
    z1, x0, front, total, row_slots, tokens_late = together(
        z1, x0, front, total, row_slots, tokens_late
    )

    z2, x1, yx0 = z_ring(z1), x_swap(z1), y_swap(x0)
    other = core_swap(tokens_late)
    total = base(1, total, total)
    z2, x1, yx0, front, total, info = together(z2, x1, yx0, front, total, info)

    def update(number, groups, before):
        return absorb(
            info,
            row_slots,
            (0, 1),
            [tokens, other],
            width,
            groups,
            KERNEL_BOUNDS[number],
            before,
            True,
        )

    z3, x2, yz2 = z_back(front), x_swap(z2), y_swap(z2)
    back = piece(1, z2)
    *state, up_a = update(0, [((front, z1, x0, z2), 0)], None)
    z3, x2, yz2, x1, back, state, total = together(z3, x2, yz2, x1, back, state, total)
    there_a = core_swap(up_a)

    zb1, x3, yx1 = z_ring(back), x_swap(z3), y_swap(x1)
    *state, up_b = update(1, [((back, yx0, yz2), 1)], state)
    zb1, x3, yx1, yz2, back, state, there_a = together(
        zb1, x3, yx1, yz2, back, state, there_a
    )
    there_b = core_swap(up_b)

    zb3, xyz2, yx3 = z_back(back), x_swap(yz2), y_swap(x3)
    *state, up_c = update(2, [((x1, z3, x2, x3), 0), ((zb1, yx1), 1)], state)
    zb3, xyz2, yx3, state, there_b = together(zb3, xyz2, yx3, state, there_b)
    there_c = core_swap(up_c)

    mine, others, up_d = update(3, [((zb3, xyz2, yx3), 1)], state)
    ups = (up_a, there_a, up_b, there_b, up_c, there_c, up_d, core_swap(up_d))
    return finish(info, row_slots, mine, core_swap(others), total, ups)


def solution(mesh):
    placed = (
        P(("groups", "req"), "tp"),
        P(("groups", "req"), None),
        P(),
        P("tp", None),
        P("req", None, "tp"),
        P("req", None, "tp"),
    )
    sizes = mesh.shape
    small = sizes["groups"] == 2 and sizes["req"] == 16 and sizes["tp"] == 1
    return jax.shard_map(
        passed_round if small else gathered,
        mesh=mesh,
        in_specs=placed,
        out_specs=P(("groups", "req"), "tp"),
        check_vma=False,
    )
```

```python
import functools

import jax
import jax.numpy as jnp
import numpy as np
from jax import lax
from jax.experimental import pallas as pl
from jax.experimental.pallas import tpu as pltpu
from jax.sharding import PartitionSpec as P

RING = (0, 1, 3, 2)
PLACE_IN_RING = (0, 1, 3, 2)
DEPTH_TILE = 1024
LANES = 128
RANK = 16

PIECES = (
    *((0, 0, 0), (1, 0, 0), (0, 1, 0), (2, 0, 0)),
    *((0, 0, 1), (0, 1, 1), (2, 0, 1)),
    *((1, 1, 0), (3, 0, 0), (2, 1, 0), (3, 1, 0), (1, 0, 1), (1, 1, 1)),
    *((3, 0, 1), (2, 1, 1), (3, 1, 1)),
)
KERNEL_BOUNDS = (0, 4, 7, 13, 16)
QUARTER_CUTS = (0, 512, 1024, 2048)
VMEM_BYTES = 64 * 1024 * 1024 - 512 * 1024


def slots_of_rows(row_adapter_index, adapter_storage_slot):
    catalog = jnp.arange(adapter_storage_slot.shape[0], dtype=jnp.int32)
    return jnp.sum(
        jnp.where(row_adapter_index == catalog[None, :], adapter_storage_slot[None, :], 0),
        axis=1,
        keepdims=True,
    )


def gathered(
    tokens,
    row_adapter_index,
    adapter_storage_slot,
    base_value_weight,
    adapter_down_weight,
    adapter_up_weight,
):
    adapter_count = adapter_storage_slot.shape[0]
    rank = adapter_down_weight.shape[1]
    slot_of = slots_of_rows(row_adapter_index, adapter_storage_slot)
    down_all = lax.all_gather(
        adapter_down_weight.reshape(-1, adapter_down_weight.shape[2]), "req", axis=0, tiled=True
    )
    up_all = lax.all_gather(
        adapter_up_weight.reshape(-1, adapter_up_weight.shape[2]), "req", axis=0, tiled=True
    )
    base_partial = jnp.dot(tokens, base_value_weight, preferred_element_type=jnp.float32)
    base_output = lax.psum_scatter(base_partial, "tp", scatter_dimension=1, tiled=True)
    shrink = lax.dot_general(
        tokens, down_all, (((1,), (1,)), ((), ())), preferred_element_type=jnp.float32
    )
    column_slot = jnp.arange(adapter_count * rank, dtype=jnp.int32) // rank
    shrink = jnp.where(slot_of == column_slot[None, :], shrink, 0.0)
    shrink = lax.psum(shrink, "tp")
    high = lax.reduce_precision(shrink, 8, 7)
    rest = shrink - high
    middle = lax.reduce_precision(rest, 8, 7)
    low = rest - middle
    lora = sum(
        jnp.dot(piece.astype(jnp.bfloat16), up_all, preferred_element_type=jnp.float32)
        for piece in (low, middle, high)
    )
    return (base_output + lora).astype(jnp.bfloat16)


def params():
    return pltpu.CompilerParams(vmem_limit_bytes=VMEM_BYTES)


def started(copies):
    for copy in copies:
        copy.start()


def awaited(copies):
    for copy in copies:
        copy.wait()


def assemble_kernel(back, info_ref, here_ref, there_ref, up_ref, out_ref, down_ref, own_ref, sems):
    y, core = info_ref[0], info_ref[1]
    place = 1 - y if back else y
    held, rank, quarter = down_ref.shape
    held //= 2
    columns = pl.ds(pl.multiple_of((2 * core + place) * quarter, quarter), quarter)
    copies = [
        pltpu.make_async_copy(
            source.at[:, :, columns], down_ref.at[pl.ds(of_core * held, held)], sems.at[n]
        )
        for n, (source, of_core) in enumerate(((here_ref, core), (there_ref, 1 - core)))
    ]
    copies.append(
        pltpu.make_async_copy(up_ref.at[pl.ds(place * (held // 2), held // 2)], own_ref, sems.at[2])
    )
    started(copies)
    awaited(copies)
    up = own_ref[...].reshape(held // 2 * rank, -1)
    rows = up.shape[0]
    for n in range(up.shape[1] // LANES):
        first = quarter + n * rows
        out_ref[first : first + rows] = up[:, n * LANES : (n + 1) * LANES]
    for n in range(0, quarter, LANES):
        block = down_ref[:, :, n : n + LANES].reshape(2 * held * rank, LANES)
        out_ref[n : n + LANES] = block.T


def assemble(back, info, here, there, up):
    held, rank, depth = here.shape
    width = up.shape[2]
    rows = depth // 4 + held // 2 * rank * width // LANES
    anywhere = pl.BlockSpec(memory_space=pl.ANY)
    return pl.pallas_call(
        functools.partial(assemble_kernel, back),
        out_shape=jax.ShapeDtypeStruct((rows, LANES), here.dtype),
        in_specs=[pl.BlockSpec(memory_space=pltpu.SMEM)] + [anywhere] * 3,
        out_specs=pl.BlockSpec(memory_space=pltpu.VMEM),
        scratch_shapes=[
            pltpu.VMEM((2 * held, rank, depth // 4), here.dtype),
            pltpu.VMEM((held // 2, rank, width), up.dtype),
            pltpu.SemaphoreType.DMA((3,)),
        ],
        compiler_params=params(),
    )(info, here, there, up)


def base_kernel(steps, tokens_ref, weight_ref, *refs):
    step = pl.program_id(0)
    more = len(refs) > 1
    out_ref = refs[1] if more else refs[0]
    copies = [pltpu.make_async_copy(refs[0], refs[2], refs[3].at[0])] if more else []
    part = jnp.dot(tokens_ref[...], weight_ref[...], preferred_element_type=jnp.float32)

    @pl.when(step == 0)
    def _():
        started(copies)
        out_ref[...] = part

    @pl.when(step > 0)
    def _():
        out_ref[...] += part

    if more:

        @pl.when(step == steps - 1)
        def _():
            awaited(copies)
            out_ref[...] += refs[2][...]


def base_part(tokens, weight, begin, end, total=None):
    rows, depth = tokens.shape
    width = weight.shape[1]
    steps, first = (end - begin) // DEPTH_TILE, begin // DEPTH_TILE
    result = jax.ShapeDtypeStruct((rows, width), jnp.float32)
    more = total is not None
    return pl.pallas_call(
        functools.partial(base_kernel, steps),
        out_shape=result,
        grid=(steps,),
        in_specs=[
            pl.BlockSpec((rows, DEPTH_TILE), lambda k: (0, first + k)),
            pl.BlockSpec((DEPTH_TILE, width), lambda k: (first + k, 0)),
        ]
        + [pl.BlockSpec(memory_space=pl.ANY)] * more,
        out_specs=pl.BlockSpec((rows, width), lambda k: (0, 0)),
        scratch_shapes=[pltpu.VMEM((rows, width), jnp.float32), pltpu.SemaphoreType.DMA((1,))]
        if more
        else [],
        cost_estimate=pl.CostEstimate(
            flops=2 * rows * width * (end - begin),
            bytes_accessed=2 * (rows + width) * (end - begin) + 4 * rows * width,
            transcendentals=0,
        ),
        compiler_params=params(),
    )(tokens, weight, *([total] if more else []))


def absorb_kernel(groups, start, sides, more, has_up, keep_up, info_ref, row_slot_ref, *refs):
    count = sum(size for size, _ in groups)
    token_refs, sources, refs = refs[: len(sides)], refs[len(sides) :][:count], refs[len(sides) + count :]
    before, refs = refs[: len(sides) * more], refs[len(sides) * more :]
    ups_before, refs = refs[:keep_up], refs[keep_up:]
    outs, refs = refs[: len(sides)], refs[len(sides) :]
    up_ref, refs = (refs[0], refs[1:]) if has_up else (None, refs)
    rows_ref, row_slot, held_refs, refs = refs[0], refs[1], refs[2 : 2 + len(before)], refs[2 + len(before) :]
    down_refs, sems = refs[:-1], refs[-1]
    rows = token_refs[0].shape[0]
    quarter = rows_ref.shape[2]
    y, core = info_ref[0], info_ref[1]
    cuts = list(zip(QUARTER_CUTS, QUARTER_CUTS[1:]))
    copies, waits = [], {}

    def begin(key, source, target):
        copy = pltpu.make_async_copy(source, target, sems.at[len(copies)])
        copies.append(copy)
        waits.setdefault(key, []).append(copy)
        copy.start()

    places = {}
    first = 0
    for n, ((size, back), down_ref) in enumerate(zip(groups, down_refs)):
        load = back not in places
        place = places.setdefault(back, len(places))
        ends = cuts + [(quarter, sources[0].shape[0])] * has_up
        for low, high in ends:
            for i in range(size):
                begin(
                    (n, low),
                    sources[first + i].at[pl.ds(low, high - low)],
                    down_ref.at[pl.ds(low, high - low), pl.ds(i * LANES, LANES)],
                )
            if not load or low == quarter:
                continue
            for i, source in enumerate(token_refs):
                column = (2 * core + (1 - y if back else y)) * quarter + low
                begin(
                    (n, low),
                    source.at[:, pl.ds(pl.multiple_of(column, QUARTER_CUTS[1]), high - low)],
                    rows_ref.at[place, pl.ds(i * rows, rows), pl.ds(low, high - low)],
                )
        first += size
    begin("late", row_slot_ref, row_slot)
    for source, target in zip(before, held_refs):
        begin("late", source, target)
    kept_rows = 0
    for source in ups_before:
        kept_rows = source.shape[0]
        begin("late", source, up_ref.at[pl.ds(0, kept_rows)])
    lane_slot = lax.broadcasted_iota(jnp.int32, (1, LANES), 1) // RANK
    state = None
    first = 0
    for n, ((size, back), down_ref) in enumerate(zip(groups, down_refs)):
        shrink = None
        for low, high in cuts:
            awaited(waits[n, low])
            part = jnp.dot(
                rows_ref[places[back], :, low:high],
                down_ref[low:high],
                preferred_element_type=jnp.float32,
            )
            shrink = part if shrink is None else shrink + part
        if n == 0:
            awaited(waits["late"])
        for i in range(size):
            lanes, which = slice(i * LANES, (i + 1) * LANES), first + i
            chip = info_ref[2 + 2 * len(PIECES) + start + which]
            wanted = lane_slot + chip * (LANES // RANK)
            kept = jnp.where(row_slot[...] == wanted, shrink[:, lanes], 0.0)
            state = kept if state is None else state + kept
        if has_up:
            awaited(waits[n, quarter])
            height = (up_ref.shape[0] - kept_rows) // count
            for i in range(size):
                lanes, which = slice(i * LANES, (i + 1) * LANES), first + i
                for j in range(up_ref.shape[1] // LANES):
                    top = quarter + j * height
                    bottom = kept_rows + which * height
                    up_ref[bottom : bottom + height, j * LANES : (j + 1) * LANES] = down_ref[
                        top : top + height, lanes
                    ]
        first += size
    for i, out_ref in enumerate(outs):
        own = state[i * rows : (i + 1) * rows]
        out_ref[...] = own + held_refs[i][...] if more else own


def absorb(info, row_slots, sides, tokens, width, groups, start, before, has_up, up_before):
    rows = tokens[0].shape[0]
    pieces = [piece for group, _ in groups for piece in group]
    sizes = [(len(group), back) for group, back in groups]
    quarter = tokens[0].shape[1] // 4
    height = pieces[0].shape[0]
    anywhere = pl.BlockSpec(memory_space=pl.ANY)
    vmem = pl.BlockSpec(memory_space=pltpu.VMEM)
    more = before is not None
    state = jax.ShapeDtypeStruct((rows, LANES), jnp.float32)
    keep_up = up_before is not None
    up_rows = len(pieces) * (height - quarter) * LANES // width
    if keep_up:
        up_rows += up_before.shape[0]
    up = jax.ShapeDtypeStruct((up_rows, width), tokens[0].dtype)
    quarters = len({back for _, back in groups})
    cuts = len(QUARTER_CUTS) - 1
    copies = len(pieces) * (cuts + has_up) + len(sides) * (quarters * cuts + more) + 1 + keep_up
    outs = (state,) * len(sides) + (up,) * has_up
    return pl.pallas_call(
        functools.partial(absorb_kernel, sizes, start, sides, more, has_up, keep_up),
        out_shape=outs,
        in_specs=[pl.BlockSpec(memory_space=pltpu.SMEM)]
        + [anywhere] * (1 + len(sides) + len(pieces) + len(sides) * more + keep_up),
        out_specs=(vmem,) * len(outs),
        scratch_shapes=[
            pltpu.VMEM((quarters, len(sides) * rows, quarter), tokens[0].dtype),
            pltpu.VMEM(row_slots.shape, row_slots.dtype),
        ]
        + [pltpu.VMEM((rows, LANES), jnp.float32)] * (len(sides) * more)
        + [pltpu.VMEM((height, size * LANES), tokens[0].dtype) for size, _ in sizes]
        + [pltpu.SemaphoreType.DMA((copies,))],
        cost_estimate=pl.CostEstimate(
            flops=2 * len(sides) * rows * len(pieces) * LANES * quarter,
            bytes_accessed=2 * len(sides) * rows * quarters * quarter
            + 2 * len(pieces) * LANES * height,
            transcendentals=0,
        ),
        compiler_params=params(),
    )(info, row_slots, *tokens, *pieces, *(before or ()), *([up_before] if keep_up else []))


def finish_kernel(count, info_ref, row_slot_ref, mine_ref, theirs_ref, total_ref, *refs):
    sources, refs = refs[:count], refs[count:]
    out_ref, row_slot, mine, theirs, total, up, sems = refs
    rows = out_ref.shape[0]
    height = up.shape[0] // (len(PIECES) * 2)
    copies = []

    def begin(source, target):
        copies.append(pltpu.make_async_copy(source, target, sems.at[len(copies)]))
        copies[-1].start()

    begin(row_slot_ref.at[pl.ds(0, rows)], row_slot)
    begin(mine_ref, mine)
    begin(theirs_ref, theirs)
    for source in sources:
        for n in range(0, source.shape[0], height):
            first = pl.multiple_of(info_ref[len(copies) - 1], height)
            begin(source.at[pl.ds(n, height)], up.at[pl.ds(first, height)])
    begin(total_ref, total)
    awaited(copies[:3])
    shrink = mine[...] + theirs[...]
    lane_slot = lax.broadcasted_iota(jnp.int32, (1, LANES), 1) // RANK
    high, low = [], []
    for n in range(up.shape[0] // LANES):
        kept = jnp.where(row_slot[...] == lane_slot + n * (LANES // RANK), shrink, 0.0)
        high.append(kept.astype(jnp.bfloat16))
        low.append((kept - high[-1].astype(jnp.float32)).astype(jnp.bfloat16))
    both = jnp.concatenate([jnp.concatenate(part, axis=1) for part in (low, high)], axis=0)
    awaited(copies[3:-1])
    lora = jnp.dot(both, up[...], preferred_element_type=jnp.float32)
    awaited(copies[-1:])
    out_ref[...] = (total[...] + (lora[:rows] + lora[rows:])).astype(out_ref.dtype)


def finish(info, row_slots, mine, theirs, total, ups):
    rows, width = total.shape
    anywhere = pl.BlockSpec(memory_space=pl.ANY)
    up_rows = sum(up.shape[0] for up in ups)
    return pl.pallas_call(
        functools.partial(finish_kernel, len(ups)),
        out_shape=jax.ShapeDtypeStruct((rows, width), jnp.bfloat16),
        in_specs=[pl.BlockSpec(memory_space=pltpu.SMEM)] + [anywhere] * (4 + len(ups)),
        out_specs=pl.BlockSpec(memory_space=pltpu.VMEM),
        scratch_shapes=[
            pltpu.VMEM((rows, 1), jnp.int32),
            pltpu.VMEM((rows, LANES), jnp.float32),
            pltpu.VMEM((rows, LANES), jnp.float32),
            pltpu.VMEM((rows, width), jnp.float32),
            pltpu.VMEM((up_rows, width), ups[0].dtype),
            pltpu.SemaphoreType.DMA((4 + 2 * len(PIECES),)),
        ],
        cost_estimate=pl.CostEstimate(
            flops=4 * rows * width * up_rows,
            bytes_accessed=6 * rows * width + 2 * up_rows * width,
            transcendentals=0,
        ),
        compiler_params=params(),
    )(info, row_slots, mine, theirs, total, *ups)


def passed_round(
    tokens,
    row_adapter_index,
    adapter_storage_slot,
    base_value_weight,
    adapter_down_weight,
    adapter_up_weight,
):
    rows, depth = tokens.shape
    held, rank, _ = adapter_down_weight.shape
    width = adapter_up_weight.shape[2]
    axes = ("groups", "req")
    planes, owners = lax.axis_size("groups"), lax.axis_size("req")
    device = lax.axis_index("groups") * owners + lax.axis_index("req")

    def permuted(array, target):
        pairs = [
            (g * owners + r, target(g, r)) for g in range(planes) for r in range(owners)
        ]
        return lax.ppermute(array, axes, pairs)

    def along_z(r, by):
        return RING[(PLACE_IN_RING[r // 4] + by) % 4] * 4 + r % 4

    z_ring = lambda array: permuted(array, lambda g, r: g * owners + along_z(r, 1))
    z_back = lambda array: permuted(array, lambda g, r: g * owners + along_z(r, -1))
    x_swap = lambda array: permuted(array, lambda g, r: g * owners + (r ^ 2))
    y_swap = lambda array: permuted(array, lambda g, r: (1 - g) * owners + r)
    core_swap = lambda array: permuted(array, lambda g, r: g * owners + (r ^ 1))

    def chip(r, piece):
        return (along_z(r, -piece[0]) ^ (2 * piece[1])) // 2

    kernels = (PIECES[: KERNEL_BOUNDS[-2]], PIECES[KERNEL_BOUNDS[-2] :])
    info_table = [
        [g, r % 2]
        + [
            chip(r, p) * LANES + core * held * rank + (g ^ p[2]) * (held // 2 * rank)
            for pieces in kernels
            for core in (r % 2, 1 - r % 2)
            for p in pieces
        ]
        + [chip(r, p) for p in PIECES]
        for g in range(planes)
        for r in range(owners)
    ]
    info = lax.dynamic_index_in_dim(
        jnp.array(np.array(info_table, np.int32)), device, 0, keepdims=False
    )

    def together(*values):
        return lax.optimization_barrier(values)

    def after(value, *others):
        return lax.optimization_barrier((value, *others))[0]

    there = core_swap(adapter_down_weight)
    row_slot = slots_of_rows(row_adapter_index, adapter_storage_slot)
    there, info, row_slot, tokens_late = together(there, info, row_slot, tokens)

    def piece(back, *others):
        return assemble(
            back, after(info, *others), adapter_down_weight, there, adapter_up_weight
        )

    front = piece(0)
    cuts = (0, depth // 2, depth)

    def base(number, before, *others):
        low, high = cuts[number : number + 2]
        return base_part(after(tokens, *others), base_value_weight, low, high, before)

    z1, x0 = z_ring(front), x_swap(front)
    other = core_swap(tokens_late)
    other_slot = core_swap(row_slot[:, 0])
    total = base(0, None, front)
    row_slots = jnp.concatenate([row_slot, other_slot[:, None]], axis=0)
    z1, x0, front, total, row_slots = together(z1, x0, front, total, row_slots)

    z2, x1, yx0 = z_ring(z1), x_swap(z1), y_swap(x0)
    total = base(1, total, total)
    z2, x1, yx0, front, other, total, info = together(z2, x1, yx0, front, other, total, info)

    def update(number, groups, before, up_before=None):
        return absorb(
            info,
            row_slots,
            (0, 1),
            [tokens, other],
            width,
            groups,
            KERNEL_BOUNDS[number],
            before,
            True,
            up_before,
        )

    z3, x2, yz2 = z_back(front), x_swap(z2), y_swap(z2)
    back = piece(1, z2)
    *state, up = update(0, [((front, z1, x0, z2), 0)], None)
    z3, x2, yz2, x1, back, state, total = together(z3, x2, yz2, x1, back, state, total)

    zb1, x3, yx1 = z_ring(back), x_swap(z3), y_swap(x1)
    *state, up = update(1, [((back, yx0, yz2), 1)], state, up)
    zb1, x3, yx1, yz2, back, state = together(zb1, x3, yx1, yz2, back, state)

    zb3, xyz2, yx3 = z_back(back), x_swap(yz2), y_swap(x3)
    *state, up = update(2, [((x1, z3, x2, x3), 0), ((zb1, yx1), 1)], state, up)
    zb3, xyz2, yx3, state = together(zb3, xyz2, yx3, state)
    there_up = core_swap(up)

    mine, others, last_up = update(3, [((zb3, xyz2, yx3), 1)], state)
    ups = (up, there_up, last_up, core_swap(last_up))
    return finish(info, row_slots, mine, core_swap(others), total, ups)


def solution(mesh):
    placed = (
        P(("groups", "req"), "tp"),
        P(("groups", "req"), None),
        P(),
        P("tp", None),
        P("req", None, "tp"),
        P("req", None, "tp"),
    )
    sizes = mesh.shape
    small = sizes["groups"] == 2 and sizes["req"] == 16 and sizes["tp"] == 1
    return jax.shard_map(
        passed_round if small else gathered,
        mesh=mesh,
        in_specs=placed,
        out_specs=P(("groups", "req"), "tp"),
        check_vma=False,
    )
```

```python
import functools

import jax
import jax.numpy as jnp
import numpy as np
from jax import lax
from jax.experimental import pallas as pl
from jax.experimental.pallas import tpu as pltpu
from jax.sharding import PartitionSpec as P

RING = (0, 1, 3, 2)
PLACE_IN_RING = (0, 1, 3, 2)
DEPTH_TILE = 1024
LANES = 128
RANK = 16

PIECES = (
    *((0, 0, 0), (1, 0, 0), (0, 1, 0), (2, 0, 0)),
    *((0, 0, 1), (0, 1, 1), (2, 0, 1)),
    *((1, 1, 0), (3, 0, 0), (2, 1, 0), (3, 1, 0), (1, 0, 1), (1, 1, 1)),
    *((3, 0, 1), (2, 1, 1), (3, 1, 1)),
)
KERNEL_BOUNDS = (0, 4, 7, 13, 16)
QUARTER_CUTS = (0, 512, 1024, 2048)
VMEM_BYTES = 64 * 1024 * 1024 - 512 * 1024


def slots_of_rows(row_adapter_index, adapter_storage_slot):
    catalog = jnp.arange(adapter_storage_slot.shape[0], dtype=jnp.int32)
    return jnp.sum(
        jnp.where(row_adapter_index == catalog[None, :], adapter_storage_slot[None, :], 0),
        axis=1,
        keepdims=True,
    )


def gathered(
    tokens,
    row_adapter_index,
    adapter_storage_slot,
    base_value_weight,
    adapter_down_weight,
    adapter_up_weight,
):
    adapter_count = adapter_storage_slot.shape[0]
    rank = adapter_down_weight.shape[1]
    slot_of = slots_of_rows(row_adapter_index, adapter_storage_slot)
    down_all = lax.all_gather(
        adapter_down_weight.reshape(-1, adapter_down_weight.shape[2]), "req", axis=0, tiled=True
    )
    up_all = lax.all_gather(
        adapter_up_weight.reshape(-1, adapter_up_weight.shape[2]), "req", axis=0, tiled=True
    )
    base_partial = jnp.dot(tokens, base_value_weight, preferred_element_type=jnp.float32)
    base_output = lax.psum_scatter(base_partial, "tp", scatter_dimension=1, tiled=True)
    shrink = lax.dot_general(
        tokens, down_all, (((1,), (1,)), ((), ())), preferred_element_type=jnp.float32
    )
    column_slot = jnp.arange(adapter_count * rank, dtype=jnp.int32) // rank
    shrink = jnp.where(slot_of == column_slot[None, :], shrink, 0.0)
    shrink = lax.psum(shrink, "tp")
    high = lax.reduce_precision(shrink, 8, 7)
    rest = shrink - high
    middle = lax.reduce_precision(rest, 8, 7)
    low = rest - middle
    lora = sum(
        jnp.dot(piece.astype(jnp.bfloat16), up_all, preferred_element_type=jnp.float32)
        for piece in (low, middle, high)
    )
    return (base_output + lora).astype(jnp.bfloat16)


def params():
    return pltpu.CompilerParams(vmem_limit_bytes=VMEM_BYTES)


def started(copies):
    for copy in copies:
        copy.start()


def awaited(copies):
    for copy in copies:
        copy.wait()


def assemble_kernel(back, info_ref, here_ref, there_ref, up_ref, out_ref, down_ref, own_ref, sems):
    y, core = info_ref[0], info_ref[1]
    place = 1 - y if back else y
    held, rank, quarter = down_ref.shape
    held //= 2
    columns = pl.ds(pl.multiple_of((2 * core + place) * quarter, quarter), quarter)
    copies = [
        pltpu.make_async_copy(
            source.at[:, :, columns], down_ref.at[pl.ds(of_core * held, held)], sems.at[n]
        )
        for n, (source, of_core) in enumerate(((here_ref, core), (there_ref, 1 - core)))
    ]
    copies.append(
        pltpu.make_async_copy(up_ref.at[pl.ds(place * (held // 2), held // 2)], own_ref, sems.at[2])
    )
    started(copies)
    awaited(copies)
    up = own_ref[...].reshape(held // 2 * rank, -1)
    rows = up.shape[0]
    for n in range(up.shape[1] // LANES):
        first = quarter + n * rows
        out_ref[first : first + rows] = up[:, n * LANES : (n + 1) * LANES]
    for n in range(0, quarter, LANES):
        block = down_ref[:, :, n : n + LANES].reshape(2 * held * rank, LANES)
        out_ref[n : n + LANES] = block.T


def assemble(back, info, here, there, up):
    held, rank, depth = here.shape
    width = up.shape[2]
    rows = depth // 4 + held // 2 * rank * width // LANES
    anywhere = pl.BlockSpec(memory_space=pl.ANY)
    return pl.pallas_call(
        functools.partial(assemble_kernel, back),
        out_shape=jax.ShapeDtypeStruct((rows, LANES), here.dtype),
        in_specs=[pl.BlockSpec(memory_space=pltpu.SMEM)] + [anywhere] * 3,
        out_specs=pl.BlockSpec(memory_space=pltpu.VMEM),
        scratch_shapes=[
            pltpu.VMEM((2 * held, rank, depth // 4), here.dtype),
            pltpu.VMEM((held // 2, rank, width), up.dtype),
            pltpu.SemaphoreType.DMA((3,)),
        ],
        compiler_params=params(),
    )(info, here, there, up)


def base_kernel(steps, tokens_ref, weight_ref, *refs):
    step = pl.program_id(0)
    more = len(refs) > 1
    out_ref = refs[1] if more else refs[0]
    copies = [pltpu.make_async_copy(refs[0], refs[2], refs[3].at[0])] if more else []
    part = jnp.dot(tokens_ref[...], weight_ref[...], preferred_element_type=jnp.float32)

    @pl.when(step == 0)
    def _():
        started(copies)
        out_ref[...] = part

    @pl.when(step > 0)
    def _():
        out_ref[...] += part

    if more:

        @pl.when(step == steps - 1)
        def _():
            awaited(copies)
            out_ref[...] += refs[2][...]


def base_part(tokens, weight, begin, end, total=None):
    rows, depth = tokens.shape
    width = weight.shape[1]
    steps, first = (end - begin) // DEPTH_TILE, begin // DEPTH_TILE
    result = jax.ShapeDtypeStruct((rows, width), jnp.float32)
    more = total is not None
    return pl.pallas_call(
        functools.partial(base_kernel, steps),
        out_shape=result,
        grid=(steps,),
        in_specs=[
            pl.BlockSpec((rows, DEPTH_TILE), lambda k: (0, first + k)),
            pl.BlockSpec((DEPTH_TILE, width), lambda k: (first + k, 0)),
        ]
        + [pl.BlockSpec(memory_space=pl.ANY)] * more,
        out_specs=pl.BlockSpec((rows, width), lambda k: (0, 0)),
        scratch_shapes=[pltpu.VMEM((rows, width), jnp.float32), pltpu.SemaphoreType.DMA((1,))]
        if more
        else [],
        cost_estimate=pl.CostEstimate(
            flops=2 * rows * width * (end - begin),
            bytes_accessed=2 * (rows + width) * (end - begin) + 4 * rows * width,
            transcendentals=0,
        ),
        compiler_params=params(),
    )(tokens, weight, *([total] if more else []))


def absorb_kernel(groups, start, sides, more, has_up, info_ref, row_slot_ref, *refs):
    count = sum(size for size, _ in groups)
    token_refs, sources, refs = refs[: len(sides)], refs[len(sides) :][:count], refs[len(sides) + count :]
    before, refs = refs[: len(sides) * more], refs[len(sides) * more :]
    outs, refs = refs[: len(sides)], refs[len(sides) :]
    up_ref, refs = (refs[0], refs[1:]) if has_up else (None, refs)
    rows_ref, row_slot, held_refs, refs = refs[0], refs[1], refs[2 : 2 + len(before)], refs[2 + len(before) :]
    down_refs, sems = refs[:-1], refs[-1]
    rows = token_refs[0].shape[0]
    quarter = rows_ref.shape[2]
    y, core = info_ref[0], info_ref[1]
    cuts = list(zip(QUARTER_CUTS, QUARTER_CUTS[1:]))
    copies, waits = [], {}

    def begin(key, source, target):
        copy = pltpu.make_async_copy(source, target, sems.at[len(copies)])
        copies.append(copy)
        waits.setdefault(key, []).append(copy)
        copy.start()

    places = {}
    first = 0
    for n, ((size, back), down_ref) in enumerate(zip(groups, down_refs)):
        load = back not in places
        place = places.setdefault(back, len(places))
        ends = cuts + [(quarter, sources[0].shape[0])] * has_up
        for low, high in ends:
            for i in range(size):
                begin(
                    (n, low),
                    sources[first + i].at[pl.ds(low, high - low)],
                    down_ref.at[pl.ds(low, high - low), pl.ds(i * LANES, LANES)],
                )
            if not load or low == quarter:
                continue
            for i, source in enumerate(token_refs):
                column = (2 * core + (1 - y if back else y)) * quarter + low
                begin(
                    (n, low),
                    source.at[:, pl.ds(pl.multiple_of(column, QUARTER_CUTS[1]), high - low)],
                    rows_ref.at[place, pl.ds(i * rows, rows), pl.ds(low, high - low)],
                )
        first += size
    begin("late", row_slot_ref, row_slot)
    for source, target in zip(before, held_refs):
        begin("late", source, target)
    lane_slot = lax.broadcasted_iota(jnp.int32, (1, LANES), 1) // RANK
    state = None
    first = 0
    for n, ((size, back), down_ref) in enumerate(zip(groups, down_refs)):
        shrink = None
        for low, high in cuts:
            awaited(waits[n, low])
            part = jnp.dot(
                rows_ref[places[back], :, low:high],
                down_ref[low:high],
                preferred_element_type=jnp.float32,
            )
            shrink = part if shrink is None else shrink + part
        if n == 0:
            awaited(waits["late"])
        for i in range(size):
            lanes, which = slice(i * LANES, (i + 1) * LANES), first + i
            chip = info_ref[2 + 2 * len(PIECES) + start + which]
            wanted = lane_slot + chip * (LANES // RANK)
            kept = jnp.where(row_slot[...] == wanted, shrink[:, lanes], 0.0)
            state = kept if state is None else state + kept
        if has_up:
            awaited(waits[n, quarter])
            height = up_ref.shape[0] // count
            for i in range(size):
                lanes, which = slice(i * LANES, (i + 1) * LANES), first + i
                for j in range(up_ref.shape[1] // LANES):
                    top = quarter + j * height
                    up_ref[
                        which * height : (which + 1) * height, j * LANES : (j + 1) * LANES
                    ] = down_ref[top : top + height, lanes]
        first += size
    for i, out_ref in enumerate(outs):
        own = state[i * rows : (i + 1) * rows]
        out_ref[...] = own + held_refs[i][...] if more else own


def absorb(info, row_slots, sides, tokens, width, groups, start, before, has_up):
    rows = tokens[0].shape[0]
    pieces = [piece for group, _ in groups for piece in group]
    sizes = [(len(group), back) for group, back in groups]
    quarter = tokens[0].shape[1] // 4
    height = pieces[0].shape[0]
    anywhere = pl.BlockSpec(memory_space=pl.ANY)
    vmem = pl.BlockSpec(memory_space=pltpu.VMEM)
    more = before is not None
    state = jax.ShapeDtypeStruct((rows, LANES), jnp.float32)
    up_rows = len(pieces) * (height - quarter) * LANES // width
    up = jax.ShapeDtypeStruct((up_rows, width), tokens[0].dtype)
    quarters = len({back for _, back in groups})
    cuts = len(QUARTER_CUTS) - 1
    copies = len(pieces) * (cuts + has_up) + len(sides) * (quarters * cuts + more) + 1
    outs = (state,) * len(sides) + (up,) * has_up
    return pl.pallas_call(
        functools.partial(absorb_kernel, sizes, start, sides, more, has_up),
        out_shape=outs,
        in_specs=[pl.BlockSpec(memory_space=pltpu.SMEM)]
        + [anywhere] * (1 + len(sides) + len(pieces) + len(sides) * more),
        out_specs=(vmem,) * len(outs),
        scratch_shapes=[
            pltpu.VMEM((quarters, len(sides) * rows, quarter), tokens[0].dtype),
            pltpu.VMEM(row_slots.shape, row_slots.dtype),
        ]
        + [pltpu.VMEM((rows, LANES), jnp.float32)] * (len(sides) * more)
        + [pltpu.VMEM((height, size * LANES), tokens[0].dtype) for size, _ in sizes]
        + [pltpu.SemaphoreType.DMA((copies,))],
        cost_estimate=pl.CostEstimate(
            flops=2 * len(sides) * rows * len(pieces) * LANES * quarter,
            bytes_accessed=2 * len(sides) * rows * quarters * quarter
            + 2 * len(pieces) * LANES * height,
            transcendentals=0,
        ),
        compiler_params=params(),
    )(info, row_slots, *tokens, *pieces, *(before or ()))


def finish_kernel(count, info_ref, row_slot_ref, mine_ref, theirs_ref, total_ref, *refs):
    sources, refs = refs[:count], refs[count:]
    out_ref, row_slot, mine, theirs, total, up, sems = refs
    rows = out_ref.shape[0]
    height = up.shape[0] // (len(PIECES) * 2)
    copies = []

    def begin(source, target):
        copies.append(pltpu.make_async_copy(source, target, sems.at[len(copies)]))
        copies[-1].start()

    begin(row_slot_ref.at[pl.ds(0, rows)], row_slot)
    begin(mine_ref, mine)
    begin(theirs_ref, theirs)
    for source in sources:
        for n in range(0, source.shape[0], height):
            first = pl.multiple_of(info_ref[len(copies) - 1], height)
            begin(source.at[pl.ds(n, height)], up.at[pl.ds(first, height)])
    begin(total_ref, total)
    awaited(copies[:3])
    shrink = mine[...] + theirs[...]
    lane_slot = lax.broadcasted_iota(jnp.int32, (1, LANES), 1) // RANK
    high, low = [], []
    for n in range(up.shape[0] // LANES):
        kept = jnp.where(row_slot[...] == lane_slot + n * (LANES // RANK), shrink, 0.0)
        high.append(kept.astype(jnp.bfloat16))
        low.append((kept - high[-1].astype(jnp.float32)).astype(jnp.bfloat16))
    both = jnp.concatenate([jnp.concatenate(part, axis=1) for part in (low, high)], axis=0)
    awaited(copies[3:-1])
    lora = jnp.dot(both, up[...], preferred_element_type=jnp.float32)
    awaited(copies[-1:])
    out_ref[...] = (total[...] + (lora[:rows] + lora[rows:])).astype(out_ref.dtype)


def finish(info, row_slots, mine, theirs, total, ups):
    rows, width = total.shape
    anywhere = pl.BlockSpec(memory_space=pl.ANY)
    up_rows = sum(up.shape[0] for up in ups)
    return pl.pallas_call(
        functools.partial(finish_kernel, len(ups)),
        out_shape=jax.ShapeDtypeStruct((rows, width), jnp.bfloat16),
        in_specs=[pl.BlockSpec(memory_space=pltpu.SMEM)] + [anywhere] * (4 + len(ups)),
        out_specs=pl.BlockSpec(memory_space=pltpu.VMEM),
        scratch_shapes=[
            pltpu.VMEM((rows, 1), jnp.int32),
            pltpu.VMEM((rows, LANES), jnp.float32),
            pltpu.VMEM((rows, LANES), jnp.float32),
            pltpu.VMEM((rows, width), jnp.float32),
            pltpu.VMEM((up_rows, width), ups[0].dtype),
            pltpu.SemaphoreType.DMA((4 + 2 * len(PIECES),)),
        ],
        cost_estimate=pl.CostEstimate(
            flops=4 * rows * width * up_rows,
            bytes_accessed=6 * rows * width + 2 * up_rows * width,
            transcendentals=0,
        ),
        compiler_params=params(),
    )(info, row_slots, mine, theirs, total, *ups)


def passed_round(
    tokens,
    row_adapter_index,
    adapter_storage_slot,
    base_value_weight,
    adapter_down_weight,
    adapter_up_weight,
):
    rows, depth = tokens.shape
    held, rank, _ = adapter_down_weight.shape
    width = adapter_up_weight.shape[2]
    axes = ("groups", "req")
    planes, owners = lax.axis_size("groups"), lax.axis_size("req")
    device = lax.axis_index("groups") * owners + lax.axis_index("req")

    def permuted(array, target):
        pairs = [
            (g * owners + r, target(g, r)) for g in range(planes) for r in range(owners)
        ]
        return lax.ppermute(array, axes, pairs)

    def along_z(r, by):
        return RING[(PLACE_IN_RING[r // 4] + by) % 4] * 4 + r % 4

    z_ring = lambda array: permuted(array, lambda g, r: g * owners + along_z(r, 1))
    z_back = lambda array: permuted(array, lambda g, r: g * owners + along_z(r, -1))
    x_swap = lambda array: permuted(array, lambda g, r: g * owners + (r ^ 2))
    y_swap = lambda array: permuted(array, lambda g, r: (1 - g) * owners + r)
    core_swap = lambda array: permuted(array, lambda g, r: g * owners + (r ^ 1))

    def chip(r, piece):
        return (along_z(r, -piece[0]) ^ (2 * piece[1])) // 2

    kernels = [PIECES[low:high] for low, high in zip(KERNEL_BOUNDS, KERNEL_BOUNDS[1:])]
    info_table = [
        [g, r % 2]
        + [
            chip(r, p) * LANES + core * held * rank + (g ^ p[2]) * (held // 2 * rank)
            for pieces in kernels
            for core in (r % 2, 1 - r % 2)
            for p in pieces
        ]
        + [chip(r, p) for p in PIECES]
        for g in range(planes)
        for r in range(owners)
    ]
    info = lax.dynamic_index_in_dim(
        jnp.array(np.array(info_table, np.int32)), device, 0, keepdims=False
    )

    def together(*values):
        return lax.optimization_barrier(values)

    def after(value, *others):
        return lax.optimization_barrier((value, *others))[0]

    there = core_swap(adapter_down_weight)
    row_slot = slots_of_rows(row_adapter_index, adapter_storage_slot)
    there, info, row_slot, tokens_late = together(there, info, row_slot, tokens)

    def piece(back, *others):
        return assemble(
            back, after(info, *others), adapter_down_weight, there, adapter_up_weight
        )

    front = piece(0)
    cuts = (0, depth // 2, depth)

    def base(number, before, *others):
        low, high = cuts[number : number + 2]
        return base_part(after(tokens, *others), base_value_weight, low, high, before)

    z1, x0 = z_ring(front), x_swap(front)
    other = core_swap(tokens_late)
    total = base(0, None, front)
    z1, x0, front, total = together(z1, x0, front, total)

    z2, x1, yx0 = z_ring(z1), x_swap(z1), y_swap(x0)
    total = base(1, total, total)
    other_slot = core_swap(after(row_slot[:, 0], total))
    z2, x1, yx0, front, other, total, info, other_slot = together(
        z2, x1, yx0, front, other, total, info, other_slot
    )
    row_slots = jnp.concatenate([row_slot, other_slot[:, None]], axis=0)

    def update(number, groups, before):
        return absorb(
            info,
            row_slots,
            (0, 1),
            [tokens, other],
            width,
            groups,
            KERNEL_BOUNDS[number],
            before,
            True,
        )

    z3, x2, yz2 = z_back(front), x_swap(z2), y_swap(z2)
    back = piece(1, z2)
    *state, up_a = update(0, [((front, z1, x0, z2), 0)], None)
    there_a = core_swap(up_a)
    z3, x2, yz2, x1, back, state, total, there_a = together(
        z3, x2, yz2, x1, back, state, total, there_a
    )

    zb1, x3, yx1 = z_ring(back), x_swap(z3), y_swap(x1)
    *state, up_b = update(1, [((back, yx0, yz2), 1)], state)
    there_b = core_swap(up_b)
    zb1, x3, yx1, yz2, back, state, there_b = together(
        zb1, x3, yx1, yz2, back, state, there_b
    )

    zb3, xyz2, yx3 = z_back(back), x_swap(yz2), y_swap(x3)
    *state, up_c = update(2, [((x1, z3, x2, x3), 0), ((zb1, yx1), 1)], state)
    zb3, xyz2, yx3, state = together(zb3, xyz2, yx3, state)
    there_c = core_swap(up_c)

    mine, others, up_d = update(3, [((zb3, xyz2, yx3), 1)], state)
    ups = (up_a, there_a, up_b, there_b, up_c, there_c, up_d, core_swap(up_d))
    return finish(info, row_slots, mine, core_swap(others), total, ups)


def solution(mesh):
    placed = (
        P(("groups", "req"), "tp"),
        P(("groups", "req"), None),
        P(),
        P("tp", None),
        P("req", None, "tp"),
        P("req", None, "tp"),
    )
    sizes = mesh.shape
    small = sizes["groups"] == 2 and sizes["req"] == 16 and sizes["tp"] == 1
    return jax.shard_map(
        passed_round if small else gathered,
        mesh=mesh,
        in_specs=placed,
        out_specs=P(("groups", "req"), "tp"),
        check_vma=False,
    )
```

```python
import functools

import jax
import jax.numpy as jnp
import numpy as np
from jax import lax
from jax.experimental import pallas as pl
from jax.experimental.pallas import tpu as pltpu
from jax.sharding import PartitionSpec as P

RING = (0, 1, 3, 2)
PLACE_IN_RING = (0, 1, 3, 2)
DEPTH_TILE = 1024
LANES = 128
RANK = 16

PIECES = (
    *((0, 0, 0), (1, 0, 0), (0, 1, 0), (2, 0, 0)),
    *((0, 0, 1), (0, 1, 1), (2, 0, 1)),
    *((1, 1, 0), (3, 0, 0), (2, 1, 0), (3, 1, 0), (1, 0, 1), (1, 1, 1)),
    *((3, 0, 1), (2, 1, 1), (3, 1, 1)),
)
KERNEL_BOUNDS = (0, 4, 7, 13, 16)
QUARTER_CUTS = (0, 512, 1024, 2048)
VMEM_BYTES = 64 * 1024 * 1024 - 512 * 1024


def slots_of_rows(row_adapter_index, adapter_storage_slot):
    catalog = jnp.arange(adapter_storage_slot.shape[0], dtype=jnp.int32)
    return jnp.sum(
        jnp.where(row_adapter_index == catalog[None, :], adapter_storage_slot[None, :], 0),
        axis=1,
        keepdims=True,
    )


def gathered(
    tokens,
    row_adapter_index,
    adapter_storage_slot,
    base_value_weight,
    adapter_down_weight,
    adapter_up_weight,
):
    adapter_count = adapter_storage_slot.shape[0]
    rank = adapter_down_weight.shape[1]
    slot_of = slots_of_rows(row_adapter_index, adapter_storage_slot)
    down_all = lax.all_gather(
        adapter_down_weight.reshape(-1, adapter_down_weight.shape[2]), "req", axis=0, tiled=True
    )
    up_all = lax.all_gather(
        adapter_up_weight.reshape(-1, adapter_up_weight.shape[2]), "req", axis=0, tiled=True
    )
    base_partial = jnp.dot(tokens, base_value_weight, preferred_element_type=jnp.float32)
    base_output = lax.psum_scatter(base_partial, "tp", scatter_dimension=1, tiled=True)
    shrink = lax.dot_general(
        tokens, down_all, (((1,), (1,)), ((), ())), preferred_element_type=jnp.float32
    )
    column_slot = jnp.arange(adapter_count * rank, dtype=jnp.int32) // rank
    shrink = jnp.where(slot_of == column_slot[None, :], shrink, 0.0)
    shrink = lax.psum(shrink, "tp")
    high = lax.reduce_precision(shrink, 8, 7)
    rest = shrink - high
    middle = lax.reduce_precision(rest, 8, 7)
    low = rest - middle
    lora = sum(
        jnp.dot(piece.astype(jnp.bfloat16), up_all, preferred_element_type=jnp.float32)
        for piece in (low, middle, high)
    )
    return (base_output + lora).astype(jnp.bfloat16)


def params():
    return pltpu.CompilerParams(vmem_limit_bytes=VMEM_BYTES)


def started(copies):
    for copy in copies:
        copy.start()


def awaited(copies):
    for copy in copies:
        copy.wait()


def assemble_kernel(back, info_ref, here_ref, there_ref, up_ref, out_ref, down_ref, own_ref, sems):
    y, core = info_ref[0], info_ref[1]
    place = 1 - y if back else y
    held, rank, quarter = down_ref.shape
    held //= 2
    columns = pl.ds(pl.multiple_of((2 * core + place) * quarter, quarter), quarter)
    copies = [
        pltpu.make_async_copy(
            source.at[:, :, columns], down_ref.at[pl.ds(of_core * held, held)], sems.at[n]
        )
        for n, (source, of_core) in enumerate(((here_ref, core), (there_ref, 1 - core)))
    ]
    copies.append(
        pltpu.make_async_copy(up_ref.at[pl.ds(place * (held // 2), held // 2)], own_ref, sems.at[2])
    )
    started(copies)
    awaited(copies)
    up = own_ref[...].reshape(held // 2 * rank, -1)
    rows = up.shape[0]
    for n in range(up.shape[1] // LANES):
        first = quarter + n * rows
        out_ref[first : first + rows] = up[:, n * LANES : (n + 1) * LANES]
    for n in range(0, quarter, LANES):
        block = down_ref[:, :, n : n + LANES].reshape(2 * held * rank, LANES)
        out_ref[n : n + LANES] = block.T


def assemble(back, info, here, there, up):
    held, rank, depth = here.shape
    width = up.shape[2]
    rows = depth // 4 + held // 2 * rank * width // LANES
    anywhere = pl.BlockSpec(memory_space=pl.ANY)
    return pl.pallas_call(
        functools.partial(assemble_kernel, back),
        out_shape=jax.ShapeDtypeStruct((rows, LANES), here.dtype),
        in_specs=[pl.BlockSpec(memory_space=pltpu.SMEM)] + [anywhere] * 3,
        out_specs=pl.BlockSpec(memory_space=pltpu.VMEM),
        scratch_shapes=[
            pltpu.VMEM((2 * held, rank, depth // 4), here.dtype),
            pltpu.VMEM((held // 2, rank, width), up.dtype),
            pltpu.SemaphoreType.DMA((3,)),
        ],
        compiler_params=params(),
    )(info, here, there, up)


def base_kernel(steps, tokens_ref, weight_ref, *refs):
    step = pl.program_id(0)
    more = len(refs) > 1
    out_ref = refs[1] if more else refs[0]
    copies = [pltpu.make_async_copy(refs[0], refs[2], refs[3].at[0])] if more else []
    part = jnp.dot(tokens_ref[...], weight_ref[...], preferred_element_type=jnp.float32)

    @pl.when(step == 0)
    def _():
        started(copies)
        out_ref[...] = part

    @pl.when(step > 0)
    def _():
        out_ref[...] += part

    if more:

        @pl.when(step == steps - 1)
        def _():
            awaited(copies)
            out_ref[...] += refs[2][...]


def base_part(tokens, weight, begin, end, total=None):
    rows, depth = tokens.shape
    width = weight.shape[1]
    steps, first = (end - begin) // DEPTH_TILE, begin // DEPTH_TILE
    result = jax.ShapeDtypeStruct((rows, width), jnp.float32)
    more = total is not None
    return pl.pallas_call(
        functools.partial(base_kernel, steps),
        out_shape=result,
        grid=(steps,),
        in_specs=[
            pl.BlockSpec((rows, DEPTH_TILE), lambda k: (0, first + k)),
            pl.BlockSpec((DEPTH_TILE, width), lambda k: (first + k, 0)),
        ]
        + [pl.BlockSpec(memory_space=pl.ANY)] * more,
        out_specs=pl.BlockSpec((rows, width), lambda k: (0, 0)),
        scratch_shapes=[pltpu.VMEM((rows, width), jnp.float32), pltpu.SemaphoreType.DMA((1,))]
        if more
        else [],
        cost_estimate=pl.CostEstimate(
            flops=2 * rows * width * (end - begin),
            bytes_accessed=2 * (rows + width) * (end - begin) + 4 * rows * width,
            transcendentals=0,
        ),
        compiler_params=params(),
    )(tokens, weight, *([total] if more else []))


def absorb_kernel(groups, start, sides, more, has_up, info_ref, row_slot_ref, *refs):
    count = sum(size for size, _ in groups)
    token_refs, sources, refs = refs[: len(sides)], refs[len(sides) :][:count], refs[len(sides) + count :]
    before, refs = refs[: len(sides) * more], refs[len(sides) * more :]
    outs, refs = refs[: len(sides)], refs[len(sides) :]
    up_ref, refs = (refs[0], refs[1:]) if has_up else (None, refs)
    rows_ref, row_slot, held_refs, refs = refs[0], refs[1], refs[2 : 2 + len(before)], refs[2 + len(before) :]
    down_refs, sems = refs[:-1], refs[-1]
    rows = token_refs[0].shape[0]
    quarter = rows_ref.shape[2]
    y, core = info_ref[0], info_ref[1]
    cuts = list(zip(QUARTER_CUTS, QUARTER_CUTS[1:]))
    copies, waits = [], {}

    def begin(key, source, target):
        copy = pltpu.make_async_copy(source, target, sems.at[len(copies)])
        copies.append(copy)
        waits.setdefault(key, []).append(copy)
        copy.start()

    places = {}
    first = 0
    for n, ((size, back), down_ref) in enumerate(zip(groups, down_refs)):
        load = back not in places
        place = places.setdefault(back, len(places))
        ends = cuts + [(quarter, sources[0].shape[0])] * has_up
        for low, high in ends:
            for i in range(size):
                begin(
                    (n, low),
                    sources[first + i].at[pl.ds(low, high - low)],
                    down_ref.at[pl.ds(low, high - low), pl.ds(i * LANES, LANES)],
                )
            if not load or low == quarter:
                continue
            for i, source in enumerate(token_refs):
                column = (2 * core + (1 - y if back else y)) * quarter + low
                begin(
                    (n, low),
                    source.at[:, pl.ds(pl.multiple_of(column, QUARTER_CUTS[1]), high - low)],
                    rows_ref.at[place, pl.ds(i * rows, rows), pl.ds(low, high - low)],
                )
        first += size
    begin("late", row_slot_ref, row_slot)
    for source, target in zip(before, held_refs):
        begin("late", source, target)
    lane_slot = lax.broadcasted_iota(jnp.int32, (1, LANES), 1) // RANK
    state = None
    first = 0
    for n, ((size, back), down_ref) in enumerate(zip(groups, down_refs)):
        shrink = None
        for low, high in cuts:
            awaited(waits[n, low])
            part = jnp.dot(
                rows_ref[places[back], :, low:high],
                down_ref[low:high],
                preferred_element_type=jnp.float32,
            )
            shrink = part if shrink is None else shrink + part
        if n == 0:
            awaited(waits["late"])
        for i in range(size):
            lanes, which = slice(i * LANES, (i + 1) * LANES), first + i
            chip = info_ref[2 + 2 * len(PIECES) + start + which]
            wanted = lane_slot + chip * (LANES // RANK)
            kept = jnp.where(row_slot[...] == wanted, shrink[:, lanes], 0.0)
            state = kept if state is None else state + kept
        if has_up:
            awaited(waits[n, quarter])
            height = up_ref.shape[0] // count
            for i in range(size):
                lanes, which = slice(i * LANES, (i + 1) * LANES), first + i
                for j in range(up_ref.shape[1] // LANES):
                    top = quarter + j * height
                    up_ref[
                        which * height : (which + 1) * height, j * LANES : (j + 1) * LANES
                    ] = down_ref[top : top + height, lanes]
        first += size
    for i, out_ref in enumerate(outs):
        own = state[i * rows : (i + 1) * rows]
        out_ref[...] = own + held_refs[i][...] if more else own


def absorb(info, row_slots, sides, tokens, width, groups, start, before, has_up):
    rows = tokens[0].shape[0]
    pieces = [piece for group, _ in groups for piece in group]
    sizes = [(len(group), back) for group, back in groups]
    quarter = tokens[0].shape[1] // 4
    height = pieces[0].shape[0]
    anywhere = pl.BlockSpec(memory_space=pl.ANY)
    vmem = pl.BlockSpec(memory_space=pltpu.VMEM)
    more = before is not None
    state = jax.ShapeDtypeStruct((rows, LANES), jnp.float32)
    up_rows = len(pieces) * (height - quarter) * LANES // width
    up = jax.ShapeDtypeStruct((up_rows, width), tokens[0].dtype)
    quarters = len({back for _, back in groups})
    cuts = len(QUARTER_CUTS) - 1
    copies = len(pieces) * (cuts + has_up) + len(sides) * (quarters * cuts + more) + 1
    outs = (state,) * len(sides) + (up,) * has_up
    return pl.pallas_call(
        functools.partial(absorb_kernel, sizes, start, sides, more, has_up),
        out_shape=outs,
        in_specs=[pl.BlockSpec(memory_space=pltpu.SMEM)]
        + [anywhere] * (1 + len(sides) + len(pieces) + len(sides) * more),
        out_specs=(vmem,) * len(outs),
        scratch_shapes=[
            pltpu.VMEM((quarters, len(sides) * rows, quarter), tokens[0].dtype),
            pltpu.VMEM(row_slots.shape, row_slots.dtype),
        ]
        + [pltpu.VMEM((rows, LANES), jnp.float32)] * (len(sides) * more)
        + [pltpu.VMEM((height, size * LANES), tokens[0].dtype) for size, _ in sizes]
        + [pltpu.SemaphoreType.DMA((copies,))],
        cost_estimate=pl.CostEstimate(
            flops=2 * len(sides) * rows * len(pieces) * LANES * quarter,
            bytes_accessed=2 * len(sides) * rows * quarters * quarter
            + 2 * len(pieces) * LANES * height,
            transcendentals=0,
        ),
        compiler_params=params(),
    )(info, row_slots, *tokens, *pieces, *(before or ()))


def finish_kernel(count, info_ref, row_slot_ref, mine_ref, theirs_ref, total_ref, *refs):
    sources, refs = refs[:count], refs[count:]
    out_ref, row_slot, mine, theirs, total, up, sems = refs
    rows = out_ref.shape[0]
    height = up.shape[0] // (len(PIECES) * 2)
    copies = []

    def begin(source, target):
        copies.append(pltpu.make_async_copy(source, target, sems.at[len(copies)]))
        copies[-1].start()

    begin(row_slot_ref.at[pl.ds(0, rows)], row_slot)
    begin(mine_ref, mine)
    begin(theirs_ref, theirs)
    for source in sources:
        for n in range(0, source.shape[0], height):
            first = pl.multiple_of(info_ref[len(copies) - 1], height)
            begin(source.at[pl.ds(n, height)], up.at[pl.ds(first, height)])
    begin(total_ref, total)
    awaited(copies[:3])
    shrink = mine[...] + theirs[...]
    lane_slot = lax.broadcasted_iota(jnp.int32, (1, LANES), 1) // RANK
    high, low = [], []
    for n in range(up.shape[0] // LANES):
        kept = jnp.where(row_slot[...] == lane_slot + n * (LANES // RANK), shrink, 0.0)
        high.append(kept.astype(jnp.bfloat16))
        low.append((kept - high[-1].astype(jnp.float32)).astype(jnp.bfloat16))
    both = jnp.concatenate([jnp.concatenate(part, axis=1) for part in (low, high)], axis=0)
    awaited(copies[3:-1])
    lora = jnp.dot(both, up[...], preferred_element_type=jnp.float32)
    awaited(copies[-1:])
    out_ref[...] = (total[...] + (lora[:rows] + lora[rows:])).astype(out_ref.dtype)


def finish(info, row_slots, mine, theirs, total, ups):
    rows, width = total.shape
    anywhere = pl.BlockSpec(memory_space=pl.ANY)
    up_rows = sum(up.shape[0] for up in ups)
    return pl.pallas_call(
        functools.partial(finish_kernel, len(ups)),
        out_shape=jax.ShapeDtypeStruct((rows, width), jnp.bfloat16),
        in_specs=[pl.BlockSpec(memory_space=pltpu.SMEM)] + [anywhere] * (4 + len(ups)),
        out_specs=pl.BlockSpec(memory_space=pltpu.VMEM),
        scratch_shapes=[
            pltpu.VMEM((rows, 1), jnp.int32),
            pltpu.VMEM((rows, LANES), jnp.float32),
            pltpu.VMEM((rows, LANES), jnp.float32),
            pltpu.VMEM((rows, width), jnp.float32),
            pltpu.VMEM((up_rows, width), ups[0].dtype),
            pltpu.SemaphoreType.DMA((4 + 2 * len(PIECES),)),
        ],
        cost_estimate=pl.CostEstimate(
            flops=4 * rows * width * up_rows,
            bytes_accessed=6 * rows * width + 2 * up_rows * width,
            transcendentals=0,
        ),
        compiler_params=params(),
    )(info, row_slots, mine, theirs, total, *ups)


def passed_round(
    tokens,
    row_adapter_index,
    adapter_storage_slot,
    base_value_weight,
    adapter_down_weight,
    adapter_up_weight,
):
    rows, depth = tokens.shape
    held, rank, _ = adapter_down_weight.shape
    width = adapter_up_weight.shape[2]
    axes = ("groups", "req")
    planes, owners = lax.axis_size("groups"), lax.axis_size("req")
    device = lax.axis_index("groups") * owners + lax.axis_index("req")

    def permuted(array, target):
        pairs = [
            (g * owners + r, target(g, r)) for g in range(planes) for r in range(owners)
        ]
        return lax.ppermute(array, axes, pairs)

    def along_z(r, by):
        return RING[(PLACE_IN_RING[r // 4] + by) % 4] * 4 + r % 4

    z_ring = lambda array: permuted(array, lambda g, r: g * owners + along_z(r, 1))
    z_back = lambda array: permuted(array, lambda g, r: g * owners + along_z(r, -1))
    x_swap = lambda array: permuted(array, lambda g, r: g * owners + (r ^ 2))
    y_swap = lambda array: permuted(array, lambda g, r: (1 - g) * owners + r)
    core_swap = lambda array: permuted(array, lambda g, r: g * owners + (r ^ 1))

    def chip(r, piece):
        return (along_z(r, -piece[0]) ^ (2 * piece[1])) // 2

    kernels = [PIECES[low:high] for low, high in zip(KERNEL_BOUNDS, KERNEL_BOUNDS[1:])]
    info_table = [
        [g, r % 2]
        + [
            chip(r, p) * LANES + core * held * rank + (g ^ p[2]) * (held // 2 * rank)
            for pieces in kernels
            for core in (r % 2, 1 - r % 2)
            for p in pieces
        ]
        + [chip(r, p) for p in PIECES]
        for g in range(planes)
        for r in range(owners)
    ]
    info = lax.dynamic_index_in_dim(
        jnp.array(np.array(info_table, np.int32)), device, 0, keepdims=False
    )

    def together(*values):
        return lax.optimization_barrier(values)

    def after(value, *others):
        return lax.optimization_barrier((value, *others))[0]

    there = core_swap(adapter_down_weight)
    row_slot = slots_of_rows(row_adapter_index, adapter_storage_slot)
    there, info, row_slot, tokens_late = together(there, info, row_slot, tokens)

    def piece(back, *others):
        return assemble(
            back, after(info, *others), adapter_down_weight, there, adapter_up_weight
        )

    front = piece(0)
    cuts = (0, 5 * DEPTH_TILE, depth)

    def base(number, before, *others):
        low, high = cuts[number : number + 2]
        return base_part(after(tokens, *others), base_value_weight, low, high, before)

    z1, x0 = z_ring(front), x_swap(front)
    other = core_swap(tokens_late)
    other_slot = core_swap(row_slot[:, 0])
    total = base(0, None, front)
    row_slots = jnp.concatenate([row_slot, other_slot[:, None]], axis=0)
    z1, x0, front, total, row_slots = together(z1, x0, front, total, row_slots)

    z2, x1, yx0 = z_ring(z1), x_swap(z1), y_swap(x0)
    total = base(1, total, total)
    z2, x1, yx0, front, other, total, info = together(z2, x1, yx0, front, other, total, info)

    def update(number, groups, before):
        return absorb(
            info,
            row_slots,
            (0, 1),
            [tokens, other],
            width,
            groups,
            KERNEL_BOUNDS[number],
            before,
            True,
        )

    z3, x2, yz2 = z_back(front), x_swap(z2), y_swap(z2)
    back = piece(1, z2)
    *state, up_a = update(0, [((front, z1, x0, z2), 0)], None)
    z3, x2, yz2, x1, back, state, total = together(z3, x2, yz2, x1, back, state, total)
    there_a = core_swap(up_a)

    zb1, x3, yx1 = z_ring(back), x_swap(z3), y_swap(x1)
    *state, up_b = update(1, [((back, yx0, yz2), 1)], state)
    zb1, x3, yx1, yz2, back, state, there_a = together(
        zb1, x3, yx1, yz2, back, state, there_a
    )
    there_b = core_swap(up_b)

    zb3, xyz2, yx3 = z_back(back), x_swap(yz2), y_swap(x3)
    *state, up_c = update(2, [((x1, z3, x2, x3), 0), ((zb1, yx1), 1)], state)
    zb3, xyz2, yx3, state, there_b = together(zb3, xyz2, yx3, state, there_b)
    there_c = core_swap(up_c)

    mine, others, up_d = update(3, [((zb3, xyz2, yx3), 1)], state)
    ups = (up_a, there_a, up_b, there_b, up_c, there_c, up_d, core_swap(up_d))
    return finish(info, row_slots, mine, core_swap(others), total, ups)


def solution(mesh):
    placed = (
        P(("groups", "req"), "tp"),
        P(("groups", "req"), None),
        P(),
        P("tp", None),
        P("req", None, "tp"),
        P("req", None, "tp"),
    )
    sizes = mesh.shape
    small = sizes["groups"] == 2 and sizes["req"] == 16 and sizes["tp"] == 1
    return jax.shard_map(
        passed_round if small else gathered,
        mesh=mesh,
        in_specs=placed,
        out_specs=P(("groups", "req"), "tp"),
        check_vma=False,
    )
```

```python
import functools

import jax
import jax.numpy as jnp
import numpy as np
from jax import lax
from jax.experimental import pallas as pl
from jax.experimental.pallas import tpu as pltpu
from jax.sharding import PartitionSpec as P

RING = (0, 1, 3, 2)
PLACE_IN_RING = (0, 1, 3, 2)
DEPTH_TILE = 1024
LANES = 128
RANK = 16

PIECES = (
    *((0, 0, 0), (1, 0, 0), (0, 1, 0), (2, 0, 0)),
    *((0, 0, 1), (0, 1, 1), (2, 0, 1)),
    *((1, 1, 0), (3, 0, 0), (2, 1, 0), (3, 1, 0), (1, 0, 1), (1, 1, 1)),
    *((3, 0, 1), (2, 1, 1), (3, 1, 1)),
)
KERNEL_BOUNDS = (0, 4, 7, 13, 16)
QUARTER_CUTS = (0, 512, 2048)
VMEM_BYTES = 64 * 1024 * 1024 - 512 * 1024


def slots_of_rows(row_adapter_index, adapter_storage_slot):
    catalog = jnp.arange(adapter_storage_slot.shape[0], dtype=jnp.int32)
    return jnp.sum(
        jnp.where(row_adapter_index == catalog[None, :], adapter_storage_slot[None, :], 0),
        axis=1,
        keepdims=True,
    )


def gathered(
    tokens,
    row_adapter_index,
    adapter_storage_slot,
    base_value_weight,
    adapter_down_weight,
    adapter_up_weight,
):
    adapter_count = adapter_storage_slot.shape[0]
    rank = adapter_down_weight.shape[1]
    slot_of = slots_of_rows(row_adapter_index, adapter_storage_slot)
    down_all = lax.all_gather(
        adapter_down_weight.reshape(-1, adapter_down_weight.shape[2]), "req", axis=0, tiled=True
    )
    up_all = lax.all_gather(
        adapter_up_weight.reshape(-1, adapter_up_weight.shape[2]), "req", axis=0, tiled=True
    )
    base_partial = jnp.dot(tokens, base_value_weight, preferred_element_type=jnp.float32)
    base_output = lax.psum_scatter(base_partial, "tp", scatter_dimension=1, tiled=True)
    shrink = lax.dot_general(
        tokens, down_all, (((1,), (1,)), ((), ())), preferred_element_type=jnp.float32
    )
    column_slot = jnp.arange(adapter_count * rank, dtype=jnp.int32) // rank
    shrink = jnp.where(slot_of == column_slot[None, :], shrink, 0.0)
    shrink = lax.psum(shrink, "tp")
    high = lax.reduce_precision(shrink, 8, 7)
    rest = shrink - high
    middle = lax.reduce_precision(rest, 8, 7)
    low = rest - middle
    lora = sum(
        jnp.dot(piece.astype(jnp.bfloat16), up_all, preferred_element_type=jnp.float32)
        for piece in (low, middle, high)
    )
    return (base_output + lora).astype(jnp.bfloat16)


def params():
    return pltpu.CompilerParams(vmem_limit_bytes=VMEM_BYTES)


def started(copies):
    for copy in copies:
        copy.start()


def awaited(copies):
    for copy in copies:
        copy.wait()


def assemble_kernel(back, info_ref, here_ref, there_ref, up_ref, out_ref, down_ref, own_ref, sems):
    y, core = info_ref[0], info_ref[1]
    place = 1 - y if back else y
    held, rank, quarter = down_ref.shape
    held //= 2
    columns = pl.ds(pl.multiple_of((2 * core + place) * quarter, quarter), quarter)
    copies = [
        pltpu.make_async_copy(
            source.at[:, :, columns], down_ref.at[pl.ds(of_core * held, held)], sems.at[n]
        )
        for n, (source, of_core) in enumerate(((here_ref, core), (there_ref, 1 - core)))
    ]
    copies.append(
        pltpu.make_async_copy(up_ref.at[pl.ds(place * (held // 2), held // 2)], own_ref, sems.at[2])
    )
    started(copies)
    awaited(copies)
    up = own_ref[...].reshape(held // 2 * rank, -1)
    rows = up.shape[0]
    for n in range(up.shape[1] // LANES):
        first = quarter + n * rows
        out_ref[first : first + rows] = up[:, n * LANES : (n + 1) * LANES]
    for n in range(0, quarter, LANES):
        block = down_ref[:, :, n : n + LANES].reshape(2 * held * rank, LANES)
        out_ref[n : n + LANES] = block.T


def assemble(back, info, here, there, up):
    held, rank, depth = here.shape
    width = up.shape[2]
    rows = depth // 4 + held // 2 * rank * width // LANES
    anywhere = pl.BlockSpec(memory_space=pl.ANY)
    return pl.pallas_call(
        functools.partial(assemble_kernel, back),
        out_shape=jax.ShapeDtypeStruct((rows, LANES), here.dtype),
        in_specs=[pl.BlockSpec(memory_space=pltpu.SMEM)] + [anywhere] * 3,
        out_specs=pl.BlockSpec(memory_space=pltpu.VMEM),
        scratch_shapes=[
            pltpu.VMEM((2 * held, rank, depth // 4), here.dtype),
            pltpu.VMEM((held // 2, rank, width), up.dtype),
            pltpu.SemaphoreType.DMA((3,)),
        ],
        compiler_params=params(),
    )(info, here, there, up)


def base_kernel(steps, tokens_ref, weight_ref, *refs):
    step = pl.program_id(0)
    more = len(refs) > 1
    out_ref = refs[1] if more else refs[0]
    copies = [pltpu.make_async_copy(refs[0], refs[2], refs[3].at[0])] if more else []
    part = jnp.dot(tokens_ref[...], weight_ref[...], preferred_element_type=jnp.float32)

    @pl.when(step == 0)
    def _():
        started(copies)
        out_ref[...] = part

    @pl.when(step > 0)
    def _():
        out_ref[...] += part

    if more:

        @pl.when(step == steps - 1)
        def _():
            awaited(copies)
            out_ref[...] += refs[2][...]


def base_part(tokens, weight, begin, end, total=None):
    rows, depth = tokens.shape
    width = weight.shape[1]
    steps, first = (end - begin) // DEPTH_TILE, begin // DEPTH_TILE
    result = jax.ShapeDtypeStruct((rows, width), jnp.float32)
    more = total is not None
    return pl.pallas_call(
        functools.partial(base_kernel, steps),
        out_shape=result,
        grid=(steps,),
        in_specs=[
            pl.BlockSpec((rows, DEPTH_TILE), lambda k: (0, first + k)),
            pl.BlockSpec((DEPTH_TILE, width), lambda k: (first + k, 0)),
        ]
        + [pl.BlockSpec(memory_space=pl.ANY)] * more,
        out_specs=pl.BlockSpec((rows, width), lambda k: (0, 0)),
        scratch_shapes=[pltpu.VMEM((rows, width), jnp.float32), pltpu.SemaphoreType.DMA((1,))]
        if more
        else [],
        cost_estimate=pl.CostEstimate(
            flops=2 * rows * width * (end - begin),
            bytes_accessed=2 * (rows + width) * (end - begin) + 4 * rows * width,
            transcendentals=0,
        ),
        compiler_params=params(),
    )(tokens, weight, *([total] if more else []))


def absorb_kernel(groups, start, sides, more, has_up, info_ref, row_slot_ref, *refs):
    count = sum(size for size, _ in groups)
    token_refs, sources, refs = refs[: len(sides)], refs[len(sides) :][:count], refs[len(sides) + count :]
    before, refs = refs[: len(sides) * more], refs[len(sides) * more :]
    outs, refs = refs[: len(sides)], refs[len(sides) :]
    up_ref, refs = (refs[0], refs[1:]) if has_up else (None, refs)
    rows_ref, row_slot, held_refs, refs = refs[0], refs[1], refs[2 : 2 + len(before)], refs[2 + len(before) :]
    down_refs, sems = refs[:-1], refs[-1]
    rows = token_refs[0].shape[0]
    quarter = rows_ref.shape[2]
    y, core = info_ref[0], info_ref[1]
    cuts = list(zip(QUARTER_CUTS, QUARTER_CUTS[1:]))
    copies, waits = [], {}

    def begin(key, source, target):
        copy = pltpu.make_async_copy(source, target, sems.at[len(copies)])
        copies.append(copy)
        waits.setdefault(key, []).append(copy)
        copy.start()

    places = {}
    first = 0
    for n, ((size, back), down_ref) in enumerate(zip(groups, down_refs)):
        load = back not in places
        place = places.setdefault(back, len(places))
        ends = cuts + [(quarter, sources[0].shape[0])] * has_up
        for low, high in ends:
            for i in range(size):
                begin(
                    (n, low),
                    sources[first + i].at[pl.ds(low, high - low)],
                    down_ref.at[pl.ds(low, high - low), pl.ds(i * LANES, LANES)],
                )
            if not load or low == quarter:
                continue
            for i, source in enumerate(token_refs):
                column = (2 * core + (1 - y if back else y)) * quarter + low
                begin(
                    (n, low),
                    source.at[:, pl.ds(pl.multiple_of(column, QUARTER_CUTS[1]), high - low)],
                    rows_ref.at[place, pl.ds(i * rows, rows), pl.ds(low, high - low)],
                )
        first += size
    begin("late", row_slot_ref, row_slot)
    for source, target in zip(before, held_refs):
        begin("late", source, target)
    lane_slot = lax.broadcasted_iota(jnp.int32, (1, LANES), 1) // RANK
    state = None
    first = 0
    for n, ((size, back), down_ref) in enumerate(zip(groups, down_refs)):
        shrink = None
        for low, high in cuts:
            awaited(waits[n, low])
            part = jnp.dot(
                rows_ref[places[back], :, low:high],
                down_ref[low:high],
                preferred_element_type=jnp.float32,
            )
            shrink = part if shrink is None else shrink + part
        if n == 0:
            awaited(waits["late"])
        for i in range(size):
            lanes, which = slice(i * LANES, (i + 1) * LANES), first + i
            chip = info_ref[2 + 2 * len(PIECES) + start + which]
            wanted = lane_slot + chip * (LANES // RANK)
            kept = jnp.where(row_slot[...] == wanted, shrink[:, lanes], 0.0)
            state = kept if state is None else state + kept
        if has_up:
            awaited(waits[n, quarter])
            height = up_ref.shape[0] // count
            for i in range(size):
                lanes, which = slice(i * LANES, (i + 1) * LANES), first + i
                for j in range(up_ref.shape[1] // LANES):
                    top = quarter + j * height
                    up_ref[
                        which * height : (which + 1) * height, j * LANES : (j + 1) * LANES
                    ] = down_ref[top : top + height, lanes]
        first += size
    for i, out_ref in enumerate(outs):
        own = state[i * rows : (i + 1) * rows]
        out_ref[...] = own + held_refs[i][...] if more else own


def absorb(info, row_slots, sides, tokens, width, groups, start, before, has_up):
    rows = tokens[0].shape[0]
    pieces = [piece for group, _ in groups for piece in group]
    sizes = [(len(group), back) for group, back in groups]
    quarter = tokens[0].shape[1] // 4
    height = pieces[0].shape[0]
    anywhere = pl.BlockSpec(memory_space=pl.ANY)
    vmem = pl.BlockSpec(memory_space=pltpu.VMEM)
    more = before is not None
    state = jax.ShapeDtypeStruct((rows, LANES), jnp.float32)
    up_rows = len(pieces) * (height - quarter) * LANES // width
    up = jax.ShapeDtypeStruct((up_rows, width), tokens[0].dtype)
    quarters = len({back for _, back in groups})
    cuts = len(QUARTER_CUTS) - 1
    copies = len(pieces) * (cuts + has_up) + len(sides) * (quarters * cuts + more) + 1
    outs = (state,) * len(sides) + (up,) * has_up
    return pl.pallas_call(
        functools.partial(absorb_kernel, sizes, start, sides, more, has_up),
        out_shape=outs,
        in_specs=[pl.BlockSpec(memory_space=pltpu.SMEM)]
        + [anywhere] * (1 + len(sides) + len(pieces) + len(sides) * more),
        out_specs=(vmem,) * len(outs),
        scratch_shapes=[
            pltpu.VMEM((quarters, len(sides) * rows, quarter), tokens[0].dtype),
            pltpu.VMEM(row_slots.shape, row_slots.dtype),
        ]
        + [pltpu.VMEM((rows, LANES), jnp.float32)] * (len(sides) * more)
        + [pltpu.VMEM((height, size * LANES), tokens[0].dtype) for size, _ in sizes]
        + [pltpu.SemaphoreType.DMA((copies,))],
        cost_estimate=pl.CostEstimate(
            flops=2 * len(sides) * rows * len(pieces) * LANES * quarter,
            bytes_accessed=2 * len(sides) * rows * quarters * quarter
            + 2 * len(pieces) * LANES * height,
            transcendentals=0,
        ),
        compiler_params=params(),
    )(info, row_slots, *tokens, *pieces, *(before or ()))


def finish_kernel(count, info_ref, row_slot_ref, mine_ref, theirs_ref, total_ref, *refs):
    sources, refs = refs[:count], refs[count:]
    out_ref, row_slot, mine, theirs, total, up, sems = refs
    rows = out_ref.shape[0]
    height = up.shape[0] // (len(PIECES) * 2)
    copies = []

    def begin(source, target):
        copies.append(pltpu.make_async_copy(source, target, sems.at[len(copies)]))
        copies[-1].start()

    begin(row_slot_ref.at[pl.ds(0, rows)], row_slot)
    begin(mine_ref, mine)
    begin(theirs_ref, theirs)
    for source in sources:
        for n in range(0, source.shape[0], height):
            first = pl.multiple_of(info_ref[len(copies) - 1], height)
            begin(source.at[pl.ds(n, height)], up.at[pl.ds(first, height)])
    begin(total_ref, total)
    awaited(copies[:3])
    shrink = mine[...] + theirs[...]
    lane_slot = lax.broadcasted_iota(jnp.int32, (1, LANES), 1) // RANK
    high, low = [], []
    for n in range(up.shape[0] // LANES):
        kept = jnp.where(row_slot[...] == lane_slot + n * (LANES // RANK), shrink, 0.0)
        high.append(kept.astype(jnp.bfloat16))
        low.append((kept - high[-1].astype(jnp.float32)).astype(jnp.bfloat16))
    both = jnp.concatenate([jnp.concatenate(part, axis=1) for part in (low, high)], axis=0)
    awaited(copies[3:-1])
    lora = jnp.dot(both, up[...], preferred_element_type=jnp.float32)
    awaited(copies[-1:])
    out_ref[...] = (total[...] + (lora[:rows] + lora[rows:])).astype(out_ref.dtype)


def finish(info, row_slots, mine, theirs, total, ups):
    rows, width = total.shape
    anywhere = pl.BlockSpec(memory_space=pl.ANY)
    up_rows = sum(up.shape[0] for up in ups)
    return pl.pallas_call(
        functools.partial(finish_kernel, len(ups)),
        out_shape=jax.ShapeDtypeStruct((rows, width), jnp.bfloat16),
        in_specs=[pl.BlockSpec(memory_space=pltpu.SMEM)] + [anywhere] * (4 + len(ups)),
        out_specs=pl.BlockSpec(memory_space=pltpu.VMEM),
        scratch_shapes=[
            pltpu.VMEM((rows, 1), jnp.int32),
            pltpu.VMEM((rows, LANES), jnp.float32),
            pltpu.VMEM((rows, LANES), jnp.float32),
            pltpu.VMEM((rows, width), jnp.float32),
            pltpu.VMEM((up_rows, width), ups[0].dtype),
            pltpu.SemaphoreType.DMA((4 + 2 * len(PIECES),)),
        ],
        cost_estimate=pl.CostEstimate(
            flops=4 * rows * width * up_rows,
            bytes_accessed=6 * rows * width + 2 * up_rows * width,
            transcendentals=0,
        ),
        compiler_params=params(),
    )(info, row_slots, mine, theirs, total, *ups)


def passed_round(
    tokens,
    row_adapter_index,
    adapter_storage_slot,
    base_value_weight,
    adapter_down_weight,
    adapter_up_weight,
):
    rows, depth = tokens.shape
    held, rank, _ = adapter_down_weight.shape
    width = adapter_up_weight.shape[2]
    axes = ("groups", "req")
    planes, owners = lax.axis_size("groups"), lax.axis_size("req")
    device = lax.axis_index("groups") * owners + lax.axis_index("req")

    def permuted(array, target):
        pairs = [
            (g * owners + r, target(g, r)) for g in range(planes) for r in range(owners)
        ]
        return lax.ppermute(array, axes, pairs)

    def along_z(r, by):
        return RING[(PLACE_IN_RING[r // 4] + by) % 4] * 4 + r % 4

    z_ring = lambda array: permuted(array, lambda g, r: g * owners + along_z(r, 1))
    z_back = lambda array: permuted(array, lambda g, r: g * owners + along_z(r, -1))
    x_swap = lambda array: permuted(array, lambda g, r: g * owners + (r ^ 2))
    y_swap = lambda array: permuted(array, lambda g, r: (1 - g) * owners + r)
    core_swap = lambda array: permuted(array, lambda g, r: g * owners + (r ^ 1))

    def chip(r, piece):
        return (along_z(r, -piece[0]) ^ (2 * piece[1])) // 2

    kernels = [PIECES[low:high] for low, high in zip(KERNEL_BOUNDS, KERNEL_BOUNDS[1:])]
    info_table = [
        [g, r % 2]
        + [
            chip(r, p) * LANES + core * held * rank + (g ^ p[2]) * (held // 2 * rank)
            for pieces in kernels
            for core in (r % 2, 1 - r % 2)
            for p in pieces
        ]
        + [chip(r, p) for p in PIECES]
        for g in range(planes)
        for r in range(owners)
    ]
    info = lax.dynamic_index_in_dim(
        jnp.array(np.array(info_table, np.int32)), device, 0, keepdims=False
    )

    def together(*values):
        return lax.optimization_barrier(values)

    def after(value, *others):
        return lax.optimization_barrier((value, *others))[0]

    there = core_swap(adapter_down_weight)
    row_slot = slots_of_rows(row_adapter_index, adapter_storage_slot)
    there, info, row_slot, tokens_late = together(there, info, row_slot, tokens)

    def piece(back, *others):
        return assemble(
            back, after(info, *others), adapter_down_weight, there, adapter_up_weight
        )

    front = piece(0)
    cuts = (0, depth // 2, depth)

    def base(number, before, *others):
        low, high = cuts[number : number + 2]
        return base_part(after(tokens, *others), base_value_weight, low, high, before)

    z1, x0 = z_ring(front), x_swap(front)
    other = core_swap(tokens_late)
    other_slot = core_swap(row_slot[:, 0])
    total = base(0, None, front)
    row_slots = jnp.concatenate([row_slot, other_slot[:, None]], axis=0)
    z1, x0, front, total, row_slots = together(z1, x0, front, total, row_slots)

    z2, x1, yx0 = z_ring(z1), x_swap(z1), y_swap(x0)
    total = base(1, total, total)
    z2, x1, yx0, front, other, total, info = together(z2, x1, yx0, front, other, total, info)

    def update(number, groups, before):
        return absorb(
            info,
            row_slots,
            (0, 1),
            [tokens, other],
            width,
            groups,
            KERNEL_BOUNDS[number],
            before,
            True,
        )

    z3, x2, yz2 = z_back(front), x_swap(z2), y_swap(z2)
    back = piece(1, z2)
    *state, up_a = update(0, [((front, z1, x0, z2), 0)], None)
    z3, x2, yz2, x1, back, state, total = together(z3, x2, yz2, x1, back, state, total)
    there_a = core_swap(up_a)

    zb1, x3, yx1 = z_ring(back), x_swap(z3), y_swap(x1)
    *state, up_b = update(1, [((back, yx0, yz2), 1)], state)
    zb1, x3, yx1, yz2, back, state, there_a = together(
        zb1, x3, yx1, yz2, back, state, there_a
    )
    there_b = core_swap(up_b)

    zb3, xyz2, yx3 = z_back(back), x_swap(yz2), y_swap(x3)
    *state, up_c = update(2, [((x1, z3, x2, x3), 0), ((zb1, yx1), 1)], state)
    zb3, xyz2, yx3, state, there_b = together(zb3, xyz2, yx3, state, there_b)
    there_c = core_swap(up_c)

    mine, others, up_d = update(3, [((zb3, xyz2, yx3), 1)], state)
    ups = (up_a, there_a, up_b, there_b, up_c, there_c, up_d, core_swap(up_d))
    return finish(info, row_slots, mine, core_swap(others), total, ups)


def solution(mesh):
    placed = (
        P(("groups", "req"), "tp"),
        P(("groups", "req"), None),
        P(),
        P("tp", None),
        P("req", None, "tp"),
        P("req", None, "tp"),
    )
    sizes = mesh.shape
    small = sizes["groups"] == 2 and sizes["req"] == 16 and sizes["tp"] == 1
    return jax.shard_map(
        passed_round if small else gathered,
        mesh=mesh,
        in_specs=placed,
        out_specs=P(("groups", "req"), "tp"),
        check_vma=False,
    )
```
